32 devices in a mesh: grp: 2 (over y), seq: 4 (over z), tp: 4 (over x, core).
Axes of the slice: x: 2, y: 2, z: 4, core: 2. Of those that a mesh axis runs over, the one named last changes fastest.
Arguments:
- ssm_input: bfloat16 [2048, 8192], P(('grp', 'seq'), 'tp'), parts along dimension 0, may hold values from -6 to 6
- bmat: bfloat16 [2048, 1024], P(('grp', 'seq'), 'tp'), parts along dimension 0, may hold values from -6 to 6
- cmat: bfloat16 [2048, 1024], P(('grp', 'seq'), 'tp'), parts along dimension 0, may hold values from -6 to 6
- dt_raw: bfloat16 [2048, 128], P(('grp', 'seq'), 'tp'), parts along dimension 0
- a_log: float32 [128], P('tp'), may hold values from -0.5 to 0.5
- d_skip: float32 [128], P('tp'), may hold values from 0.5 to 1.5
- prompt_len: int32 [16], P('grp'), parts along dimension 0, may hold values from 1 to 1024, as said below
- owner: int32 [16], P('grp'), parts along dimension 0, may hold values from 0 to 3, as said below
- dec_x: bfloat16 [8, 4, 4, 8192], P(('grp', 'seq'), None, None, 'tp'), parts along dimension 0, may hold values from -6 to 6
- dec_b: bfloat16 [8, 4, 4, 1024], P(('grp', 'seq'), None, None, 'tp'), parts along dimension 0, may hold values from -6 to 6
- dec_c: bfloat16 [8, 4, 4, 1024], P(('grp', 'seq'), None, None, 'tp'), parts along dimension 0, may hold values from -6 to 6
- dec_dt: bfloat16 [8, 4, 4, 128], P(('grp', 'seq'), None, None, 'tp'), parts along dimension 0
Outputs:
- prefill_out: bfloat16 [2048, 8192], P(('grp', 'seq'), 'tp'), parts along dimension 0
- decode_out: bfloat16 [8, 4, 4, 8192], P(('grp', 'seq'), None, None, 'tp'), parts along dimension 0
The draws below stay inside these ranges and needn't reach their ends.
There are 2 independent parts, one for each index of `grp`. The reference program is written for one: setup_inputs(seed, part) draws one part's arguments, and reference() takes and returns one part's arrays. A program takes and returns all parts, laid end to end along the dimension named above; an argument that names none is the same for every part. Nothing has to cross between parts.
Inputs may be any that keep to these rules, and one draw needn't show every extreme that they name: `prompt_len`: no two requests have both the same owner and the same 256-position part of the prompt holding their last prompt position. Each owner decodes at most 4 requests and each part holds the last position of at most 4; some owner and some part reach that in every draw. `owner`: every index of seq owns at least one request.
All inputs are finite; a program needn't handle non-finite values.
Results may differ from the reference program's by a relative error of at most 0.0055.
Values may be sent and summed in bfloat16 or wider, within the bound.
No kernel may reach another device: no remote copies, remote signals or barrier semaphores. Data moves between devices by JAX's collectives and lax.ppermute only.
A program may use at most 128 MiB of HBM per device.

```python
import jax
import jax.numpy as jnp
from jax import lax

H = 128
P_SIZE = 64
N = 128
G = 8
SPAN = 128
STEPS = 4
SLICE_LENGTH = 256
INPUT_LENGTH = 1024
REQUEST_COUNT = 8
N_SEQ = 4


def head_levels(key, share_slow):
    kind_key = jax.random.fold_in(key, 101)
    level_key = jax.random.fold_in(key, 102)
    slow = jax.random.uniform(kind_key, (H,)) < share_slow
    spread = jax.random.uniform(level_key, (H,))
    slow_level = jnp.exp(jnp.log(0.1) + spread * (jnp.log(0.6) - jnp.log(0.1))) / SLICE_LENGTH
    fast_level = jnp.exp(jnp.log(1.0 / 50.0) + spread * (jnp.log(1.0 / 30.0) - jnp.log(1.0 / 50.0)))
    return jnp.where(slow, slow_level, fast_level)


def draw_dt_raw(key, part):
    share_slow = 0.5
    levels = head_levels(key, share_slow)
    block_key = jax.random.fold_in(key, 103)
    rough_key = jax.random.fold_in(key, 104)
    main_random_seed = jax.random.fold_in(key, 105)
    auxiliary_random_seed = jax.random.fold_in(key, 106)
    strength_key = jax.random.fold_in(key, 107)
    block_count = INPUT_LENGTH // SLICE_LENGTH
    factor = jnp.exp(jax.random.uniform(block_key, (block_count, H), minval=jnp.log(0.5), maxval=jnp.log(2.0)))
    factor = jnp.repeat(factor, SLICE_LENGTH, axis=0)
    noise = jax.random.truncated_normal(rough_key, -2.5, 2.5, (INPUT_LENGTH, H))
    destination_device = levels[None, :] * factor * jnp.exp(0.5 * noise)
    front_stretch = jax.random.randint(main_random_seed, (), 0, SLICE_LENGTH)
    closing_stretch = jax.random.randint(auxiliary_random_seed, (), SLICE_LENGTH, INPUT_LENGTH)
    assignment_table = jnp.arange(INPUT_LENGTH)
    input_stretch = (assignment_table == front_stretch) | (assignment_table == closing_stretch)
    magnitude_level = jax.random.uniform(strength_key, (INPUT_LENGTH, H), minval=0.2, maxval=0.5)
    destination_device = jnp.where(input_stretch[:, None], magnitude_level, destination_device)
    return jnp.log(jnp.expm1(destination_device)).astype(jnp.bfloat16)


def draw_dec_dt(key, part):
    share_slow = 0.5
    levels = head_levels(key, share_slow)
    rough_key = jax.random.fold_in(key, 108)
    noise = jax.random.truncated_normal(rough_key, -2.5, 2.5, (N_SEQ, N_SEQ, STEPS, H))
    destination_device = levels * jnp.exp(0.5 * noise)
    return jnp.log(jnp.expm1(destination_device)).astype(jnp.bfloat16)


def request_table(key):
    count = N_SEQ
    pairs = count * count
    owner_key = jax.random.fold_in(key, 201)
    source_key = jax.random.fold_in(key, 202)
    score_key = jax.random.fold_in(key, 203)
    offset_key = jax.random.fold_in(key, 204)
    complete_owner = jax.random.randint(owner_key, (), 0, count)
    complete_source = jax.random.randint(source_key, (), 0, count)
    numbers = jnp.arange(pairs, dtype=jnp.int32)
    row_lookup = numbers // count
    column_lookup = numbers % count
    score_values = jax.random.randint(score_key, (pairs,), 0, 2 ** 30 // pairs) * pairs + numbers
    extra_score = jnp.where((row_lookup == complete_owner) | (column_lookup == complete_source), 2 ** 30, 0)
    sorted_ranking, picked_heads = lax.top_k(score_values + extra_score, REQUEST_COUNT)
    owners = picked_heads // count
    sources = picked_heads % count
    offsets = jax.random.randint(offset_key, (REQUEST_COUNT,), 1, SLICE_LENGTH + 1)
    lengths = sources * SLICE_LENGTH + offsets
    return (owners.astype(jnp.int32), lengths.astype(jnp.int32))


def draw_prompt_len(key, part):
    return request_table(key)[1]


def draw_owner(key, part):
    return request_table(key)[0]


def shard_levels(stream_key, shape, split, low, largest):
    factor_of = 1.0
    for position, blocks in split:
        draws = jax.random.uniform(jax.random.fold_in(jax.random.fold_in(stream_key, 6), position), (blocks,), jnp.float32, low / len(split), largest / len(split))
        factor_of = factor_of * jnp.repeat(jnp.exp(draws), shape[position] // blocks).reshape((-1,) + (1,) * (len(shape) - 1 - position))
    return factor_of


def bell_draw(rng, extent, scale, most, shards=(), held_as=jnp.bfloat16):
    result = scale * jax.random.normal(rng, extent, jnp.float32)
    if shards:
        result = result * shard_levels(rng, extent, shards, -0.22, 0.18)
    return jnp.clip(result, -most, most).astype(held_as)


def setup_inputs(seed: int = 0, part: int = 0) -> dict:
    key_list = jax.random.split(jax.random.key(seed), 13)
    part_keys = jax.random.split(jax.random.fold_in(key_list[12], part), 13)
    return {
        "ssm_input": bell_draw(part_keys[0], (INPUT_LENGTH, H * P_SIZE), 1.0, 6.0, ((0, 4), (1, 4))),
        "bmat": bell_draw(part_keys[1], (INPUT_LENGTH, G * N), 1.0, 6.0, ((0, 4), (1, 4))),
        "cmat": bell_draw(part_keys[2], (INPUT_LENGTH, G * N), 1.0, 6.0, ((0, 4), (1, 4))),
        "dt_raw": draw_dt_raw(jax.random.fold_in(jax.random.fold_in(key_list[12], part), 71), part),
        "a_log": jnp.clip(jax.random.uniform(key_list[4], (H,), jnp.float32, -0.5, 0.5) * shard_levels(key_list[4], (H,), ((0, 4),), -0.4, 0.0), -0.5, 0.5),
        "d_skip": jnp.clip(0.5 + 1.0 * jax.random.uniform(key_list[5], (H,), jnp.float32) ** shard_levels(key_list[5], (H,), ((0, 4),), -0.2, 0.2), 0.5, 1.5),
        "prompt_len": draw_prompt_len(jax.random.fold_in(jax.random.fold_in(key_list[12], part), 71), part),
        "owner": draw_owner(jax.random.fold_in(jax.random.fold_in(key_list[12], part), 71), part),
        "dec_x": bell_draw(part_keys[8], (N_SEQ, N_SEQ, STEPS, H * P_SIZE), 1.0, 6.0, ((0, 4), (3, 4))),
        "dec_b": bell_draw(part_keys[9], (N_SEQ, N_SEQ, STEPS, G * N), 1.0, 6.0, ((0, 4), (3, 4))),
        "dec_c": bell_draw(part_keys[10], (N_SEQ, N_SEQ, STEPS, G * N), 1.0, 6.0, ((0, 4), (3, 4))),
        "dec_dt": draw_dec_dt(jax.random.fold_in(jax.random.fold_in(key_list[12], part), 71), part),
    }


def reference(ssm_input, bmat, cmat, dt_raw, a_log, d_skip, prompt_len, owner, dec_x, dec_b, dec_c, dec_dt):
    highest = lax.Precision.HIGHEST
    span_count = INPUT_LENGTH // SPAN
    per_group = H // G
    step_size = jax.nn.softplus(dt_raw.astype(jnp.float32))
    log_decay = -jnp.exp(a_log)[None, :] * step_size
    cumulative = jnp.cumsum(log_decay.reshape(span_count, SPAN, H), axis=1)
    step_spans = step_size.reshape(span_count, SPAN, H)
    x_spans = ssm_input.reshape(span_count, SPAN, H, P_SIZE)
    b_spans = bmat.reshape(span_count, SPAN, G, N)
    c_spans = cmat.reshape(span_count, SPAN, G, N)
    causal = jnp.arange(SPAN)[:, None] >= jnp.arange(SPAN)[None, :]

    def span_pass(state, items):
        x_part, b_part, c_part, cum_part, step_part = items
        score_values = jnp.einsum('tgn,sgn->gts', c_part.astype(jnp.float32), b_part.astype(jnp.float32), precision=highest)
        head_scores = jnp.repeat(score_values, per_group, axis=0)
        spread = cum_part.T[:, :, None] - cum_part.T[:, None, :]
        decay = jnp.where(causal[None], jnp.exp(jnp.where(causal[None], spread, 0.0)), 0.0)
        weights = (head_scores * decay * step_part.T[:, None, :]).astype(jnp.bfloat16)
        inner = jnp.einsum('hts,shp->thp', weights.astype(jnp.float32), x_part.astype(jnp.float32), precision=highest)
        b_heads = jnp.repeat(b_part, per_group, axis=1).astype(jnp.float32)
        scaled = (b_heads * (jnp.exp(cum_part[-1][None, :] - cum_part) * step_part)[:, :, None]).astype(jnp.bfloat16)
        span_state = jnp.einsum('shp,shn->hpn', x_part.astype(jnp.float32), scaled.astype(jnp.float32), precision=highest)
        carried = jnp.einsum('tgn,gjpn->tgjp', c_part.astype(jnp.float32), state.reshape(G, per_group, P_SIZE, N), precision=highest).reshape(SPAN, H, P_SIZE)
        outer = jnp.exp(cum_part)[:, :, None] * carried
        output = (inner + outer + d_skip[None, :, None] * x_part.astype(jnp.float32)).astype(jnp.bfloat16)
        following = jnp.exp(cum_part[-1])[:, None, None] * state + span_state
        return following, (output, state)

    initial = jnp.zeros((H, P_SIZE, N), jnp.float32)
    ending, (outputs, starts) = lax.scan(span_pass, initial, (x_spans, b_spans, c_spans, cumulative, step_spans))
    prefill_out = outputs.reshape(INPUT_LENGTH, H * P_SIZE)
    rate_scale = jnp.exp(a_log)
    positions = jnp.arange(SPAN)

    def request_pass(request):
        last_token = (prompt_len[request] - 1).astype(jnp.int32)
        span_index = (last_token // SPAN).astype(jnp.int32)
        offset = (last_token % SPAN).astype(jnp.int32)
        x_part = lax.dynamic_index_in_dim(x_spans, span_index, 0, keepdims=False)
        b_part = lax.dynamic_index_in_dim(b_spans, span_index, 0, keepdims=False)
        cum_part = lax.dynamic_index_in_dim(cumulative, span_index, 0, keepdims=False)
        step_part = lax.dynamic_index_in_dim(step_spans, span_index, 0, keepdims=False)
        state = lax.dynamic_index_in_dim(starts, span_index, 0, keepdims=False)
        cum_last = lax.dynamic_index_in_dim(cum_part, offset, 0, keepdims=False)
        upto = positions[:, None] <= offset
        weight = jnp.where(upto, jnp.exp(jnp.where(upto, cum_last[None, :] - cum_part, 0.0)) * step_part, 0.0)
        b_heads = jnp.repeat(b_part, per_group, axis=1).astype(jnp.float32)
        scaled = (b_heads * weight[:, :, None]).astype(jnp.bfloat16)
        local_sum = jnp.einsum('shp,shn->hpn', x_part.astype(jnp.float32), scaled.astype(jnp.float32), precision=highest)
        handed = (jnp.exp(cum_last)[:, None, None] * state + local_sum).astype(jnp.bfloat16)
        source = (last_token // SLICE_LENGTH).astype(jnp.int32)
        holder = owner[request].astype(jnp.int32)
        slot_x = dec_x[holder, source]
        slot_b = dec_b[holder, source]
        slot_c = dec_c[holder, source]
        slot_step = dec_dt[holder, source]
        hidden = handed.astype(jnp.float32)
        rows = []
        for turn in range(STEPS):
            step_now = jax.nn.softplus(slot_step[turn].astype(jnp.float32))
            x_now = slot_x[turn].reshape(H, P_SIZE).astype(jnp.float32)
            b_now = jnp.repeat(slot_b[turn].reshape(G, N), per_group, axis=0).astype(jnp.float32)
            c_now = jnp.repeat(slot_c[turn].reshape(G, N), per_group, axis=0).astype(jnp.float32)
            hidden = jnp.exp(-rate_scale * step_now)[:, None, None] * hidden + (step_now[:, None] * x_now)[:, :, None] * b_now[:, None, :]
            reading = jnp.einsum('hpn,hn->hp', hidden, c_now, precision=highest) + d_skip[:, None] * x_now
            rows.append(reading.reshape(H * P_SIZE))
        return jnp.stack(rows).astype(jnp.bfloat16)

    decoded = lax.map(request_pass, jnp.arange(REQUEST_COUNT, dtype=jnp.int32))
    sources = ((prompt_len - 1) // SLICE_LENGTH).astype(jnp.int32)
    decode_out = jnp.zeros((N_SEQ, N_SEQ, STEPS, H * P_SIZE), jnp.bfloat16).at[owner.astype(jnp.int32), sources].set(decoded)
    return (prefill_out, decode_out)
```

```python
import functools
import math

import jax
import jax.numpy as jnp
from jax import lax
from jax.experimental import pallas as pl
from jax.experimental.pallas import tpu as pltpu
from jax.sharding import PartitionSpec as P

H = 128
P_SIZE = 64
N = 128
G = 8
SPAN = 128
STEPS = 4
LOG2E = math.log2(math.e)
F32 = jnp.float32
BF16 = jnp.bfloat16
VMEM_LIMIT = 32 * 1024 * 1024


def softplus(value):
    small = jnp.exp(-jnp.abs(value))
    series = small * (1.0 - small * (0.5 - small * (1.0 / 3.0 - small * 0.25)))
    return jnp.maximum(value, 0.0) + jnp.where(small < 0.02, series, jnp.log(1.0 + small))


def dot(left, right, left_dim=1, right_dim=0):
    return lax.dot_general(
        left, right, (((left_dim,), (right_dim,)), ((), ())), preferred_element_type=F32
    )


def split(value, pieces):
    result = []
    for _ in range(pieces):
        piece = value.astype(BF16)
        result.append(piece)
        value = value - piece.astype(F32)
    return result


def exact_dot(ones, value, pieces=3, left_dim=1):
    return sum(dot(ones, piece, left_dim) for piece in split(value, pieces))


def spread_matrix(heads, first, width):
    lane = lax.broadcasted_iota(jnp.int32, (heads, width), 1) + first
    head = lax.broadcasted_iota(jnp.int32, (heads, width), 0)
    return jnp.where(lane // P_SIZE == head, 1.0, 0.0).astype(BF16)


def over_lanes(value, first, width, pieces=2):
    return exact_dot_right(value, spread_matrix(value.shape[1], first, width), pieces)


def exact_dot_right(value, ones, pieces):
    return sum(dot(piece, ones) for piece in split(value, pieces))


def state_kernel(
    x_ref, b_ref, dt_ref, a_ref, d_ref,
    total_ref, sent_ref, decay_ref, skip_ref, cum_ref, far_ref, row_ref,
):
    tokens, heads = dt_ref.shape
    spans = tokens // SPAN
    chunks, _, width = total_ref.shape
    step = softplus(dt_ref[...].astype(F32))
    rate = step * (jnp.exp(a_ref[...]) * -LOG2E)
    t_index = lax.broadcasted_iota(jnp.int32, (SPAN, SPAN), 0)
    s_index = lax.broadcasted_iota(jnp.int32, (SPAN, SPAN), 1)
    lower = jnp.where(t_index >= s_index, 1.0, 0.0).astype(BF16)
    cums, ends = [], []
    for i in range(spans):
        cum = exact_dot(lower, rate[i * SPAN : (i + 1) * SPAN])
        cums.append(cum)
        ends.append(cum[SPAN - 1 : SPAN, :])
    before = jnp.zeros_like(ends[0])
    for i in range(spans):
        cum_ref[i * SPAN : (i + 1) * SPAN, :] = cums[i]
        far_ref[i * SPAN : (i + 1) * SPAN, :] = cums[i] + before
        before = before + ends[i]
    log_step = jnp.log2(step)
    rows = log_step - jnp.concatenate(cums, axis=0)
    row_ref[...] = rows.T
    after = jnp.zeros_like(ends[0])
    weights = [None] * spans
    for i in reversed(range(spans)):
        after = after + ends[i]
        weights[i] = jnp.exp2(after - cums[i]) * step[i * SPAN : (i + 1) * SPAN]
    weight = jnp.concatenate(weights, axis=0)
    per_group = H // G
    for k in range(chunks):
        first = k * width
        g = first // (per_group * P_SIZE)
        lanes = slice(first, first + width)
        scaled = (x_ref[:, lanes].astype(F32) * over_lanes(weight, first, width)).astype(BF16)
        total = dot(b_ref[:, g * N : (g + 1) * N], scaled, 0, 0)
        total_ref[k] = total
        sent_ref[k] = total.astype(BF16)
        decay_ref[k] = over_lanes(jnp.exp2(after), first, width, 3)
        skip_ref[:, lanes] = over_lanes(d_ref[...], first, width, 3)


def inner_kernel(
    x_ref, b_ref, c_ref, cum_ref, far_ref, row_ref, skip_ref, spot_ref, ask_ref,
    inner_ref, local_ref, gain_ref,
):
    tokens, heads = cum_ref.shape
    spans = tokens // SPAN
    asks = ask_ref.shape[0]
    per_group = H // G
    groups = heads // per_group
    t_index = lax.broadcasted_iota(jnp.int32, (SPAN, SPAN), 0)
    s_index = lax.broadcasted_iota(jnp.int32, (SPAN, SPAN), 1)
    causal = t_index >= s_index
    spot = spot_ref[...]
    position = lax.broadcasted_iota(jnp.int32, (asks, tokens), 1)
    picked = jnp.where(position == spot, 1.0, 0.0).astype(BF16)
    cum = cum_ref[...]
    rows = row_ref[...]
    near_ask = exact_dot(picked, cum)
    far_ask = exact_dot(picked, far_ref[...])
    gain_ref[...] = far_ask
    upto = position <= spot
    ends = [cum[(i + 1) * SPAN - 1 : (i + 1) * SPAN, :] for i in range(spans)]
    ask_columns = []
    for j in range(spans):
        start = sum(ends[:j], jnp.zeros_like(ends[0]))
        later = far_ask - start
        ask_columns.append(jnp.where(spot < (j + 1) * SPAN, near_ask, later))
    row_ends = [rows[:, 0:1] * 0.0]
    lane = lax.broadcasted_iota(jnp.int32, (1, 2 * P_SIZE), 1)
    first_half = lane < P_SIZE
    for g in range(groups):
        b_part = b_ref[:, g * N : (g + 1) * N]
        c_part = c_ref[:, g * N : (g + 1) * N]
        scores = dot(c_part, b_part, 1, 1)
        ask_scores = dot(ask_ref[:, g * N : (g + 1) * N], b_part, 1, 1)
        for pair in range(per_group // 2):
            h0 = g * per_group + 2 * pair
            lanes = slice(h0 * P_SIZE, (h0 + 2) * P_SIZE)
            x_part = x_ref[:, lanes]
            zero = jnp.zeros_like(x_part)
            halves = (jnp.where(first_half, x_part, zero), jnp.where(first_half, zero, x_part))
            weights = [[None, None] for _ in range(spans)]
            for e in range(2):
                h = h0 + e
                row = rows[h : h + 1, :]
                for i in range(spans):
                    column = jnp.broadcast_to(
                        cum[i * SPAN : (i + 1) * SPAN, h : h + 1], (SPAN, SPAN)
                    )
                    parts = []
                    for j in range(i + 1):
                        shift = row[:, j * SPAN : (j + 1) * SPAN]
                        for m in range(j, i):
                            shift = shift + ends[m][:, h : h + 1]
                        score = scores[i * SPAN : (i + 1) * SPAN, j * SPAN : (j + 1) * SPAN]
                        part = score * jnp.exp2(column + shift)
                        if i == j:
                            part = jnp.where(causal, part, 0.0)
                        parts.append(part.astype(BF16))
                    if i == spans - 1:
                        asked = []
                        for j in range(spans):
                            span = slice(j * SPAN, (j + 1) * SPAN)
                            part = ask_scores[:, span] * jnp.exp2(
                                ask_columns[j][:, h : h + 1] + row[:, span]
                            )
                            asked.append(jnp.where(upto[:, span], part, 0.0).astype(BF16))
                        parts = [
                            jnp.concatenate([part, ask], axis=0) for part, ask in zip(parts, asked)
                        ]
                    weights[i][e] = jnp.concatenate(parts, axis=1) if i else parts[0]
            skip = skip_ref[:, lanes]
            for i in range(spans):
                reach = (i + 1) * SPAN
                left = jnp.concatenate(weights[i], axis=1)
                right = jnp.concatenate([half[:reach] for half in halves], axis=0)
                result = dot(left, right)
                mine = slice(i * SPAN, (i + 1) * SPAN)
                inner_ref[mine, lanes] = result[:SPAN] + skip * x_part[mine].astype(F32)
                if i == spans - 1:
                    local_ref[:, lanes] = result[SPAN:]


def outer_kernel(c_ref, ask_ref, far_ref, gain_ref, inner_ref, local_ref, *rest):
    carry_refs, (out_ref, read_ref) = rest[:-2], rest[-2:]
    chunks = len(carry_refs)
    tokens, heads = far_ref.shape
    width = out_ref.shape[1] // chunks
    per_group = H // G
    gain = jnp.exp2(far_ref[...])
    ask_gain = jnp.exp2(gain_ref[...])
    for k in range(chunks):
        first = k * width
        g = first // (per_group * P_SIZE)
        lanes = slice(first, first + width)
        state = carry_refs[k][...]
        carried = dot(c_ref[:, g * N : (g + 1) * N], state)
        out = inner_ref[:, lanes] + over_lanes(gain, first, width) * carried
        out_ref[:, lanes] = out.astype(BF16)
        ask_carried = dot(ask_ref[:, g * N : (g + 1) * N], state)
        read_ref[:, lanes] = local_ref[:, lanes] + over_lanes(ask_gain, first, width) * ask_carried


def fresh_kernel(x_ref, b_ref, c_ref, dt_ref, a_ref, d_ref, fresh_ref, keep_ref):
    rows, heads = dt_ref.shape
    per_group = H // G
    groups = heads // per_group
    width = x_ref.shape[1]
    turn = lax.broadcasted_iota(jnp.int32, (rows, 1), 0) % STEPS
    step = softplus(dt_ref[...].astype(F32))
    rate = step * (jnp.exp(a_ref[...]) * -LOG2E)

    def earlier(value, gap):
        if not gap:
            return value
        moved = jnp.concatenate([jnp.zeros_like(value[:gap]), value[:-gap]], axis=0)
        return jnp.where(turn >= gap, moved, 0.0)

    running = sum(earlier(rate, gap) for gap in range(STEPS))
    keep_ref[...] = over_lanes(jnp.exp2(running), 0, width)
    x_values = x_ref[...].astype(F32)
    b_values = b_ref[...].astype(F32)
    c_values = c_ref[...].astype(F32)
    head = lax.broadcasted_iota(jnp.int32, (rows, heads), 1)
    fresh = over_lanes(d_ref[...], 0, width, 3) * x_values
    since = jnp.zeros_like(rate)
    for gap in range(STEPS):
        if gap:
            since = since + earlier(rate, gap - 1)
        products = c_values * earlier(b_values, gap)
        pair = jnp.zeros((rows, heads), F32)
        for g in range(groups):
            score = jnp.sum(products[:, g * N : (g + 1) * N], axis=1, keepdims=True)
            pair = jnp.where(head // per_group == g, score, pair)
        factor = jnp.where(turn >= gap, jnp.exp2(since) * earlier(step, gap) * pair, 0.0)
        fresh = fresh + over_lanes(factor, 0, width) * earlier(x_values, gap)
    fresh_ref[...] = fresh


def call(kernel, out_shape, flops, moved):
    return pl.pallas_call(
        kernel,
        out_shape=out_shape,
        compiler_params=pltpu.CompilerParams(vmem_limit_bytes=VMEM_LIMIT),
        cost_estimate=pl.CostEstimate(flops=flops, bytes_accessed=moved, transcendentals=0),
    )


def shards(
    ssm_input, bmat, cmat, dt_raw, a_log, d_skip, prompt_len, owner, dec_x, dec_b, dec_c, dec_dt
):
    seq_count = lax.axis_size("seq")
    my_index = lax.axis_index("seq")
    token_count, heads = dt_raw.shape
    groups = heads // (H // G)
    lanes = heads * P_SIZE
    rows = seq_count * STEPS
    chunks = 2 * groups if seq_count <= 4 else groups
    width = lanes // chunks
    shape = jax.ShapeDtypeStruct
    a_row = a_log.reshape(1, heads)
    d_row = d_skip.reshape(1, heads)

    total, sent, decay, skip, cum, far, row = call(
        state_kernel,
        (
            shape((chunks, N, width), F32),
            shape((chunks, N, width), BF16),
            shape((chunks, 1, width), F32),
            shape((1, lanes), F32),
            shape((token_count, heads), F32),
            shape((token_count, heads), F32),
            shape((heads, token_count), F32),
        ),
        2 * token_count * N * lanes,
        4 * token_count * lanes,
    )(ssm_input, bmat, dt_raw, a_row, d_row)

    carry = [None] * chunks
    moving = [sent[k] for k in range(chunks)]
    for hop in range(1, seq_count):
        for k in range(chunks):
            got = lax.ppermute(moving[k], "seq", [(hop - 1, hop)])
            carry[k] = got if hop == 1 else carry[k] + got
            if hop < seq_count - 1:
                moving[k] = (got.astype(F32) * decay[k] + total[k]).astype(BF16)

    asked = lax.all_to_all(dec_c[0], "seq", split_axis=0, concat_axis=0, tiled=True)
    ask = asked.reshape(rows, groups * N)
    last_token = prompt_len - 1
    sources = last_token // token_count
    indices = jnp.arange(seq_count, dtype=jnp.int32)
    mine = (sources == my_index)[None, :] & (owner[None, :] == indices[:, None])
    offsets = jnp.sum(jnp.where(mine, last_token[None, :] - my_index * token_count, 0), axis=1)
    spot = jnp.repeat(offsets, STEPS).reshape(rows, 1).astype(jnp.int32)

    inner, local, gain = call(
        inner_kernel,
        (
            shape((token_count, lanes), F32),
            shape((rows, lanes), F32),
            shape((rows, heads), F32),
        ),
        4 * token_count * token_count * lanes,
        16 * token_count * lanes,
    )(ssm_input, bmat, cmat, cum, far, row, skip, spot, ask)

    fresh, keep = call(
        fresh_kernel,
        (shape((rows, lanes), F32), shape((rows, lanes), F32)),
        64 * rows * lanes,
        16 * rows * lanes,
    )(
        dec_x.reshape(rows, lanes),
        dec_b.reshape(rows, groups * N),
        dec_c.reshape(rows, groups * N),
        dec_dt.reshape(rows, heads),
        a_row,
        d_row,
    )

    prefill, reading = call(
        outer_kernel,
        (shape((token_count, lanes), BF16), shape((rows, lanes), F32)),
        2 * token_count * N * lanes,
        8 * token_count * lanes,
    )(cmat, ask, far, gain, inner, local, *carry)

    back = lax.all_to_all(
        reading.reshape(seq_count, STEPS, lanes), "seq", split_axis=0, concat_axis=0, tiled=True
    )
    held = jnp.any((owner == my_index)[None, :] & (sources[None, :] == indices[:, None]), axis=1)
    decoded = back * keep.reshape(seq_count, STEPS, lanes) + fresh.reshape(seq_count, STEPS, lanes)
    decoded = jnp.where(held[:, None, None], decoded, 0.0).astype(BF16)
    return (prefill, decoded[None])


def solution(mesh):
    placed = (
        P(("grp", "seq"), "tp"),
        P(("grp", "seq"), "tp"),
        P(("grp", "seq"), "tp"),
        P(("grp", "seq"), "tp"),
        P("tp"),
        P("tp"),
        P("grp"),
        P("grp"),
        P(("grp", "seq"), None, None, "tp"),
        P(("grp", "seq"), None, None, "tp"),
        P(("grp", "seq"), None, None, "tp"),
        P(("grp", "seq"), None, None, "tp"),
    )
    return jax.shard_map(
        shards,
        mesh=mesh,
        in_specs=placed,
        out_specs=(P(("grp", "seq"), "tp"), P(("grp", "seq"), None, None, "tp")),
        check_vma=False,
    )
```

```python
import functools
import math

import jax
import jax.numpy as jnp
from jax import lax
from jax.experimental import pallas as pl
from jax.experimental.pallas import tpu as pltpu
from jax.sharding import PartitionSpec as P

H = 128
P_SIZE = 64
N = 128
G = 8
SPAN = 128
STEPS = 4
LOG2E = math.log2(math.e)
F32 = jnp.float32
BF16 = jnp.bfloat16
CHUNKS = 8
LAG = 2
VMEM_LIMIT = 32 * 1024 * 1024


def softplus(value):
    small = jnp.exp(-jnp.abs(value))
    series = small * (1.0 - small * (0.5 - small * (1.0 / 3.0 - small * 0.25)))
    return jnp.maximum(value, 0.0) + jnp.where(small < 0.02, series, jnp.log(1.0 + small))


def dot(left, right, left_dim=1, right_dim=0):
    return lax.dot_general(
        left, right, (((left_dim,), (right_dim,)), ((), ())), preferred_element_type=F32
    )


def split(value, pieces):
    result = []
    for _ in range(pieces):
        piece = value.astype(BF16)
        result.append(piece)
        value = value - piece.astype(F32)
    return result


def exact_dot(ones, value, pieces=3, left_dim=1):
    return sum(dot(ones, piece, left_dim) for piece in split(value, pieces))


def spread_matrix(heads, first, width):
    lane = lax.broadcasted_iota(jnp.int32, (heads, width), 1) + first
    head = lax.broadcasted_iota(jnp.int32, (heads, width), 0)
    return jnp.where(lane // P_SIZE == head, 1.0, 0.0).astype(BF16)


def over_lanes(value, first, width, pieces=2):
    return exact_dot_right(value, spread_matrix(value.shape[1], first, width), pieces)


def exact_dot_right(value, ones, pieces):
    return sum(dot(piece, ones) for piece in split(value, pieces))


def shape(dims, dtype=F32):
    return jax.ShapeDtypeStruct(dims, dtype)


def call(kernel, out_shape, flops, moved, **options):
    return pl.pallas_call(
        kernel,
        out_shape=out_shape,
        compiler_params=pltpu.CompilerParams(vmem_limit_bytes=VMEM_LIMIT),
        cost_estimate=pl.CostEstimate(flops=flops, bytes_accessed=moved, transcendentals=0),
        **options,
    )


def triangle(keep):
    row = lax.broadcasted_iota(jnp.int32, (SPAN, SPAN), 0)
    column = lax.broadcasted_iota(jnp.int32, (SPAN, SPAN), 1)
    return jnp.where(keep(row, column), 1.0, 0.0).astype(BF16)


def state_kernel(
    x_hbm, b_hbm, dt_hbm, a_hbm, c_hbm, *rest,
):
    moving_refs = rest[:LAG]
    total_ref, decay_ref, cum_ref, row_ref = rest[LAG : LAG + 4]
    x_ref, b_ref, dt_ref, a_ref, sems = rest[LAG + 4 :]
    heads, tokens = dt_ref.shape
    spans = tokens // SPAN
    chunks, _, width = total_ref.shape
    per_group = H // G
    first_copies = [
        pltpu.make_async_copy(dt_hbm, dt_ref, sems.at[0]),
        pltpu.make_async_copy(a_hbm, a_ref, sems.at[1]),
        pltpu.make_async_copy(b_hbm, b_ref, sems.at[2]),
        pltpu.make_async_copy(c_hbm, moving_refs[0].at[N:, : c_hbm.shape[1]], sems.at[3]),
    ]
    x_copies = []
    for k in range(chunks):
        lanes = slice(k * width, (k + 1) * width)
        x_copies.append(
            pltpu.make_async_copy(x_hbm.at[:, lanes], x_ref.at[:, lanes], sems.at[4 + k])
        )
    for copy in first_copies[:3] + x_copies + first_copies[3:]:
        copy.start()
    upper = triangle(lambda s, t: s <= t)
    eye = lax.broadcasted_iota(jnp.int32, (heads, heads), 0) == lax.broadcasted_iota(
        jnp.int32, (heads, heads), 1
    )
    first_copies[0].wait()
    first_copies[1].wait()
    a_column = jnp.sum(jnp.where(eye, a_ref[...], 0.0), axis=1, keepdims=True)
    step = softplus(dt_ref[...].astype(F32))
    rate = step * (jnp.exp(a_column) * -LOG2E)
    cums = [exact_dot_right(rate[:, i * SPAN : (i + 1) * SPAN], upper, 3) for i in range(spans)]
    ends = [cum[:, SPAN - 1 : SPAN] for cum in cums]
    after = jnp.zeros_like(ends[0])
    weights = [None] * spans
    for i in reversed(range(spans)):
        after = after + ends[i]
        weights[i] = jnp.exp2(after - cums[i]) * step[:, i * SPAN : (i + 1) * SPAN]
    weight = jnp.concatenate(weights, axis=1).T
    whole = jnp.sum(jnp.where(eye, jnp.exp2(after), 0.0), axis=0, keepdims=True)
    first_copies[2].wait()
    turned = [
        b_ref[:, g * N : (g + 1) * N].astype(F32).T.astype(BF16)
        for g in range(heads // per_group)
    ]
    for k in range(chunks):
        first = k * width
        lanes = slice(first, first + width)
        x_copies[k].wait()
        scaled = (x_ref[:, lanes].astype(F32) * over_lanes(weight, first, width)).astype(BF16)
        total = dot(turned[first // (per_group * P_SIZE)], scaled)
        total_ref[k] = total
        if k < LAG:
            moving_refs[k][:N] = total.astype(BF16)
        decay_ref[k] = over_lanes(whole, first, width, 3)
    cum = jnp.concatenate(cums, axis=1)
    cum_ref[...] = cum
    row_ref[...] = jnp.log2(step) - cum
    first_copies[3].wait()


def pass_kernel(step, total_ref, decay_ref, got_ref, *rest):
    (moving_ref, carry_ref) = rest[-2:]
    chunks = total_ref.shape[0]
    me = lax.axis_index("seq")
    wanted = step - LAG * me
    k = jnp.clip(wanted, 0, chunks - 1)
    slot = jnp.where((me > 0) & (wanted == k), k, chunks)
    if len(rest) == 2:
        carry_ref[...] = jnp.zeros_like(carry_ref)
    got = jnp.where(me > 0, got_ref[:N].astype(F32), 0.0)
    moving_ref[:N] = (total_ref[k] + decay_ref[k] * got).astype(BF16)
    carry_ref[slot] = got_ref[:N]
    if moving_ref.shape[0] > N:
        moving_ref[N:] = got_ref[N:]


def inner_kernel(
    g, x_ref, b_ref, c_ref, cum_ref, row_ref, d_ref, spot_ref, own_ref, *rest
):
    ask_refs = rest[:-4]
    inner_ref, local_ref, gain_ref, asked_ref = rest[-4:]
    heads, tokens = cum_ref.shape
    spans = tokens // SPAN
    asks = own_ref.shape[0]
    per_group = H // G
    me = lax.axis_index("seq")
    names = slice(g * N, (g + 1) * N)
    blocks = [own_ref[:, names]] + [ref[N:, names] for ref in ask_refs]
    row_index = lax.broadcasted_iota(jnp.int32, (asks, asks * len(blocks)), 0)
    block_index = lax.broadcasted_iota(jnp.int32, (asks, asks * len(blocks)), 1)
    wanted = (row_index // STEPS) * asks + me * STEPS + row_index % STEPS
    chosen = jnp.where(block_index == wanted, 1.0, 0.0).astype(BF16)
    asked = dot(chosen, jnp.concatenate(blocks, axis=0)).astype(BF16)
    asked_ref[...] = asked
    t_index = lax.broadcasted_iota(jnp.int32, (SPAN, SPAN), 0)
    s_index = lax.broadcasted_iota(jnp.int32, (SPAN, SPAN), 1)
    causal = t_index >= s_index
    spot = spot_ref[...]
    position = lax.broadcasted_iota(jnp.int32, (asks, tokens), 1)
    picked = jnp.where(position == spot, 1.0, 0.0).astype(BF16)
    rows = row_ref[...]
    cum = cum_ref[...].T
    ends = [cum[(i + 1) * SPAN - 1 : (i + 1) * SPAN, :] for i in range(spans)]
    near_ask = exact_dot(picked, cum)
    upto = position <= spot
    starts = [jnp.zeros_like(ends[0])]
    for i in range(spans):
        starts.append(starts[i] + ends[i])
    ask_start = starts[0]
    for i in range(1, spans):
        ask_start = jnp.where(spot >= i * SPAN, starts[i], ask_start)
    gain_ref[...] = near_ask + ask_start
    ask_columns = []
    for j in range(spans):
        column = near_ask
        for i in range(j + 1, spans):
            between = sum(ends[j + 1 : i], ends[j])
            column = jnp.where(spot // SPAN == i, near_ask + between, column)
        ask_columns.append(column)
    first_half = lax.broadcasted_iota(jnp.int32, (1, 2 * P_SIZE), 1) < P_SIZE
    b_part = b_ref[:, names]
    scores = dot(c_ref[:, names], b_part, 1, 1)
    ask_scores = dot(asked, b_part, 1, 1)
    for pair in range(per_group // 2):
        h0 = g * per_group + 2 * pair
        lanes = slice(h0 * P_SIZE, (h0 + 2) * P_SIZE)
        here = slice(2 * pair * P_SIZE, (2 * pair + 2) * P_SIZE)
        x_part = x_ref[:, lanes]
        zero = jnp.zeros_like(x_part)
        halves = (jnp.where(first_half, x_part, zero), jnp.where(first_half, zero, x_part))
        weights = [[None, None] for _ in range(spans)]
        for e in range(2):
            h = h0 + e
            row = rows[h : h + 1, :]
            for i in range(spans):
                column = jnp.broadcast_to(cum[i * SPAN : (i + 1) * SPAN, h : h + 1], (SPAN, SPAN))
                parts = []
                for j in range(i + 1):
                    shift = row[:, j * SPAN : (j + 1) * SPAN]
                    for m in range(j, i):
                        shift = shift + ends[m][:, h : h + 1]
                    score = scores[i * SPAN : (i + 1) * SPAN, j * SPAN : (j + 1) * SPAN]
                    part = score * jnp.exp2(column + shift)
                    if i == j:
                        part = jnp.where(causal, part, 0.0)
                    parts.append(part.astype(BF16))
                if i == spans - 1:
                    for j in range(spans):
                        span = slice(j * SPAN, (j + 1) * SPAN)
                        part = ask_scores[:, span] * jnp.exp2(
                            ask_columns[j][:, h : h + 1] + row[:, span]
                        )
                        part = jnp.where(upto[:, span], part, 0.0).astype(BF16)
                        parts[j] = jnp.concatenate([parts[j], part], axis=0)
                weights[i][e] = jnp.concatenate(parts, axis=1) if i else parts[0]
        skip = jnp.where(first_half, d_ref[:, h0 : h0 + 1], d_ref[:, h0 + 1 : h0 + 2])
        for i in range(spans):
            reach = (i + 1) * SPAN
            left = jnp.concatenate(weights[i], axis=1)
            right = jnp.concatenate([half[:reach] for half in halves], axis=0)
            result = dot(left, right)
            mine = slice(i * SPAN, (i + 1) * SPAN)
            inner_ref[mine, here] = result[:SPAN] + skip * x_part[mine].astype(F32)
            if i == spans - 1:
                local_ref[:, here] = result[SPAN:]


def read_kernel(groups, gain_ref, carry_in_ref, *rest):
    asked_refs, local_refs = rest[:groups], rest[groups : 2 * groups]
    got_refs = rest[2 * groups : 2 * groups + LAG]
    carry_ref, read_refs = rest[2 * groups + LAG], rest[2 * groups + LAG + 1 :]
    chunks, _, width = carry_ref.shape
    chunks = chunks - 1
    count = len(read_refs)
    me = lax.axis_index("seq")
    for i, got_ref in enumerate(got_refs):
        wanted = chunks + LAG * (count - 1) - LAG + i - LAG * me
        k = jnp.clip(wanted, 0, chunks - 1)
        carry_ref[jnp.where((me > 0) & (wanted == k), k, chunks)] = got_ref[:N]
    gain = jnp.exp2(gain_ref[...])
    per_group = H // G
    for k in range(chunks):
        first = k * width
        g = first // (per_group * P_SIZE)
        here = slice(first - g * per_group * P_SIZE, first - g * per_group * P_SIZE + width)
        carried = dot(asked_refs[g][...], carry_ref[k])
        reading = local_refs[g][:, here] + over_lanes(gain, first, width) * carried
        for r in range(count):
            read_refs[r][:, first : first + width] = reading[r * STEPS : (r + 1) * STEPS]


def outer_kernel(groups, c_ref, cum_ref, carry_ref, *rest):
    inner_refs, out_hbm, out_ref, sems = rest[:groups], rest[-3], rest[-2], rest[-1]
    heads, tokens = cum_ref.shape
    spans = tokens // SPAN
    chunks, _, width = carry_ref.shape
    chunks = chunks - 1
    per_group = H // G
    start = jnp.zeros((heads, 1), F32)
    gains = []
    for i in range(spans):
        cum = cum_ref[:, i * SPAN : (i + 1) * SPAN]
        gains.append(jnp.exp2(cum + start))
        start = start + cum[:, SPAN - 1 : SPAN]
    gain = jnp.concatenate(gains, axis=1).T
    copies = []
    for k in range(chunks):
        first = k * width
        g = first // (per_group * P_SIZE)
        lanes = slice(first, first + width)
        here = slice(first - g * per_group * P_SIZE, first - g * per_group * P_SIZE + width)
        carried = dot(c_ref[:, g * N : (g + 1) * N], carry_ref[k])
        out = inner_refs[g][:, here] + over_lanes(gain, first, width) * carried
        out_ref[:, lanes] = out.astype(BF16)
        copies.append(
            pltpu.make_async_copy(out_ref.at[:, lanes], out_hbm.at[:, lanes], sems.at[k])
        )
        copies[k].start()
    for copy in copies:
        copy.wait()


def fresh_kernel(x_ref, b_ref, c_ref, dt_ref, a_ref, d_ref, keep_ref, fresh_ref):
    rows, heads = dt_ref.shape
    per_group = H // G
    groups = heads // per_group
    width = x_ref.shape[1]
    turn = lax.broadcasted_iota(jnp.int32, (rows, 1), 0) % STEPS
    step = softplus(dt_ref[...].astype(F32))
    rate = step * (jnp.exp(a_ref[...]) * -LOG2E)

    def earlier(value, gap):
        if not gap:
            return value
        moved = jnp.concatenate([jnp.zeros_like(value[:gap]), value[:-gap]], axis=0)
        return jnp.where(turn >= gap, moved, 0.0)

    running = sum(earlier(rate, gap) for gap in range(STEPS))
    keep = over_lanes(jnp.exp2(running), 0, width)
    x_values = x_ref[...].astype(F32)
    b_values = b_ref[...].astype(F32)
    c_values = c_ref[...].astype(F32)
    head = lax.broadcasted_iota(jnp.int32, (rows, heads), 1)
    fresh = over_lanes(d_ref[...], 0, width, 3) * x_values
    since = jnp.zeros_like(rate)
    for gap in range(STEPS):
        if gap:
            since = since + earlier(rate, gap - 1)
        products = c_values * earlier(b_values, gap)
        pair = jnp.zeros((rows, heads), F32)
        for g in range(groups):
            score = jnp.sum(products[:, g * N : (g + 1) * N], axis=1, keepdims=True)
            pair = jnp.where(head // per_group == g, score, pair)
        factor = jnp.where(turn >= gap, jnp.exp2(since) * earlier(step, gap) * pair, 0.0)
        fresh = fresh + over_lanes(factor, 0, width) * earlier(x_values, gap)
    for i in range(rows // STEPS):
        keep_ref[i] = keep[i * STEPS : (i + 1) * STEPS]
        fresh_ref[i] = fresh[i * STEPS : (i + 1) * STEPS]


def finish_kernel(held_ref, keep_ref, fresh_ref, *rest):
    back_refs, out_ref = rest[:-1], rest[-1]
    count = len(back_refs)
    me = lax.axis_index("seq")
    for r in range(count):
        source = lax.rem(me + r, count)
        value = back_refs[r][...] * keep_ref[source] + fresh_ref[source]
        out_ref[source] = jnp.where(held_ref[source] > 0, value, 0.0).astype(BF16)


def shards(
    ssm_input, bmat, cmat, dt_raw, a_log, d_skip, prompt_len, owner, dec_x, dec_b, dec_c, dec_dt
):
    count = lax.axis_size("seq")
    me = lax.axis_index("seq")
    tokens, heads = dt_raw.shape
    groups = heads // (H // G)
    names = groups * N
    lanes = heads * P_SIZE
    group_lanes = lanes // groups
    rows = count * STEPS
    width = lanes // CHUNKS
    a_row = a_log.reshape(1, heads)
    d_row = d_skip.reshape(1, heads)
    own = dec_c.reshape(rows, names)
    anywhere = pl.BlockSpec(memory_space=pl.ANY)
    steps = CHUNKS + LAG * (count - 2)

    def carries_asks(s):
        return s % LAG == 0 and s // LAG < count - 1

    def sent_shape(s):
        return shape((N + rows * carries_asks(s), width), BF16)

    *moving, total, decay, cum, row = call(
        state_kernel,
        tuple(sent_shape(s) for s in range(LAG))
        + (
            shape((CHUNKS, N, width)),
            shape((CHUNKS, 1, width)),
            shape((heads, tokens)),
            shape((heads, tokens)),
        ),
        2 * tokens * N * lanes,
        4 * tokens * lanes,
        in_specs=[anywhere] * 5,
        scratch_shapes=[
            pltpu.VMEM((tokens, lanes), BF16),
            pltpu.VMEM((tokens, names), BF16),
            pltpu.VMEM((heads, tokens), BF16),
            pltpu.VMEM((1, heads), F32),
            pltpu.SemaphoreType.DMA((4 + CHUNKS,)),
        ],
    )(ssm_input, bmat, dt_raw.T, a_row, own)

    ring = [(d, (d + 1) % count) for d in range(count)]
    got = []
    carry = None
    for s in range(steps):
        if s >= LAG:
            before = () if carry is None else (carry,)
            sent, carry = call(
                functools.partial(pass_kernel, s),
                (sent_shape(s), shape((CHUNKS + 1, N, width), BF16)),
                2 * N * width,
                8 * N * width,
                input_output_aliases={3: 1} if before else {},
            )(total, decay, got[s - LAG], *before)
            moving.append(sent)
        got.append(lax.ppermute(moving[s], "seq", ring))

    last_token = prompt_len - 1
    sources = last_token // tokens
    indices = jnp.arange(count, dtype=jnp.int32)
    owners = (me - indices) % count
    mine = (sources == me)[None, :] & (owner[None, :] == owners[:, None])
    offsets = jnp.sum(jnp.where(mine, last_token[None, :] - me * tokens, 0), axis=1)
    spot = jnp.repeat(offsets, STEPS).reshape(rows, 1).astype(jnp.int32)
    held = jnp.any((owner == me)[None, :] & (sources[None, :] == indices[:, None]), axis=1)

    ask_blocks = [got[s] for s in range(steps) if carries_asks(s)]
    inner, local, asked = [], [], []
    for g in range(groups):
        inner_g, local_g, gain, asked_g = call(
            functools.partial(inner_kernel, g),
            (
                shape((tokens, group_lanes)),
                shape((rows, group_lanes)),
                shape((rows, heads)),
                shape((rows, N), BF16),
            ),
            4 * tokens * tokens * group_lanes,
            16 * tokens * group_lanes,
        )(ssm_input, bmat, cmat, cum, row, d_row, spot, own, *ask_blocks)
        inner.append(inner_g)
        local.append(local_g)
        asked.append(asked_g)

    keep, fresh = call(
        fresh_kernel,
        (shape((count, STEPS, lanes)), shape((count, STEPS, lanes))),
        64 * rows * lanes,
        16 * rows * lanes,
    )(
        dec_x.reshape(rows, lanes),
        dec_b.reshape(rows, names),
        own,
        dec_dt.reshape(rows, heads),
        a_row,
        d_row,
    )

    carry, *reading = call(
        functools.partial(read_kernel, groups),
        (shape(carry.shape, BF16),) + (shape((STEPS, lanes)),) * count,
        2 * rows * N * lanes,
        4 * N * lanes,
        input_output_aliases={1: 0},
    )(gain, carry, *asked, *local, *got[steps - LAG :])
    back = [reading[0]]
    for r in range(1, count):
        there = [(d, (d - r) % count) for d in range(count)]
        back.append(lax.ppermute(reading[r], "seq", there))

    prefill = call(
        functools.partial(outer_kernel, groups),
        shape((tokens, lanes), BF16),
        2 * tokens * N * lanes,
        8 * tokens * lanes,
        out_specs=anywhere,
        scratch_shapes=[
            pltpu.VMEM((tokens, lanes), BF16),
            pltpu.SemaphoreType.DMA((CHUNKS,)),
        ],
    )(cmat, cum, carry, *inner)

    decoded = call(
        finish_kernel,
        shape((count, STEPS, lanes), BF16),
        4 * rows * lanes,
        16 * rows * lanes,
        in_specs=[pl.BlockSpec(memory_space=pltpu.SMEM)]
        + [pl.BlockSpec(memory_space=pltpu.VMEM)] * (2 + count),
    )(held.astype(jnp.int32), keep, fresh, *back)
    return (prefill, decoded[None])


def solution(mesh):
    placed = (
        P(("grp", "seq"), "tp"),
        P(("grp", "seq"), "tp"),
        P(("grp", "seq"), "tp"),
        P(("grp", "seq"), "tp"),
        P("tp"),
        P("tp"),
        P("grp"),
        P("grp"),
        P(("grp", "seq"), None, None, "tp"),
        P(("grp", "seq"), None, None, "tp"),
        P(("grp", "seq"), None, None, "tp"),
        P(("grp", "seq"), None, None, "tp"),
    )
    return jax.shard_map(
        shards,
        mesh=mesh,
        in_specs=placed,
        out_specs=(P(("grp", "seq"), "tp"), P(("grp", "seq"), None, None, "tp")),
        check_vma=False,
    )
```

```python
import functools
import math

import jax
import jax.numpy as jnp
from jax import lax
from jax.experimental import pallas as pl
from jax.experimental.pallas import tpu as pltpu
from jax.sharding import PartitionSpec as P

H = 128
P_SIZE = 64
N = 128
G = 8
SPAN = 128
STEPS = 4
LOG2E = math.log2(math.e)
F32 = jnp.float32
BF16 = jnp.bfloat16
CHUNKS = 4
VMEM_LIMIT = 32 * 1024 * 1024


def softplus(value):
    small = jnp.exp(-jnp.abs(value))
    series = small * (1.0 - small * (0.5 - small * (1.0 / 3.0 - small * 0.25)))
    return jnp.maximum(value, 0.0) + jnp.where(small < 0.02, series, jnp.log(1.0 + small))


def dot(left, right, left_dim=1, right_dim=0):
    return lax.dot_general(
        left, right, (((left_dim,), (right_dim,)), ((), ())), preferred_element_type=F32
    )


def split(value, pieces):
    result = []
    for _ in range(pieces):
        piece = value.astype(BF16)
        result.append(piece)
        value = value - piece.astype(F32)
    return result


def exact_dot(ones, value, pieces=3, left_dim=1):
    return sum(dot(ones, piece, left_dim) for piece in split(value, pieces))


def spread_matrix(heads, first, width):
    lane = lax.broadcasted_iota(jnp.int32, (heads, width), 1) + first
    head = lax.broadcasted_iota(jnp.int32, (heads, width), 0)
    return jnp.where(lane // P_SIZE == head, 1.0, 0.0).astype(BF16)


def over_lanes(value, first, width, pieces=2):
    return exact_dot_right(value, spread_matrix(value.shape[1], first, width), pieces)


def exact_dot_right(value, ones, pieces):
    return sum(dot(piece, ones) for piece in split(value, pieces))


def shape(dims, dtype=F32):
    return jax.ShapeDtypeStruct(dims, dtype)


def call(kernel, out_shape, flops, moved, **options):
    return pl.pallas_call(
        kernel,
        out_shape=out_shape,
        compiler_params=pltpu.CompilerParams(vmem_limit_bytes=VMEM_LIMIT),
        cost_estimate=pl.CostEstimate(flops=flops, bytes_accessed=moved, transcendentals=0),
        **options,
    )


def triangle(keep):
    row = lax.broadcasted_iota(jnp.int32, (SPAN, SPAN), 0)
    column = lax.broadcasted_iota(jnp.int32, (SPAN, SPAN), 1)
    return jnp.where(keep(row, column), 1.0, 0.0).astype(BF16)


def state_kernel(
    x_hbm, b_hbm, dt_hbm, a_hbm, total_ref, sent_ref, decay_ref, cum_ref, row_ref,
    x_ref, b_ref, dt_ref, a_ref, sems,
):
    heads, tokens = dt_ref.shape
    spans = tokens // SPAN
    chunks, _, width = total_ref.shape
    per_group = H // G
    groups = heads // per_group
    group_lanes = per_group * P_SIZE
    copies = [
        pltpu.make_async_copy(dt_hbm, dt_ref, sems.at[0]),
        pltpu.make_async_copy(a_hbm, a_ref, sems.at[1]),
        pltpu.make_async_copy(b_hbm, b_ref, sems.at[2]),
    ]
    for g in range(groups):
        lanes = slice(g * group_lanes, (g + 1) * group_lanes)
        copies.append(
            pltpu.make_async_copy(x_hbm.at[:, lanes], x_ref.at[:, lanes], sems.at[3 + g])
        )
    for copy in copies:
        copy.start()
    upper = triangle(lambda s, t: s <= t)
    eye = lax.broadcasted_iota(jnp.int32, (heads, heads), 0) == lax.broadcasted_iota(
        jnp.int32, (heads, heads), 1
    )
    copies[0].wait()
    copies[1].wait()
    a_column = jnp.sum(jnp.where(eye, a_ref[...], 0.0), axis=1, keepdims=True)
    step = softplus(dt_ref[...].astype(F32))
    rate = step * (jnp.exp(a_column) * -LOG2E)
    cums = [exact_dot_right(rate[:, i * SPAN : (i + 1) * SPAN], upper, 3) for i in range(spans)]
    ends = [cum[:, SPAN - 1 : SPAN] for cum in cums]
    after = jnp.zeros_like(ends[0])
    weights = [None] * spans
    for i in reversed(range(spans)):
        after = after + ends[i]
        weights[i] = jnp.exp2(after - cums[i]) * step[:, i * SPAN : (i + 1) * SPAN]
    weight = jnp.concatenate(weights, axis=1).T
    whole = jnp.sum(jnp.where(eye, jnp.exp2(after), 0.0), axis=0, keepdims=True)
    cum = jnp.concatenate(cums, axis=1)
    cum_ref[...] = cum
    row_ref[...] = jnp.log2(step) - cum
    copies[2].wait()
    for g in range(groups):
        turned = b_ref[:, g * N : (g + 1) * N].astype(F32).T.astype(BF16)
        copies[3 + g].wait()
        for k in range(chunks):
            first = k * width
            if first // group_lanes != g:
                continue
            lanes = slice(first, first + width)
            scaled = (x_ref[:, lanes].astype(F32) * over_lanes(weight, first, width)).astype(BF16)
            total = dot(turned, scaled)
            total_ref[k] = total
            sent_ref[k] = total.astype(BF16)
            decay_ref[k] = over_lanes(whole, first, width, 3)


def pass_kernel(hop, k, got_ref, total_ref, decay_ref, *rest):
    moving_ref, carry_ref = rest[-2:]
    first = hop == 1 and k == 0
    if first:
        carry_ref[...] = jnp.zeros_like(carry_ref)
    got = got_ref[...]
    moving_ref[...] = (total_ref[...] + decay_ref[...] * got.astype(F32)).astype(BF16)

    @pl.when(lax.axis_index("seq") == hop)
    def _():
        carry_ref[k] = got


def pair_halves(x_part):
    first_half = lax.broadcasted_iota(jnp.int32, (1, 2 * P_SIZE), 1) < P_SIZE
    zero = jnp.zeros_like(x_part)
    return jnp.where(first_half, x_part, zero), jnp.where(first_half, zero, x_part)


def span_starts(cum, spans):
    ends = [cum[(i + 1) * SPAN - 1 : (i + 1) * SPAN, :] for i in range(spans)]
    starts = [jnp.zeros_like(ends[0])]
    for i in range(spans):
        starts.append(starts[i] + ends[i])
    return ends, starts


def inner_kernel(g, x_ref, b_ref, c_ref, cum_ref, row_ref, d_ref, *rest):
    inner_ref = rest[-1]
    heads, tokens = cum_ref.shape
    spans = tokens // SPAN
    per_group = H // G
    names = slice(g * N, (g + 1) * N)
    t_index = lax.broadcasted_iota(jnp.int32, (SPAN, SPAN), 0)
    s_index = lax.broadcasted_iota(jnp.int32, (SPAN, SPAN), 1)
    causal = t_index >= s_index
    rows = row_ref[...]
    cum = cum_ref[...].T
    ends, _ = span_starts(cum, spans)
    first_half = lax.broadcasted_iota(jnp.int32, (1, 2 * P_SIZE), 1) < P_SIZE
    scores = dot(c_ref[:, names], b_ref[:, names], 1, 1)
    for pair in range(per_group // 2):
        h0 = g * per_group + 2 * pair
        lanes = slice(h0 * P_SIZE, (h0 + 2) * P_SIZE)
        here = slice(2 * pair * P_SIZE, (2 * pair + 2) * P_SIZE)
        x_part = x_ref[:, lanes]
        halves = pair_halves(x_part)
        weights = [[None, None] for _ in range(spans)]
        for e in range(2):
            h = h0 + e
            row = rows[h : h + 1, :]
            for i in range(spans):
                column = jnp.broadcast_to(cum[i * SPAN : (i + 1) * SPAN, h : h + 1], (SPAN, SPAN))
                parts = []
                for j in range(i + 1):
                    shift = row[:, j * SPAN : (j + 1) * SPAN]
                    for m in range(j, i):
                        shift = shift + ends[m][:, h : h + 1]
                    score = scores[i * SPAN : (i + 1) * SPAN, j * SPAN : (j + 1) * SPAN]
                    part = score * jnp.exp2(column + shift)
                    if i == j:
                        part = jnp.where(causal, part, 0.0)
                    parts.append(part.astype(BF16))
                weights[i][e] = jnp.concatenate(parts, axis=1) if i else parts[0]
        skip = jnp.where(first_half, d_ref[:, h0 : h0 + 1], d_ref[:, h0 + 1 : h0 + 2])
        for i in range(spans):
            reach = (i + 1) * SPAN
            left = jnp.concatenate(weights[i], axis=1)
            right = jnp.concatenate([half[:reach] for half in halves], axis=0)
            mine = slice(i * SPAN, (i + 1) * SPAN)
            inner_ref[mine, here] = dot(left, right) + skip * x_part[mine].astype(F32)


def ask_kernel(count, x_ref, b_ref, cum_ref, row_ref, spot_ref, *rest):
    ask_refs = rest[:count]
    local_ref, gain_ref, asked_ref = rest[-3:]
    heads, tokens = cum_ref.shape
    spans = tokens // SPAN
    asks = local_ref.shape[0]
    per_group = H // G
    groups = heads // per_group
    me = lax.axis_index("seq")
    asked = jnp.concatenate([ref[me].astype(F32) for ref in ask_refs], axis=0).astype(BF16)
    asked_ref[...] = asked
    spot = spot_ref[...]
    position = lax.broadcasted_iota(jnp.int32, (asks, tokens), 1)
    picked = jnp.where(position == spot, 1.0, 0.0).astype(BF16)
    upto = position <= spot
    rows = row_ref[...]
    cum = cum_ref[...].T
    ends, starts = span_starts(cum, spans)
    near_ask = exact_dot(picked, cum)
    ask_start = starts[0]
    for i in range(1, spans):
        ask_start = jnp.where(spot >= i * SPAN, starts[i], ask_start)
    gain_ref[...] = near_ask + ask_start
    columns = []
    for j in range(spans):
        column = near_ask
        for i in range(j + 1, spans):
            column = jnp.where(spot // SPAN == i, near_ask + sum(ends[j + 1 : i], ends[j]), column)
        columns.append(column)
    for g in range(groups):
        names = slice(g * N, (g + 1) * N)
        scores = jnp.where(upto, dot(asked[:, names], b_ref[:, names], 1, 1), 0.0)
        for pair in range(per_group // 2):
            h0 = g * per_group + 2 * pair
            lanes = slice(h0 * P_SIZE, (h0 + 2) * P_SIZE)
            parts = []
            for h in (h0, h0 + 1):
                for j in range(spans):
                    span = slice(j * SPAN, (j + 1) * SPAN)
                    part = scores[:, span] * jnp.exp2(columns[j][:, h : h + 1] + rows[h : h + 1, span])
                    parts.append(jnp.where(upto[:, span], part, 0.0).astype(BF16))
            right = jnp.concatenate(pair_halves(x_ref[:, lanes]), axis=0)
            local_ref[:, lanes] = dot(jnp.concatenate(parts, axis=1), right)


def read_kernel(chunks, gain_ref, asked_ref, local_ref, carry_ref, *rest):
    got_refs, read_refs = rest[: len(chunks)], rest[len(chunks) :]
    width = got_refs[0].shape[1]
    count = len(read_refs)
    last = lax.axis_index("seq") == count - 1
    gain = jnp.exp2(gain_ref[...])
    for i, k in enumerate(chunks):
        first = k * width
        g = first // (H // G * P_SIZE)
        state = jnp.where(last, got_refs[i][...], carry_ref[k])
        carried = dot(asked_ref[:, g * N : (g + 1) * N], state)
        reading = local_ref[:, first : first + width] + over_lanes(gain, first, width) * carried
        here = slice(i * width, (i + 1) * width)
        for r in range(count):
            read_refs[r][:, here] = reading[r * STEPS : (r + 1) * STEPS]


def outer_kernel(chunks, count, c_ref, cum_ref, carry_ref, *rest):
    got_refs = rest[: len(chunks)]
    inner_refs = rest[len(chunks) : -3]
    out_hbm, out_ref, sems = rest[-3:]
    heads, tokens = cum_ref.shape
    spans = tokens // SPAN
    width = got_refs[0].shape[1]
    group_lanes = H // G * P_SIZE
    last = lax.axis_index("seq") == count - 1
    start = jnp.zeros((heads, 1), F32)
    gains = []
    for i in range(spans):
        cum = cum_ref[:, i * SPAN : (i + 1) * SPAN]
        gains.append(jnp.exp2(cum + start))
        start = start + cum[:, SPAN - 1 : SPAN]
    gain = jnp.concatenate(gains, axis=1).T
    copies = []
    for i, k in enumerate(chunks):
        first = k * width
        g = first // group_lanes
        state = jnp.where(last, got_refs[i][...], carry_ref[k])
        carried = dot(c_ref[:, g * N : (g + 1) * N], state)
        inner = inner_refs[g][:, first - g * group_lanes : first - g * group_lanes + width]
        out_ref[i] = (inner + over_lanes(gain, first, width) * carried).astype(BF16)
        copies.append(
            pltpu.make_async_copy(out_ref.at[i], out_hbm.at[:, first : first + width], sems.at[i])
        )
        copies[i].start()
    for copy in copies:
        copy.wait()


def fresh_kernel(x_ref, b_ref, c_ref, dt_ref, a_ref, d_ref, *rest):
    keep_ref, fresh_ref = rest[-2:]
    count, _, heads = dt_ref.shape
    rows = count * STEPS
    per_group = H // G
    groups = heads // per_group
    width = x_ref.shape[2]

    def flat(ref):
        return jnp.concatenate([ref[i].astype(F32) for i in range(count)], axis=0)

    turn = lax.broadcasted_iota(jnp.int32, (rows, 1), 0) % STEPS
    step = softplus(flat(dt_ref))
    rate = step * (jnp.exp(a_ref[...]) * -LOG2E)

    def earlier(value, gap):
        if not gap:
            return value
        moved = jnp.concatenate([jnp.zeros_like(value[:gap]), value[:-gap]], axis=0)
        return jnp.where(turn >= gap, moved, 0.0)

    running = sum(earlier(rate, gap) for gap in range(STEPS))
    keep = over_lanes(jnp.exp2(running), 0, width)
    x_values = flat(x_ref)
    b_values = flat(b_ref)
    c_values = flat(c_ref)
    head = lax.broadcasted_iota(jnp.int32, (rows, heads), 1)
    fresh = over_lanes(d_ref[...], 0, width, 3) * x_values
    since = jnp.zeros_like(rate)
    for gap in range(STEPS):
        if gap:
            since = since + earlier(rate, gap - 1)
        products = c_values * earlier(b_values, gap)
        pair = jnp.zeros((rows, heads), F32)
        for g in range(groups):
            score = jnp.sum(products[:, g * N : (g + 1) * N], axis=1, keepdims=True)
            pair = jnp.where(head // per_group == g, score, pair)
        factor = jnp.where(turn >= gap, jnp.exp2(since) * earlier(step, gap) * pair, 0.0)
        fresh = fresh + over_lanes(factor, 0, width) * earlier(x_values, gap)
    for i in range(rows // STEPS):
        keep_ref[i] = keep[i * STEPS : (i + 1) * STEPS]
        fresh_ref[i] = fresh[i * STEPS : (i + 1) * STEPS]


def finish_kernel(held_ref, keep_ref, fresh_ref, *rest):
    back_refs, out_ref = rest[:-1], rest[-1]
    count = len(back_refs)
    me = lax.axis_index("seq")
    for r in range(count):
        source = lax.rem(me + r, count)
        value = back_refs[r][...] * keep_ref[source] + fresh_ref[source]
        out_ref[source] = jnp.where(held_ref[source] > 0, value, 0.0).astype(BF16)


def shards(
    ssm_input, bmat, cmat, dt_raw, a_log, d_skip, prompt_len, owner, dec_x, dec_b, dec_c, dec_dt
):
    count = lax.axis_size("seq")
    me = lax.axis_index("seq")
    tokens, heads = dt_raw.shape
    groups = heads // (H // G)
    names = groups * N
    lanes = heads * P_SIZE
    group_lanes = lanes // groups
    rows = count * STEPS
    chunks = CHUNKS if count <= 4 else groups
    width = lanes // chunks
    a_row = a_log.reshape(1, heads)
    d_row = d_skip.reshape(1, heads)
    anywhere = pl.BlockSpec(memory_space=pl.ANY)
    in_hbm = pl.BlockSpec(memory_space=pltpu.HBM)
    in_vmem = pl.BlockSpec(memory_space=pltpu.VMEM)

    total, sent, decay, cum, row = call(
        state_kernel,
        (
            shape((chunks, N, width)),
            shape((chunks, N, width), BF16),
            shape((chunks, 1, width)),
            shape((heads, tokens)),
            shape((heads, tokens)),
        ),
        2 * tokens * N * lanes,
        4 * tokens * lanes,
        in_specs=[in_hbm] * 4,
        scratch_shapes=[
            pltpu.VMEM((tokens, lanes), BF16),
            pltpu.VMEM((tokens, names), BF16),
            pltpu.VMEM((heads, tokens), BF16),
            pltpu.VMEM((1, heads), F32),
            pltpu.SemaphoreType.DMA((3 + groups,)),
        ],
    )(ssm_input, bmat, dt_raw.T, a_row)

    def swap(value, hop):
        pairs = {hop - 1: hop, hop: hop - 1}
        return lax.ppermute(value, "seq", [(d, pairs.get(d, d)) for d in range(count)])

    def shift(value, by):
        return lax.ppermute(value, "seq", [(d, (d + by) % count) for d in range(count)])

    got = {(1, k): swap(sent[k], 1) for k in range(chunks)}
    asks = [dec_c[0]] + [shift(dec_c[0], r) for r in range(1, count)]

    last_token = prompt_len - 1
    sources = last_token // tokens
    indices = jnp.arange(count, dtype=jnp.int32)
    owners = (me - indices) % count
    mine = (sources == me)[None, :] & (owner[None, :] == owners[:, None])
    offsets = jnp.sum(jnp.where(mine, last_token[None, :] - me * tokens, 0), axis=1)
    spot = jnp.repeat(offsets, STEPS).reshape(rows, 1).astype(jnp.int32)
    held = jnp.any((owner == me)[None, :] & (sources[None, :] == indices[:, None]), axis=1)

    def inner_part(g, *after):
        return call(
            functools.partial(inner_kernel, g),
            shape((tokens, group_lanes)),
            2 * tokens * tokens * group_lanes,
            16 * tokens * group_lanes,
            in_specs=[in_vmem] * 6 + [anywhere] * len(after),
        )(ssm_input, bmat, cmat, cum, row, d_row, *after)

    def ask_part(*after):
        return call(
            functools.partial(ask_kernel, count),
            (shape((rows, lanes)), shape((rows, heads)), shape((rows, names), BF16)),
            2 * rows * tokens * lanes,
            4 * tokens * lanes,
            in_specs=[in_vmem] * (5 + count) + [anywhere] * len(after),
        )(ssm_input, bmat, cum, row, spot, *asks, *after)

    def fresh_part(*after):
        return call(
            fresh_kernel,
            (shape((count, STEPS, lanes)), shape((count, STEPS, lanes))),
            64 * rows * lanes,
            16 * rows * lanes,
            in_specs=[in_vmem] * 6 + [anywhere] * len(after),
        )(dec_x[0], dec_b[0], dec_c[0], dec_dt[0], a_row, d_row, *after)

    order = sorted(
        (k + hop, hop, k) for hop in range(1, count - 1) for k in range(chunks)
    )
    work = [functools.partial(inner_part, g) for g in range(groups)] + [ask_part, fresh_part]
    results = [work[0]()]
    carry = None
    tie = None
    for place, (_, hop, k) in enumerate(order):
        if 0 < place < len(work):
            results.append(work[place](tie))
        after = jax.tree.leaves(results[place])[:1] if place < len(results) else []
        held_before = [] if carry is None else [carry]
        moving, carry = call(
            functools.partial(pass_kernel, hop, k),
            (shape((N, width), BF16), shape((chunks, N, width), BF16)),
            2 * N * width,
            8 * N * width,
            in_specs=[in_vmem] * (3 + len(held_before)) + [anywhere] * len(after),
            input_output_aliases={3: 1} if held_before else {},
        )(got[hop, k], total[k], decay[k], *held_before, *after)
        got[hop + 1, k] = swap(moving, hop + 1)
        tie = moving
    *inner, (local, gain, asked), (keep, fresh) = results
    arrived = [got[count - 1, k] for k in range(chunks)]

    all_chunks = tuple(range(chunks))
    reading = call(
        functools.partial(read_kernel, all_chunks),
        (shape((STEPS, lanes)),) * count,
        2 * rows * N * lanes,
        4 * N * lanes,
    )(gain, asked, local, carry, *arrived)
    back = [reading[0]] + [None] * (count - 1)
    for r in reversed(range(1, count)):
        back[r] = shift(reading[r], -r)

    prefill = call(
        functools.partial(outer_kernel, all_chunks, count),
        shape((tokens, lanes), BF16),
        2 * tokens * N * lanes,
        8 * tokens * lanes,
        out_specs=in_hbm,
        scratch_shapes=[
            pltpu.VMEM((chunks, tokens, width), BF16),
            pltpu.SemaphoreType.DMA((chunks,)),
        ],
    )(cmat, cum, carry, *arrived, *inner)

    decoded = call(
        finish_kernel,
        shape((count, STEPS, lanes), BF16),
        4 * rows * lanes,
        16 * rows * lanes,
        in_specs=[pl.BlockSpec(memory_space=pltpu.SMEM)] + [in_vmem] * (2 + count),
    )(held.astype(jnp.int32), keep, fresh, *back)
    return (prefill, decoded[None])


def solution(mesh):
    placed = (
        P(("grp", "seq"), "tp"),
        P(("grp", "seq"), "tp"),
        P(("grp", "seq"), "tp"),
        P(("grp", "seq"), "tp"),
        P("tp"),
        P("tp"),
        P("grp"),
        P("grp"),
        P(("grp", "seq"), None, None, "tp"),
        P(("grp", "seq"), None, None, "tp"),
        P(("grp", "seq"), None, None, "tp"),
        P(("grp", "seq"), None, None, "tp"),
    )
    return jax.shard_map(
        shards,
        mesh=mesh,
        in_specs=placed,
        out_specs=(P(("grp", "seq"), "tp"), P(("grp", "seq"), None, None, "tp")),
        check_vma=False,
    )
```

```python
import functools
import math

import jax
import jax.numpy as jnp
from jax import lax
from jax.experimental import pallas as pl
from jax.experimental.pallas import tpu as pltpu
from jax.sharding import PartitionSpec as P

H = 128
P_SIZE = 64
N = 128
G = 8
SPAN = 128
STEPS = 4
LOG2E = math.log2(math.e)
F32 = jnp.float32
BF16 = jnp.bfloat16
CHUNKS = 4
VMEM_LIMIT = 32 * 1024 * 1024


def softplus(value):
    small = jnp.exp(-jnp.abs(value))
    series = small * (1.0 - small * (0.5 - small * (1.0 / 3.0 - small * 0.25)))
    return jnp.maximum(value, 0.0) + jnp.where(small < 0.02, series, jnp.log(1.0 + small))


def dot(left, right, left_dim=1, right_dim=0):
    return lax.dot_general(
        left, right, (((left_dim,), (right_dim,)), ((), ())), preferred_element_type=F32
    )


def split(value, pieces):
    result = []
    for _ in range(pieces):
        piece = value.astype(BF16)
        result.append(piece)
        value = value - piece.astype(F32)
    return result


def exact_dot(ones, value, pieces=3, left_dim=1):
    return sum(dot(ones, piece, left_dim) for piece in split(value, pieces))


def spread_matrix(heads, first, width):
    lane = lax.broadcasted_iota(jnp.int32, (heads, width), 1) + first
    head = lax.broadcasted_iota(jnp.int32, (heads, width), 0)
    return jnp.where(lane // P_SIZE == head, 1.0, 0.0).astype(BF16)


def over_lanes(value, first, width, pieces=2):
    return exact_dot_right(value, spread_matrix(value.shape[1], first, width), pieces)


def exact_dot_right(value, ones, pieces):
    return sum(dot(piece, ones) for piece in split(value, pieces))


def shape(dims, dtype=F32):
    return pltpu.VMEM(dims, dtype)


def pinned(value, space=pltpu.VMEM):
    return pltpu.with_memory_space_constraint(value, space)


def call(kernel, out_shape, flops, moved, **options):
    return pl.pallas_call(
        kernel,
        out_shape=out_shape,
        compiler_params=pltpu.CompilerParams(vmem_limit_bytes=VMEM_LIMIT),
        cost_estimate=pl.CostEstimate(flops=flops, bytes_accessed=moved, transcendentals=0),
        **options,
    )


def triangle(keep):
    row = lax.broadcasted_iota(jnp.int32, (SPAN, SPAN), 0)
    column = lax.broadcasted_iota(jnp.int32, (SPAN, SPAN), 1)
    return jnp.where(keep(row, column), 1.0, 0.0).astype(BF16)


def state_kernel(
    x_hbm, b_hbm, dt_hbm, a_hbm, asked_hbm, total_ref, decay_ref, cum_ref, row_ref,
    x_ref, b_ref, asked_ref, *rest,
):
    sent_refs, (dt_ref, a_ref, sems) = rest[:-3], rest[-3:]
    heads, tokens = dt_ref.shape
    spans = tokens // SPAN
    chunks, _, width = total_ref.shape
    per_group = H // G
    groups = heads // per_group
    group_lanes = per_group * P_SIZE
    copies = [
        pltpu.make_async_copy(dt_hbm, dt_ref, sems.at[0]),
        pltpu.make_async_copy(a_hbm, a_ref, sems.at[1]),
        pltpu.make_async_copy(b_hbm, b_ref, sems.at[2]),
    ]
    for g in range(groups):
        lanes = slice(g * group_lanes, (g + 1) * group_lanes)
        copies.append(
            pltpu.make_async_copy(x_hbm.at[:, lanes], x_ref.at[:, lanes], sems.at[3 + g])
        )
    copies.append(pltpu.make_async_copy(asked_hbm, asked_ref, sems.at[3 + groups]))
    for copy in copies:
        copy.start()
    upper = triangle(lambda s, t: s <= t)
    eye = lax.broadcasted_iota(jnp.int32, (heads, heads), 0) == lax.broadcasted_iota(
        jnp.int32, (heads, heads), 1
    )
    copies[0].wait()
    copies[1].wait()
    a_column = jnp.sum(jnp.where(eye, a_ref[...], 0.0), axis=1, keepdims=True)
    step = softplus(dt_ref[...].astype(F32))
    rate = step * (jnp.exp(a_column) * -LOG2E)
    cums = [exact_dot_right(rate[:, i * SPAN : (i + 1) * SPAN], upper, 3) for i in range(spans)]
    ends = [cum[:, SPAN - 1 : SPAN] for cum in cums]
    after = jnp.zeros_like(ends[0])
    weights = [None] * spans
    for i in reversed(range(spans)):
        after = after + ends[i]
        weights[i] = jnp.exp2(after - cums[i]) * step[:, i * SPAN : (i + 1) * SPAN]
    weight = jnp.concatenate(weights, axis=1).T
    whole = jnp.sum(jnp.where(eye, jnp.exp2(after), 0.0), axis=0, keepdims=True)
    cum = jnp.concatenate(cums, axis=1)
    cum_ref[...] = cum
    row_ref[...] = jnp.log2(step) - cum
    copies[2].wait()
    for g in range(groups):
        turned = b_ref[:, g * N : (g + 1) * N].astype(F32).T.astype(BF16)
        copies[3 + g].wait()
        for k in range(chunks):
            first = k * width
            if first // group_lanes != g:
                continue
            lanes = slice(first, first + width)
            scaled = (x_ref[:, lanes].astype(F32) * over_lanes(weight, first, width)).astype(BF16)
            total = dot(turned, scaled)
            total_ref[k] = total
            sent_refs[k][...] = total.astype(BF16)
            decay_ref[k] = over_lanes(whole, first, width, 3)
    copies[-1].wait()


def pass_kernel(hop, k, got_ref, total_ref, decay_ref, *rest):
    moving_ref, carry_ref = rest[-2:]
    first = hop == 1 and k == 0
    if first:
        carry_ref[...] = jnp.zeros_like(carry_ref)
    got = got_ref[...]
    moving_ref[...] = (total_ref[k] + decay_ref[k] * got.astype(F32)).astype(BF16)

    @pl.when(lax.axis_index("seq") == hop)
    def _():
        carry_ref[k] = got


def pair_halves(x_part):
    first_half = lax.broadcasted_iota(jnp.int32, (1, 2 * P_SIZE), 1) < P_SIZE
    zero = jnp.zeros_like(x_part)
    return jnp.where(first_half, x_part, zero), jnp.where(first_half, zero, x_part)


def span_starts(cum, spans):
    ends = [cum[(i + 1) * SPAN - 1 : (i + 1) * SPAN, :] for i in range(spans)]
    starts = [jnp.zeros_like(ends[0])]
    for i in range(spans):
        starts.append(starts[i] + ends[i])
    return ends, starts


def inner_kernel(g, x_ref, b_ref, c_ref, cum_ref, row_ref, d_ref, *rest):
    inner_ref = rest[-1]
    if g == 0:
        asked_ref, handed_ref, inner_ref = rest
        handed_ref[...] = asked_ref[...]
    heads, tokens = cum_ref.shape
    spans = tokens // SPAN
    per_group = H // G
    names = slice(g * N, (g + 1) * N)
    t_index = lax.broadcasted_iota(jnp.int32, (SPAN, SPAN), 0)
    s_index = lax.broadcasted_iota(jnp.int32, (SPAN, SPAN), 1)
    causal = t_index >= s_index
    rows = row_ref[...]
    cum = cum_ref[...].T
    ends, _ = span_starts(cum, spans)
    first_half = lax.broadcasted_iota(jnp.int32, (1, 2 * P_SIZE), 1) < P_SIZE
    scores = dot(c_ref[:, names], b_ref[:, names], 1, 1)
    for pair in range(per_group // 2):
        h0 = g * per_group + 2 * pair
        lanes = slice(h0 * P_SIZE, (h0 + 2) * P_SIZE)
        here = slice(2 * pair * P_SIZE, (2 * pair + 2) * P_SIZE)
        x_part = x_ref[:, lanes]
        halves = pair_halves(x_part)
        weights = [[None, None] for _ in range(spans)]
        for e in range(2):
            h = h0 + e
            row = rows[h : h + 1, :]
            for i in range(spans):
                column = jnp.broadcast_to(cum[i * SPAN : (i + 1) * SPAN, h : h + 1], (SPAN, SPAN))
                parts = []
                for j in range(i + 1):
                    shift = row[:, j * SPAN : (j + 1) * SPAN]
                    for m in range(j, i):
                        shift = shift + ends[m][:, h : h + 1]
                    score = scores[i * SPAN : (i + 1) * SPAN, j * SPAN : (j + 1) * SPAN]
                    part = score * jnp.exp2(column + shift)
                    if i == j:
                        part = jnp.where(causal, part, 0.0)
                    parts.append(part.astype(BF16))
                weights[i][e] = jnp.concatenate(parts, axis=1) if i else parts[0]
        skip = jnp.where(first_half, d_ref[:, h0 : h0 + 1], d_ref[:, h0 + 1 : h0 + 2])
        for i in range(spans):
            reach = (i + 1) * SPAN
            left = jnp.concatenate(weights[i], axis=1)
            right = jnp.concatenate([half[:reach] for half in halves], axis=0)
            mine = slice(i * SPAN, (i + 1) * SPAN)
            inner_ref[mine, here] = dot(left, right) + skip * x_part[mine].astype(F32)


def ask_kernel(count, x_ref, b_ref, cum_ref, row_ref, len_ref, owner_ref, *rest):
    ask_refs = rest[:count]
    local_ref, gain_ref, asked_ref = rest[-3:]
    heads, tokens = cum_ref.shape
    spans = tokens // SPAN
    asks = local_ref.shape[0]
    per_group = H // G
    groups = heads // per_group
    me = lax.axis_index("seq")
    asked = jnp.concatenate([ref[me].astype(F32) for ref in ask_refs], axis=0).astype(BF16)
    asked_ref[...] = asked
    block = lax.broadcasted_iota(jnp.int32, (asks, 1), 0) // STEPS
    spot = len_ref[...] - 1 - me * tokens
    mine = (owner_ref[...] == lax.rem(me + count - block, count)) & (spot >= 0) & (spot < tokens)
    spot = jnp.sum(jnp.where(mine, spot, 0).astype(F32), axis=1, keepdims=True).astype(jnp.int32)
    position = lax.broadcasted_iota(jnp.int32, (asks, tokens), 1)
    picked = jnp.where(position == spot, 1.0, 0.0).astype(BF16)
    upto = position <= spot
    rows = row_ref[...]
    cum = cum_ref[...].T
    ends, starts = span_starts(cum, spans)
    near_ask = exact_dot(picked, cum)
    ask_start = starts[0]
    for i in range(1, spans):
        ask_start = jnp.where(spot >= i * SPAN, starts[i], ask_start)
    gain_ref[...] = near_ask + ask_start
    columns = []
    for j in range(spans):
        column = near_ask
        for i in range(j + 1, spans):
            column = jnp.where(spot // SPAN == i, near_ask + sum(ends[j + 1 : i], ends[j]), column)
        columns.append(column)
    for g in range(groups):
        names = slice(g * N, (g + 1) * N)
        scores = jnp.where(upto, dot(asked[:, names], b_ref[:, names], 1, 1), 0.0)
        for pair in range(per_group // 2):
            h0 = g * per_group + 2 * pair
            lanes = slice(h0 * P_SIZE, (h0 + 2) * P_SIZE)
            parts = []
            for h in (h0, h0 + 1):
                for j in range(spans):
                    span = slice(j * SPAN, (j + 1) * SPAN)
                    part = scores[:, span] * jnp.exp2(columns[j][:, h : h + 1] + rows[h : h + 1, span])
                    parts.append(jnp.where(upto[:, span], part, 0.0).astype(BF16))
            right = jnp.concatenate(pair_halves(x_ref[:, lanes]), axis=0)
            local_ref[:, lanes] = dot(jnp.concatenate(parts, axis=1), right)


def read_kernel(chunks, filed, gain_ref, asked_ref, local_ref, carry_ref, *rest):
    got_refs, rest = rest[: len(chunks)], rest[len(chunks) :]
    read_refs = rest[len(rest) // 2 :] if filed else rest
    width = got_refs[0].shape[1]
    count = len(read_refs)
    last = lax.axis_index("seq") == count - 1
    gain = jnp.exp2(gain_ref[...])
    for got_ref, k in zip(got_refs, chunks):
        first = k * width
        g = first // (H // G * P_SIZE)
        state = jnp.where(last, got_ref[...], carry_ref[k])
        carried = dot(asked_ref[:, g * N : (g + 1) * N], state)
        reading = local_ref[:, first : first + width] + over_lanes(gain, first, width) * carried
        for r in range(count):
            read_refs[r][:, first : first + width] = reading[r * STEPS : (r + 1) * STEPS]


def outer_kernel(chunks, count, c_ref, cum_ref, carry_ref, *rest):
    got_refs = rest[: len(chunks)]
    inner_refs = rest[len(chunks) :]
    out_hbm, out_ref, sems = rest[-3:]
    heads, tokens = cum_ref.shape
    spans = tokens // SPAN
    width = got_refs[0].shape[1]
    group_lanes = H // G * P_SIZE
    last = lax.axis_index("seq") == count - 1
    start = jnp.zeros((heads, 1), F32)
    gains = []
    for i in range(spans):
        cum = cum_ref[:, i * SPAN : (i + 1) * SPAN]
        gains.append(jnp.exp2(cum + start))
        start = start + cum[:, SPAN - 1 : SPAN]
    gain = jnp.concatenate(gains, axis=1).T
    copies = []
    for i, k in enumerate(chunks):
        first = k * width
        g = first // group_lanes
        state = jnp.where(last, got_refs[i][...], carry_ref[k])
        carried = dot(c_ref[:, g * N : (g + 1) * N], state)
        inner = inner_refs[g][:, first - g * group_lanes : first - g * group_lanes + width]
        out_ref[i] = (inner + over_lanes(gain, first, width) * carried).astype(BF16)
        copies.append(
            pltpu.make_async_copy(out_ref.at[i], out_hbm.at[:, first : first + width], sems.at[i])
        )
        copies[i].start()
    for copy in copies:
        copy.wait()


def fresh_kernel(tokens, x_ref, b_ref, c_ref, dt_ref, a_ref, d_ref, len_ref, owner_ref, *rest):
    keep_ref, fresh_ref, held_ref = rest[-3:]
    count, _, heads = dt_ref.shape
    rows = count * STEPS
    place = lax.broadcasted_iota(jnp.int32, (rows, 1), 0) // STEPS * tokens
    spot = len_ref[...] - 1 - place
    mine = (owner_ref[...] == lax.axis_index("seq")) & (spot >= 0) & (spot < tokens)
    held = jnp.sum(jnp.where(mine, 1.0, 0.0), axis=1, keepdims=True)
    held = jnp.broadcast_to(held, (rows, held_ref.shape[2]))
    per_group = H // G
    groups = heads // per_group
    width = x_ref.shape[2]

    def flat(ref):
        return jnp.concatenate([ref[i].astype(F32) for i in range(count)], axis=0)

    turn = lax.broadcasted_iota(jnp.int32, (rows, 1), 0) % STEPS
    step = softplus(flat(dt_ref))
    rate = step * (jnp.exp(a_ref[...]) * -LOG2E)

    def earlier(value, gap):
        if not gap:
            return value
        moved = jnp.concatenate([jnp.zeros_like(value[:gap]), value[:-gap]], axis=0)
        return jnp.where(turn >= gap, moved, 0.0)

    running = sum(earlier(rate, gap) for gap in range(STEPS))
    keep = over_lanes(jnp.exp2(running), 0, width)
    x_values = flat(x_ref)
    b_values = flat(b_ref)
    c_values = flat(c_ref)
    head = lax.broadcasted_iota(jnp.int32, (rows, heads), 1)
    fresh = over_lanes(d_ref[...], 0, width, 3) * x_values
    since = jnp.zeros_like(rate)
    for gap in range(STEPS):
        if gap:
            since = since + earlier(rate, gap - 1)
        products = c_values * earlier(b_values, gap)
        pair = jnp.zeros((rows, heads), F32)
        for g in range(groups):
            score = jnp.sum(products[:, g * N : (g + 1) * N], axis=1, keepdims=True)
            pair = jnp.where(head // per_group == g, score, pair)
        factor = jnp.where(turn >= gap, jnp.exp2(since) * earlier(step, gap) * pair, 0.0)
        fresh = fresh + over_lanes(factor, 0, width) * earlier(x_values, gap)
    for i in range(rows // STEPS):
        keep_ref[i] = keep[i * STEPS : (i + 1) * STEPS]
        fresh_ref[i] = fresh[i * STEPS : (i + 1) * STEPS]
        held_ref[i] = held[i * STEPS : (i + 1) * STEPS]


def finish_kernel(keep_ref, fresh_ref, held_ref, *rest):
    back_refs, out_ref = rest[:-1], rest[-1]
    count = len(back_refs)
    me = lax.axis_index("seq")
    for r in range(count):
        source = lax.rem(me + r, count)
        value = back_refs[r][...] * keep_ref[source] + fresh_ref[source]
        held = held_ref[source][:, :1] > 0.0
        out_ref[source] = jnp.where(held, value, 0.0).astype(BF16)


def shards(
    ssm_input, bmat, cmat, dt_raw, a_log, d_skip, prompt_len, owner, dec_x, dec_b, dec_c, dec_dt
):
    count = lax.axis_size("seq")
    tensor = lax.axis_size("tp")
    tokens, heads = dt_raw.shape
    groups = heads // (H // G)
    names = groups * N
    lanes = heads * P_SIZE
    group_lanes = lanes // groups
    rows = count * STEPS
    chunks = CHUNKS if count <= 4 else groups
    width = lanes // chunks
    a_row = a_log.reshape(1, heads)
    d_row = d_skip.reshape(1, heads)
    len_row = prompt_len.reshape(1, -1)
    owner_row = owner.reshape(1, -1)
    anywhere = pl.BlockSpec(memory_space=pl.ANY)
    in_hbm = pl.BlockSpec(memory_space=pltpu.HBM)
    in_vmem = pl.BlockSpec(memory_space=pltpu.VMEM)
    sent_shape = shape((N, width), BF16)
    asked_shape = shape((count, STEPS, names), BF16)

    total, decay, cum, row, x_here, b_here, asked_here, *sent = call(
        state_kernel,
        (
            shape((chunks, N, width)),
            shape((chunks, 1, width)),
            shape((heads, tokens)),
            shape((heads, tokens)),
            shape((tokens, lanes), BF16),
            shape((tokens, names), BF16),
            asked_shape,
        )
        + (sent_shape,) * chunks,
        2 * tokens * N * lanes,
        4 * tokens * lanes,
        in_specs=[in_hbm] * 5,
        scratch_shapes=[
            pltpu.VMEM((heads, tokens), BF16),
            pltpu.VMEM((1, heads), F32),
            pltpu.SemaphoreType.DMA((4 + groups,)),
        ],
    )(
        pinned(ssm_input, pltpu.HBM),
        pinned(bmat, pltpu.HBM),
        pinned(dt_raw.T, pltpu.HBM),
        pinned(a_row, pltpu.HBM),
        pinned(dec_c[0], pltpu.HBM),
    )

    def forward(value, hop):
        pairs = []
        for d in range(count):
            other = d + 1 if (d - hop) % 2 else d - 1
            for t in range(tensor):
                alone = not 0 <= other < count
                there = d * tensor + (t ^ 1) if alone else other * tensor + t
                pairs.append((d * tensor + t, there))
        return lax.ppermute(value, ("seq", "tp"), pairs)

    def shift(value, by):
        return lax.ppermute(value, "seq", [(d, (d + by) % count) for d in range(count)])

    got = {(1, k): forward(sent[k], 1) for k in range(chunks)}

    def inner_part(g):
        more = (asked_here,) if g == 0 else ()
        inner_shape = shape((tokens, group_lanes))
        return call(
            functools.partial(inner_kernel, g),
            (asked_shape, inner_shape) if g == 0 else inner_shape,
            2 * tokens * tokens * group_lanes,
            16 * tokens * group_lanes,
        )(x_here, b_here, cmat, cum, row, d_row, *more)

    handed, first_inner = inner_part(0)
    inner = [first_inner] + [inner_part(g) for g in range(1, groups)]
    asks = [handed] + [shift(handed, r) for r in range(1, count)]

    def ask_part(*after):
        return call(
            functools.partial(ask_kernel, count),
            (shape((rows, lanes)), shape((rows, heads)), shape((rows, names), BF16)),
            2 * rows * tokens * lanes,
            4 * tokens * lanes,
            in_specs=[in_vmem] * (6 + count) + [anywhere] * len(after),
        )(x_here, b_here, cum, row, len_row, owner_row, *asks, *after)

    def fresh_part(*after):
        return call(
            functools.partial(fresh_kernel, tokens),
            (shape((count, STEPS, lanes)),) * 2 + (shape((count, STEPS, 128)),),
            64 * rows * lanes,
            16 * rows * lanes,
            in_specs=[in_vmem] * 8 + [anywhere] * len(after),
        )(dec_x[0], dec_b[0], asked_here, dec_dt[0], a_row, d_row, len_row, owner_row, *after)

    order = sorted((k + hop, hop, k) for hop in range(1, count - 1) for k in range(chunks))
    work = {1: ask_part, 2: fresh_part}
    results = {}
    after = inner
    carry = tie = None
    for place, (_, hop, k) in enumerate(order):
        if place in work:
            results[place] = work[place](tie)
            after = results[place][:1]
        held_before = [] if carry is None else [carry]
        moving, carry = call(
            functools.partial(pass_kernel, hop, k),
            (sent_shape, shape((chunks, N, width), BF16)),
            2 * N * width,
            8 * N * width,
            in_specs=[in_vmem] * (3 + len(held_before)) + [anywhere] * len(after),
            input_output_aliases={3: 1} if held_before else {},
        )(got[hop, k], total, decay, *held_before, *after)
        got[hop + 1, k] = forward(moving, hop + 1)
        tie, after = moving, []
    local, gain, asked = results[1]
    keep, fresh, held = results[2]

    def read_part(part, before):
        return call(
            functools.partial(read_kernel, part, bool(before)),
            (shape((STEPS, lanes)),) * count,
            2 * rows * N * lanes,
            4 * N * lanes,
            input_output_aliases={4 + len(part) + r: r for r in range(len(before))},
        )(gain, asked, local, carry, *[got[count - 1, k] for k in part], *before)

    def outer_part(part, before):
        return call(
            functools.partial(outer_kernel, part, count),
            pltpu.HBM((tokens, lanes), BF16),
            2 * tokens * N * lanes,
            8 * tokens * lanes,
            in_specs=[in_vmem] * (3 + len(part) + groups) + [in_hbm] * len(before),
            out_specs=in_hbm,
            scratch_shapes=[
                pltpu.VMEM((len(part), tokens, width), BF16),
                pltpu.SemaphoreType.DMA((len(part),)),
            ],
            input_output_aliases={3 + len(part) + groups: 0} if before else {},
        )(cmat, cum, carry, *[got[count - 1, k] for k in part], *inner, *before)

    early, late = tuple(range(chunks - 1)), (chunks - 1,)
    prefill = outer_part(early, [])
    reading = read_part(early, [])
    reading = read_part(late, reading)
    back = [reading[0]] + [None] * (count - 1)
    for r in reversed(range(1, count)):
        back[r] = shift(reading[r], -r)
    prefill = outer_part(late, [prefill])

    decoded = call(
        finish_kernel,
        jax.ShapeDtypeStruct((count, STEPS, lanes), BF16),
        4 * rows * lanes,
        16 * rows * lanes,
    )(keep, fresh, held, *back)
    return (prefill, decoded[None])


def solution(mesh):
    placed = (
        P(("grp", "seq"), "tp"),
        P(("grp", "seq"), "tp"),
        P(("grp", "seq"), "tp"),
        P(("grp", "seq"), "tp"),
        P("tp"),
        P("tp"),
        P("grp"),
        P("grp"),
        P(("grp", "seq"), None, None, "tp"),
        P(("grp", "seq"), None, None, "tp"),
        P(("grp", "seq"), None, None, "tp"),
        P(("grp", "seq"), None, None, "tp"),
    )
    return jax.shard_map(
        shards,
        mesh=mesh,
        in_specs=placed,
        out_specs=(P(("grp", "seq"), "tp"), P(("grp", "seq"), None, None, "tp")),
        check_vma=False,
    )
```

```python
import functools
import math

import jax
import jax.numpy as jnp
from jax import lax
from jax.experimental import pallas as pl
from jax.experimental.pallas import tpu as pltpu
from jax.sharding import PartitionSpec as P

H = 128
P_SIZE = 64
N = 128
G = 8
SPAN = 128
STEPS = 4
LOG2E = math.log2(math.e)
F32 = jnp.float32
BF16 = jnp.bfloat16
CHUNKS = 4
VMEM_LIMIT = 32 * 1024 * 1024


def softplus(value):
    small = jnp.exp(-jnp.abs(value))
    series = small * (1.0 - small * (0.5 - small * (1.0 / 3.0 - small * 0.25)))
    return jnp.maximum(value, 0.0) + jnp.where(small < 0.02, series, jnp.log(1.0 + small))


def dot(left, right, left_dim=1, right_dim=0):
    return lax.dot_general(
        left, right, (((left_dim,), (right_dim,)), ((), ())), preferred_element_type=F32
    )


def split(value, pieces):
    result = []
    for _ in range(pieces):
        piece = value.astype(BF16)
        result.append(piece)
        value = value - piece.astype(F32)
    return result


def exact_dot(ones, value, pieces=3, left_dim=1):
    return sum(dot(ones, piece, left_dim) for piece in split(value, pieces))


def spread_matrix(heads, first, width):
    lane = lax.broadcasted_iota(jnp.int32, (heads, width), 1) + first
    head = lax.broadcasted_iota(jnp.int32, (heads, width), 0)
    return jnp.where(lane // P_SIZE == head, 1.0, 0.0).astype(BF16)


def over_lanes(value, first, width, pieces=2):
    return exact_dot_right(value, spread_matrix(value.shape[1], first, width), pieces)


def exact_dot_right(value, ones, pieces):
    return sum(dot(piece, ones) for piece in split(value, pieces))


def shape(dims, dtype=F32):
    return pltpu.VMEM(dims, dtype)


def pinned(value, space=pltpu.VMEM):
    return pltpu.with_memory_space_constraint(value, space)


def call(kernel, out_shape, flops, moved, **options):
    return pl.pallas_call(
        kernel,
        out_shape=out_shape,
        compiler_params=pltpu.CompilerParams(vmem_limit_bytes=VMEM_LIMIT),
        cost_estimate=pl.CostEstimate(flops=flops, bytes_accessed=moved, transcendentals=0),
        **options,
    )


def triangle(keep):
    row = lax.broadcasted_iota(jnp.int32, (SPAN, SPAN), 0)
    column = lax.broadcasted_iota(jnp.int32, (SPAN, SPAN), 1)
    return jnp.where(keep(row, column), 1.0, 0.0).astype(BF16)


def state_kernel(kept, chunks, ride, *refs):
    hbm, refs = refs[: kept + 1], refs[kept + 1 :]
    here, refs = refs[:kept], refs[kept:]
    total_ref, decay_ref, cum_ref, row_ref = refs[:4]
    sent_refs, (dt_ref, sems) = refs[4 : 4 + chunks], refs[4 + chunks :]
    x_ref, b_ref, a_ref, asked_ref = here[:4]
    heads, tokens = dt_ref.shape
    spans = tokens // SPAN
    width = total_ref.shape[2]
    per_group = H // G
    groups = heads // per_group
    group_lanes = per_group * P_SIZE
    dt_copy = pltpu.make_async_copy(hbm[kept], dt_ref, sems.at[0])
    copies = [
        pltpu.make_async_copy(hbm[i], here[i], sems.at[i]) for i in range(1, kept)
    ]
    x_copies = []
    for g in range(groups):
        lanes = slice(g * group_lanes, (g + 1) * group_lanes)
        x_copies.append(
            pltpu.make_async_copy(hbm[0].at[:, lanes], x_ref.at[:, lanes], sems.at[kept + g])
        )
    for copy in [dt_copy, copies[1], copies[0], *x_copies, *copies[2:]]:
        copy.start()
    upper = triangle(lambda s, t: s <= t)
    eye = lax.broadcasted_iota(jnp.int32, (heads, heads), 0) == lax.broadcasted_iota(
        jnp.int32, (heads, heads), 1
    )
    dt_copy.wait()
    copies[1].wait()
    a_column = jnp.sum(jnp.where(eye, a_ref[...], 0.0), axis=1, keepdims=True)
    step = softplus(dt_ref[...].astype(F32))
    rate = step * (jnp.exp(a_column) * -LOG2E)
    cums = [exact_dot_right(rate[:, i * SPAN : (i + 1) * SPAN], upper, 3) for i in range(spans)]
    ends = [cum[:, SPAN - 1 : SPAN] for cum in cums]
    after = jnp.zeros_like(ends[0])
    weights = [None] * spans
    for i in reversed(range(spans)):
        after = after + ends[i]
        weights[i] = jnp.exp2(after - cums[i]) * step[:, i * SPAN : (i + 1) * SPAN]
    weight = jnp.concatenate(weights, axis=1).T
    whole = jnp.sum(jnp.where(eye, jnp.exp2(after), 0.0), axis=0, keepdims=True)
    cum = jnp.concatenate(cums, axis=1)
    cum_ref[...] = cum
    row_ref[...] = jnp.log2(step) - cum
    copies[0].wait()
    for g in range(groups):
        turned = b_ref[:, g * N : (g + 1) * N].astype(F32).T.astype(BF16)
        x_copies[g].wait()
        for k in range(chunks):
            first = k * width
            if first // group_lanes != g:
                continue
            lanes = slice(first, first + width)
            scaled = (x_ref[:, lanes].astype(F32) * over_lanes(weight, first, width)).astype(BF16)
            total = dot(turned, scaled)
            total_ref[k] = total
            sent_refs[k][:N] = total.astype(BF16)
            decay_ref[k] = over_lanes(whole, first, width, 3)
    for copy in copies[2:]:
        copy.wait()
    if ride:
        own = flat(asked_ref).astype(BF16)
        sent_refs[0][N:] = jnp.concatenate([own, own], axis=1)


def flat(ref):
    return jnp.concatenate([ref[i].astype(F32) for i in range(ref.shape[0])], axis=0)


def pass_kernel(hop, k, ride, got_ref, total_ref, decay_ref, *rest):
    moving_ref, carry_ref = rest[-2:]
    me = lax.axis_index("seq")
    if hop == 1 and k == 0:
        carry_ref[...] = jnp.zeros_like(carry_ref)
    got = got_ref[:N]
    moving_ref[:N] = (total_ref[k] + decay_ref[k] * got.astype(F32)).astype(BF16)

    @pl.when(me == hop)
    def _():
        carry_ref[k] = got

    if ride and k == 0:
        tail = got_ref[N:]
        if hop == 1:
            own = rest[0][N:]
            names = tail.shape[1] // 2
            lane = lax.broadcasted_iota(jnp.int32, tail.shape, 1)
            mine = (lane // names) == lax.rem(me, 2)
            tail = jnp.where(mine, own.astype(F32), tail.astype(F32)).astype(BF16)
        moving_ref[N:] = tail


def pair_halves(x_part):
    first_half = lax.broadcasted_iota(jnp.int32, (1, 2 * P_SIZE), 1) < P_SIZE
    zero = jnp.zeros_like(x_part)
    return jnp.where(first_half, x_part, zero), jnp.where(first_half, zero, x_part)


def span_starts(cum, spans):
    ends = [cum[(i + 1) * SPAN - 1 : (i + 1) * SPAN, :] for i in range(spans)]
    starts = [jnp.zeros_like(ends[0])]
    for i in range(spans):
        starts.append(starts[i] + ends[i])
    return ends, starts


def inner_kernel(g, x_ref, b_ref, c_ref, cum_ref, row_ref, d_ref, *rest):
    inner_ref = rest[-1]
    if len(rest) > 1:
        asked_ref, handed_ref, inner_ref = rest
        handed_ref[...] = asked_ref[...]
    heads, tokens = cum_ref.shape
    spans = tokens // SPAN
    per_group = H // G
    names = slice(g * N, (g + 1) * N)
    t_index = lax.broadcasted_iota(jnp.int32, (SPAN, SPAN), 0)
    s_index = lax.broadcasted_iota(jnp.int32, (SPAN, SPAN), 1)
    causal = t_index >= s_index
    rows = row_ref[...]
    cum = cum_ref[...].T
    ends, _ = span_starts(cum, spans)
    first_half = lax.broadcasted_iota(jnp.int32, (1, 2 * P_SIZE), 1) < P_SIZE
    scores = dot(c_ref[:, names], b_ref[:, names], 1, 1)
    for pair in range(per_group // 2):
        h0 = g * per_group + 2 * pair
        lanes = slice(h0 * P_SIZE, (h0 + 2) * P_SIZE)
        here = slice(2 * pair * P_SIZE, (2 * pair + 2) * P_SIZE)
        x_part = x_ref[:, lanes]
        halves = pair_halves(x_part)
        weights = [[None, None] for _ in range(spans)]
        for e in range(2):
            h = h0 + e
            row = rows[h : h + 1, :]
            for i in range(spans):
                column = jnp.broadcast_to(cum[i * SPAN : (i + 1) * SPAN, h : h + 1], (SPAN, SPAN))
                parts = []
                for j in range(i + 1):
                    shift = row[:, j * SPAN : (j + 1) * SPAN]
                    for m in range(j, i):
                        shift = shift + ends[m][:, h : h + 1]
                    score = scores[i * SPAN : (i + 1) * SPAN, j * SPAN : (j + 1) * SPAN]
                    part = score * jnp.exp2(column + shift)
                    if i == j:
                        part = jnp.where(causal, part, 0.0)
                    parts.append(part.astype(BF16))
                weights[i][e] = jnp.concatenate(parts, axis=1) if i else parts[0]
        skip = jnp.where(first_half, d_ref[:, h0 : h0 + 1], d_ref[:, h0 + 1 : h0 + 2])
        for i in range(spans):
            reach = (i + 1) * SPAN
            left = jnp.concatenate(weights[i], axis=1)
            right = jnp.concatenate([half[:reach] for half in halves], axis=0)
            mine = slice(i * SPAN, (i + 1) * SPAN)
            inner_ref[mine, here] = dot(left, right) + skip * x_part[mine].astype(F32)


def ask_kernel(count, ride, x_ref, b_ref, cum_ref, row_ref, len_ref, owner_ref, *rest):
    local_ref, gain_ref, next_ref = rest[-3:]
    heads, tokens = cum_ref.shape
    spans = tokens // SPAN
    asks = local_ref.shape[0]
    per_group = H // G
    groups = heads // per_group
    me = lax.axis_index("seq")
    if ride:
        near, middle, far = [ref[N:].astype(F32) for ref in rest[:3]]
        far = jnp.where((me == 1) | (me == 2), middle, far)
        halves = (jnp.where(me < 2, near, far), jnp.where(me < 2, far, near))
        names = near.shape[1] // 2
        blocks = [half[:, i * names : (i + 1) * names] for half in halves for i in range(2)]
    else:
        blocks = [flat(ref) for ref in rest[:count]]
    blocks = jnp.concatenate(blocks, axis=0).astype(BF16)
    row = lax.broadcasted_iota(jnp.int32, (asks, asks * count), 0)
    column = lax.broadcasted_iota(jnp.int32, (asks, asks * count), 1)
    place = row // STEPS
    if ride:
        place = lax.rem(me + count - place, count)

    def of_source(source):
        wanted = place * asks + source * STEPS + row % STEPS
        return dot(jnp.where(column == wanted, 1.0, 0.0).astype(BF16), blocks).astype(BF16)

    asked = of_source(me)
    next_ref[...] = of_source(lax.rem(me + 1, count))
    block = lax.broadcasted_iota(jnp.int32, (asks, 1), 0) // STEPS
    spot = len_ref[...] - 1 - me * tokens
    mine = (owner_ref[...] == lax.rem(me + count - block, count)) & (spot >= 0) & (spot < tokens)
    spot = jnp.sum(jnp.where(mine, spot, 0).astype(F32), axis=1, keepdims=True).astype(jnp.int32)
    position = lax.broadcasted_iota(jnp.int32, (asks, tokens), 1)
    picked = jnp.where(position == spot, 1.0, 0.0).astype(BF16)
    upto = position <= spot
    rows = row_ref[...]
    cum = cum_ref[...].T
    ends, starts = span_starts(cum, spans)
    near_ask = exact_dot(picked, cum)
    ask_start = starts[0]
    for i in range(1, spans):
        ask_start = jnp.where(spot >= i * SPAN, starts[i], ask_start)
    gain = near_ask + ask_start
    gain_ref[...] = jnp.concatenate([gain] * (gain_ref.shape[1] // heads), axis=1)
    columns = []
    for j in range(spans):
        column = near_ask
        for i in range(j + 1, spans):
            column = jnp.where(spot // SPAN == i, near_ask + sum(ends[j + 1 : i], ends[j]), column)
        columns.append(column)
    for g in range(groups):
        names = slice(g * N, (g + 1) * N)
        scores = jnp.where(upto, dot(asked[:, names], b_ref[:, names], 1, 1), 0.0)
        for pair in range(per_group // 2):
            h0 = g * per_group + 2 * pair
            lanes = slice(h0 * P_SIZE, (h0 + 2) * P_SIZE)
            parts = []
            for h in (h0, h0 + 1):
                for j in range(spans):
                    span = slice(j * SPAN, (j + 1) * SPAN)
                    part = scores[:, span] * jnp.exp2(columns[j][:, h : h + 1] + rows[h : h + 1, span])
                    parts.append(jnp.where(upto[:, span], part, 0.0).astype(BF16))
            right = jnp.concatenate(pair_halves(x_ref[:, lanes]), axis=0)
            local_ref[:, lanes] = dot(jnp.concatenate(parts, axis=1), right)


def message_kernel(count, chunks, local_ref, gain_ref, next_ref, *rest):
    moving_refs, message_refs = rest[:-count], rest[-count:]
    me = lax.axis_index("seq")
    lanes = local_ref.shape[1]
    width = lanes // chunks
    for k in range(chunks):
        first = k * width
        g = first // (H // G * P_SIZE)
        state = moving_refs[k][:N].astype(F32)
        for hop in range(1, count - 1):
            state = jnp.where(me == hop, moving_refs[hop * chunks + k][:N].astype(F32), state)
        reading = dot(next_ref[:, g * N : (g + 1) * N], state.astype(BF16))
        for r in range(count):
            message_refs[r][:, first : first + width] = reading[r * STEPS : (r + 1) * STEPS]
    for r in range(count):
        mine = slice(r * STEPS, (r + 1) * STEPS)
        message_refs[r][:, lanes : 2 * lanes] = local_ref[mine]
        message_refs[r][:, 2 * lanes :] = gain_ref[mine]


def outer_kernel(chunks, count, c_ref, cum_ref, carry_ref, *rest):
    got_refs = rest[: len(chunks)]
    inner_refs = rest[len(chunks) :]
    out_hbm, token_ref, out_ref, sems = rest[-4:]
    token_ref[...] = jnp.zeros_like(token_ref)
    heads, tokens = cum_ref.shape
    spans = tokens // SPAN
    width = got_refs[0].shape[1]
    group_lanes = H // G * P_SIZE
    last = lax.axis_index("seq") == count - 1
    start = jnp.zeros((heads, 1), F32)
    gains = []
    for i in range(spans):
        cum = cum_ref[:, i * SPAN : (i + 1) * SPAN]
        gains.append(jnp.exp2(cum + start))
        start = start + cum[:, SPAN - 1 : SPAN]
    gain = jnp.concatenate(gains, axis=1).T
    copies = []
    for i, k in enumerate(chunks):
        first = k * width
        g = first // group_lanes
        state = jnp.where(last, got_refs[i][:N], carry_ref[k])
        carried = dot(c_ref[:, g * N : (g + 1) * N], state)
        inner = inner_refs[g][:, first - g * group_lanes : first - g * group_lanes + width]
        out_ref[i] = (inner + over_lanes(gain, first, width) * carried).astype(BF16)
        copies.append(
            pltpu.make_async_copy(out_ref.at[i], out_hbm.at[:, first : first + width], sems.at[i])
        )
        copies[i].start()
    for copy in copies:
        copy.wait()


def fresh_kernel(tokens, x_ref, b_ref, c_ref, dt_ref, a_ref, d_ref, len_ref, owner_ref, *rest):
    keep_ref, fresh_ref, held_ref = rest[-3:]
    count, _, heads = dt_ref.shape
    rows = count * STEPS
    place = lax.broadcasted_iota(jnp.int32, (rows, 1), 0) // STEPS * tokens
    spot = len_ref[...] - 1 - place
    mine = (owner_ref[...] == lax.axis_index("seq")) & (spot >= 0) & (spot < tokens)
    held = jnp.sum(jnp.where(mine, 1.0, 0.0), axis=1, keepdims=True)
    held = jnp.broadcast_to(held, (rows, held_ref.shape[2]))
    per_group = H // G
    groups = heads // per_group
    width = x_ref.shape[2]
    turn = lax.broadcasted_iota(jnp.int32, (rows, 1), 0) % STEPS
    step = softplus(flat(dt_ref))
    rate = step * (jnp.exp(a_ref[...]) * -LOG2E)

    def earlier(value, gap):
        if not gap:
            return value
        moved = jnp.concatenate([jnp.zeros_like(value[:gap]), value[:-gap]], axis=0)
        return jnp.where(turn >= gap, moved, 0.0)

    running = sum(earlier(rate, gap) for gap in range(STEPS))
    keep = over_lanes(jnp.exp2(running), 0, width)
    x_values = flat(x_ref)
    b_values = flat(b_ref)
    c_values = flat(c_ref)
    head = lax.broadcasted_iota(jnp.int32, (rows, heads), 1)
    fresh = over_lanes(d_ref[...], 0, width, 3) * x_values
    since = jnp.zeros_like(rate)
    for gap in range(STEPS):
        if gap:
            since = since + earlier(rate, gap - 1)
        products = c_values * earlier(b_values, gap)
        pair = jnp.zeros((rows, heads), F32)
        for g in range(groups):
            score = jnp.sum(products[:, g * N : (g + 1) * N], axis=1, keepdims=True)
            pair = jnp.where(head // per_group == g, score, pair)
        factor = jnp.where(turn >= gap, jnp.exp2(since) * earlier(step, gap) * pair, 0.0)
        fresh = fresh + over_lanes(factor, 0, width) * earlier(x_values, gap)
    for i in range(rows // STEPS):
        keep_ref[i] = keep[i * STEPS : (i + 1) * STEPS]
        fresh_ref[i] = fresh[i * STEPS : (i + 1) * STEPS]
        held_ref[i] = held[i * STEPS : (i + 1) * STEPS]


def finish_kernel(keep_ref, fresh_ref, held_ref, *rest):
    back_refs, out_ref = rest[:-2], rest[-1]
    count = len(back_refs)
    lanes = keep_ref.shape[2]
    me = lax.axis_index("seq")
    gain = jnp.concatenate([ref[:, 2 * lanes :] for ref in back_refs], axis=0)
    gain = over_lanes(jnp.exp2(gain[:, : lanes // P_SIZE]), 0, lanes)
    for r in range(count):
        source = lax.rem(me + r, count)
        carried = gain[r * STEPS : (r + 1) * STEPS] * back_refs[r - 1][:, :lanes]
        reading = back_refs[r][:, lanes : 2 * lanes] + jnp.where(source > 0, carried, 0.0)
        value = reading * keep_ref[source] + fresh_ref[source]
        held = held_ref[source][:, :1] > 0.0
        out_ref[source] = jnp.where(held, value, 0.0).astype(BF16)


def shards(
    ssm_input, bmat, cmat, dt_raw, a_log, d_skip, prompt_len, owner, dec_x, dec_b, dec_c, dec_dt
):
    count = lax.axis_size("seq")
    tensor = lax.axis_size("tp")
    tokens, heads = dt_raw.shape
    groups = heads // (H // G)
    names = groups * N
    lanes = heads * P_SIZE
    group_lanes = lanes // groups
    rows = count * STEPS
    chunks = CHUNKS if count <= 4 else groups
    width = lanes // chunks
    anywhere = pl.BlockSpec(memory_space=pl.ANY)
    in_hbm = pl.BlockSpec(memory_space=pltpu.HBM)
    in_vmem = pl.BlockSpec(memory_space=pltpu.VMEM)
    ride = count == 4 and width == 2 * names

    def sent_shape(k):
        return shape((N + rows * (ride and k == 0), width), BF16)

    inputs = [
        ssm_input,
        bmat,
        a_log.reshape(1, heads),
        dec_c[0],
        cmat,
        d_skip.reshape(1, heads),
        prompt_len.reshape(1, -1),
        owner.reshape(1, -1),
        dec_x[0],
        dec_b[0],
        dec_dt[0],
    ]
    results = call(
        functools.partial(state_kernel, len(inputs), chunks, ride),
        tuple(shape(value.shape, value.dtype) for value in inputs)
        + (
            shape((chunks, N, width)),
            shape((chunks, 1, width)),
            shape((heads, tokens)),
            shape((heads, tokens)),
        )
        + tuple(sent_shape(k) for k in range(chunks)),
        2 * tokens * N * lanes,
        4 * tokens * lanes,
        in_specs=[in_hbm] * (len(inputs) + 1),
        scratch_shapes=[
            pltpu.VMEM((heads, tokens), BF16),
            pltpu.SemaphoreType.DMA((len(inputs) + groups,)),
        ],
    )(*[pinned(value, pltpu.HBM) for value in inputs + [dt_raw.T]])
    x, b, a_row, asked_here, c, d_row, len_row, owner_row, x_dec, b_dec, dt_dec = results[:11]
    total, decay, cum, row, *sent = results[11:]

    def forward(value, hop):
        pairs = []
        for d in range(count):
            other = d + 1 if (d - hop) % 2 else d - 1
            for t in range(tensor):
                alone = not 0 <= other < count
                there = d * tensor + (t ^ 1) if alone else other * tensor + t
                pairs.append((d * tensor + t, there))
        return lax.ppermute(value, ("seq", "tp"), pairs)

    def shift(value, by):
        return lax.ppermute(value, "seq", [(d, (d + by) % count) for d in range(count)])

    got = {(1, k): forward(sent[k], 1) for k in range(chunks)}
    moving = {(1, k): sent[k] for k in range(chunks)}

    def inner_part(g):
        more = (asked_here,) if g == 0 and not ride else ()
        inner_shape = shape((tokens, group_lanes))
        return call(
            functools.partial(inner_kernel, g),
            (shape(asked_here.shape, BF16), inner_shape) if more else inner_shape,
            2 * tokens * tokens * group_lanes,
            16 * tokens * group_lanes,
        )(x, b, c, cum, row, d_row, *more)

    inner = [inner_part(g) for g in range(groups)]
    if not ride:
        handed, inner[0] = inner[0]
        asks = [handed] + [shift(handed, r) for r in range(1, count)]

    def ask_part(*after):
        blocks = (moving[2, 0], got[2, 0], got[3, 0]) if ride else asks
        return call(
            functools.partial(ask_kernel, count, ride),
            (shape((rows, lanes)), shape((rows, 128)), shape((rows, names), BF16)),
            2 * rows * tokens * lanes,
            4 * tokens * lanes,
            in_specs=[in_vmem] * (6 + len(blocks)) + [anywhere] * len(after),
        )(x, b, cum, row, len_row, owner_row, *blocks, *after)

    def fresh_part(*after):
        return call(
            functools.partial(fresh_kernel, tokens),
            (shape((count, STEPS, lanes)),) * 2 + (shape((count, STEPS, 128)),),
            64 * rows * lanes,
            16 * rows * lanes,
            in_specs=[in_vmem] * 8 + [anywhere] * len(after),
        )(x_dec, b_dec, asked_here, dt_dec, a_row, d_row, len_row, owner_row, *after)

    def outer_part(part, carry, before):
        return call(
            functools.partial(outer_kernel, part, count),
            (pltpu.HBM((tokens, lanes), BF16), shape((8, 128))),
            2 * tokens * N * lanes,
            8 * tokens * lanes,
            in_specs=[in_vmem] * (3 + len(part) + groups) + [in_hbm] * len(before),
            out_specs=(in_hbm, in_vmem),
            scratch_shapes=[
                pltpu.VMEM((len(part), tokens, width), BF16),
                pltpu.SemaphoreType.DMA((len(part),)),
            ],
            input_output_aliases={3 + len(part) + groups: 0} if before else {},
        )(c, cum, carry, *[got[count - 1, k] for k in part], *inner, *before)

    order = sorted((k + hop, hop, k) for hop in range(1, count - 1) for k in range(chunks))
    early, late = tuple(range(chunks // 2)), tuple(range(chunks // 2, chunks))
    after = inner
    carry = tie = None
    for _, hop, k in order:
        if (hop, k) == (1, 1):
            keep, fresh, held = fresh_part(tie)
            after = [keep]
        if (hop, k) == (count - 2, chunks - 2):
            local, gain, asked_next = ask_part(tie)
            after = [gain]
        if (hop, k) == (count - 2, chunks - 1):
            prefill, token = outer_part(early, carry, [])
            after = [token]
        tail = [sent[0]] if ride and (hop, k) == (1, 0) else []
        filed = [] if carry is None else [carry]
        moving[hop + 1, k], carry = call(
            functools.partial(pass_kernel, hop, k, ride),
            (sent_shape(k), shape((chunks, N, width), BF16)),
            2 * N * width,
            8 * N * width,
            in_specs=[in_vmem] * (3 + len(filed) + len(tail)) + [anywhere] * len(after),
            input_output_aliases={3: 1} if filed else {},
        )(got[hop, k], total, decay, *filed, *tail, *after)
        got[hop + 1, k] = forward(moving[hop + 1, k], hop + 1)
        tie, after = moving[hop + 1, k], []

    message = call(
        functools.partial(message_kernel, count, chunks),
        (shape((STEPS, 2 * lanes + 128)),) * count,
        2 * rows * N * lanes,
        4 * N * lanes,
    )(local, gain, asked_next, *[moving[hop, k] for hop in range(1, count) for k in range(chunks)])
    back = [message[0]] + [None] * (count - 1)
    for r in reversed(range(1, count)):
        back[r] = shift(message[r], -r)
    prefill, token = outer_part(late, carry, [prefill])

    decoded = call(
        finish_kernel,
        jax.ShapeDtypeStruct((count, STEPS, lanes), BF16),
        4 * rows * lanes,
        16 * rows * lanes,
        in_specs=[in_vmem] * (3 + count) + [anywhere],
    )(keep, fresh, held, *back, token)
    return (prefill, decoded[None])


def solution(mesh):
    placed = (
        P(("grp", "seq"), "tp"),
        P(("grp", "seq"), "tp"),
        P(("grp", "seq"), "tp"),
        P(("grp", "seq"), "tp"),
        P("tp"),
        P("tp"),
        P("grp"),
        P("grp"),
        P(("grp", "seq"), None, None, "tp"),
        P(("grp", "seq"), None, None, "tp"),
        P(("grp", "seq"), None, None, "tp"),
        P(("grp", "seq"), None, None, "tp"),
    )
    return jax.shard_map(
        shards,
        mesh=mesh,
        in_specs=placed,
        out_specs=(P(("grp", "seq"), "tp"), P(("grp", "seq"), None, None, "tp")),
        check_vma=False,
    )
```

```python
import functools
import math

import jax
import jax.numpy as jnp
from jax import lax
from jax.experimental import pallas as pl
from jax.experimental.pallas import tpu as pltpu
from jax.sharding import PartitionSpec as P

H = 128
P_SIZE = 64
N = 128
G = 8
SPAN = 128
STEPS = 4
LOG2E = math.log2(math.e)
F32 = jnp.float32
BF16 = jnp.bfloat16
CHUNKS = 4
VMEM_LIMIT = 32 * 1024 * 1024


def softplus(value):
    small = jnp.exp(-jnp.abs(value))
    series = small * (1.0 - small * (0.5 - small * (1.0 / 3.0 - small * 0.25)))
    return jnp.maximum(value, 0.0) + jnp.where(small < 0.02, series, jnp.log(1.0 + small))


def dot(left, right, left_dim=1, right_dim=0):
    return lax.dot_general(
        left, right, (((left_dim,), (right_dim,)), ((), ())), preferred_element_type=F32
    )


def split(value, pieces):
    result = []
    for _ in range(pieces):
        piece = value.astype(BF16)
        result.append(piece)
        value = value - piece.astype(F32)
    return result


def exact_dot(ones, value, pieces=3, left_dim=1):
    return sum(dot(ones, piece, left_dim) for piece in split(value, pieces))


def spread_matrix(heads, first, width):
    lane = lax.broadcasted_iota(jnp.int32, (heads, width), 1) + first
    head = lax.broadcasted_iota(jnp.int32, (heads, width), 0)
    return jnp.where(lane // P_SIZE == head, 1.0, 0.0).astype(BF16)


def over_lanes(value, first, width, pieces=2):
    return exact_dot_right(value, spread_matrix(value.shape[1], first, width), pieces)


def exact_dot_right(value, ones, pieces):
    return sum(dot(piece, ones) for piece in split(value, pieces))


def shape(dims, dtype=F32):
    return pltpu.VMEM(dims, dtype)


def pinned(value, space=pltpu.VMEM):
    return pltpu.with_memory_space_constraint(value, space)


def call(kernel, out_shape, **options):
    return pl.pallas_call(
        kernel,
        out_shape=out_shape,
        compiler_params=pltpu.CompilerParams(vmem_limit_bytes=VMEM_LIMIT),
        cost_estimate=pl.CostEstimate(flops=1, bytes_accessed=1, transcendentals=0),
        **options,
    )


def triangle(keep):
    row = lax.broadcasted_iota(jnp.int32, (SPAN, SPAN), 0)
    column = lax.broadcasted_iota(jnp.int32, (SPAN, SPAN), 1)
    return jnp.where(keep(row, column), 1.0, 0.0).astype(BF16)


def chunk_total(k, x_ref, turned, weight, whole, total_ref, sent_ref, decay_ref):
    width = total_ref.shape[1]
    first = k * width
    scaled = x_ref[:, first : first + width].astype(F32) * over_lanes(weight, first, width)
    total = dot(turned, scaled.astype(BF16))
    total_ref[...] = total
    sent_ref[:N] = total.astype(BF16)
    decay_ref[...] = over_lanes(whole, first, width, 3)


def first_kernel(kept, ride, *refs):
    hbm, refs = refs[: kept + 1], refs[kept + 1 :]
    here, refs = refs[:kept], refs[kept:]
    cum_ref, row_ref, weight_ref, whole_ref, turned_ref = refs[:5]
    total_ref, sent_ref, decay_ref, dt_ref, sems = refs[5:]
    x_ref, b_ref, a_ref, asked_ref = here[:4]
    heads, tokens = dt_ref.shape
    spans = tokens // SPAN
    width = total_ref.shape[1]
    dt_copy = pltpu.make_async_copy(hbm[kept], dt_ref, sems.at[0])
    copies = [pltpu.make_async_copy(hbm[i], here[i], sems.at[i]) for i in range(1, kept)]
    x_copies = [
        pltpu.make_async_copy(hbm[0].at[:, lanes], x_ref.at[:, lanes], sems.at[kept + i])
        for i, lanes in enumerate((slice(0, width), slice(width, x_ref.shape[1])))
    ]
    for copy in [dt_copy, copies[1], copies[0], *x_copies, *copies[2:]]:
        copy.start()
    upper = triangle(lambda s, t: s <= t)
    eye = lax.broadcasted_iota(jnp.int32, (heads, heads), 0) == lax.broadcasted_iota(
        jnp.int32, (heads, heads), 1
    )
    dt_copy.wait()
    copies[1].wait()
    a_column = jnp.sum(jnp.where(eye, a_ref[...], 0.0), axis=1, keepdims=True)
    step = softplus(dt_ref[...].astype(F32))
    rate = step * (jnp.exp(a_column) * -LOG2E)
    cums = [exact_dot_right(rate[:, i * SPAN : (i + 1) * SPAN], upper, 3) for i in range(spans)]
    ends = [cum[:, SPAN - 1 : SPAN] for cum in cums]
    after = jnp.zeros_like(ends[0])
    weights = [None] * spans
    for i in reversed(range(spans)):
        after = after + ends[i]
        weights[i] = jnp.exp2(after - cums[i]) * step[:, i * SPAN : (i + 1) * SPAN]
    weight = jnp.concatenate(weights, axis=1).T
    whole = jnp.sum(jnp.where(eye, jnp.exp2(after), 0.0), axis=0, keepdims=True)
    weight_ref[...] = weight
    whole_ref[...] = whole
    copies[0].wait()
    turned = b_ref[:, :N].astype(F32).T.astype(BF16)
    x_copies[0].wait()
    chunk_total(0, x_ref, turned, weight, whole, total_ref, sent_ref, decay_ref)
    turned_ref[0] = turned
    for g in range(1, turned_ref.shape[0]):
        turned_ref[g] = b_ref[:, g * N : (g + 1) * N].astype(F32).T.astype(BF16)
    cum = jnp.concatenate(cums, axis=1)
    cum_ref[...] = cum
    row_ref[...] = jnp.log2(step) - cum
    x_copies[1].wait()
    for copy in copies[2:]:
        copy.wait()
    if ride:
        own = flat(asked_ref).astype(BF16)
        sent_ref[N:] = jnp.concatenate([own, own], axis=1)


def state_kernel(k, x_ref, turned_ref, weight_ref, whole_ref, *rest):
    total_ref, sent_ref, decay_ref = rest[-3:]
    g = k * total_ref.shape[1] // (H // G * P_SIZE)
    chunk_total(
        k, x_ref, turned_ref[g], weight_ref[...], whole_ref[...], total_ref, sent_ref, decay_ref
    )


def flat(ref):
    return jnp.concatenate([ref[i].astype(F32) for i in range(ref.shape[0])], axis=0)


def pass_kernel(hop, k, ride, got_ref, total_ref, decay_ref, *rest):
    moving_ref, carry_ref = rest[-2:]
    me = lax.axis_index("seq")
    if hop == 1 and k == 0:
        carry_ref[...] = jnp.zeros_like(carry_ref)
    got = got_ref[:N]
    moving_ref[:N] = (total_ref[...] + decay_ref[...] * got.astype(F32)).astype(BF16)

    @pl.when(me == hop)
    def _():
        carry_ref[k] = got

    if ride and k == 0:
        tail = got_ref[N:]
        if hop == 1:
            own = rest[0][N:]
            names = tail.shape[1] // 2
            lane = lax.broadcasted_iota(jnp.int32, tail.shape, 1)
            mine = (lane // names) == lax.rem(me, 2)
            tail = jnp.where(mine, own.astype(F32), tail.astype(F32)).astype(BF16)
        moving_ref[N:] = tail


def pair_halves(x_part):
    first_half = lax.broadcasted_iota(jnp.int32, (1, 2 * P_SIZE), 1) < P_SIZE
    zero = jnp.zeros_like(x_part)
    return jnp.where(first_half, x_part, zero), jnp.where(first_half, zero, x_part)


def span_starts(cum, spans):
    ends = [cum[(i + 1) * SPAN - 1 : (i + 1) * SPAN, :] for i in range(spans)]
    starts = [jnp.zeros_like(ends[0])]
    for i in range(spans):
        starts.append(starts[i] + ends[i])
    return ends, starts


def inner_kernel(g, x_ref, b_ref, c_ref, cum_ref, row_ref, d_ref, *rest):
    inner_ref = rest[-1]
    heads, tokens = cum_ref.shape
    spans = tokens // SPAN
    per_group = H // G
    names = slice(g * N, (g + 1) * N)
    t_index = lax.broadcasted_iota(jnp.int32, (SPAN, SPAN), 0)
    s_index = lax.broadcasted_iota(jnp.int32, (SPAN, SPAN), 1)
    causal = t_index >= s_index
    rows = row_ref[...]
    cum = cum_ref[...].T
    ends, _ = span_starts(cum, spans)
    first_half = lax.broadcasted_iota(jnp.int32, (1, 2 * P_SIZE), 1) < P_SIZE
    scores = dot(c_ref[:, names], b_ref[:, names], 1, 1)
    for pair in range(per_group // 2):
        h0 = g * per_group + 2 * pair
        lanes = slice(h0 * P_SIZE, (h0 + 2) * P_SIZE)
        here = slice(2 * pair * P_SIZE, (2 * pair + 2) * P_SIZE)
        x_part = x_ref[:, lanes]
        halves = pair_halves(x_part)
        weights = [[None, None] for _ in range(spans)]
        for e in range(2):
            h = h0 + e
            row = rows[h : h + 1, :]
            for i in range(spans):
                column = jnp.broadcast_to(cum[i * SPAN : (i + 1) * SPAN, h : h + 1], (SPAN, SPAN))
                parts = []
                for j in range(i + 1):
                    shift = row[:, j * SPAN : (j + 1) * SPAN]
                    for m in range(j, i):
                        shift = shift + ends[m][:, h : h + 1]
                    score = scores[i * SPAN : (i + 1) * SPAN, j * SPAN : (j + 1) * SPAN]
                    part = score * jnp.exp2(column + shift)
                    if i == j:
                        part = jnp.where(causal, part, 0.0)
                    parts.append(part.astype(BF16))
                weights[i][e] = jnp.concatenate(parts, axis=1) if i else parts[0]
        skip = jnp.where(first_half, d_ref[:, h0 : h0 + 1], d_ref[:, h0 + 1 : h0 + 2])
        for i in range(spans):
            reach = (i + 1) * SPAN
            left = jnp.concatenate(weights[i], axis=1)
            right = jnp.concatenate([half[:reach] for half in halves], axis=0)
            mine = slice(i * SPAN, (i + 1) * SPAN)
            inner_ref[mine, here] = dot(left, right) + skip * x_part[mine].astype(F32)


def ask_kernel(count, ride, x_ref, b_ref, cum_ref, row_ref, len_ref, owner_ref, *rest):
    local_ref, gain_ref, asked_ref = rest[-3:]
    heads, tokens = cum_ref.shape
    spans = tokens // SPAN
    asks = local_ref.shape[0]
    per_group = H // G
    groups = heads // per_group
    me = lax.axis_index("seq")
    if ride:
        near, middle, far = [ref[N:].astype(F32) for ref in rest[:3]]
        far = jnp.where((me == 1) | (me == 2), middle, far)
        halves = (jnp.where(me < 2, near, far), jnp.where(me < 2, far, near))
        names = near.shape[1] // 2
        blocks = [half[:, i * names : (i + 1) * names] for half in halves for i in range(2)]
    else:
        blocks = [flat(ref) for ref in rest[:count]]
    blocks = jnp.concatenate(blocks, axis=0).astype(BF16)
    row = lax.broadcasted_iota(jnp.int32, (asks, asks * count), 0)
    column = lax.broadcasted_iota(jnp.int32, (asks, asks * count), 1)
    place = row // STEPS
    wanted = place * asks + me * STEPS + row % STEPS
    asked = dot(jnp.where(column == wanted, 1.0, 0.0).astype(BF16), blocks).astype(BF16)
    asked_ref[...] = asked
    block = lax.broadcasted_iota(jnp.int32, (asks, 1), 0) // STEPS
    spot = len_ref[...] - 1 - me * tokens
    mine = (owner_ref[...] == (block if ride else lax.rem(me + count - block, count))) & (spot >= 0) & (spot < tokens)
    spot = jnp.sum(jnp.where(mine, spot, 0).astype(F32), axis=1, keepdims=True).astype(jnp.int32)
    position = lax.broadcasted_iota(jnp.int32, (asks, tokens), 1)
    picked = jnp.where(position == spot, 1.0, 0.0).astype(BF16)
    upto = position <= spot
    rows = row_ref[...]
    cum = cum_ref[...].T
    ends, starts = span_starts(cum, spans)
    near_ask = exact_dot(picked, cum)
    ask_start = starts[0]
    for i in range(1, spans):
        ask_start = jnp.where(spot >= i * SPAN, starts[i], ask_start)
    gain_ref[...] = jnp.exp2(near_ask + ask_start)
    columns = []
    for j in range(spans):
        column = near_ask
        for i in range(j + 1, spans):
            column = jnp.where(spot // SPAN == i, near_ask + sum(ends[j + 1 : i], ends[j]), column)
        columns.append(column)
    for g in range(groups):
        names = slice(g * N, (g + 1) * N)
        scores = jnp.where(upto, dot(asked[:, names], b_ref[:, names], 1, 1), 0.0)
        for pair in range(per_group // 2):
            h0 = g * per_group + 2 * pair
            lanes = slice(h0 * P_SIZE, (h0 + 2) * P_SIZE)
            parts = []
            for h in (h0, h0 + 1):
                for j in range(spans):
                    span = slice(j * SPAN, (j + 1) * SPAN)
                    part = scores[:, span] * jnp.exp2(columns[j][:, h : h + 1] + rows[h : h + 1, span])
                    parts.append(jnp.where(upto[:, span], part, 0.0).astype(BF16))
            right = jnp.concatenate(pair_halves(x_ref[:, lanes]), axis=0)
            local_ref[:, lanes] = dot(jnp.concatenate(parts, axis=1), right)


def read_kernel(count, chunks, ops, final, local_ref, gain_ref, asked_ref, carry_ref, *rest):
    got_refs, rest = rest[: chunks * final], rest[chunks * final :]
    read_refs = rest[-(len(ops) + final) :]
    me = lax.axis_index("seq")
    lanes = local_ref.shape[1]
    width = lanes // chunks
    for k in range(chunks):
        first = k * width
        here = slice(first, first + width)
        g = first // (H // G * P_SIZE)
        state = carry_ref[k]
        if final:
            state = jnp.where(me == count - 1, got_refs[k][:N], state)
        carried = dot(asked_ref[:, g * N : (g + 1) * N], state)
        reading = local_ref[:, here] + over_lanes(gain_ref[...], first, width) * carried
        parts = [reading[r * STEPS : (r + 1) * STEPS] for r in range(count)]
        for (one, other), read_ref in zip(ops, read_refs):
            part = parts[other]
            if one != other:
                part = jnp.where(me == one, part, parts[one])
            read_ref[:, here] = part
        if final:
            own = parts[0]
            for r in range(1, count):
                own = jnp.where(me == r, parts[r], own)
            read_refs[-1][:, here] = own


def outer_kernel(parts, count, c_ref, cum_ref, carry_ref, *rest):
    final = len(parts) > 1
    part = parts[-1]
    got_refs = rest[: len(part)]
    inner_refs = rest[len(part) : len(part) + cum_ref.shape[0] // (H // G)]
    if final:
        early_ref, out_hbm, token_ref, out_ref, sems = rest[-5:]
        token_ref[...] = jnp.zeros_like(token_ref)
    else:
        out_ref = rest[-1]
    heads, tokens = cum_ref.shape
    spans = tokens // SPAN
    width = got_refs[0].shape[1]
    group_lanes = H // G * P_SIZE
    copies = []

    def send(source, k):
        lanes = slice(k * width, (k + 1) * width)
        copies.append(pltpu.make_async_copy(source, out_hbm.at[:, lanes], sems.at[k]))
        copies[-1].start()

    if final:
        for i, k in enumerate(parts[0]):
            send(early_ref.at[i], k)
    last = lax.axis_index("seq") == count - 1
    start = jnp.zeros((heads, 1), F32)
    gains = []
    for i in range(spans):
        cum = cum_ref[:, i * SPAN : (i + 1) * SPAN]
        gains.append(jnp.exp2(cum + start))
        start = start + cum[:, SPAN - 1 : SPAN]
    gain = jnp.concatenate(gains, axis=1).T
    for i, k in enumerate(part):
        first = k * width
        g = first // group_lanes
        state = jnp.where(last, got_refs[i][:N], carry_ref[k])
        carried = dot(c_ref[:, g * N : (g + 1) * N], state)
        inner = inner_refs[g][:, first - g * group_lanes : first - g * group_lanes + width]
        out_ref[i] = (inner + over_lanes(gain, first, width) * carried).astype(BF16)
        if final:
            send(out_ref.at[i], k)
    for copy in copies:
        copy.wait()


def fresh_kernel(tokens, x_ref, b_ref, c_ref, dt_ref, a_ref, d_ref, len_ref, owner_ref, *rest):
    keep_ref, fresh_ref, held_ref = rest[-3:]
    count, _, heads = dt_ref.shape
    rows = count * STEPS
    place = lax.broadcasted_iota(jnp.int32, (rows, 1), 0) // STEPS * tokens
    spot = len_ref[...] - 1 - place
    mine = (owner_ref[...] == lax.axis_index("seq")) & (spot >= 0) & (spot < tokens)
    held = jnp.sum(jnp.where(mine, 1.0, 0.0), axis=1, keepdims=True)
    held = jnp.broadcast_to(held, (rows, held_ref.shape[2]))
    per_group = H // G
    groups = heads // per_group
    width = x_ref.shape[2]
    turn = lax.broadcasted_iota(jnp.int32, (rows, 1), 0) % STEPS
    step = softplus(flat(dt_ref))
    rate = step * (jnp.exp(a_ref[...]) * -LOG2E)

    def earlier(value, gap):
        if not gap:
            return value
        moved = jnp.concatenate([jnp.zeros_like(value[:gap]), value[:-gap]], axis=0)
        return jnp.where(turn >= gap, moved, 0.0)

    running = sum(earlier(rate, gap) for gap in range(STEPS))
    keep = over_lanes(jnp.exp2(running), 0, width)
    x_values = flat(x_ref)
    b_values = flat(b_ref)
    c_values = flat(c_ref)
    head = lax.broadcasted_iota(jnp.int32, (rows, heads), 1)
    fresh = over_lanes(d_ref[...], 0, width, 3) * x_values
    since = jnp.zeros_like(rate)
    for gap in range(STEPS):
        if gap:
            since = since + earlier(rate, gap - 1)
        products = c_values * earlier(b_values, gap)
        pair = jnp.zeros((rows, heads), F32)
        for g in range(groups):
            score = jnp.sum(products[:, g * N : (g + 1) * N], axis=1, keepdims=True)
            pair = jnp.where(head // per_group == g, score, pair)
        factor = jnp.where(turn >= gap, jnp.exp2(since) * earlier(step, gap) * pair, 0.0)
        fresh = fresh + over_lanes(factor, 0, width) * earlier(x_values, gap)
    for i in range(rows // STEPS):
        keep_ref[i] = keep[i * STEPS : (i + 1) * STEPS]
        fresh_ref[i] = fresh[i * STEPS : (i + 1) * STEPS]
        held_ref[i] = held[i * STEPS : (i + 1) * STEPS]


def finish_kernel(ops, keep_ref, fresh_ref, held_ref, *rest):
    count = keep_ref.shape[0]
    back_refs, own_ref, out_ref = rest[: len(ops)], rest[len(ops)], rest[-1]
    me = lax.axis_index("seq")

    def finish(source, reading):
        value = reading * keep_ref[source] + fresh_ref[source]
        held = held_ref[source][:, :1] > 0.0
        out_ref[source] = jnp.where(held, value, 0.0).astype(BF16)

    if isinstance(ops[0], tuple):
        for source in range(count):
            reading = own_ref[...]
            for (one, other), back_ref in zip(ops, back_refs):
                if source in (one, other):
                    owner = one + other - source
                    reading = jnp.where(me == owner, back_ref[...], reading)
            finish(source, reading)
    else:
        finish(me, own_ref[...])
        for r, back_ref in zip(ops, back_refs):
            finish(lax.rem(me + r, count), back_ref[...])


def shards(
    ssm_input, bmat, cmat, dt_raw, a_log, d_skip, prompt_len, owner, dec_x, dec_b, dec_c, dec_dt
):
    count = lax.axis_size("seq")
    tensor = lax.axis_size("tp")
    tokens, heads = dt_raw.shape
    groups = heads // (H // G)
    names = groups * N
    lanes = heads * P_SIZE
    group_lanes = lanes // groups
    rows = count * STEPS
    chunks = CHUNKS if count <= 4 else groups
    width = lanes // chunks
    anywhere = pl.BlockSpec(memory_space=pl.ANY)
    in_hbm = pl.BlockSpec(memory_space=pltpu.HBM)
    in_vmem = pl.BlockSpec(memory_space=pltpu.VMEM)
    ride = count == 4 and width == 2 * names

    def sent_shape(k):
        return shape((N + rows * (ride and k == 0), width), BF16)

    inputs = [
        ssm_input,
        bmat,
        a_log.reshape(1, heads),
        dec_c[0],
        cmat,
        d_skip.reshape(1, heads),
        prompt_len.reshape(1, -1),
        owner.reshape(1, -1),
        dec_x[0],
        dec_b[0],
        dec_dt[0],
    ]
    chunk_shapes = [
        (shape((N, width)), sent_shape(k), shape((1, width))) for k in range(chunks)
    ]
    results = call(
        functools.partial(first_kernel, len(inputs), ride),
        tuple(shape(value.shape, value.dtype) for value in inputs)
        + (
            shape((heads, tokens)),
            shape((heads, tokens)),
            shape((tokens, heads)),
            shape((1, heads)),
            shape((groups, N, tokens), BF16),
        )
        + chunk_shapes[0],
        in_specs=[in_hbm] * (len(inputs) + 1),
        scratch_shapes=[
            pltpu.VMEM((heads, tokens), BF16),
            pltpu.SemaphoreType.DMA((len(inputs) + 2,)),
        ],
    )(*[pinned(value, pltpu.HBM) for value in inputs + [dt_raw.T]])
    x, b, a_row, asked_here, c, d_row, len_row, owner_row, x_dec, b_dec, dt_dec = results[:11]
    cum, row, weight, whole, turned = results[11:16]
    total, sent, decay = ([value] for value in results[16:])

    def state_part(k, tie):
        part = call(
            functools.partial(state_kernel, k),
            chunk_shapes[k],
            in_specs=[in_vmem] * 4 + [anywhere],
        )(x, turned, weight, whole, tie)
        for values, value in zip((total, sent, decay), part):
            values.append(value)

    def swap(value, *couples):
        partner = {}
        for one, other in couples:
            partner.update({one: other, other: one})
        pairs = []
        for d in range(count):
            for t in range(tensor):
                there = partner[d] * tensor + t if d in partner else d * tensor + (t ^ 1)
                pairs.append((d * tensor + t, there))
        return lax.ppermute(value, ("seq", "tp"), pairs)

    def forward(value, hop, k):
        rides = ride and k == 0 and hop != 2
        return swap(value, *([(0, 1), (2, 3)] if rides else [(hop - 1, hop)]))

    def shift(value, by):
        return lax.ppermute(value, "seq", [(d, (d + by) % count) for d in range(count)])

    def inner_part(g, *after):
        return call(
            functools.partial(inner_kernel, g),
            shape((tokens, group_lanes)),
            in_specs=[in_vmem] * 6 + [anywhere] * len(after),
        )(x, b, c, cum, row, d_row, *after)

    def ask_part(*after):
        blocks = (moving[2, 0], got[2, 0], got[3, 0]) if ride else asks
        return call(
            functools.partial(ask_kernel, count, ride),
            (shape((rows, lanes)), shape((rows, heads)), shape((rows, names), BF16)),
            in_specs=[in_vmem] * (6 + len(blocks)) + [anywhere] * len(after),
        )(x, b, cum, row, len_row, owner_row, *blocks, *after)

    def fresh_part(*after):
        return call(
            functools.partial(fresh_kernel, tokens),
            (shape((count, STEPS, lanes)),) * 2 + (shape((count, STEPS, 128)),),
            in_specs=[in_vmem] * 8 + [anywhere] * len(after),
        )(x_dec, b_dec, asked_here, dt_dec, a_row, d_row, len_row, owner_row, *after)

    def outer_part(parts, carry, before, *after):
        part = parts[-1]
        out = shape((len(part), tokens, width), BF16)
        operands = [c, cum, carry, *[got[count - 1, k] for k in part], *inner, *before]
        return call(
            functools.partial(outer_kernel, parts, count),
            (pltpu.HBM((tokens, lanes), BF16), shape((8, 128))) if before else out,
            in_specs=[in_vmem] * len(operands) + [anywhere] * len(after),
            out_specs=(in_hbm, in_vmem) if before else in_vmem,
            scratch_shapes=[out, pltpu.SemaphoreType.DMA((chunks,))] if before else [],
        )(*operands, *after)

    def read_part(ops, final, *after):
        arrived = [got[count - 1, k] for k in range(chunks)] if final else []
        operands = [local, gain, asked, carry, *arrived]
        return call(
            functools.partial(read_kernel, count, chunks, ops, final),
            (shape((STEPS, lanes)),) * (len(ops) + final),
            in_specs=[in_vmem] * len(operands) + [anywhere] * len(after),
        )(*operands, *after)

    got = {(1, 0): forward(sent[0], 1, 0)}
    moving = {}
    inner = [inner_part(0)]
    state_part(1, inner[0])
    got[1, 1] = forward(sent[1], 1, 1)
    inner += [inner_part(g, sent[1]) for g in range(1, groups)]
    if not ride:
        asks = [asked_here] + [shift(asked_here, r) for r in range(1, count)]
    order = sorted((k + hop, hop, k) for hop in range(1, count - 1) for k in range(chunks))
    early, late = tuple(range(chunks // 2)), tuple(range(chunks // 2, chunks))
    after = inner[-1:]
    carry = tie = None
    for _, hop, k in order:
        if (hop, k) == (1, 1):
            keep, fresh, held = fresh_part(tie)
            after = [keep]
        if (hop, k) == (count - 2, chunks - 2):
            local, gain, asked = ask_part(tie)
            after = [gain]
        if (hop, k) == (count - 2, chunks - 1):
            outer = outer_part((early,), carry, [], tie)
            after = [outer]
        tail = [sent[0]] if ride and (hop, k) == (1, 0) else []
        filed = [] if carry is None else [carry]
        moving[hop + 1, k], carry = call(
            functools.partial(pass_kernel, hop, k, ride),
            (sent_shape(k), shape((chunks, N, width), BF16)),
            in_specs=[in_vmem] * (3 + len(filed) + len(tail)) + [anywhere] * len(after),
            input_output_aliases={3: 1} if filed else {},
        )(got[hop, k], total[k], decay[k], *filed, *tail, *after)
        got[hop + 1, k] = forward(moving[hop + 1, k], hop + 1, k)
        tie, after = moving[hop + 1, k], []
        if hop == 1 and k + 2 < chunks:
            state_part(k + 2, tie)
            got[1, k + 2] = forward(sent[k + 2], 1, k + 2)

    back = []
    if ride:
        ops = [(0, 1), (0, 2), (1, 2)]
        first_readings = read_part(ops, False, tie, got[count - 1, chunks - 2])
        for (one, other), value in zip(ops, first_readings):
            back.append(swap(value, (one, other)))
        ends = [(0, 3), (1, 3), (2, 3)]
        *reading, own = read_part(ends, True, first_readings[0])
        for (one, other), value in zip(ends, reading):
            back.append(swap(value, (one, other)))
        ops = ops + ends
    else:
        *reading, own = read_part([(r, r) for r in range(count)], True)
        ops = list(range(1, count))
        back, own = [shift(reading[r], -r) for r in ops], reading[0]
    prefill, token = outer_part((early, late), carry, [outer])

    decoded = call(
        functools.partial(finish_kernel, ops),
        jax.ShapeDtypeStruct((count, STEPS, lanes), BF16),
        in_specs=[in_vmem] * (4 + len(ops)) + [anywhere],
    )(keep, fresh, held, *back, own, token)
    return (prefill, decoded[None])


def solution(mesh):
    placed = (
        P(("grp", "seq"), "tp"),
        P(("grp", "seq"), "tp"),
        P(("grp", "seq"), "tp"),
        P(("grp", "seq"), "tp"),
        P("tp"),
        P("tp"),
        P("grp"),
        P("grp"),
        P(("grp", "seq"), None, None, "tp"),
        P(("grp", "seq"), None, None, "tp"),
        P(("grp", "seq"), None, None, "tp"),
        P(("grp", "seq"), None, None, "tp"),
    )
    return jax.shard_map(
        shards,
        mesh=mesh,
        in_specs=placed,
        out_specs=(P(("grp", "seq"), "tp"), P(("grp", "seq"), None, None, "tp")),
        check_vma=False,
    )
```

```python
import functools
import math

import jax
import jax.numpy as jnp
from jax import lax
from jax.experimental import pallas as pl
from jax.experimental.pallas import tpu as pltpu
from jax.sharding import PartitionSpec as P

H = 128
P_SIZE = 64
N = 128
G = 8
SPAN = 128
STEPS = 4
LOG2E = math.log2(math.e)
F32 = jnp.float32
BF16 = jnp.bfloat16
CHUNKS = 4
VMEM_LIMIT = 32 * 1024 * 1024


def softplus(value):
    small = jnp.exp(-jnp.abs(value))
    series = small * (1.0 - small * (0.5 - small * (1.0 / 3.0 - small * 0.25)))
    return jnp.maximum(value, 0.0) + jnp.where(small < 0.02, series, jnp.log(1.0 + small))


def dot(left, right, left_dim=1, right_dim=0):
    return lax.dot_general(
        left, right, (((left_dim,), (right_dim,)), ((), ())), preferred_element_type=F32
    )


def split(value, pieces):
    result = []
    for _ in range(pieces):
        piece = value.astype(BF16)
        result.append(piece)
        value = value - piece.astype(F32)
    return result


def exact_dot(ones, value, pieces=3, left_dim=1):
    return sum(dot(ones, piece, left_dim) for piece in split(value, pieces))


def spread_matrix(heads, first, width):
    lane = lax.broadcasted_iota(jnp.int32, (heads, width), 1) + first
    head = lax.broadcasted_iota(jnp.int32, (heads, width), 0)
    return jnp.where(lane // P_SIZE == head, 1.0, 0.0).astype(BF16)


def over_lanes(value, first, width, pieces=2):
    return exact_dot_right(value, spread_matrix(value.shape[1], first, width), pieces)


def exact_dot_right(value, ones, pieces):
    return sum(dot(piece, ones) for piece in split(value, pieces))


def shape(dims, dtype=F32):
    return pltpu.VMEM(dims, dtype)


def pinned(value, space=pltpu.VMEM):
    return pltpu.with_memory_space_constraint(value, space)


def call(kernel, out_shape, flops=1, **options):
    return pl.pallas_call(
        kernel,
        out_shape=out_shape,
        compiler_params=pltpu.CompilerParams(vmem_limit_bytes=VMEM_LIMIT),
        cost_estimate=pl.CostEstimate(flops=flops, bytes_accessed=1, transcendentals=0),
        **options,
    )


def triangle(keep):
    row = lax.broadcasted_iota(jnp.int32, (SPAN, SPAN), 0)
    column = lax.broadcasted_iota(jnp.int32, (SPAN, SPAN), 1)
    return jnp.where(keep(row, column), 1.0, 0.0).astype(BF16)


def chunk_total(k, x_ref, turned, weight, whole, total_ref, decay_ref):
    width = total_ref.shape[1]
    first = k * width
    scaled = x_ref[:, first : first + width].astype(F32) * over_lanes(weight, first, width)
    total_ref[...] = dot(turned, scaled.astype(BF16))
    decay_ref[...] = over_lanes(whole, first, width, 3)


def first_kernel(kept, ride, *refs):
    hbm, refs = refs[: kept + 1], refs[kept + 1 :]
    here, refs = refs[:kept], refs[kept:]
    cum_ref, row_ref, weight_ref, whole_ref, turned_ref = refs[:5]
    total_ref, decay_ref, sent_ref, dt_ref, sems = refs[5:]
    x_ref, b_ref, a_ref, asked_ref = here[:4]
    heads, tokens = dt_ref.shape
    spans = tokens // SPAN
    width = total_ref.shape[1]
    dt_copy = pltpu.make_async_copy(hbm[kept], dt_ref, sems.at[0])
    copies = [pltpu.make_async_copy(hbm[i], here[i], sems.at[i]) for i in range(1, kept)]
    x_copies = [
        pltpu.make_async_copy(hbm[0].at[:, lanes], x_ref.at[:, lanes], sems.at[kept + i])
        for i, lanes in enumerate((slice(0, width), slice(width, x_ref.shape[1])))
    ]
    for copy in [dt_copy, copies[1], copies[0], *x_copies, *copies[2:]]:
        copy.start()
    upper = triangle(lambda s, t: s <= t)
    eye = lax.broadcasted_iota(jnp.int32, (heads, heads), 0) == lax.broadcasted_iota(
        jnp.int32, (heads, heads), 1
    )
    dt_copy.wait()
    copies[1].wait()
    a_column = jnp.sum(jnp.where(eye, a_ref[...], 0.0), axis=1, keepdims=True)
    step = softplus(dt_ref[...].astype(F32))
    rate = step * (jnp.exp(a_column) * -LOG2E)
    cums = [exact_dot_right(rate[:, i * SPAN : (i + 1) * SPAN], upper, 3) for i in range(spans)]
    ends = [cum[:, SPAN - 1 : SPAN] for cum in cums]
    after = jnp.zeros_like(ends[0])
    weights = [None] * spans
    for i in reversed(range(spans)):
        after = after + ends[i]
        weights[i] = jnp.exp2(after - cums[i]) * step[:, i * SPAN : (i + 1) * SPAN]
    weight = jnp.concatenate(weights, axis=1).T
    whole = jnp.sum(jnp.where(eye, jnp.exp2(after), 0.0), axis=0, keepdims=True)
    weight_ref[...] = weight
    whole_ref[...] = whole
    copies[0].wait()
    turned = b_ref[:, :N].astype(F32).T.astype(BF16)
    x_copies[0].wait()
    chunk_total(0, x_ref, turned, weight, whole, total_ref, decay_ref)
    sent_ref[:N] = total_ref[...].astype(BF16)
    turned_ref[0] = turned
    for g in range(1, turned_ref.shape[0]):
        turned_ref[g] = b_ref[:, g * N : (g + 1) * N].astype(F32).T.astype(BF16)
    cum = jnp.concatenate(cums, axis=1)
    cum_ref[...] = cum
    row_ref[...] = jnp.log2(step) - cum
    x_copies[1].wait()
    for copy in copies[2:]:
        copy.wait()
    if ride:
        own = flat(asked_ref).astype(BF16)
        sent_ref[N:] = jnp.concatenate([own, own], axis=1)


def state_kernel(part, first, x_ref, turned_ref, weight_ref, whole_ref, *rest):
    results = rest[-2 * len(part) - first :]
    for i, k in enumerate(part):
        total_ref, decay_ref = results[2 * i : 2 * i + 2]
        g = k * total_ref.shape[1] // (H // G * P_SIZE)
        chunk_total(k, x_ref, turned_ref[g], weight_ref[...], whole_ref[...], total_ref, decay_ref)
    if first:
        results[-1][...] = results[0][...].astype(BF16)


def flat(ref):
    return jnp.concatenate([ref[i].astype(F32) for i in range(ref.shape[0])], axis=0)


def token_kernel(got_ref, tie_ref, token_ref):
    token_ref[...] = jnp.zeros_like(token_ref)


def pass_kernel(hop, k, tail, more, got_ref, total_ref, decay_ref, *rest):
    extra, (moving_ref, carry_ref) = rest, rest[-2 - more : len(rest) - more]
    me = lax.axis_index("seq")
    if hop == 1 and k == 0:
        carry_ref[...] = jnp.zeros_like(carry_ref)
    else:
        extra = extra[1:]
    got = got_ref[:N]
    moving_ref[:N] = (total_ref[...] + decay_ref[...] * got.astype(F32)).astype(BF16)

    @pl.when(me == hop)
    def _():
        carry_ref[k] = got

    if more:
        rest[-1][...] = extra[0][...].astype(BF16)
        extra = extra[1:]
    if tail:
        rows = extra[0][N:]
        if hop == 1:
            lane = lax.broadcasted_iota(jnp.int32, rows.shape, 1)
            mine = (lane // (rows.shape[1] // 2)) == lax.rem(me, 2)
            rows = jnp.where(mine, rows.astype(F32), got_ref[N:].astype(F32)).astype(BF16)
        moving_ref[N:] = rows


def pair_halves(x_part):
    first_half = lax.broadcasted_iota(jnp.int32, (1, 2 * P_SIZE), 1) < P_SIZE
    zero = jnp.zeros_like(x_part)
    return jnp.where(first_half, x_part, zero), jnp.where(first_half, zero, x_part)


def span_starts(cum, spans):
    ends = [cum[(i + 1) * SPAN - 1 : (i + 1) * SPAN, :] for i in range(spans)]
    starts = [jnp.zeros_like(ends[0])]
    for i in range(spans):
        starts.append(starts[i] + ends[i])
    return ends, starts


def inner_kernel(g, x_ref, b_ref, c_ref, cum_ref, row_ref, d_ref, *rest):
    inner_ref = rest[-1]
    heads, tokens = cum_ref.shape
    spans = tokens // SPAN
    per_group = H // G
    names = slice(g * N, (g + 1) * N)
    t_index = lax.broadcasted_iota(jnp.int32, (SPAN, SPAN), 0)
    s_index = lax.broadcasted_iota(jnp.int32, (SPAN, SPAN), 1)
    causal = t_index >= s_index
    rows = row_ref[...]
    cum = cum_ref[...].T
    ends, _ = span_starts(cum, spans)
    first_half = lax.broadcasted_iota(jnp.int32, (1, 2 * P_SIZE), 1) < P_SIZE
    scores = dot(c_ref[:, names], b_ref[:, names], 1, 1)
    for pair in range(per_group // 2):
        h0 = g * per_group + 2 * pair
        lanes = slice(h0 * P_SIZE, (h0 + 2) * P_SIZE)
        here = slice(2 * pair * P_SIZE, (2 * pair + 2) * P_SIZE)
        x_part = x_ref[:, lanes]
        halves = pair_halves(x_part)
        weights = [[None, None] for _ in range(spans)]
        for e in range(2):
            h = h0 + e
            row = rows[h : h + 1, :]
            for i in range(spans):
                column = jnp.broadcast_to(cum[i * SPAN : (i + 1) * SPAN, h : h + 1], (SPAN, SPAN))
                parts = []
                for j in range(i + 1):
                    shift = row[:, j * SPAN : (j + 1) * SPAN]
                    for m in range(j, i):
                        shift = shift + ends[m][:, h : h + 1]
                    score = scores[i * SPAN : (i + 1) * SPAN, j * SPAN : (j + 1) * SPAN]
                    part = score * jnp.exp2(column + shift)
                    if i == j:
                        part = jnp.where(causal, part, 0.0)
                    parts.append(part.astype(BF16))
                weights[i][e] = jnp.concatenate(parts, axis=1) if i else parts[0]
        skip = jnp.where(first_half, d_ref[:, h0 : h0 + 1], d_ref[:, h0 + 1 : h0 + 2])
        for i in range(spans):
            reach = (i + 1) * SPAN
            left = jnp.concatenate(weights[i], axis=1)
            right = jnp.concatenate([half[:reach] for half in halves], axis=0)
            mine = slice(i * SPAN, (i + 1) * SPAN)
            inner_ref[mine, here] = dot(left, right) + skip * x_part[mine].astype(F32)


def ask_kernel(count, ride, x_ref, b_ref, cum_ref, row_ref, len_ref, owner_ref, *rest):
    local_ref, gain_ref, asked_ref = rest[-3:]
    heads, tokens = cum_ref.shape
    spans = tokens // SPAN
    asks = local_ref.shape[0]
    per_group = H // G
    groups = heads // per_group
    me = lax.axis_index("seq")
    if ride:
        near, middle, far = [ref[N:].astype(F32) for ref in rest[:3]]
        far = jnp.where((me == 1) | (me == 2), middle, far)
        halves = (jnp.where(me < 2, near, far), jnp.where(me < 2, far, near))
        names = near.shape[1] // 2
        blocks = [half[:, i * names : (i + 1) * names] for half in halves for i in range(2)]
    else:
        blocks = [flat(ref) for ref in rest[:count]]
    blocks = jnp.concatenate(blocks, axis=0).astype(BF16)
    row = lax.broadcasted_iota(jnp.int32, (asks, asks * count), 0)
    column = lax.broadcasted_iota(jnp.int32, (asks, asks * count), 1)
    place = row // STEPS
    wanted = place * asks + me * STEPS + row % STEPS
    asked = dot(jnp.where(column == wanted, 1.0, 0.0).astype(BF16), blocks).astype(BF16)
    asked_ref[...] = asked
    block = lax.broadcasted_iota(jnp.int32, (asks, 1), 0) // STEPS
    spot = len_ref[...] - 1 - me * tokens
    mine = (owner_ref[...] == (block if ride else lax.rem(me + count - block, count))) & (spot >= 0) & (spot < tokens)
    spot = jnp.sum(jnp.where(mine, spot, 0).astype(F32), axis=1, keepdims=True).astype(jnp.int32)
    position = lax.broadcasted_iota(jnp.int32, (asks, tokens), 1)
    picked = jnp.where(position == spot, 1.0, 0.0).astype(BF16)
    upto = position <= spot
    rows = row_ref[...]
    cum = cum_ref[...].T
    ends, starts = span_starts(cum, spans)
    near_ask = exact_dot(picked, cum)
    ask_start = starts[0]
    for i in range(1, spans):
        ask_start = jnp.where(spot >= i * SPAN, starts[i], ask_start)
    gain_ref[...] = jnp.exp2(near_ask + ask_start)
    columns = []
    for j in range(spans):
        column = near_ask
        for i in range(j + 1, spans):
            column = jnp.where(spot // SPAN == i, near_ask + sum(ends[j + 1 : i], ends[j]), column)
        columns.append(column)
    for g in range(groups):
        names = slice(g * N, (g + 1) * N)
        scores = jnp.where(upto, dot(asked[:, names], b_ref[:, names], 1, 1), 0.0)
        for pair in range(per_group // 2):
            h0 = g * per_group + 2 * pair
            lanes = slice(h0 * P_SIZE, (h0 + 2) * P_SIZE)
            parts = []
            for h in (h0, h0 + 1):
                for j in range(spans):
                    span = slice(j * SPAN, (j + 1) * SPAN)
                    part = scores[:, span] * jnp.exp2(columns[j][:, h : h + 1] + rows[h : h + 1, span])
                    parts.append(jnp.where(upto[:, span], part, 0.0).astype(BF16))
            right = jnp.concatenate(pair_halves(x_ref[:, lanes]), axis=0)
            local_ref[:, lanes] = dot(jnp.concatenate(parts, axis=1), right)


def read_kernel(count, chunks, ops, final, local_ref, gain_ref, asked_ref, carry_ref, *rest):
    got_refs, rest = rest[: chunks * final], rest[chunks * final :]
    read_refs = rest[-(len(ops) + final) :]
    me = lax.axis_index("seq")
    lanes = local_ref.shape[1]
    width = lanes // chunks
    for k in range(chunks):
        first = k * width
        here = slice(first, first + width)
        g = first // (H // G * P_SIZE)
        state = carry_ref[k]
        if final:
            state = jnp.where(me == count - 1, got_refs[k][:N], state)
        carried = dot(asked_ref[:, g * N : (g + 1) * N], state)
        reading = local_ref[:, here] + over_lanes(gain_ref[...], first, width) * carried
        parts = [reading[r * STEPS : (r + 1) * STEPS] for r in range(count)]
        for (one, other), read_ref in zip(ops, read_refs):
            part = parts[other]
            if one != other:
                part = jnp.where(me == one, part, parts[one])
            read_ref[:, here] = part.astype(read_ref.dtype)
        if final:
            own = parts[0]
            for r in range(1, count):
                own = jnp.where(me == r, parts[r], own)
            read_refs[-1][:, here] = own


def outer_kernel(parts, count, c_ref, cum_ref, carry_ref, *rest):
    final = len(parts) > 1
    part = parts[-1]
    got_refs = rest[: len(part)]
    inner_refs = rest[len(part) : len(part) + cum_ref.shape[0] // (H // G)]
    if final:
        early_ref, out_hbm, token_ref, out_ref, sems = rest[-5:]
        token_ref[...] = jnp.zeros_like(token_ref)
    else:
        out_ref = rest[-1]
    heads, tokens = cum_ref.shape
    spans = tokens // SPAN
    width = got_refs[0].shape[1]
    group_lanes = H // G * P_SIZE
    copies = []

    def send(source, k):
        lanes = slice(k * width, (k + 1) * width)
        copies.append(pltpu.make_async_copy(source, out_hbm.at[:, lanes], sems.at[k]))
        copies[-1].start()

    if final:
        for i, k in enumerate(parts[0]):
            send(early_ref.at[i], k)
    last = lax.axis_index("seq") == count - 1
    start = jnp.zeros((heads, 1), F32)
    gains = []
    for i in range(spans):
        cum = cum_ref[:, i * SPAN : (i + 1) * SPAN]
        gains.append(jnp.exp2(cum + start))
        start = start + cum[:, SPAN - 1 : SPAN]
    gain = jnp.concatenate(gains, axis=1).T
    for i, k in enumerate(part):
        first = k * width
        g = first // group_lanes
        state = jnp.where(last, got_refs[i][:N], carry_ref[k])
        carried = dot(c_ref[:, g * N : (g + 1) * N], state)
        inner = inner_refs[g][:, first - g * group_lanes : first - g * group_lanes + width]
        out_ref[i] = (inner + over_lanes(gain, first, width) * carried).astype(BF16)
        if final:
            send(out_ref.at[i], k)
    for copy in copies:
        copy.wait()


def fresh_kernel(tokens, x_ref, b_ref, c_ref, dt_ref, a_ref, d_ref, len_ref, owner_ref, *rest):
    keep_ref, fresh_ref, held_ref = rest[-3:]
    count, _, heads = dt_ref.shape
    rows = count * STEPS
    place = lax.broadcasted_iota(jnp.int32, (rows, 1), 0) // STEPS * tokens
    spot = len_ref[...] - 1 - place
    mine = (owner_ref[...] == lax.axis_index("seq")) & (spot >= 0) & (spot < tokens)
    held = jnp.sum(jnp.where(mine, 1.0, 0.0), axis=1, keepdims=True)
    held = jnp.broadcast_to(held, (rows, held_ref.shape[2]))
    per_group = H // G
    groups = heads // per_group
    width = x_ref.shape[2]
    turn = lax.broadcasted_iota(jnp.int32, (rows, 1), 0) % STEPS
    step = softplus(flat(dt_ref))
    rate = step * (jnp.exp(a_ref[...]) * -LOG2E)

    def earlier(value, gap):
        if not gap:
            return value
        moved = jnp.concatenate([jnp.zeros_like(value[:gap]), value[:-gap]], axis=0)
        return jnp.where(turn >= gap, moved, 0.0)

    running = sum(earlier(rate, gap) for gap in range(STEPS))
    keep = over_lanes(jnp.exp2(running), 0, width)
    x_values = flat(x_ref)
    b_values = flat(b_ref)
    c_values = flat(c_ref)
    head = lax.broadcasted_iota(jnp.int32, (rows, heads), 1)
    fresh = over_lanes(d_ref[...], 0, width, 3) * x_values
    since = jnp.zeros_like(rate)
    for gap in range(STEPS):
        if gap:
            since = since + earlier(rate, gap - 1)
        products = c_values * earlier(b_values, gap)
        pair = jnp.zeros((rows, heads), F32)
        for g in range(groups):
            score = jnp.sum(products[:, g * N : (g + 1) * N], axis=1, keepdims=True)
            pair = jnp.where(head // per_group == g, score, pair)
        factor = jnp.where(turn >= gap, jnp.exp2(since) * earlier(step, gap) * pair, 0.0)
        fresh = fresh + over_lanes(factor, 0, width) * earlier(x_values, gap)
    for i in range(rows // STEPS):
        keep_ref[i] = keep[i * STEPS : (i + 1) * STEPS]
        fresh_ref[i] = fresh[i * STEPS : (i + 1) * STEPS]
        held_ref[i] = held[i * STEPS : (i + 1) * STEPS]


def finish_kernel(ops, keep_ref, fresh_ref, held_ref, *rest):
    count = keep_ref.shape[0]
    back_refs, own_ref, out_ref = rest[: len(ops)], rest[len(ops)], rest[-1]
    me = lax.axis_index("seq")

    def finish(source, reading):
        value = reading * keep_ref[source] + fresh_ref[source]
        held = held_ref[source][:, :1] > 0.0
        out_ref[source] = jnp.where(held, value, 0.0).astype(BF16)

    if isinstance(ops[0], tuple):
        for source in range(count):
            reading = own_ref[...]
            for (one, other), back_ref in zip(ops, back_refs):
                if source in (one, other):
                    owner = one + other - source
                    reading = jnp.where(me == owner, back_ref[...].astype(F32), reading)
            finish(source, reading)
    else:
        finish(me, own_ref[...])
        for r, back_ref in zip(ops, back_refs):
            finish(lax.rem(me + r, count), back_ref[...].astype(F32))


def shards(
    ssm_input, bmat, cmat, dt_raw, a_log, d_skip, prompt_len, owner, dec_x, dec_b, dec_c, dec_dt
):
    count = lax.axis_size("seq")
    tensor = lax.axis_size("tp")
    tokens, heads = dt_raw.shape
    groups = heads // (H // G)
    names = groups * N
    lanes = heads * P_SIZE
    group_lanes = lanes // groups
    rows = count * STEPS
    chunks = CHUNKS if count <= 4 else groups
    width = lanes // chunks
    anywhere = pl.BlockSpec(memory_space=pl.ANY)
    in_hbm = pl.BlockSpec(memory_space=pltpu.HBM)
    in_vmem = pl.BlockSpec(memory_space=pltpu.VMEM)
    ride = count == 4 and width == 2 * names

    def sent_shape(hop, k):
        tail = ride and (hop, k) in ((1, 0), (2, 0), (3, 2))
        return shape((N + rows * tail, width), BF16)

    inputs = [
        ssm_input,
        bmat,
        a_log.reshape(1, heads),
        dec_c[0],
        cmat,
        d_skip.reshape(1, heads),
        prompt_len.reshape(1, -1),
        owner.reshape(1, -1),
        dec_x[0],
        dec_b[0],
        dec_dt[0],
    ]
    chunk_shapes = (shape((N, width)), shape((1, width)))
    results = call(
        functools.partial(first_kernel, len(inputs), ride),
        tuple(shape(value.shape, value.dtype) for value in inputs)
        + (
            shape((heads, tokens)),
            shape((heads, tokens)),
            shape((tokens, heads)),
            shape((1, heads)),
            shape((groups, N, tokens), BF16),
        )
        + chunk_shapes
        + (sent_shape(1, 0),),
        in_specs=[in_hbm] * (len(inputs) + 1),
        scratch_shapes=[
            pltpu.VMEM((heads, tokens), BF16),
            pltpu.SemaphoreType.DMA((len(inputs) + 2,)),
        ],
    )(*[pinned(value, pltpu.HBM) for value in inputs + [dt_raw.T]])
    x, b, a_row, asked_here, c, d_row, len_row, owner_row, x_dec, b_dec, dt_dec = results[:11]
    cum, row, weight, whole, turned = results[11:16]
    total, decay = [results[16]], [results[17]]
    sent = {0: results[18]}

    def state_part(part, tie):
        first = part[0] == 1
        out = call(
            functools.partial(state_kernel, part, first),
            chunk_shapes * len(part) + (sent_shape(1, 1),) * first,
            in_specs=[in_vmem] * 4 + [anywhere],
        )(x, turned, weight, whole, tie)
        total.extend(out[0 : 2 * len(part) : 2])
        decay.extend(out[1 : 2 * len(part) : 2])
        if first:
            sent[1] = out[-1]

    def swap(value, *couples):
        partner = {}
        for one, other in couples:
            partner.update({one: other, other: one})
        pairs = []
        for d in range(count):
            for t in range(tensor):
                there = partner[d] * tensor + t if d in partner else d * tensor + (t ^ 1)
                pairs.append((d * tensor + t, there))
        return lax.ppermute(value, ("seq", "tp"), pairs)

    def forward(value, hop, k):
        rides = ride and (hop, k) in ((1, 0), (3, 2))
        return swap(value, *([(0, 1), (2, 3)] if rides else [(hop - 1, hop)]))

    def shift(value, by):
        return lax.ppermute(value, "seq", [(d, (d + by) % count) for d in range(count)])

    def inner_part(g, *after):
        return call(
            functools.partial(inner_kernel, g),
            shape((tokens, group_lanes)),
            in_specs=[in_vmem] * 6 + [anywhere] * len(after),
        )(x, b, c, cum, row, d_row, *after)

    def ask_part(*after):
        blocks = (moving[2, 0], got[2, 0], got[3, 2]) if ride else asks
        return call(
            functools.partial(ask_kernel, count, ride),
            (shape((rows, lanes)), shape((rows, heads)), shape((rows, names), BF16)),
            in_specs=[in_vmem] * (6 + len(blocks)) + [anywhere] * len(after),
        )(x, b, cum, row, len_row, owner_row, *blocks, *after)

    def fresh_part(*after):
        return call(
            functools.partial(fresh_kernel, tokens),
            (shape((count, STEPS, lanes)),) * 2 + (shape((count, STEPS, 128)),),
            in_specs=[in_vmem] * 8 + [anywhere] * len(after),
        )(x_dec, b_dec, asked_here, dt_dec, a_row, d_row, len_row, owner_row, *after)

    def outer_part(parts, carry, before, *after):
        part = parts[-1]
        out = shape((len(part), tokens, width), BF16)
        operands = [c, cum, carry, *[got[count - 1, k] for k in part], *inner, *before]
        return call(
            functools.partial(outer_kernel, parts, count),
            (pltpu.HBM((tokens, lanes), BF16), shape((8, 128))) if before else out,
            in_specs=[in_vmem] * len(operands) + [anywhere] * len(after),
            out_specs=(in_hbm, in_vmem) if before else in_vmem,
            scratch_shapes=[out, pltpu.SemaphoreType.DMA((chunks,))] if before else [],
        )(*operands, *after)

    def read_part(ops, final, *after):
        arrived = [got[count - 1, k] for k in range(chunks)] if final else []
        operands = [local, gain, asked, carry, *arrived]
        return call(
            functools.partial(read_kernel, count, chunks, ops, final),
            (shape((STEPS, lanes), BF16),) * len(ops) + (shape((STEPS, lanes)),) * final,
            in_specs=[in_vmem] * len(operands) + [anywhere] * len(after),
        )(*operands, *after)

    got = {(1, 0): forward(sent[0], 1, 0)}
    moving = {}
    inner = [inner_part(0)]
    for g in range(1, groups):
        inner.append(inner_part(g, inner[-1]))
    state_part([1], inner[-1])
    got[1, 1] = forward(sent[1], 1, 1)
    if chunks > 2:
        state_part(list(range(2, chunks)), sent[1])
    keep, fresh, held = fresh_part(total[-1])
    if not ride:
        asks = [asked_here] + [shift(asked_here, r) for r in range(1, count)]
    order = sorted((k + hop, hop, k) for hop in range(1, count - 1) for k in range(chunks))
    carry = tie = None
    for _, hop, k in order:
        tail = {(1, 0): sent[0], (2, 2): got.get((2, 0))}.get((hop, k)) if ride else None
        more = hop == 1 and k + 2 < chunks
        operands = [got[hop, k], total[k], decay[k]]
        operands += [] if carry is None else [carry]
        operands += total[k + 2 : k + 3] * more + [tail] * (tail is not None)
        after = [keep] if carry is None else []
        if hop == count - 2 and k > 1:
            after.append(
                call(
                    token_kernel, shape((8, 128)), flops=10**9, in_specs=[anywhere] * 2
                )(got[hop + 1, k - 2], tie)
            )
        moving[hop + 1, k], carry, *following = call(
            functools.partial(pass_kernel, hop, k, tail is not None, more),
            (sent_shape(hop + 1, k), shape((chunks, N, width), BF16))
            + (sent_shape(1, k + 2),) * more,
            in_specs=[in_vmem] * len(operands) + [anywhere] * len(after),
            input_output_aliases={} if carry is None else {3: 1},
        )(*operands, *after)
        got[hop + 1, k] = forward(moving[hop + 1, k], hop + 1, k)
        tie = moving[hop + 1, k]
        if more:
            got[1, k + 2] = forward(following[0], 1, k + 2)

    early, late = tuple(range(chunks // 2)), tuple(range(chunks // 2, chunks))
    local, gain, asked = ask_part(tie)

    back = []
    if ride:
        ops, ends = [(0, 1), (0, 2), (1, 2)], [(0, 3), (1, 3), (2, 3)]
        reading = read_part(ops, False)
        for couple, value in zip(ops, reading):
            back.append(swap(value, couple))
        outer = outer_part((early,), carry, [], reading[0])
        *reading, own = read_part(ends, True, outer, *back)
        for couple, value in zip(ends, reading):
            back.append(swap(value, couple))
        ops = ops + ends
    else:
        outer = outer_part((early,), carry, [])
        *reading, own = read_part([(r, r) for r in range(count)], True)
        ops = list(range(1, count))
        back = [shift(reading[r], -r) for r in ops]
        own = reading[0].astype(F32)
    prefill, token = outer_part((early, late), carry, [outer])

    decoded = call(
        functools.partial(finish_kernel, ops),
        jax.ShapeDtypeStruct((count, STEPS, lanes), BF16),
        in_specs=[in_vmem] * (4 + len(ops)) + [anywhere],
    )(keep, fresh, held, *back, own, token)
    return (prefill, decoded[None])


def solution(mesh):
    placed = (
        P(("grp", "seq"), "tp"),
        P(("grp", "seq"), "tp"),
        P(("grp", "seq"), "tp"),
        P(("grp", "seq"), "tp"),
        P("tp"),
        P("tp"),
        P("grp"),
        P("grp"),
        P(("grp", "seq"), None, None, "tp"),
        P(("grp", "seq"), None, None, "tp"),
        P(("grp", "seq"), None, None, "tp"),
        P(("grp", "seq"), None, None, "tp"),
    )
    return jax.shard_map(
        shards,
        mesh=mesh,
        in_specs=placed,
        out_specs=(P(("grp", "seq"), "tp"), P(("grp", "seq"), None, None, "tp")),
        check_vma=False,
    )
```

```python
import functools
import math

import jax
import jax.numpy as jnp
from jax import lax
from jax.experimental import pallas as pl
from jax.experimental.pallas import tpu as pltpu
from jax.sharding import PartitionSpec as P

H = 128
P_SIZE = 64
N = 128
G = 8
SPAN = 128
STEPS = 4
LOG2E = math.log2(math.e)
F32 = jnp.float32
BF16 = jnp.bfloat16
CHUNKS = 4
COSTS = {(2, 2): 10**9}
VMEM_LIMIT = 32 * 1024 * 1024


def softplus(value):
    small = jnp.exp(-jnp.abs(value))
    series = small * (1.0 - small * (0.5 - small * (1.0 / 3.0 - small * 0.25)))
    return jnp.maximum(value, 0.0) + jnp.where(small < 0.02, series, jnp.log(1.0 + small))


def dot(left, right, left_dim=1, right_dim=0):
    return lax.dot_general(
        left, right, (((left_dim,), (right_dim,)), ((), ())), preferred_element_type=F32
    )


def split(value, pieces):
    result = []
    for _ in range(pieces):
        piece = value.astype(BF16)
        result.append(piece)
        value = value - piece.astype(F32)
    return result


def exact_dot(ones, value, pieces=3, left_dim=1):
    return sum(dot(ones, piece, left_dim) for piece in split(value, pieces))


def spread_matrix(heads, first, width):
    lane = lax.broadcasted_iota(jnp.int32, (heads, width), 1) + first
    head = lax.broadcasted_iota(jnp.int32, (heads, width), 0)
    return jnp.where(lane // P_SIZE == head, 1.0, 0.0).astype(BF16)


def over_lanes(value, first, width, pieces=2):
    return exact_dot_right(value, spread_matrix(value.shape[1], first, width), pieces)


def exact_dot_right(value, ones, pieces):
    return sum(dot(piece, ones) for piece in split(value, pieces))


def shape(dims, dtype=F32):
    return pltpu.VMEM(dims, dtype)


def pinned(value, space=pltpu.VMEM):
    return pltpu.with_memory_space_constraint(value, space)


def call(kernel, out_shape, flops=1, **options):
    name = getattr(kernel, "func", kernel).__name__
    return pl.pallas_call(
        kernel,
        name=name,
        out_shape=out_shape,
        compiler_params=pltpu.CompilerParams(vmem_limit_bytes=VMEM_LIMIT),
        cost_estimate=pl.CostEstimate(flops=flops, bytes_accessed=1, transcendentals=0),
        **options,
    )


def triangle(keep):
    row = lax.broadcasted_iota(jnp.int32, (SPAN, SPAN), 0)
    column = lax.broadcasted_iota(jnp.int32, (SPAN, SPAN), 1)
    return jnp.where(keep(row, column), 1.0, 0.0).astype(BF16)


def chunk_total(k, x_ref, turned, weight, whole, total_ref, decay_ref):
    width = total_ref.shape[1]
    first = k * width
    scaled = x_ref[:, first : first + width].astype(F32) * over_lanes(weight, first, width)
    total_ref[...] = dot(turned, scaled.astype(BF16))
    decay_ref[...] = over_lanes(whole, first, width, 3)


def first_kernel(kept, *refs):
    hbm, refs = refs[: kept + 1], refs[kept + 1 :]
    here, refs = refs[:kept], refs[kept:]
    cum_ref, row_ref, weight_ref, whole_ref, turned_ref = refs[:5]
    total_ref, decay_ref, sent_ref, own_ref, dt_ref, sems = refs[5:]
    x_ref, b_ref, a_ref, asked_ref = here[:4]
    heads, tokens = dt_ref.shape
    spans = tokens // SPAN
    width = total_ref.shape[1]
    dt_copy = pltpu.make_async_copy(hbm[kept], dt_ref, sems.at[0])
    copies = [pltpu.make_async_copy(hbm[i], here[i], sems.at[i]) for i in range(1, kept)]
    x_copies = [
        pltpu.make_async_copy(hbm[0].at[:, lanes], x_ref.at[:, lanes], sems.at[kept + i])
        for i, lanes in enumerate((slice(0, width), slice(width, x_ref.shape[1])))
    ]
    for copy in [dt_copy, copies[1], copies[0], *x_copies, *copies[2:]]:
        copy.start()
    upper = triangle(lambda s, t: s <= t)
    eye = lax.broadcasted_iota(jnp.int32, (heads, heads), 0) == lax.broadcasted_iota(
        jnp.int32, (heads, heads), 1
    )
    dt_copy.wait()
    copies[1].wait()
    a_column = jnp.sum(jnp.where(eye, a_ref[...], 0.0), axis=1, keepdims=True)
    step = softplus(dt_ref[...].astype(F32))
    rate = step * (jnp.exp(a_column) * -LOG2E)
    cums = [exact_dot_right(rate[:, i * SPAN : (i + 1) * SPAN], upper, 3) for i in range(spans)]
    ends = [cum[:, SPAN - 1 : SPAN] for cum in cums]
    after = jnp.zeros_like(ends[0])
    weights = [None] * spans
    for i in reversed(range(spans)):
        after = after + ends[i]
        weights[i] = jnp.exp2(after - cums[i]) * step[:, i * SPAN : (i + 1) * SPAN]
    weight = jnp.concatenate(weights, axis=1).T
    whole = jnp.sum(jnp.where(eye, jnp.exp2(after), 0.0), axis=0, keepdims=True)
    weight_ref[...] = weight
    whole_ref[...] = whole
    copies[0].wait()
    turned = b_ref[:, :N].astype(F32).T.astype(BF16)
    x_copies[0].wait()
    chunk_total(0, x_ref, turned, weight, whole, total_ref, decay_ref)
    sent_ref[...] = total_ref[...].astype(BF16)
    turned_ref[0] = turned
    for g in range(1, turned_ref.shape[0]):
        turned_ref[g] = b_ref[:, g * N : (g + 1) * N].astype(F32).T.astype(BF16)
    cum = jnp.concatenate(cums, axis=1)
    cum_ref[...] = cum
    row_ref[...] = jnp.log2(step) - cum
    x_copies[1].wait()
    for copy in copies[2:]:
        copy.wait()
    own = flat(asked_ref).astype(BF16)
    own_ref[...] = jnp.concatenate([own, own], axis=1)


def state_kernel(part, x_ref, turned_ref, weight_ref, whole_ref, *rest):
    results = rest[-2 * len(part) - 1 :]
    for i, k in enumerate(part):
        total_ref, decay_ref = results[2 * i : 2 * i + 2]
        g = k * total_ref.shape[1] // (H // G * P_SIZE)
        chunk_total(k, x_ref, turned_ref[g], weight_ref[...], whole_ref[...], total_ref, decay_ref)
    results[-1][...] = results[0][...].astype(BF16)


def flat(ref):
    return jnp.concatenate([ref[i].astype(F32) for i in range(ref.shape[0])], axis=0)


def token_kernel(got_ref, tie_ref, token_ref):
    token_ref[...] = jnp.zeros_like(token_ref)


def pass_kernel(hop, k, tail, more, opening, got_ref, total_ref, decay_ref, *rest):
    results = rest[-2 - more - opening :]
    extra, (moving_ref, carry_ref) = rest, results[:2]
    me = lax.axis_index("seq")
    if hop == 1 and k == 0:
        carry_ref[...] = jnp.zeros_like(carry_ref)
    else:
        extra = extra[1:]
    got = got_ref[:N]
    moving_ref[:N] = (total_ref[...] + decay_ref[...] * got.astype(F32)).astype(BF16)

    @pl.when(me == hop)
    def _():
        carry_ref[k] = got

    if more:
        results[2][...] = extra[0][...].astype(BF16)
        extra = extra[1:]
    if opening:
        results[-1][...] = extra[0][...]
    if tail and hop == 1:
        own, other = extra[0][...].astype(F32), extra[1][...].astype(F32)
        lane = lax.broadcasted_iota(jnp.int32, own.shape, 1)
        mine = (lane // (own.shape[1] // 2)) == lax.rem(me, 2)
        moving_ref[N:] = jnp.where(mine, own, other).astype(BF16)
    elif tail:
        moving_ref[N:] = got_ref[N:]


def pair_halves(x_part):
    first_half = lax.broadcasted_iota(jnp.int32, (1, 2 * P_SIZE), 1) < P_SIZE
    zero = jnp.zeros_like(x_part)
    return jnp.where(first_half, x_part, zero), jnp.where(first_half, zero, x_part)


def span_starts(cum, spans):
    ends = [cum[(i + 1) * SPAN - 1 : (i + 1) * SPAN, :] for i in range(spans)]
    starts = [jnp.zeros_like(ends[0])]
    for i in range(spans):
        starts.append(starts[i] + ends[i])
    return ends, starts


def inner_kernel(g, x_ref, b_ref, c_ref, cum_ref, row_ref, d_ref, *rest):
    inner_ref = rest[-1]
    heads, tokens = cum_ref.shape
    spans = tokens // SPAN
    per_group = H // G
    names = slice(g * N, (g + 1) * N)
    t_index = lax.broadcasted_iota(jnp.int32, (SPAN, SPAN), 0)
    s_index = lax.broadcasted_iota(jnp.int32, (SPAN, SPAN), 1)
    causal = t_index >= s_index
    rows = row_ref[...]
    cum = cum_ref[...].T
    ends, _ = span_starts(cum, spans)
    first_half = lax.broadcasted_iota(jnp.int32, (1, 2 * P_SIZE), 1) < P_SIZE
    scores = dot(c_ref[:, names], b_ref[:, names], 1, 1)
    for pair in range(per_group // 2):
        h0 = g * per_group + 2 * pair
        lanes = slice(h0 * P_SIZE, (h0 + 2) * P_SIZE)
        here = slice(2 * pair * P_SIZE, (2 * pair + 2) * P_SIZE)
        x_part = x_ref[:, lanes]
        halves = pair_halves(x_part)
        weights = [[None, None] for _ in range(spans)]
        for e in range(2):
            h = h0 + e
            row = rows[h : h + 1, :]
            for i in range(spans):
                column = jnp.broadcast_to(cum[i * SPAN : (i + 1) * SPAN, h : h + 1], (SPAN, SPAN))
                parts = []
                for j in range(i + 1):
                    shift = row[:, j * SPAN : (j + 1) * SPAN]
                    for m in range(j, i):
                        shift = shift + ends[m][:, h : h + 1]
                    score = scores[i * SPAN : (i + 1) * SPAN, j * SPAN : (j + 1) * SPAN]
                    part = score * jnp.exp2(column + shift)
                    if i == j:
                        part = jnp.where(causal, part, 0.0)
                    parts.append(part.astype(BF16))
                weights[i][e] = jnp.concatenate(parts, axis=1) if i else parts[0]
        skip = jnp.where(first_half, d_ref[:, h0 : h0 + 1], d_ref[:, h0 + 1 : h0 + 2])
        for i in range(spans):
            reach = (i + 1) * SPAN
            left = jnp.concatenate(weights[i], axis=1)
            right = jnp.concatenate([half[:reach] for half in halves], axis=0)
            mine = slice(i * SPAN, (i + 1) * SPAN)
            inner_ref[mine, here] = dot(left, right) + skip * x_part[mine].astype(F32)


def ask_kernel(count, ride, x_ref, b_ref, cum_ref, row_ref, len_ref, owner_ref, *rest):
    local_ref, gain_ref, asked_ref = rest[-3:]
    heads, tokens = cum_ref.shape
    spans = tokens // SPAN
    asks = local_ref.shape[0]
    per_group = H // G
    groups = heads // per_group
    me = lax.axis_index("seq")
    if ride:
        near, middle, far = [ref[N:].astype(F32) for ref in rest[:3]]
        far = jnp.where((me == 1) | (me == 2), middle, far)
        halves = (jnp.where(me < 2, near, far), jnp.where(me < 2, far, near))
        names = near.shape[1] // 2
        blocks = [half[:, i * names : (i + 1) * names] for half in halves for i in range(2)]
    else:
        blocks = [flat(ref) for ref in rest[:count]]
    blocks = jnp.concatenate(blocks, axis=0).astype(BF16)
    row = lax.broadcasted_iota(jnp.int32, (asks, asks * count), 0)
    column = lax.broadcasted_iota(jnp.int32, (asks, asks * count), 1)
    place = row // STEPS
    wanted = place * asks + me * STEPS + row % STEPS
    asked = dot(jnp.where(column == wanted, 1.0, 0.0).astype(BF16), blocks).astype(BF16)
    asked_ref[...] = asked
    block = lax.broadcasted_iota(jnp.int32, (asks, 1), 0) // STEPS
    spot = len_ref[...] - 1 - me * tokens
    mine = (owner_ref[...] == (block if ride else lax.rem(me + count - block, count))) & (spot >= 0) & (spot < tokens)
    spot = jnp.sum(jnp.where(mine, spot, 0).astype(F32), axis=1, keepdims=True).astype(jnp.int32)
    position = lax.broadcasted_iota(jnp.int32, (asks, tokens), 1)
    picked = jnp.where(position == spot, 1.0, 0.0).astype(BF16)
    upto = position <= spot
    rows = row_ref[...]
    cum = cum_ref[...].T
    ends, starts = span_starts(cum, spans)
    near_ask = exact_dot(picked, cum)
    ask_start = starts[0]
    for i in range(1, spans):
        ask_start = jnp.where(spot >= i * SPAN, starts[i], ask_start)
    gain_ref[...] = jnp.exp2(near_ask + ask_start)
    columns = []
    for j in range(spans):
        column = near_ask
        for i in range(j + 1, spans):
            column = jnp.where(spot // SPAN == i, near_ask + sum(ends[j + 1 : i], ends[j]), column)
        columns.append(column)
    for g in range(groups):
        names = slice(g * N, (g + 1) * N)
        scores = jnp.where(upto, dot(asked[:, names], b_ref[:, names], 1, 1), 0.0)
        for pair in range(per_group // 2):
            h0 = g * per_group + 2 * pair
            lanes = slice(h0 * P_SIZE, (h0 + 2) * P_SIZE)
            parts = []
            for h in (h0, h0 + 1):
                for j in range(spans):
                    span = slice(j * SPAN, (j + 1) * SPAN)
                    part = scores[:, span] * jnp.exp2(columns[j][:, h : h + 1] + rows[h : h + 1, span])
                    parts.append(jnp.where(upto[:, span], part, 0.0).astype(BF16))
            right = jnp.concatenate(pair_halves(x_ref[:, lanes]), axis=0)
            local_ref[:, lanes] = dot(jnp.concatenate(parts, axis=1), right)


def read_kernel(count, chunks, ops, final, local_ref, gain_ref, asked_ref, carry_ref, *rest):
    got_refs, rest = rest[: chunks * final], rest[chunks * final :]
    read_refs = rest[-(len(ops) + final) :]
    me = lax.axis_index("seq")
    lanes = local_ref.shape[1]
    width = lanes // chunks
    for k in range(chunks):
        first = k * width
        here = slice(first, first + width)
        g = first // (H // G * P_SIZE)
        state = carry_ref[k]
        if final:
            state = jnp.where(me == count - 1, got_refs[k][:N], state)
        carried = dot(asked_ref[:, g * N : (g + 1) * N], state)
        reading = local_ref[:, here] + over_lanes(gain_ref[...], first, width) * carried
        parts = [reading[r * STEPS : (r + 1) * STEPS] for r in range(count)]
        for (one, other), read_ref in zip(ops, read_refs):
            part = parts[other]
            if one != other:
                part = jnp.where(me == one, part, parts[one])
            read_ref[:, here] = part.astype(read_ref.dtype)
        if final:
            own = parts[0]
            for r in range(1, count):
                own = jnp.where(me == r, parts[r], own)
            read_refs[-1][:, here] = own


def outer_kernel(parts, count, c_ref, cum_ref, carry_ref, *rest):
    final = len(parts) > 1
    part = parts[-1]
    got_refs = rest[: len(part)]
    inner_refs = rest[len(part) : len(part) + cum_ref.shape[0] // (H // G)]
    if final:
        early_ref, out_hbm, token_ref, out_ref, sems = rest[-5:]
        token_ref[...] = jnp.zeros_like(token_ref)
    else:
        out_ref = rest[-1]
    heads, tokens = cum_ref.shape
    spans = tokens // SPAN
    width = got_refs[0].shape[1]
    group_lanes = H // G * P_SIZE
    copies = []

    def send(source, k):
        lanes = slice(k * width, (k + 1) * width)
        copies.append(pltpu.make_async_copy(source, out_hbm.at[:, lanes], sems.at[k]))
        copies[-1].start()

    if final:
        for i, k in enumerate(parts[0]):
            send(early_ref.at[i], k)
    last = lax.axis_index("seq") == count - 1
    start = jnp.zeros((heads, 1), F32)
    gains = []
    for i in range(spans):
        cum = cum_ref[:, i * SPAN : (i + 1) * SPAN]
        gains.append(jnp.exp2(cum + start))
        start = start + cum[:, SPAN - 1 : SPAN]
    gain = jnp.concatenate(gains, axis=1).T
    for i, k in enumerate(part):
        first = k * width
        g = first // group_lanes
        state = jnp.where(last, got_refs[i][:N], carry_ref[k])
        carried = dot(c_ref[:, g * N : (g + 1) * N], state)
        inner = inner_refs[g][:, first - g * group_lanes : first - g * group_lanes + width]
        out_ref[i] = (inner + over_lanes(gain, first, width) * carried).astype(BF16)
        if final:
            send(out_ref.at[i], k)
    for copy in copies:
        copy.wait()


def fresh_kernel(tokens, x_ref, b_ref, c_ref, dt_ref, a_ref, d_ref, len_ref, owner_ref, *rest):
    keep_ref, fresh_ref, held_ref = rest[-3:]
    count, _, heads = dt_ref.shape
    rows = count * STEPS
    place = lax.broadcasted_iota(jnp.int32, (rows, 1), 0) // STEPS * tokens
    spot = len_ref[...] - 1 - place
    mine = (owner_ref[...] == lax.axis_index("seq")) & (spot >= 0) & (spot < tokens)
    held = jnp.sum(jnp.where(mine, 1.0, 0.0), axis=1, keepdims=True)
    held = jnp.broadcast_to(held, (rows, held_ref.shape[2]))
    per_group = H // G
    groups = heads // per_group
    width = x_ref.shape[2]
    turn = lax.broadcasted_iota(jnp.int32, (rows, 1), 0) % STEPS
    step = softplus(flat(dt_ref))
    rate = step * (jnp.exp(a_ref[...]) * -LOG2E)

    def earlier(value, gap):
        if not gap:
            return value
        moved = jnp.concatenate([jnp.zeros_like(value[:gap]), value[:-gap]], axis=0)
        return jnp.where(turn >= gap, moved, 0.0)

    running = sum(earlier(rate, gap) for gap in range(STEPS))
    keep = over_lanes(jnp.exp2(running), 0, width)
    x_values = flat(x_ref)
    b_values = flat(b_ref)
    c_values = flat(c_ref)
    head = lax.broadcasted_iota(jnp.int32, (rows, heads), 1)
    fresh = over_lanes(d_ref[...], 0, width, 3) * x_values
    since = jnp.zeros_like(rate)
    for gap in range(STEPS):
        if gap:
            since = since + earlier(rate, gap - 1)
        products = c_values * earlier(b_values, gap)
        pair = jnp.zeros((rows, heads), F32)
        for g in range(groups):
            score = jnp.sum(products[:, g * N : (g + 1) * N], axis=1, keepdims=True)
            pair = jnp.where(head // per_group == g, score, pair)
        factor = jnp.where(turn >= gap, jnp.exp2(since) * earlier(step, gap) * pair, 0.0)
        fresh = fresh + over_lanes(factor, 0, width) * earlier(x_values, gap)
    for i in range(rows // STEPS):
        keep_ref[i] = keep[i * STEPS : (i + 1) * STEPS]
        fresh_ref[i] = fresh[i * STEPS : (i + 1) * STEPS]
        held_ref[i] = held[i * STEPS : (i + 1) * STEPS]


def finish_kernel(ops, keep_ref, fresh_ref, held_ref, *rest):
    count = keep_ref.shape[0]
    back_refs, own_ref, out_ref = rest[: len(ops)], rest[len(ops)], rest[-1]
    me = lax.axis_index("seq")

    def finish(source, reading):
        value = reading * keep_ref[source] + fresh_ref[source]
        held = held_ref[source][:, :1] > 0.0
        out_ref[source] = jnp.where(held, value, 0.0).astype(BF16)

    if isinstance(ops[0], tuple):
        for source in range(count):
            reading = own_ref[...]
            for (one, other), back_ref in zip(ops, back_refs):
                if source in (one, other):
                    owner = one + other - source
                    reading = jnp.where(me == owner, back_ref[...].astype(F32), reading)
            finish(source, reading)
    else:
        finish(me, own_ref[...])
        for r, back_ref in zip(ops, back_refs):
            finish(lax.rem(me + r, count), back_ref[...].astype(F32))


def shards(
    ssm_input, bmat, cmat, dt_raw, a_log, d_skip, prompt_len, owner, dec_x, dec_b, dec_c, dec_dt
):
    count = lax.axis_size("seq")
    tensor = lax.axis_size("tp")
    tokens, heads = dt_raw.shape
    groups = heads // (H // G)
    names = groups * N
    lanes = heads * P_SIZE
    group_lanes = lanes // groups
    rows = count * STEPS
    chunks = CHUNKS if count <= 4 else groups
    width = lanes // chunks
    anywhere = pl.BlockSpec(memory_space=pl.ANY)
    in_hbm = pl.BlockSpec(memory_space=pltpu.HBM)
    in_vmem = pl.BlockSpec(memory_space=pltpu.VMEM)
    ride = count == 4 and width == 2 * names

    def sent_shape(hop, k):
        tail = ride and k == 1 and hop > 1
        return shape((N + rows * tail, width), BF16)

    inputs = [
        ssm_input,
        bmat,
        a_log.reshape(1, heads),
        dec_c[0],
        cmat,
        d_skip.reshape(1, heads),
        prompt_len.reshape(1, -1),
        owner.reshape(1, -1),
        dec_x[0],
        dec_b[0],
        dec_dt[0],
    ]
    chunk_shapes = (shape((N, width)), shape((1, width)))
    own_shape = shape((rows, 2 * names), BF16)
    results = call(
        functools.partial(first_kernel, len(inputs)),
        tuple(shape(value.shape, value.dtype) for value in inputs)
        + (
            shape((heads, tokens)),
            shape((heads, tokens)),
            shape((tokens, heads)),
            shape((1, heads)),
            shape((groups, N, tokens), BF16),
        )
        + chunk_shapes
        + (sent_shape(1, 0), own_shape),
        in_specs=[in_hbm] * (len(inputs) + 1),
        scratch_shapes=[
            pltpu.VMEM((heads, tokens), BF16),
            pltpu.SemaphoreType.DMA((len(inputs) + 2,)),
        ],
    )(*[pinned(value, pltpu.HBM) for value in inputs + [dt_raw.T]])
    x, b, a_row, asked_here, c, d_row, len_row, owner_row, x_dec, b_dec, dt_dec = results[:11]
    cum, row, weight, whole, turned = results[11:16]
    total, decay = [results[16]], [results[17]]
    sent = {0: results[18]}
    own = results[19]

    def state_part(part, tie):
        out = call(
            functools.partial(state_kernel, part),
            chunk_shapes * len(part) + (sent_shape(1, 1),),
            in_specs=[in_vmem] * 4 + [anywhere],
        )(x, turned, weight, whole, tie)
        total.extend(out[0 : 2 * len(part) : 2])
        decay.extend(out[1 : 2 * len(part) : 2])
        return out[-1]

    def swap(value, *couples):
        partner = {}
        for one, other in couples:
            partner.update({one: other, other: one})
        pairs = []
        for d in range(count):
            for t in range(tensor):
                there = partner[d] * tensor + t if d in partner else d * tensor + (t ^ 1)
                pairs.append((d * tensor + t, there))
        return lax.ppermute(value, ("seq", "tp"), pairs)

    def forward(value, hop, k):
        rides = ride and (hop, k) == (3, 1)
        with jax.named_scope(f"hop{hop}_chunk{k}"):
            return swap(value, *([(0, 1), (2, 3)] if rides else [(hop - 1, hop)]))

    def shift(value, by):
        return lax.ppermute(value, "seq", [(d, (d + by) % count) for d in range(count)])

    def inner_part(g, *after):
        return call(
            functools.partial(inner_kernel, g),
            shape((tokens, group_lanes)),
            in_specs=[in_vmem] * 6 + [anywhere] * len(after),
        )(x, b, c, cum, row, d_row, *after)

    def ask_part(*after):
        blocks = (moving[2, 1], got[2, 1], got[3, 1]) if ride else asks
        return call(
            functools.partial(ask_kernel, count, ride),
            (shape((rows, lanes)), shape((rows, heads)), shape((rows, names), BF16)),
            flops=10**9,
            in_specs=[in_vmem] * (6 + len(blocks)) + [anywhere] * len(after),
        )(x, b, cum, row, len_row, owner_row, *blocks, *after)

    def fresh_part(*after):
        return call(
            functools.partial(fresh_kernel, tokens),
            (shape((count, STEPS, lanes)),) * 2 + (shape((count, STEPS, 128)),),
            in_specs=[in_vmem] * 8 + [anywhere] * len(after),
        )(x_dec, b_dec, asked_here, dt_dec, a_row, d_row, len_row, owner_row, *after)

    def outer_part(parts, carry, before, *after):
        part = parts[-1]
        out = shape((len(part), tokens, width), BF16)
        operands = [c, cum, carry, *[got[count - 1, k] for k in part], *inner, *before]
        return call(
            functools.partial(outer_kernel, parts, count),
            (pltpu.HBM((tokens, lanes), BF16), shape((8, 128))) if before else out,
            in_specs=[in_vmem] * len(operands) + [anywhere] * len(after),
            out_specs=(in_hbm, in_vmem) if before else in_vmem,
            scratch_shapes=[out, pltpu.SemaphoreType.DMA((chunks,))] if before else [],
        )(*operands, *after)

    def read_part(ops, final, *after):
        arrived = [got[count - 1, k] for k in range(chunks)] if final else []
        operands = [local, gain, asked, carry, *arrived]
        return call(
            functools.partial(read_kernel, count, chunks, ops, final),
            (shape((STEPS, lanes), BF16),) * len(ops) + (shape((STEPS, lanes)),) * final,
            in_specs=[in_vmem] * len(operands) + [anywhere] * len(after),
        )(*operands, *after)

    got = {(1, 0): forward(sent[0], 1, 0)}
    moving = {}
    inner = [inner_part(0)]
    for g in range(1, groups):
        inner.append(inner_part(g, inner[-1]))
    sent[1] = state_part(list(range(1, chunks)), inner[-1])
    got[1, 1] = forward(sent[1], 1, 1)
    if not ride:
        asks = [asked_here] + [shift(asked_here, r) for r in range(1, count)]
    order = sorted((k + hop, hop, k) for hop in range(1, count - 1) for k in range(chunks))
    carry = tie = other = None
    for _, hop, k in order:
        tail = ride and k == 1
        more = hop == 1 and k + 2 < chunks
        operands = [got[hop, k], total[k], decay[k]]
        operands += [] if carry is None else [carry]
        opening = ride and (hop, k) == (1, 0)
        operands += total[k + 2 : k + 3] * more + [own] * opening
        operands += [own, other] * (tail and hop == 1)
        after = []
        if hop == count - 2 and k == chunks - 1:
            local, gain, asked = ask_part(tie)
            after = [gain]
        elif hop == count - 2 and k > 1:
            after = [
                call(
                    token_kernel, shape((8, 128)), flops=10**9, in_specs=[anywhere] * 2
                )(got[hop + 1, k - 2], tie)
            ]
        moving[hop + 1, k], carry, *following = call(
            functools.partial(pass_kernel, hop, k, tail, more, opening),
            (sent_shape(hop + 1, k), shape((chunks, N, width), BF16))
            + (sent_shape(1, k + 2),) * more
            + (own_shape,) * opening,
            flops=COSTS.get((hop, k), 1),
            in_specs=[in_vmem] * len(operands) + [anywhere] * len(after),
            input_output_aliases={} if carry is None else {3: 1},
        )(*operands, *after)
        got[hop + 1, k] = forward(moving[hop + 1, k], hop + 1, k)
        tie = moving[hop + 1, k]
        if more:
            got[1, k + 2] = forward(following[0], 1, k + 2)
        if ride and (hop, k) == (1, 0):
            other = swap(following[-1], (0, 1), (2, 3))

    early, late = tuple(range(chunks // 2)), tuple(range(chunks // 2, chunks))

    back = []
    if ride:
        ops, ends = [(0, 1), (0, 2), (1, 2)], [(0, 3), (1, 3), (2, 3)]
        reading = read_part(ops, False)
        for couple, value in zip(ops, reading):
            back.append(swap(value, couple))
        outer = outer_part((early,), carry, [], reading[0])
        keep, fresh, held = fresh_part(outer)
        *reading, mine = read_part(ends, True, keep, *back)
        for couple, value in zip(ends, reading):
            back.append(swap(value, couple))
        ops = ops + ends
    else:
        outer = outer_part((early,), carry, [])
        keep, fresh, held = fresh_part(outer)
        *reading, mine = read_part([(r, r) for r in range(count)], True)
        ops = list(range(1, count))
        back = [shift(reading[r], -r) for r in ops]
        mine = reading[0].astype(F32)
    prefill, token = outer_part((early, late), carry, [outer])

    decoded = call(
        functools.partial(finish_kernel, ops),
        jax.ShapeDtypeStruct((count, STEPS, lanes), BF16),
        in_specs=[in_vmem] * (4 + len(ops)) + [anywhere],
    )(keep, fresh, held, *back, mine, token)
    return (prefill, decoded[None])


def solution(mesh):
    placed = (
        P(("grp", "seq"), "tp"),
        P(("grp", "seq"), "tp"),
        P(("grp", "seq"), "tp"),
        P(("grp", "seq"), "tp"),
        P("tp"),
        P("tp"),
        P("grp"),
        P("grp"),
        P(("grp", "seq"), None, None, "tp"),
        P(("grp", "seq"), None, None, "tp"),
        P(("grp", "seq"), None, None, "tp"),
        P(("grp", "seq"), None, None, "tp"),
    )
    return jax.shard_map(
        shards,
        mesh=mesh,
        in_specs=placed,
        out_specs=(P(("grp", "seq"), "tp"), P(("grp", "seq"), None, None, "tp")),
        check_vma=False,
    )
```

```python
import functools
import math

import jax
import jax.numpy as jnp
from jax import lax
from jax.experimental import pallas as pl
from jax.experimental.pallas import tpu as pltpu
from jax.sharding import PartitionSpec as P

H = 128
P_SIZE = 64
N = 128
G = 8
SPAN = 128
STEPS = 4
LOG2E = math.log2(math.e)
F32 = jnp.float32
BF16 = jnp.bfloat16
CHUNKS = 4
TOKEN_COST = 5 * 10**8
VMEM_LIMIT = 32 * 1024 * 1024


def softplus(value):
    small = jnp.exp(-jnp.abs(value))
    series = small * (1.0 - small * (0.5 - small * (1.0 / 3.0 - small * 0.25)))
    return jnp.maximum(value, 0.0) + jnp.where(small < 0.02, series, jnp.log(1.0 + small))


def dot(left, right, left_dim=1, right_dim=0):
    return lax.dot_general(
        left, right, (((left_dim,), (right_dim,)), ((), ())), preferred_element_type=F32
    )


def split(value, pieces):
    result = []
    for _ in range(pieces):
        piece = value.astype(BF16)
        result.append(piece)
        value = value - piece.astype(F32)
    return result


def exact_dot(ones, value, pieces=3, left_dim=1):
    return sum(dot(ones, piece, left_dim) for piece in split(value, pieces))


def spread_matrix(heads, first, width):
    lane = lax.broadcasted_iota(jnp.int32, (heads, width), 1) + first
    head = lax.broadcasted_iota(jnp.int32, (heads, width), 0)
    return jnp.where(lane // P_SIZE == head, 1.0, 0.0).astype(BF16)


def over_lanes(value, first, width, pieces=2):
    return exact_dot_right(value, spread_matrix(value.shape[1], first, width), pieces)


def exact_dot_right(value, ones, pieces):
    return sum(dot(piece, ones) for piece in split(value, pieces))


def shape(dims, dtype=F32):
    return pltpu.VMEM(dims, dtype)


def pinned(value, space=pltpu.VMEM):
    return pltpu.with_memory_space_constraint(value, space)


def call(kernel, out_shape, flops=1, **options):
    name = getattr(kernel, "func", kernel).__name__
    return pl.pallas_call(
        kernel,
        name=name,
        out_shape=out_shape,
        compiler_params=pltpu.CompilerParams(vmem_limit_bytes=VMEM_LIMIT),
        cost_estimate=pl.CostEstimate(flops=flops, bytes_accessed=1, transcendentals=0),
        **options,
    )


def triangle(keep):
    row = lax.broadcasted_iota(jnp.int32, (SPAN, SPAN), 0)
    column = lax.broadcasted_iota(jnp.int32, (SPAN, SPAN), 1)
    return jnp.where(keep(row, column), 1.0, 0.0).astype(BF16)


def chunk_total(k, x_ref, turned, weight, whole, total_ref, decay_ref):
    width = total_ref.shape[1]
    first = k * width
    scaled = x_ref[:, first : first + width].astype(F32) * over_lanes(weight, first, width)
    total_ref[...] = dot(turned, scaled.astype(BF16))
    decay_ref[...] = over_lanes(whole, first, width, 3)


def first_kernel(kept, *refs):
    hbm, refs = refs[: kept + 1], refs[kept + 1 :]
    here, refs = refs[:kept], refs[kept:]
    cum_ref, row_ref, weight_ref, whole_ref, turned_ref = refs[:5]
    total_ref, decay_ref, sent_ref, dt_ref, sems = refs[5:]
    x_ref, b_ref, a_ref = here[:3]
    heads, tokens = dt_ref.shape
    spans = tokens // SPAN
    width = total_ref.shape[1]
    dt_copy = pltpu.make_async_copy(hbm[kept], dt_ref, sems.at[0])
    copies = [pltpu.make_async_copy(hbm[i], here[i], sems.at[i]) for i in range(1, kept)]
    x_copies = [
        pltpu.make_async_copy(hbm[0].at[:, lanes], x_ref.at[:, lanes], sems.at[kept + i])
        for i, lanes in enumerate((slice(0, width), slice(width, x_ref.shape[1])))
    ]
    for copy in [dt_copy, copies[1], copies[0], *x_copies, *copies[2:]]:
        copy.start()
    upper = triangle(lambda s, t: s <= t)
    eye = lax.broadcasted_iota(jnp.int32, (heads, heads), 0) == lax.broadcasted_iota(
        jnp.int32, (heads, heads), 1
    )
    dt_copy.wait()
    copies[1].wait()
    a_column = jnp.sum(jnp.where(eye, a_ref[...], 0.0), axis=1, keepdims=True)
    step = softplus(dt_ref[...].astype(F32))
    rate = step * (jnp.exp(a_column) * -LOG2E)
    cums = [exact_dot_right(rate[:, i * SPAN : (i + 1) * SPAN], upper, 3) for i in range(spans)]
    ends = [cum[:, SPAN - 1 : SPAN] for cum in cums]
    after = jnp.zeros_like(ends[0])
    weights = [None] * spans
    for i in reversed(range(spans)):
        after = after + ends[i]
        weights[i] = jnp.exp2(after - cums[i]) * step[:, i * SPAN : (i + 1) * SPAN]
    weight = jnp.concatenate(weights, axis=1).T
    whole = jnp.sum(jnp.where(eye, jnp.exp2(after), 0.0), axis=0, keepdims=True)
    weight_ref[...] = weight
    whole_ref[...] = whole
    copies[0].wait()
    turned = b_ref[:, :N].astype(F32).T.astype(BF16)
    x_copies[0].wait()
    chunk_total(0, x_ref, turned, weight, whole, total_ref, decay_ref)
    sent_ref[...] = total_ref[...].astype(BF16)
    turned_ref[0] = turned
    for g in range(1, turned_ref.shape[0]):
        turned_ref[g] = b_ref[:, g * N : (g + 1) * N].astype(F32).T.astype(BF16)
    cum = jnp.concatenate(cums, axis=1)
    cum_ref[...] = cum
    row_ref[...] = jnp.log2(step) - cum
    x_copies[1].wait()
    for copy in copies[2:]:
        copy.wait()


def state_kernel(part, x_ref, turned_ref, weight_ref, whole_ref, *rest):
    results = rest[-2 * len(part) - 1 :]
    for i, k in enumerate(part):
        total_ref, decay_ref = results[2 * i : 2 * i + 2]
        g = k * total_ref.shape[1] // (H // G * P_SIZE)
        chunk_total(k, x_ref, turned_ref[g], weight_ref[...], whole_ref[...], total_ref, decay_ref)
    results[-1][...] = results[0][...].astype(BF16)


def flat(ref):
    return jnp.concatenate([ref[i].astype(F32) for i in range(ref.shape[0])], axis=0)


def token_kernel(*refs):
    refs[-1][...] = jnp.zeros_like(refs[-1])


def pass_kernel(hop, k, more, got_ref, total_ref, decay_ref, *rest):
    moving_ref, carry_ref = rest[len(rest) - 2 - more : len(rest) - more]
    if hop == 1 and k == 0:
        following_ref = rest[0]
        carry_ref[...] = jnp.zeros_like(carry_ref)
    else:
        following_ref = rest[1]
    got = got_ref[...]
    moving_ref[...] = (total_ref[...] + decay_ref[...] * got.astype(F32)).astype(BF16)

    @pl.when(lax.axis_index("seq") == hop)
    def _():
        carry_ref[k] = got

    if more:
        rest[-1][...] = following_ref[...].astype(BF16)


def pair_halves(x_part):
    first_half = lax.broadcasted_iota(jnp.int32, (1, 2 * P_SIZE), 1) < P_SIZE
    zero = jnp.zeros_like(x_part)
    return jnp.where(first_half, x_part, zero), jnp.where(first_half, zero, x_part)


def span_starts(cum, spans):
    ends = [cum[(i + 1) * SPAN - 1 : (i + 1) * SPAN, :] for i in range(spans)]
    starts = [jnp.zeros_like(ends[0])]
    for i in range(spans):
        starts.append(starts[i] + ends[i])
    return ends, starts


def inner_kernel(g, x_ref, b_ref, c_ref, cum_ref, row_ref, d_ref, *rest):
    inner_ref = rest[-1]
    heads, tokens = cum_ref.shape
    spans = tokens // SPAN
    per_group = H // G
    names = slice(g * N, (g + 1) * N)
    t_index = lax.broadcasted_iota(jnp.int32, (SPAN, SPAN), 0)
    s_index = lax.broadcasted_iota(jnp.int32, (SPAN, SPAN), 1)
    causal = t_index >= s_index
    rows = row_ref[...]
    cum = cum_ref[...].T
    ends, _ = span_starts(cum, spans)
    first_half = lax.broadcasted_iota(jnp.int32, (1, 2 * P_SIZE), 1) < P_SIZE
    scores = dot(c_ref[:, names], b_ref[:, names], 1, 1)
    for pair in range(per_group // 2):
        h0 = g * per_group + 2 * pair
        lanes = slice(h0 * P_SIZE, (h0 + 2) * P_SIZE)
        here = slice(2 * pair * P_SIZE, (2 * pair + 2) * P_SIZE)
        x_part = x_ref[:, lanes]
        halves = pair_halves(x_part)
        weights = [[None, None] for _ in range(spans)]
        for e in range(2):
            h = h0 + e
            row = rows[h : h + 1, :]
            for i in range(spans):
                column = jnp.broadcast_to(cum[i * SPAN : (i + 1) * SPAN, h : h + 1], (SPAN, SPAN))
                parts = []
                for j in range(i + 1):
                    shift = row[:, j * SPAN : (j + 1) * SPAN]
                    for m in range(j, i):
                        shift = shift + ends[m][:, h : h + 1]
                    score = scores[i * SPAN : (i + 1) * SPAN, j * SPAN : (j + 1) * SPAN]
                    part = score * jnp.exp2(column + shift)
                    if i == j:
                        part = jnp.where(causal, part, 0.0)
                    parts.append(part.astype(BF16))
                weights[i][e] = jnp.concatenate(parts, axis=1) if i else parts[0]
        skip = jnp.where(first_half, d_ref[:, h0 : h0 + 1], d_ref[:, h0 + 1 : h0 + 2])
        for i in range(spans):
            reach = (i + 1) * SPAN
            left = jnp.concatenate(weights[i], axis=1)
            right = jnp.concatenate([half[:reach] for half in halves], axis=0)
            mine = slice(i * SPAN, (i + 1) * SPAN)
            inner_ref[mine, here] = dot(left, right) + skip * x_part[mine].astype(F32)


def ask_kernel(x_ref, b_ref, cum_ref, row_ref, len_ref, owner_ref, asked_here_ref, *rest):
    local_ref, gain_ref, asked_ref = rest[-3:]
    heads, tokens = cum_ref.shape
    spans = tokens // SPAN
    asks = local_ref.shape[0]
    per_group = H // G
    groups = heads // per_group
    me = lax.axis_index("seq")
    blocks = [asked_here_ref[r, me].astype(F32) for r in range(asks // STEPS)]
    asked = jnp.concatenate(blocks, axis=0).astype(BF16)
    asked_ref[...] = asked
    block = lax.broadcasted_iota(jnp.int32, (asks, 1), 0) // STEPS
    spot = len_ref[...] - 1 - me * tokens
    mine = (owner_ref[...] == block) & (spot >= 0) & (spot < tokens)
    spot = jnp.sum(jnp.where(mine, spot, 0).astype(F32), axis=1, keepdims=True).astype(jnp.int32)
    position = lax.broadcasted_iota(jnp.int32, (asks, tokens), 1)
    picked = jnp.where(position == spot, 1.0, 0.0).astype(BF16)
    upto = position <= spot
    rows = row_ref[...]
    cum = cum_ref[...].T
    ends, starts = span_starts(cum, spans)
    near_ask = exact_dot(picked, cum)
    ask_start = starts[0]
    for i in range(1, spans):
        ask_start = jnp.where(spot >= i * SPAN, starts[i], ask_start)
    gain_ref[...] = jnp.exp2(near_ask + ask_start)
    columns = []
    for j in range(spans):
        column = near_ask
        for i in range(j + 1, spans):
            column = jnp.where(spot // SPAN == i, near_ask + sum(ends[j + 1 : i], ends[j]), column)
        columns.append(column)
    for g in range(groups):
        names = slice(g * N, (g + 1) * N)
        scores = jnp.where(upto, dot(asked[:, names], b_ref[:, names], 1, 1), 0.0)
        for pair in range(per_group // 2):
            h0 = g * per_group + 2 * pair
            lanes = slice(h0 * P_SIZE, (h0 + 2) * P_SIZE)
            parts = []
            for h in (h0, h0 + 1):
                for j in range(spans):
                    span = slice(j * SPAN, (j + 1) * SPAN)
                    part = scores[:, span] * jnp.exp2(columns[j][:, h : h + 1] + rows[h : h + 1, span])
                    parts.append(jnp.where(upto[:, span], part, 0.0).astype(BF16))
            right = jnp.concatenate(pair_halves(x_ref[:, lanes]), axis=0)
            local_ref[:, lanes] = dot(jnp.concatenate(parts, axis=1), right)


def read_kernel(count, chunks, ops, final, local_ref, gain_ref, asked_ref, carry_ref, *rest):
    got_refs, rest = rest[: chunks * final], rest[chunks * final :]
    read_refs = rest[-(len(ops) + final) :]
    me = lax.axis_index("seq")
    lanes = local_ref.shape[1]
    width = lanes // chunks
    for k in range(chunks):
        first = k * width
        here = slice(first, first + width)
        g = first // (H // G * P_SIZE)
        state = carry_ref[k]
        if final:
            state = jnp.where(me == count - 1, got_refs[k][...], state)
        carried = dot(asked_ref[:, g * N : (g + 1) * N], state)
        reading = local_ref[:, here] + over_lanes(gain_ref[...], first, width) * carried
        parts = [reading[r * STEPS : (r + 1) * STEPS] for r in range(count)]
        for op, read_ref in zip(ops, read_refs):
            if isinstance(op, tuple):
                part = jnp.where(me == op[0], parts[op[1]], parts[op[0]])
            else:
                part = parts[0]
                for r in range(1, count):
                    part = jnp.where(lax.rem(me + count - op, count) == r, parts[r], part)
            read_ref[:, here] = part.astype(read_ref.dtype)
        if final:
            own = parts[0]
            for r in range(1, count):
                own = jnp.where(me == r, parts[r], own)
            read_refs[-1][:, here] = own


def outer_kernel(parts, count, c_ref, cum_ref, carry_ref, *rest):
    final = len(parts) > 1
    part = parts[-1]
    got_refs = rest[: len(part)]
    inner_refs = rest[len(part) : len(part) + cum_ref.shape[0] // (H // G)]
    if final:
        early_ref, out_hbm, token_ref, out_ref, sems = rest[-5:]
        token_ref[...] = jnp.zeros_like(token_ref)
    else:
        out_ref = rest[-1]
    heads, tokens = cum_ref.shape
    spans = tokens // SPAN
    width = got_refs[0].shape[1]
    group_lanes = H // G * P_SIZE
    copies = []

    def send(source, k):
        lanes = slice(k * width, (k + 1) * width)
        copies.append(pltpu.make_async_copy(source, out_hbm.at[:, lanes], sems.at[k]))
        copies[-1].start()

    if final:
        for i, k in enumerate(parts[0]):
            send(early_ref.at[i], k)
    last = lax.axis_index("seq") == count - 1
    start = jnp.zeros((heads, 1), F32)
    gains = []
    for i in range(spans):
        cum = cum_ref[:, i * SPAN : (i + 1) * SPAN]
        gains.append(jnp.exp2(cum + start))
        start = start + cum[:, SPAN - 1 : SPAN]
    gain = jnp.concatenate(gains, axis=1).T
    for i, k in enumerate(part):
        first = k * width
        g = first // group_lanes
        state = jnp.where(last, got_refs[i][...], carry_ref[k])
        carried = dot(c_ref[:, g * N : (g + 1) * N], state)
        inner = inner_refs[g][:, first - g * group_lanes : first - g * group_lanes + width]
        out_ref[i] = (inner + over_lanes(gain, first, width) * carried).astype(BF16)
        if final:
            send(out_ref.at[i], k)
    for copy in copies:
        copy.wait()


def fresh_kernel(tokens, x_ref, b_ref, c_ref, dt_ref, a_ref, d_ref, len_ref, owner_ref, *rest):
    keep_ref, fresh_ref, held_ref = rest[-3:]
    count, _, heads = dt_ref.shape
    rows = count * STEPS
    place = lax.broadcasted_iota(jnp.int32, (rows, 1), 0) // STEPS * tokens
    spot = len_ref[...] - 1 - place
    mine = (owner_ref[...] == lax.axis_index("seq")) & (spot >= 0) & (spot < tokens)
    held = jnp.sum(jnp.where(mine, 1.0, 0.0), axis=1, keepdims=True)
    held = jnp.broadcast_to(held, (rows, held_ref.shape[2]))
    per_group = H // G
    groups = heads // per_group
    width = x_ref.shape[2]
    turn = lax.broadcasted_iota(jnp.int32, (rows, 1), 0) % STEPS
    step = softplus(flat(dt_ref))
    rate = step * (jnp.exp(a_ref[...]) * -LOG2E)

    def earlier(value, gap):
        if not gap:
            return value
        moved = jnp.concatenate([jnp.zeros_like(value[:gap]), value[:-gap]], axis=0)
        return jnp.where(turn >= gap, moved, 0.0)

    running = sum(earlier(rate, gap) for gap in range(STEPS))
    keep = over_lanes(jnp.exp2(running), 0, width)
    x_values = flat(x_ref)
    b_values = flat(b_ref)
    c_values = flat(c_ref)
    head = lax.broadcasted_iota(jnp.int32, (rows, heads), 1)
    fresh = over_lanes(d_ref[...], 0, width, 3) * x_values
    since = jnp.zeros_like(rate)
    for gap in range(STEPS):
        if gap:
            since = since + earlier(rate, gap - 1)
        products = c_values * earlier(b_values, gap)
        pair = jnp.zeros((rows, heads), F32)
        for g in range(groups):
            score = jnp.sum(products[:, g * N : (g + 1) * N], axis=1, keepdims=True)
            pair = jnp.where(head // per_group == g, score, pair)
        factor = jnp.where(turn >= gap, jnp.exp2(since) * earlier(step, gap) * pair, 0.0)
        fresh = fresh + over_lanes(factor, 0, width) * earlier(x_values, gap)
    for i in range(rows // STEPS):
        keep_ref[i] = keep[i * STEPS : (i + 1) * STEPS]
        fresh_ref[i] = fresh[i * STEPS : (i + 1) * STEPS]
        held_ref[i] = held[i * STEPS : (i + 1) * STEPS]


def finish_kernel(ops, keep_ref, fresh_ref, held_ref, *rest):
    count = keep_ref.shape[0]
    back_refs, own_ref, out_ref = rest[: len(ops)], rest[len(ops)], rest[-1]
    me = lax.axis_index("seq")

    def finish(source, reading):
        value = reading * keep_ref[source] + fresh_ref[source]
        held = held_ref[source][:, :1] > 0.0
        out_ref[source] = jnp.where(held, value, 0.0).astype(BF16)

    if isinstance(ops[0], tuple):
        for source in range(count):
            reading = own_ref[...]
            for (one, other), back_ref in zip(ops, back_refs):
                if source in (one, other):
                    owner = one + other - source
                    reading = jnp.where(me == owner, back_ref[...].astype(F32), reading)
            finish(source, reading)
    else:
        finish(me, own_ref[...])
        for r, back_ref in zip(ops, back_refs):
            finish(lax.rem(me + r, count), back_ref[...].astype(F32))


def shards(
    ssm_input, bmat, cmat, dt_raw, a_log, d_skip, prompt_len, owner, dec_x, dec_b, dec_c, dec_dt
):
    count = lax.axis_size("seq")
    tensor = lax.axis_size("tp")
    tokens, heads = dt_raw.shape
    groups = heads // (H // G)
    names = groups * N
    lanes = heads * P_SIZE
    group_lanes = lanes // groups
    rows = count * STEPS
    chunks = CHUNKS if count <= 4 else groups
    width = lanes // chunks
    anywhere = pl.BlockSpec(memory_space=pl.ANY)
    in_hbm = pl.BlockSpec(memory_space=pltpu.HBM)
    in_vmem = pl.BlockSpec(memory_space=pltpu.VMEM)
    sent_shape = shape((N, width), BF16)
    inputs = [
        ssm_input,
        bmat,
        a_log.reshape(1, heads),
        dec_c[0],
        cmat,
        d_skip.reshape(1, heads),
        prompt_len.reshape(1, -1),
        owner.reshape(1, -1),
        dec_x[0],
        dec_b[0],
        dec_dt[0],
    ]
    chunk_shapes = (shape((N, width)), shape((1, width)))
    results = call(
        functools.partial(first_kernel, len(inputs)),
        tuple(shape(value.shape, value.dtype) for value in inputs)
        + (
            shape((heads, tokens)),
            shape((heads, tokens)),
            shape((tokens, heads)),
            shape((1, heads)),
            shape((groups, N, tokens), BF16),
        )
        + chunk_shapes
        + (sent_shape,),
        in_specs=[in_hbm] * (len(inputs) + 1),
        scratch_shapes=[
            pltpu.VMEM((heads, tokens), BF16),
            pltpu.SemaphoreType.DMA((len(inputs) + 2,)),
        ],
    )(*[pinned(value, pltpu.HBM) for value in inputs + [dt_raw.T]])
    x, b, a_row, asked_here, c, d_row, len_row, owner_row, x_dec, b_dec, dt_dec = results[:11]
    cum, row, weight, whole, turned = results[11:16]
    total, decay = [results[16]], [results[17]]
    all_asked = lax.all_gather(dec_c[0], "seq")
    sent = {0: results[18]}

    def state_part(part, tie):
        out = call(
            functools.partial(state_kernel, part),
            chunk_shapes * len(part) + (sent_shape,),
            in_specs=[in_vmem] * 4 + [anywhere],
        )(x, turned, weight, whole, tie)
        total.extend(out[0 : 2 * len(part) : 2])
        decay.extend(out[1 : 2 * len(part) : 2])
        return out[-1]

    def swap(value, *couples):
        partner = {}
        for one, other in couples:
            partner.update({one: other, other: one})
        pairs = []
        for d in range(count):
            for t in range(tensor):
                there = partner[d] * tensor + t if d in partner else d * tensor + (t ^ 1)
                pairs.append((d * tensor + t, there))
        return lax.ppermute(value, ("seq", "tp"), pairs)

    def forward(value, hop, k):
        with jax.named_scope(f"hop{hop}_chunk{k}"):
            return swap(value, (hop - 1, hop))

    def shift(value, by):
        return lax.ppermute(value, "seq", [(d, (d + by) % count) for d in range(count)])

    def inner_part(g, *after):
        return call(
            functools.partial(inner_kernel, g),
            shape((tokens, group_lanes)),
            in_specs=[in_vmem] * 6 + [anywhere] * len(after),
        )(x, b, c, cum, row, d_row, *after)

    def ask_part(*after):
        return call(
            ask_kernel,
            (shape((rows, lanes)), shape((rows, heads)), shape((rows, names), BF16)),
            in_specs=[in_vmem] * 7 + [anywhere] * len(after),
        )(x, b, cum, row, len_row, owner_row, all_asked, *after)

    def token(*after, flops=1):
        return call(
            token_kernel, shape((8, 128)), flops=flops, in_specs=[anywhere] * len(after)
        )(*after)

    def fresh_part(*after):
        return call(
            functools.partial(fresh_kernel, tokens),
            (shape((count, STEPS, lanes)),) * 2 + (shape((count, STEPS, 128)),),
            in_specs=[in_vmem] * 8 + [anywhere] * len(after),
        )(x_dec, b_dec, asked_here, dt_dec, a_row, d_row, len_row, owner_row, *after)

    def outer_part(parts, carry, before, *after):
        part = parts[-1]
        out = shape((len(part), tokens, width), BF16)
        operands = [c, cum, carry, *[got[count - 1, k] for k in part], *inner, *before]
        return call(
            functools.partial(outer_kernel, parts, count),
            (pltpu.HBM((tokens, lanes), BF16), shape((8, 128))) if before else out,
            in_specs=[in_vmem] * len(operands) + [anywhere] * len(after),
            out_specs=(in_hbm, in_vmem) if before else in_vmem,
            scratch_shapes=[out, pltpu.SemaphoreType.DMA((chunks,))] if before else [],
        )(*operands, *after)

    def read_part(ops, final, *after):
        arrived = [got[count - 1, k] for k in range(chunks)] if final else []
        operands = [local, gain, asked, carry, *arrived]
        return call(
            functools.partial(read_kernel, count, chunks, ops, final),
            (shape((STEPS, lanes), BF16),) * len(ops) + (shape((STEPS, lanes)),) * final,
            in_specs=[in_vmem] * len(operands) + [anywhere] * len(after),
        )(*operands, *after)

    got = {(1, 0): forward(sent[0], 1, 0)}
    inner = [inner_part(0)]
    for g in range(1, groups):
        inner.append(inner_part(g, inner[-1]))
    sent[1] = state_part(list(range(1, chunks)), inner[-1])
    got[1, 1] = forward(sent[1], 1, 1)
    order = sorted((k + hop, hop, k) for hop in range(1, count - 1) for k in range(chunks))
    carry = tie = None
    for _, hop, k in order:
        more = hop == 1 and k + 2 < chunks
        operands = [got[hop, k], total[k], decay[k]]
        operands += [] if carry is None else [carry]
        operands += total[k + 2 : k + 3] * more
        after = []
        if hop == count - 2 and k > 1:
            after = [token(got[hop + 1, k - 2], tie, flops=TOKEN_COST)]
        tie, carry, *following = call(
            functools.partial(pass_kernel, hop, k, more),
            (sent_shape, shape((chunks, N, width), BF16)) + (sent_shape,) * more,
            in_specs=[in_vmem] * len(operands) + [anywhere] * len(after),
            input_output_aliases={} if carry is None else {3: 1},
        )(*operands, *after)
        got[hop + 1, k] = forward(tie, hop + 1, k)
        if more:
            got[1, k + 2] = forward(following[0], 1, k + 2)

    early, late = tuple(range(chunks // 2)), tuple(range(chunks // 2, chunks))
    four = count == 4
    local, gain, asked = ask_part(tie)
    back, ops = [], [(0, 2), (1, 2), (0, 1)] if four else []
    if four:
        reading = read_part(ops, False)
        for couple, value in zip(ops, reading):
            back.append(swap(value, couple))
    outer = outer_part((early,), carry, [], reading[0] if four else asked)
    keep, fresh, held = fresh_part(outer)
    order_token = token(got[count - 1, chunks - 2], keep, flops=TOKEN_COST)
    ends = [(0, 3), (1, 3), (2, 3)] if four else list(range(1, count))
    *reading, mine = read_part(ends, True, order_token, *back)
    for op, value in zip(ends, reading):
        back.append(swap(value, op) if four else shift(value, -op))
    ops = ops + ends
    prefill, end_token = outer_part((early, late), carry, [outer])

    decoded = call(
        functools.partial(finish_kernel, ops),
        jax.ShapeDtypeStruct((count, STEPS, lanes), BF16),
        in_specs=[in_vmem] * (4 + len(ops)) + [anywhere],
    )(keep, fresh, held, *back, mine, end_token)
    return (prefill, decoded[None])


def solution(mesh):
    placed = (
        P(("grp", "seq"), "tp"),
        P(("grp", "seq"), "tp"),
        P(("grp", "seq"), "tp"),
        P(("grp", "seq"), "tp"),
        P("tp"),
        P("tp"),
        P("grp"),
        P("grp"),
        P(("grp", "seq"), None, None, "tp"),
        P(("grp", "seq"), None, None, "tp"),
        P(("grp", "seq"), None, None, "tp"),
        P(("grp", "seq"), None, None, "tp"),
    )
    return jax.shard_map(
        shards,
        mesh=mesh,
        in_specs=placed,
        out_specs=(P(("grp", "seq"), "tp"), P(("grp", "seq"), None, None, "tp")),
        check_vma=False,
    )
```

```python
import functools
import math

import jax
import jax.numpy as jnp
from jax import lax
from jax.experimental import pallas as pl
from jax.experimental.pallas import tpu as pltpu
from jax.sharding import PartitionSpec as P

H = 128
P_SIZE = 64
N = 128
G = 8
SPAN = 128
STEPS = 4
LOG2E = math.log2(math.e)
F32 = jnp.float32
BF16 = jnp.bfloat16
CHUNKS = 4
TOKEN_COST = 5 * 10**8
PASS_COST = 5 * 10**8
VMEM_LIMIT = 32 * 1024 * 1024


def softplus(value):
    small = jnp.exp(-jnp.abs(value))
    series = small * (1.0 - small * (0.5 - small * (1.0 / 3.0 - small * 0.25)))
    return jnp.maximum(value, 0.0) + jnp.where(small < 0.02, series, jnp.log(1.0 + small))


def dot(left, right, left_dim=1, right_dim=0):
    return lax.dot_general(
        left, right, (((left_dim,), (right_dim,)), ((), ())), preferred_element_type=F32
    )


def split(value, pieces):
    result = []
    for _ in range(pieces):
        piece = value.astype(BF16)
        result.append(piece)
        value = value - piece.astype(F32)
    return result


def exact_dot(ones, value, pieces=3, left_dim=1):
    return sum(dot(ones, piece, left_dim) for piece in split(value, pieces))


def spread_matrix(heads, first, width):
    lane = lax.broadcasted_iota(jnp.int32, (heads, width), 1) + first
    head = lax.broadcasted_iota(jnp.int32, (heads, width), 0)
    return jnp.where(lane // P_SIZE == head, 1.0, 0.0).astype(BF16)


def over_lanes(value, first, width, pieces=2):
    return exact_dot_right(value, spread_matrix(value.shape[1], first, width), pieces)


def exact_dot_right(value, ones, pieces):
    return sum(dot(piece, ones) for piece in split(value, pieces))


def shape(dims, dtype=F32):
    return pltpu.VMEM(dims, dtype)


def pinned(value, space=pltpu.VMEM):
    return pltpu.with_memory_space_constraint(value, space)


def call(kernel, out_shape, flops=1, **options):
    name = getattr(kernel, "func", kernel).__name__
    return pl.pallas_call(
        kernel,
        name=name,
        out_shape=out_shape,
        compiler_params=pltpu.CompilerParams(vmem_limit_bytes=VMEM_LIMIT),
        cost_estimate=pl.CostEstimate(flops=flops, bytes_accessed=1, transcendentals=0),
        **options,
    )


def triangle(keep):
    row = lax.broadcasted_iota(jnp.int32, (SPAN, SPAN), 0)
    column = lax.broadcasted_iota(jnp.int32, (SPAN, SPAN), 1)
    return jnp.where(keep(row, column), 1.0, 0.0).astype(BF16)


def chunk_total(k, x_ref, turned, weight, whole, total_ref, decay_ref):
    width = total_ref.shape[1]
    first = k * width
    scaled = x_ref[:, first : first + width].astype(F32) * over_lanes(weight, first, width)
    total_ref[...] = dot(turned, scaled.astype(BF16))
    decay_ref[...] = over_lanes(whole, first, width, 3)


def first_kernel(kept, *refs):
    hbm, refs = refs[: kept + 1], refs[kept + 1 :]
    here, refs = refs[:kept], refs[kept:]
    cum_ref, row_ref, weight_ref, whole_ref, turned_ref = refs[:5]
    total_ref, decay_ref, sent_ref, dt_ref, sems = refs[5:]
    x_ref, b_ref, a_ref = here[:3]
    heads, tokens = dt_ref.shape
    spans = tokens // SPAN
    width = total_ref.shape[1]
    dt_copy = pltpu.make_async_copy(hbm[kept], dt_ref, sems.at[0])
    copies = [pltpu.make_async_copy(hbm[i], here[i], sems.at[i]) for i in range(1, kept)]
    x_copies = [
        pltpu.make_async_copy(hbm[0].at[:, lanes], x_ref.at[:, lanes], sems.at[kept + i])
        for i, lanes in enumerate((slice(0, width), slice(width, x_ref.shape[1])))
    ]
    for copy in [dt_copy, copies[1], copies[0], *x_copies, *copies[2:]]:
        copy.start()
    upper = triangle(lambda s, t: s <= t)
    eye = lax.broadcasted_iota(jnp.int32, (heads, heads), 0) == lax.broadcasted_iota(
        jnp.int32, (heads, heads), 1
    )
    dt_copy.wait()
    copies[1].wait()
    a_column = jnp.sum(jnp.where(eye, a_ref[...], 0.0), axis=1, keepdims=True)
    step = softplus(dt_ref[...].astype(F32))
    rate = step * (jnp.exp(a_column) * -LOG2E)
    cums = [exact_dot_right(rate[:, i * SPAN : (i + 1) * SPAN], upper, 3) for i in range(spans)]
    ends = [cum[:, SPAN - 1 : SPAN] for cum in cums]
    after = jnp.zeros_like(ends[0])
    weights = [None] * spans
    for i in reversed(range(spans)):
        after = after + ends[i]
        weights[i] = jnp.exp2(after - cums[i]) * step[:, i * SPAN : (i + 1) * SPAN]
    weight = jnp.concatenate(weights, axis=1).T
    whole = jnp.sum(jnp.where(eye, jnp.exp2(after), 0.0), axis=0, keepdims=True)
    weight_ref[...] = weight
    whole_ref[...] = whole
    copies[0].wait()
    turned = b_ref[:, :N].astype(F32).T.astype(BF16)
    x_copies[0].wait()
    chunk_total(0, x_ref, turned, weight, whole, total_ref, decay_ref)
    sent_ref[...] = total_ref[...].astype(BF16)
    turned_ref[0] = turned
    for g in range(1, turned_ref.shape[0]):
        turned_ref[g] = b_ref[:, g * N : (g + 1) * N].astype(F32).T.astype(BF16)
    cum = jnp.concatenate(cums, axis=1)
    cum_ref[...] = cum
    row_ref[...] = jnp.log2(step) - cum
    x_copies[1].wait()
    for copy in copies[2:]:
        copy.wait()


def state_kernel(part, x_ref, turned_ref, weight_ref, whole_ref, asked_ref, *rest):
    results = rest[-2 * len(part) - 1 :]
    for i, k in enumerate(part):
        total_ref, decay_ref = results[2 * i : 2 * i + 2]
        g = k * total_ref.shape[1] // (H // G * P_SIZE)
        chunk_total(k, x_ref, turned_ref[g], weight_ref[...], whole_ref[...], total_ref, decay_ref)
    results[-1][:N] = results[0][...].astype(BF16)
    if results[-1].shape[0] > N:
        own = flat(asked_ref).astype(BF16)
        results[-1][N:] = jnp.concatenate([own, own], axis=1)


def flat(ref):
    return jnp.concatenate([ref[i].astype(F32) for i in range(ref.shape[0])], axis=0)


def token_kernel(*refs):
    refs[-1][...] = jnp.zeros_like(refs[-1])


def pass_kernel(hop, k, more, got_ref, total_ref, decay_ref, *rest):
    moving_ref, carry_ref = rest[len(rest) - 2 - more : len(rest) - more]
    me = lax.axis_index("seq")
    if hop == 1 and k == 0:
        following_ref = rest[0]
        carry_ref[...] = jnp.zeros_like(carry_ref)
    else:
        following_ref = rest[1]
    got = got_ref[:N]
    moving_ref[:N] = (total_ref[...] + decay_ref[...] * got.astype(F32)).astype(BF16)
    if got_ref.shape[0] > N:
        tail = got_ref[N:]
        if hop == 1:
            own = rest[1 + more][N:].astype(F32)
            lane = lax.broadcasted_iota(jnp.int32, own.shape, 1)
            mine = (lane // (own.shape[1] // 2)) == lax.rem(me, 2)
            tail = jnp.where(mine, own, tail.astype(F32)).astype(BF16)
        moving_ref[N:] = tail

    @pl.when(me == hop)
    def _():
        carry_ref[k] = got

    if more:
        rest[-1][...] = following_ref[...].astype(BF16)


def pair_halves(x_part):
    first_half = lax.broadcasted_iota(jnp.int32, (1, 2 * P_SIZE), 1) < P_SIZE
    zero = jnp.zeros_like(x_part)
    return jnp.where(first_half, x_part, zero), jnp.where(first_half, zero, x_part)


def span_starts(cum, spans):
    ends = [cum[(i + 1) * SPAN - 1 : (i + 1) * SPAN, :] for i in range(spans)]
    starts = [jnp.zeros_like(ends[0])]
    for i in range(spans):
        starts.append(starts[i] + ends[i])
    return ends, starts


def inner_kernel(g, x_ref, b_ref, c_ref, cum_ref, row_ref, d_ref, *rest):
    inner_ref = rest[-1]
    heads, tokens = cum_ref.shape
    spans = tokens // SPAN
    per_group = H // G
    names = slice(g * N, (g + 1) * N)
    t_index = lax.broadcasted_iota(jnp.int32, (SPAN, SPAN), 0)
    s_index = lax.broadcasted_iota(jnp.int32, (SPAN, SPAN), 1)
    causal = t_index >= s_index
    rows = row_ref[...]
    cum = cum_ref[...].T
    ends, _ = span_starts(cum, spans)
    first_half = lax.broadcasted_iota(jnp.int32, (1, 2 * P_SIZE), 1) < P_SIZE
    scores = dot(c_ref[:, names], b_ref[:, names], 1, 1)
    for pair in range(per_group // 2):
        h0 = g * per_group + 2 * pair
        lanes = slice(h0 * P_SIZE, (h0 + 2) * P_SIZE)
        here = slice(2 * pair * P_SIZE, (2 * pair + 2) * P_SIZE)
        x_part = x_ref[:, lanes]
        halves = pair_halves(x_part)
        weights = [[None, None] for _ in range(spans)]
        for e in range(2):
            h = h0 + e
            row = rows[h : h + 1, :]
            for i in range(spans):
                column = jnp.broadcast_to(cum[i * SPAN : (i + 1) * SPAN, h : h + 1], (SPAN, SPAN))
                parts = []
                for j in range(i + 1):
                    shift = row[:, j * SPAN : (j + 1) * SPAN]
                    for m in range(j, i):
                        shift = shift + ends[m][:, h : h + 1]
                    score = scores[i * SPAN : (i + 1) * SPAN, j * SPAN : (j + 1) * SPAN]
                    part = score * jnp.exp2(column + shift)
                    if i == j:
                        part = jnp.where(causal, part, 0.0)
                    parts.append(part.astype(BF16))
                weights[i][e] = jnp.concatenate(parts, axis=1) if i else parts[0]
        skip = jnp.where(first_half, d_ref[:, h0 : h0 + 1], d_ref[:, h0 + 1 : h0 + 2])
        for i in range(spans):
            reach = (i + 1) * SPAN
            left = jnp.concatenate(weights[i], axis=1)
            right = jnp.concatenate([half[:reach] for half in halves], axis=0)
            mine = slice(i * SPAN, (i + 1) * SPAN)
            inner_ref[mine, here] = dot(left, right) + skip * x_part[mine].astype(F32)


def ask_kernel(ride, x_ref, b_ref, cum_ref, row_ref, len_ref, owner_ref, *rest):
    local_ref, gain_ref, asked_ref = rest[-3:]
    heads, tokens = cum_ref.shape
    spans = tokens // SPAN
    asks = local_ref.shape[0]
    per_group = H // G
    groups = heads // per_group
    me = lax.axis_index("seq")
    if ride:
        near, middle, far = [ref[N:].astype(F32) for ref in rest[:3]]
        far = jnp.where((me == 1) | (me == 2), middle, far)
        halves = (jnp.where(me < 2, near, far), jnp.where(me < 2, far, near))
        names = near.shape[1] // 2
        blocks = [half[:, i * names : (i + 1) * names] for half in halves for i in range(2)]
        blocks = jnp.concatenate(blocks, axis=0).astype(BF16)
        row = lax.broadcasted_iota(jnp.int32, (asks, blocks.shape[0]), 0)
        column = lax.broadcasted_iota(jnp.int32, (asks, blocks.shape[0]), 1)
        wanted = row // STEPS * asks + me * STEPS + row % STEPS
        asked = dot(jnp.where(column == wanted, 1.0, 0.0).astype(BF16), blocks).astype(BF16)
    else:
        blocks = [rest[0][r, me].astype(F32) for r in range(asks // STEPS)]
        asked = jnp.concatenate(blocks, axis=0).astype(BF16)
    asked_ref[...] = asked
    block = lax.broadcasted_iota(jnp.int32, (asks, 1), 0) // STEPS
    spot = len_ref[...] - 1 - me * tokens
    mine = (owner_ref[...] == block) & (spot >= 0) & (spot < tokens)
    spot = jnp.sum(jnp.where(mine, spot, 0).astype(F32), axis=1, keepdims=True).astype(jnp.int32)
    position = lax.broadcasted_iota(jnp.int32, (asks, tokens), 1)
    picked = jnp.where(position == spot, 1.0, 0.0).astype(BF16)
    upto = position <= spot
    rows = row_ref[...]
    cum = cum_ref[...].T
    ends, starts = span_starts(cum, spans)
    near_ask = exact_dot(picked, cum)
    ask_start = starts[0]
    for i in range(1, spans):
        ask_start = jnp.where(spot >= i * SPAN, starts[i], ask_start)
    gain_ref[...] = jnp.exp2(near_ask + ask_start)
    columns = []
    for j in range(spans):
        column = near_ask
        for i in range(j + 1, spans):
            column = jnp.where(spot // SPAN == i, near_ask + sum(ends[j + 1 : i], ends[j]), column)
        columns.append(column)
    for g in range(groups):
        names = slice(g * N, (g + 1) * N)
        scores = jnp.where(upto, dot(asked[:, names], b_ref[:, names], 1, 1), 0.0)
        for pair in range(per_group // 2):
            h0 = g * per_group + 2 * pair
            lanes = slice(h0 * P_SIZE, (h0 + 2) * P_SIZE)
            parts = []
            for h in (h0, h0 + 1):
                for j in range(spans):
                    span = slice(j * SPAN, (j + 1) * SPAN)
                    part = scores[:, span] * jnp.exp2(columns[j][:, h : h + 1] + rows[h : h + 1, span])
                    parts.append(jnp.where(upto[:, span], part, 0.0).astype(BF16))
            right = jnp.concatenate(pair_halves(x_ref[:, lanes]), axis=0)
            local_ref[:, lanes] = dot(jnp.concatenate(parts, axis=1), right)


def read_kernel(count, chunks, ops, final, local_ref, gain_ref, asked_ref, carry_ref, *rest):
    got_refs, rest = rest[: chunks * final], rest[chunks * final :]
    read_refs = rest[-(len(ops) + final) :]
    me = lax.axis_index("seq")
    lanes = local_ref.shape[1]
    width = lanes // chunks
    for k in range(chunks):
        first = k * width
        here = slice(first, first + width)
        g = first // (H // G * P_SIZE)
        state = carry_ref[k]
        if final:
            state = jnp.where(me == count - 1, got_refs[k][:N], state)
        carried = dot(asked_ref[:, g * N : (g + 1) * N], state)
        reading = local_ref[:, here] + over_lanes(gain_ref[...], first, width) * carried
        parts = [reading[r * STEPS : (r + 1) * STEPS] for r in range(count)]
        for op, read_ref in zip(ops, read_refs):
            if isinstance(op, tuple):
                part = jnp.where(me == op[0], parts[op[1]], parts[op[0]])
            else:
                part = parts[0]
                for r in range(1, count):
                    part = jnp.where(lax.rem(me + count - op, count) == r, parts[r], part)
            read_ref[:, here] = part.astype(read_ref.dtype)
        if final:
            own = parts[0]
            for r in range(1, count):
                own = jnp.where(me == r, parts[r], own)
            read_refs[-1][:, here] = own


def outer_kernel(parts, count, c_ref, cum_ref, carry_ref, *rest):
    final = len(parts) > 1
    part = parts[-1]
    got_refs = rest[: len(part)]
    inner_refs = rest[len(part) : len(part) + cum_ref.shape[0] // (H // G)]
    if final:
        early_ref, out_hbm, token_ref, out_ref, sems = rest[-5:]
        token_ref[...] = jnp.zeros_like(token_ref)
    else:
        out_ref = rest[-1]
    heads, tokens = cum_ref.shape
    spans = tokens // SPAN
    width = got_refs[0].shape[1]
    group_lanes = H // G * P_SIZE
    copies = []

    def send(source, k):
        lanes = slice(k * width, (k + 1) * width)
        copies.append(pltpu.make_async_copy(source, out_hbm.at[:, lanes], sems.at[k]))
        copies[-1].start()

    if final:
        for i, k in enumerate(parts[0]):
            send(early_ref.at[i], k)
    last = lax.axis_index("seq") == count - 1
    start = jnp.zeros((heads, 1), F32)
    gains = []
    for i in range(spans):
        cum = cum_ref[:, i * SPAN : (i + 1) * SPAN]
        gains.append(jnp.exp2(cum + start))
        start = start + cum[:, SPAN - 1 : SPAN]
    gain = jnp.concatenate(gains, axis=1).T
    for i, k in enumerate(part):
        first = k * width
        g = first // group_lanes
        state = jnp.where(last, got_refs[i][:N], carry_ref[k])
        carried = dot(c_ref[:, g * N : (g + 1) * N], state)
        inner = inner_refs[g][:, first - g * group_lanes : first - g * group_lanes + width]
        out_ref[i] = (inner + over_lanes(gain, first, width) * carried).astype(BF16)
        if final:
            send(out_ref.at[i], k)
    for copy in copies:
        copy.wait()


def fresh_kernel(tokens, x_ref, b_ref, c_ref, dt_ref, a_ref, d_ref, len_ref, owner_ref, *rest):
    keep_ref, fresh_ref, held_ref = rest[-3:]
    count, _, heads = dt_ref.shape
    rows = count * STEPS
    place = lax.broadcasted_iota(jnp.int32, (rows, 1), 0) // STEPS * tokens
    spot = len_ref[...] - 1 - place
    mine = (owner_ref[...] == lax.axis_index("seq")) & (spot >= 0) & (spot < tokens)
    held = jnp.sum(jnp.where(mine, 1.0, 0.0), axis=1, keepdims=True)
    held = jnp.broadcast_to(held, (rows, held_ref.shape[2]))
    per_group = H // G
    groups = heads // per_group
    width = x_ref.shape[2]
    turn = lax.broadcasted_iota(jnp.int32, (rows, 1), 0) % STEPS
    step = softplus(flat(dt_ref))
    rate = step * (jnp.exp(a_ref[...]) * -LOG2E)

    def earlier(value, gap):
        if not gap:
            return value
        moved = jnp.concatenate([jnp.zeros_like(value[:gap]), value[:-gap]], axis=0)
        return jnp.where(turn >= gap, moved, 0.0)

    running = sum(earlier(rate, gap) for gap in range(STEPS))
    keep = over_lanes(jnp.exp2(running), 0, width)
    x_values = flat(x_ref)
    b_values = flat(b_ref)
    c_values = flat(c_ref)
    head = lax.broadcasted_iota(jnp.int32, (rows, heads), 1)
    fresh = over_lanes(d_ref[...], 0, width, 3) * x_values
    since = jnp.zeros_like(rate)
    for gap in range(STEPS):
        if gap:
            since = since + earlier(rate, gap - 1)
        products = c_values * earlier(b_values, gap)
        pair = jnp.zeros((rows, heads), F32)
        for g in range(groups):
            score = jnp.sum(products[:, g * N : (g + 1) * N], axis=1, keepdims=True)
            pair = jnp.where(head // per_group == g, score, pair)
        factor = jnp.where(turn >= gap, jnp.exp2(since) * earlier(step, gap) * pair, 0.0)
        fresh = fresh + over_lanes(factor, 0, width) * earlier(x_values, gap)
    for i in range(rows // STEPS):
        keep_ref[i] = keep[i * STEPS : (i + 1) * STEPS]
        fresh_ref[i] = fresh[i * STEPS : (i + 1) * STEPS]
        held_ref[i] = held[i * STEPS : (i + 1) * STEPS]


def finish_kernel(ops, keep_ref, fresh_ref, held_ref, *rest):
    count = keep_ref.shape[0]
    back_refs, own_ref, out_ref = rest[: len(ops)], rest[len(ops)], rest[-1]
    me = lax.axis_index("seq")

    def finish(source, reading):
        value = reading * keep_ref[source] + fresh_ref[source]
        held = held_ref[source][:, :1] > 0.0
        out_ref[source] = jnp.where(held, value, 0.0).astype(BF16)

    if isinstance(ops[0], tuple):
        for source in range(count):
            reading = own_ref[...]
            for (one, other), back_ref in zip(ops, back_refs):
                if source in (one, other):
                    owner = one + other - source
                    reading = jnp.where(me == owner, back_ref[...].astype(F32), reading)
            finish(source, reading)
    else:
        finish(me, own_ref[...])
        for r, back_ref in zip(ops, back_refs):
            finish(lax.rem(me + r, count), back_ref[...].astype(F32))


def shards(
    ssm_input, bmat, cmat, dt_raw, a_log, d_skip, prompt_len, owner, dec_x, dec_b, dec_c, dec_dt
):
    count = lax.axis_size("seq")
    tensor = lax.axis_size("tp")
    tokens, heads = dt_raw.shape
    groups = heads // (H // G)
    names = groups * N
    lanes = heads * P_SIZE
    group_lanes = lanes // groups
    rows = count * STEPS
    chunks = CHUNKS if count <= 4 else groups
    width = lanes // chunks
    anywhere = pl.BlockSpec(memory_space=pl.ANY)
    in_hbm = pl.BlockSpec(memory_space=pltpu.HBM)
    in_vmem = pl.BlockSpec(memory_space=pltpu.VMEM)
    ride = count == 4 and width == 2 * names

    def sent_shape(k):
        return shape((N + rows * (ride and k == 1), width), BF16)

    inputs = [
        ssm_input,
        bmat,
        a_log.reshape(1, heads),
        dec_c[0],
        cmat,
        d_skip.reshape(1, heads),
        prompt_len.reshape(1, -1),
        owner.reshape(1, -1),
        dec_x[0],
        dec_b[0],
        dec_dt[0],
    ]
    chunk_shapes = (shape((N, width)), shape((1, width)))
    results = call(
        functools.partial(first_kernel, len(inputs)),
        tuple(shape(value.shape, value.dtype) for value in inputs)
        + (
            shape((heads, tokens)),
            shape((heads, tokens)),
            shape((tokens, heads)),
            shape((1, heads)),
            shape((groups, N, tokens), BF16),
        )
        + chunk_shapes
        + (sent_shape(0),),
        in_specs=[in_hbm] * (len(inputs) + 1),
        scratch_shapes=[
            pltpu.VMEM((heads, tokens), BF16),
            pltpu.SemaphoreType.DMA((len(inputs) + 2,)),
        ],
    )(*[pinned(value, pltpu.HBM) for value in inputs + [dt_raw.T]])
    x, b, a_row, asked_here, c, d_row, len_row, owner_row, x_dec, b_dec, dt_dec = results[:11]
    cum, row, weight, whole, turned = results[11:16]
    total, decay = [results[16]], [results[17]]
    all_asked = None if ride else lax.all_gather(dec_c[0], "seq")
    sent = {0: results[18]}

    def state_part(part, tie):
        out = call(
            functools.partial(state_kernel, part),
            chunk_shapes * len(part) + (sent_shape(1),),
            in_specs=[in_vmem] * 5 + [anywhere],
        )(x, turned, weight, whole, asked_here, tie)
        total.extend(out[0 : 2 * len(part) : 2])
        decay.extend(out[1 : 2 * len(part) : 2])
        return out[-1]

    def swap(value, *couples):
        partner = {}
        for one, other in couples:
            partner.update({one: other, other: one})
        pairs = []
        for d in range(count):
            for t in range(tensor):
                there = partner[d] * tensor + t if d in partner else d * tensor + (t ^ 1)
                pairs.append((d * tensor + t, there))
        return lax.ppermute(value, ("seq", "tp"), pairs)

    def forward(value, hop, k):
        with jax.named_scope(f"hop{hop}_chunk{k}"):
            rides = ride and k == 1 and hop != 2
            return swap(value, *([(0, 1), (2, 3)] if rides else [(hop - 1, hop)]))

    def shift(value, by):
        return lax.ppermute(value, "seq", [(d, (d + by) % count) for d in range(count)])

    def inner_part(g, *after):
        return call(
            functools.partial(inner_kernel, g),
            shape((tokens, group_lanes)),
            in_specs=[in_vmem] * 6 + [anywhere] * len(after),
        )(x, b, c, cum, row, d_row, *after)

    def ask_part(*after):
        blocks = (moving[2, 1], got[2, 1], got[3, 1]) if ride else (all_asked,)
        return call(
            functools.partial(ask_kernel, ride),
            (shape((rows, lanes)), shape((rows, heads)), shape((rows, names), BF16)),
            in_specs=[in_vmem] * (6 + len(blocks)) + [anywhere] * len(after),
        )(x, b, cum, row, len_row, owner_row, *blocks, *after)

    def token(*after, flops=1):
        return call(
            token_kernel, shape((8, 128)), flops=flops, in_specs=[anywhere] * len(after)
        )(*after)

    def fresh_part(*after):
        return call(
            functools.partial(fresh_kernel, tokens),
            (shape((count, STEPS, lanes)),) * 2 + (shape((count, STEPS, 128)),),
            in_specs=[in_vmem] * 8 + [anywhere] * len(after),
        )(x_dec, b_dec, asked_here, dt_dec, a_row, d_row, len_row, owner_row, *after)

    def outer_part(parts, carry, before, *after):
        part = parts[-1]
        out = shape((len(part), tokens, width), BF16)
        operands = [c, cum, carry, *[got[count - 1, k] for k in part], *inner, *before]
        return call(
            functools.partial(outer_kernel, parts, count),
            (pltpu.HBM((tokens, lanes), BF16), shape((8, 128))) if before else out,
            in_specs=[in_vmem] * len(operands) + [anywhere] * len(after),
            out_specs=(in_hbm, in_vmem) if before else in_vmem,
            scratch_shapes=[out, pltpu.SemaphoreType.DMA((chunks,))] if before else [],
        )(*operands, *after)

    def read_part(ops, final, *after):
        arrived = [got[count - 1, k] for k in range(chunks)] if final else []
        operands = [local, gain, asked, carry, *arrived]
        return call(
            functools.partial(read_kernel, count, chunks, ops, final),
            (shape((STEPS, lanes), BF16),) * len(ops) + (shape((STEPS, lanes)),) * final,
            in_specs=[in_vmem] * len(operands) + [anywhere] * len(after),
        )(*operands, *after)

    got = {(1, 0): forward(sent[0], 1, 0)}
    inner = [inner_part(0)]
    for g in range(1, groups):
        inner.append(inner_part(g, inner[-1]))
    sent[1] = state_part(list(range(1, chunks)), inner[-1])
    got[1, 1] = forward(sent[1], 1, 1)
    order = sorted((k + hop, hop, k) for hop in range(1, count - 1) for k in range(chunks))
    moving = {}
    carry = tie = None
    for _, hop, k in order:
        more = hop == 1 and k + 2 < chunks
        operands = [got[hop, k], total[k], decay[k]]
        operands += [] if carry is None else [carry]
        operands += total[k + 2 : k + 3] * more + [sent[1]] * (ride and (hop, k) == (1, 1))
        after = []
        if hop == count - 2 and k > 1:
            after = [token(got[hop + 1, k - 2], tie, flops=TOKEN_COST)]
        tie, carry, *following = call(
            functools.partial(pass_kernel, hop, k, more),
            (sent_shape(k), shape((chunks, N, width), BF16)) + (sent_shape(k + 2),) * more,
            flops=PASS_COST if k % 2 == 0 else 1,
            in_specs=[in_vmem] * len(operands) + [anywhere] * len(after),
            input_output_aliases={} if carry is None else {3: 1},
        )(*operands, *after)
        moving[hop + 1, k] = tie
        got[hop + 1, k] = forward(tie, hop + 1, k)
        if more:
            got[1, k + 2] = forward(following[0], 1, k + 2)

    early, late = tuple(range(chunks // 2)), tuple(range(chunks // 2, chunks))
    four = count == 4
    local, gain, asked = ask_part(tie)
    back, ops = [], [(0, 2), (1, 2), (0, 1)] if four else []
    if four:
        reading = read_part(ops, False)
        for couple, value in zip(ops, reading):
            back.append(swap(value, couple))
    outer = outer_part((early,), carry, [], reading[0] if four else asked)
    keep, fresh, held = fresh_part(outer)
    order_token = token(got[count - 1, chunks - 2], keep, flops=TOKEN_COST)
    ends = [(0, 3), (1, 3), (2, 3)] if four else list(range(1, count))
    *reading, mine = read_part(ends, True, order_token, *back)
    for op, value in zip(ends, reading):
        back.append(swap(value, op) if four else shift(value, -op))
    ops = ops + ends
    prefill, end_token = outer_part((early, late), carry, [outer])

    decoded = call(
        functools.partial(finish_kernel, ops),
        jax.ShapeDtypeStruct((count, STEPS, lanes), BF16),
        in_specs=[in_vmem] * (4 + len(ops)) + [anywhere],
    )(keep, fresh, held, *back, mine, end_token)
    return (prefill, decoded[None])


def solution(mesh):
    placed = (
        P(("grp", "seq"), "tp"),
        P(("grp", "seq"), "tp"),
        P(("grp", "seq"), "tp"),
        P(("grp", "seq"), "tp"),
        P("tp"),
        P("tp"),
        P("grp"),
        P("grp"),
        P(("grp", "seq"), None, None, "tp"),
        P(("grp", "seq"), None, None, "tp"),
        P(("grp", "seq"), None, None, "tp"),
        P(("grp", "seq"), None, None, "tp"),
    )
    return jax.shard_map(
        shards,
        mesh=mesh,
        in_specs=placed,
        out_specs=(P(("grp", "seq"), "tp"), P(("grp", "seq"), None, None, "tp")),
        check_vma=False,
    )
```

```python
import functools
import math

import jax
import jax.numpy as jnp
from jax import lax
from jax.experimental import pallas as pl
from jax.experimental.pallas import tpu as pltpu
from jax.sharding import PartitionSpec as P

H = 128
P_SIZE = 64
N = 128
G = 8
SPAN = 128
STEPS = 4
LOG2E = math.log2(math.e)
F32 = jnp.float32
BF16 = jnp.bfloat16
CHUNKS = 4
TOKEN_COST = 10**8
PASS_COST = 5 * 10**8
VMEM_LIMIT = 32 * 1024 * 1024


def softplus(value):
    small = jnp.exp(-jnp.abs(value))
    series = small * (1.0 - small * (0.5 - small * (1.0 / 3.0 - small * 0.25)))
    return jnp.maximum(value, 0.0) + jnp.where(small < 0.02, series, jnp.log(1.0 + small))


def dot(left, right, left_dim=1, right_dim=0):
    return lax.dot_general(
        left, right, (((left_dim,), (right_dim,)), ((), ())), preferred_element_type=F32
    )


def split(value, pieces):
    result = []
    for _ in range(pieces):
        piece = value.astype(BF16)
        result.append(piece)
        value = value - piece.astype(F32)
    return result


def exact_dot(ones, value, pieces=3, left_dim=1):
    return sum(dot(ones, piece, left_dim) for piece in split(value, pieces))


def spread_matrix(heads, first, width):
    lane = lax.broadcasted_iota(jnp.int32, (heads, width), 1) + first
    head = lax.broadcasted_iota(jnp.int32, (heads, width), 0)
    return jnp.where(lane // P_SIZE == head, 1.0, 0.0).astype(BF16)


def over_lanes(value, first, width, pieces=2):
    return exact_dot_right(value, spread_matrix(value.shape[1], first, width), pieces)


def exact_dot_right(value, ones, pieces):
    return sum(dot(piece, ones) for piece in split(value, pieces))


def shape(dims, dtype=F32):
    return pltpu.VMEM(dims, dtype)


def pinned(value, space=pltpu.VMEM):
    return pltpu.with_memory_space_constraint(value, space)


def call(kernel, out_shape, flops=1, **options):
    name = getattr(kernel, "func", kernel).__name__
    return pl.pallas_call(
        kernel,
        name=name,
        out_shape=out_shape,
        compiler_params=pltpu.CompilerParams(vmem_limit_bytes=VMEM_LIMIT),
        cost_estimate=pl.CostEstimate(flops=flops, bytes_accessed=1, transcendentals=0),
        **options,
    )


def triangle(keep):
    row = lax.broadcasted_iota(jnp.int32, (SPAN, SPAN), 0)
    column = lax.broadcasted_iota(jnp.int32, (SPAN, SPAN), 1)
    return jnp.where(keep(row, column), 1.0, 0.0).astype(BF16)


def chunk_total(k, x_ref, turned, weight, whole, total_ref, decay_ref):
    width = total_ref.shape[1]
    first = k * width
    scaled = x_ref[:, first : first + width].astype(F32) * over_lanes(weight, first, width)
    total_ref[...] = dot(turned, scaled.astype(BF16))
    decay_ref[...] = over_lanes(whole, first, width, 3)


def first_kernel(kept, *refs):
    hbm, refs = refs[: kept + 1], refs[kept + 1 :]
    here, refs = refs[:kept], refs[kept:]
    cum_ref, row_ref, weight_ref, whole_ref, turned_ref = refs[:5]
    total_ref, decay_ref, sent_ref, dt_ref, sems = refs[5:]
    x_ref, b_ref, a_ref = here[:3]
    heads, tokens = dt_ref.shape
    spans = tokens // SPAN
    width = total_ref.shape[1]
    dt_copy = pltpu.make_async_copy(hbm[kept], dt_ref, sems.at[0])
    copies = [pltpu.make_async_copy(hbm[i], here[i], sems.at[i]) for i in range(1, kept)]
    x_copies = [
        pltpu.make_async_copy(hbm[0].at[:, lanes], x_ref.at[:, lanes], sems.at[kept + i])
        for i, lanes in enumerate((slice(0, width), slice(width, x_ref.shape[1])))
    ]
    for copy in [dt_copy, copies[1], copies[0], *x_copies, *copies[2:]]:
        copy.start()
    upper = triangle(lambda s, t: s <= t)
    eye = lax.broadcasted_iota(jnp.int32, (heads, heads), 0) == lax.broadcasted_iota(
        jnp.int32, (heads, heads), 1
    )
    dt_copy.wait()
    copies[1].wait()
    a_column = jnp.sum(jnp.where(eye, a_ref[...], 0.0), axis=1, keepdims=True)
    step = softplus(dt_ref[...].astype(F32))
    rate = step * (jnp.exp(a_column) * -LOG2E)
    cums = [exact_dot_right(rate[:, i * SPAN : (i + 1) * SPAN], upper, 3) for i in range(spans)]
    ends = [cum[:, SPAN - 1 : SPAN] for cum in cums]
    after = jnp.zeros_like(ends[0])
    weights = [None] * spans
    for i in reversed(range(spans)):
        after = after + ends[i]
        weights[i] = jnp.exp2(after - cums[i]) * step[:, i * SPAN : (i + 1) * SPAN]
    weight = jnp.concatenate(weights, axis=1).T
    whole = jnp.sum(jnp.where(eye, jnp.exp2(after), 0.0), axis=0, keepdims=True)
    weight_ref[...] = weight
    whole_ref[...] = whole
    copies[0].wait()
    turned = b_ref[:, :N].astype(F32).T.astype(BF16)
    x_copies[0].wait()
    chunk_total(0, x_ref, turned, weight, whole, total_ref, decay_ref)
    sent_ref[:N] = total_ref[...].astype(BF16)
    turned_ref[0] = turned
    for g in range(1, turned_ref.shape[0]):
        turned_ref[g] = b_ref[:, g * N : (g + 1) * N].astype(F32).T.astype(BF16)
    cum = jnp.concatenate(cums, axis=1)
    cum_ref[...] = cum
    row_ref[...] = jnp.log2(step) - cum
    x_copies[1].wait()
    for copy in copies[2:]:
        copy.wait()
    if sent_ref.shape[0] > N:
        own = flat(here[3]).astype(BF16)
        sent_ref[N:] = jnp.concatenate([own, own], axis=1)


def state_kernel(part, x_ref, turned_ref, weight_ref, whole_ref, *rest):
    results = rest[-2 * len(part) - 1 :]
    for i, k in enumerate(part):
        total_ref, decay_ref = results[2 * i : 2 * i + 2]
        g = k * total_ref.shape[1] // (H // G * P_SIZE)
        chunk_total(k, x_ref, turned_ref[g], weight_ref[...], whole_ref[...], total_ref, decay_ref)
    results[-1][...] = results[0][...].astype(BF16)


def flat(ref):
    return jnp.concatenate([ref[i].astype(F32) for i in range(ref.shape[0])], axis=0)


def token_kernel(*refs):
    refs[-1][...] = jnp.zeros_like(refs[-1])


def pass_kernel(hop, k, more, got_ref, total_ref, decay_ref, *rest):
    moving_ref, carry_ref = rest[len(rest) - 2 - more : len(rest) - more]
    me = lax.axis_index("seq")
    if hop == 1 and k == 0:
        following_ref = rest[0]
        carry_ref[...] = jnp.zeros_like(carry_ref)
    else:
        following_ref = rest[1]
    got = got_ref[:N]
    moving_ref[:N] = (total_ref[...] + decay_ref[...] * got.astype(F32)).astype(BF16)
    if moving_ref.shape[0] > N and hop == 1:
        own, other = [ref[N:].astype(F32) for ref in rest[1 + more : 3 + more]]
        lane = lax.broadcasted_iota(jnp.int32, own.shape, 1)
        mine = (lane // (own.shape[1] // 2)) == lax.rem(me, 2)
        moving_ref[N:] = jnp.where(mine, own, other).astype(BF16)
    elif moving_ref.shape[0] > N:
        moving_ref[N:] = got_ref[N:]

    @pl.when(me == hop)
    def _():
        carry_ref[k] = got

    if more:
        rest[-1][...] = following_ref[...].astype(BF16)


def pair_halves(x_part):
    first_half = lax.broadcasted_iota(jnp.int32, (1, 2 * P_SIZE), 1) < P_SIZE
    zero = jnp.zeros_like(x_part)
    return jnp.where(first_half, x_part, zero), jnp.where(first_half, zero, x_part)


def span_starts(cum, spans):
    ends = [cum[(i + 1) * SPAN - 1 : (i + 1) * SPAN, :] for i in range(spans)]
    starts = [jnp.zeros_like(ends[0])]
    for i in range(spans):
        starts.append(starts[i] + ends[i])
    return ends, starts


def inner_kernel(g, x_ref, b_ref, c_ref, cum_ref, row_ref, d_ref, *rest):
    inner_ref = rest[-1]
    heads, tokens = cum_ref.shape
    spans = tokens // SPAN
    per_group = H // G
    names = slice(g * N, (g + 1) * N)
    t_index = lax.broadcasted_iota(jnp.int32, (SPAN, SPAN), 0)
    s_index = lax.broadcasted_iota(jnp.int32, (SPAN, SPAN), 1)
    causal = t_index >= s_index
    rows = row_ref[...]
    cum = cum_ref[...].T
    ends, _ = span_starts(cum, spans)
    first_half = lax.broadcasted_iota(jnp.int32, (1, 2 * P_SIZE), 1) < P_SIZE
    scores = dot(c_ref[:, names], b_ref[:, names], 1, 1)
    for pair in range(per_group // 2):
        h0 = g * per_group + 2 * pair
        lanes = slice(h0 * P_SIZE, (h0 + 2) * P_SIZE)
        here = slice(2 * pair * P_SIZE, (2 * pair + 2) * P_SIZE)
        x_part = x_ref[:, lanes]
        halves = pair_halves(x_part)
        weights = [[None, None] for _ in range(spans)]
        for e in range(2):
            h = h0 + e
            row = rows[h : h + 1, :]
            for i in range(spans):
                column = jnp.broadcast_to(cum[i * SPAN : (i + 1) * SPAN, h : h + 1], (SPAN, SPAN))
                parts = []
                for j in range(i + 1):
                    shift = row[:, j * SPAN : (j + 1) * SPAN]
                    for m in range(j, i):
                        shift = shift + ends[m][:, h : h + 1]
                    score = scores[i * SPAN : (i + 1) * SPAN, j * SPAN : (j + 1) * SPAN]
                    part = score * jnp.exp2(column + shift)
                    if i == j:
                        part = jnp.where(causal, part, 0.0)
                    parts.append(part.astype(BF16))
                weights[i][e] = jnp.concatenate(parts, axis=1) if i else parts[0]
        skip = jnp.where(first_half, d_ref[:, h0 : h0 + 1], d_ref[:, h0 + 1 : h0 + 2])
        for i in range(spans):
            reach = (i + 1) * SPAN
            left = jnp.concatenate(weights[i], axis=1)
            right = jnp.concatenate([half[:reach] for half in halves], axis=0)
            mine = slice(i * SPAN, (i + 1) * SPAN)
            inner_ref[mine, here] = dot(left, right) + skip * x_part[mine].astype(F32)


def ask_kernel(ride, x_ref, b_ref, cum_ref, row_ref, len_ref, owner_ref, *rest):
    local_ref, gain_ref, asked_ref = rest[-3:]
    heads, tokens = cum_ref.shape
    spans = tokens // SPAN
    asks = local_ref.shape[0]
    per_group = H // G
    groups = heads // per_group
    me = lax.axis_index("seq")
    if ride:
        near, middle, far = [ref[N:].astype(F32) for ref in rest[:3]]
        far = jnp.where((me == 1) | (me == 2), middle, far)
        halves = (jnp.where(me < 2, near, far), jnp.where(me < 2, far, near))
        names = near.shape[1] // 2
        blocks = [half[:, i * names : (i + 1) * names] for half in halves for i in range(2)]
        blocks = jnp.concatenate(blocks, axis=0).astype(BF16)
        row = lax.broadcasted_iota(jnp.int32, (asks, blocks.shape[0]), 0)
        column = lax.broadcasted_iota(jnp.int32, (asks, blocks.shape[0]), 1)
        wanted = row // STEPS * asks + me * STEPS + row % STEPS
        asked = dot(jnp.where(column == wanted, 1.0, 0.0).astype(BF16), blocks).astype(BF16)
    else:
        blocks = [rest[0][r, me].astype(F32) for r in range(asks // STEPS)]
        asked = jnp.concatenate(blocks, axis=0).astype(BF16)
    asked_ref[...] = asked
    block = lax.broadcasted_iota(jnp.int32, (asks, 1), 0) // STEPS
    spot = len_ref[...] - 1 - me * tokens
    mine = (owner_ref[...] == block) & (spot >= 0) & (spot < tokens)
    spot = jnp.sum(jnp.where(mine, spot, 0).astype(F32), axis=1, keepdims=True).astype(jnp.int32)
    position = lax.broadcasted_iota(jnp.int32, (asks, tokens), 1)
    picked = jnp.where(position == spot, 1.0, 0.0).astype(BF16)
    upto = position <= spot
    rows = row_ref[...]
    cum = cum_ref[...].T
    ends, starts = span_starts(cum, spans)
    near_ask = exact_dot(picked, cum)
    ask_start = starts[0]
    for i in range(1, spans):
        ask_start = jnp.where(spot >= i * SPAN, starts[i], ask_start)
    gain_ref[...] = jnp.exp2(near_ask + ask_start)
    columns = []
    for j in range(spans):
        column = near_ask
        for i in range(j + 1, spans):
            column = jnp.where(spot // SPAN == i, near_ask + sum(ends[j + 1 : i], ends[j]), column)
        columns.append(column)
    for g in range(groups):
        names = slice(g * N, (g + 1) * N)
        scores = jnp.where(upto, dot(asked[:, names], b_ref[:, names], 1, 1), 0.0)
        for pair in range(per_group // 2):
            h0 = g * per_group + 2 * pair
            lanes = slice(h0 * P_SIZE, (h0 + 2) * P_SIZE)
            parts = []
            for h in (h0, h0 + 1):
                for j in range(spans):
                    span = slice(j * SPAN, (j + 1) * SPAN)
                    part = scores[:, span] * jnp.exp2(columns[j][:, h : h + 1] + rows[h : h + 1, span])
                    parts.append(jnp.where(upto[:, span], part, 0.0).astype(BF16))
            right = jnp.concatenate(pair_halves(x_ref[:, lanes]), axis=0)
            local_ref[:, lanes] = dot(jnp.concatenate(parts, axis=1), right)


def read_kernel(count, chunks, ops, final, local_ref, gain_ref, asked_ref, carry_ref, *rest):
    got_refs, rest = rest[: chunks * final], rest[chunks * final :]
    read_refs = rest[-(len(ops) + final) :]
    me = lax.axis_index("seq")
    lanes = local_ref.shape[1]
    width = lanes // chunks
    for k in range(chunks):
        first = k * width
        here = slice(first, first + width)
        g = first // (H // G * P_SIZE)
        state = carry_ref[k]
        if final:
            state = jnp.where(me == count - 1, got_refs[k][:N], state)
        carried = dot(asked_ref[:, g * N : (g + 1) * N], state)
        reading = local_ref[:, here] + over_lanes(gain_ref[...], first, width) * carried
        parts = [reading[r * STEPS : (r + 1) * STEPS] for r in range(count)]
        for op, read_ref in zip(ops, read_refs):
            if isinstance(op, tuple):
                part = jnp.where(me == op[0], parts[op[1]], parts[op[0]])
            else:
                part = parts[0]
                for r in range(1, count):
                    part = jnp.where(lax.rem(me + count - op, count) == r, parts[r], part)
            read_ref[:, here] = part.astype(read_ref.dtype)
        if final:
            own = parts[0]
            for r in range(1, count):
                own = jnp.where(me == r, parts[r], own)
            read_refs[-1][:, here] = own


def outer_kernel(parts, count, c_ref, cum_ref, carry_ref, *rest):
    final = len(parts) > 1
    part = parts[-1]
    got_refs = rest[: len(part)]
    inner_refs = rest[len(part) : len(part) + cum_ref.shape[0] // (H // G)]
    if final:
        early_ref, out_hbm, token_ref, out_ref, sems = rest[-5:]
        token_ref[...] = jnp.zeros_like(token_ref)
    else:
        out_ref = rest[-1]
    heads, tokens = cum_ref.shape
    spans = tokens // SPAN
    width = got_refs[0].shape[1]
    group_lanes = H // G * P_SIZE
    copies = []

    def send(source, k):
        lanes = slice(k * width, (k + 1) * width)
        copies.append(pltpu.make_async_copy(source, out_hbm.at[:, lanes], sems.at[k]))
        copies[-1].start()

    if final:
        for i, k in enumerate(parts[0]):
            send(early_ref.at[i], k)
    last = lax.axis_index("seq") == count - 1
    start = jnp.zeros((heads, 1), F32)
    gains = []
    for i in range(spans):
        cum = cum_ref[:, i * SPAN : (i + 1) * SPAN]
        gains.append(jnp.exp2(cum + start))
        start = start + cum[:, SPAN - 1 : SPAN]
    gain = jnp.concatenate(gains, axis=1).T
    for i, k in enumerate(part):
        first = k * width
        g = first // group_lanes
        state = jnp.where(last, got_refs[i][:N], carry_ref[k])
        carried = dot(c_ref[:, g * N : (g + 1) * N], state)
        inner = inner_refs[g][:, first - g * group_lanes : first - g * group_lanes + width]
        out_ref[i] = (inner + over_lanes(gain, first, width) * carried).astype(BF16)
        if final:
            send(out_ref.at[i], k)
    for copy in copies:
        copy.wait()


def fresh_kernel(tokens, x_ref, b_ref, c_ref, dt_ref, a_ref, d_ref, len_ref, owner_ref, *rest):
    keep_ref, fresh_ref, held_ref = rest[-3:]
    count, _, heads = dt_ref.shape
    rows = count * STEPS
    place = lax.broadcasted_iota(jnp.int32, (rows, 1), 0) // STEPS * tokens
    spot = len_ref[...] - 1 - place
    mine = (owner_ref[...] == lax.axis_index("seq")) & (spot >= 0) & (spot < tokens)
    held = jnp.sum(jnp.where(mine, 1.0, 0.0), axis=1, keepdims=True)
    held = jnp.broadcast_to(held, (rows, held_ref.shape[2]))
    per_group = H // G
    groups = heads // per_group
    width = x_ref.shape[2]
    turn = lax.broadcasted_iota(jnp.int32, (rows, 1), 0) % STEPS
    step = softplus(flat(dt_ref))
    rate = step * (jnp.exp(a_ref[...]) * -LOG2E)

    def earlier(value, gap):
        if not gap:
            return value
        moved = jnp.concatenate([jnp.zeros_like(value[:gap]), value[:-gap]], axis=0)
        return jnp.where(turn >= gap, moved, 0.0)

    running = sum(earlier(rate, gap) for gap in range(STEPS))
    keep = over_lanes(jnp.exp2(running), 0, width)
    x_values = flat(x_ref)
    b_values = flat(b_ref)
    c_values = flat(c_ref)
    head = lax.broadcasted_iota(jnp.int32, (rows, heads), 1)
    fresh = over_lanes(d_ref[...], 0, width, 3) * x_values
    since = jnp.zeros_like(rate)
    for gap in range(STEPS):
        if gap:
            since = since + earlier(rate, gap - 1)
        products = c_values * earlier(b_values, gap)
        pair = jnp.zeros((rows, heads), F32)
        for g in range(groups):
            score = jnp.sum(products[:, g * N : (g + 1) * N], axis=1, keepdims=True)
            pair = jnp.where(head // per_group == g, score, pair)
        factor = jnp.where(turn >= gap, jnp.exp2(since) * earlier(step, gap) * pair, 0.0)
        fresh = fresh + over_lanes(factor, 0, width) * earlier(x_values, gap)
    for i in range(rows // STEPS):
        keep_ref[i] = keep[i * STEPS : (i + 1) * STEPS]
        fresh_ref[i] = fresh[i * STEPS : (i + 1) * STEPS]
        held_ref[i] = held[i * STEPS : (i + 1) * STEPS]


def finish_kernel(ops, keep_ref, fresh_ref, held_ref, *rest):
    count = keep_ref.shape[0]
    back_refs, own_ref, out_ref = rest[: len(ops)], rest[len(ops)], rest[-1]
    me = lax.axis_index("seq")

    def finish(source, reading):
        value = reading * keep_ref[source] + fresh_ref[source]
        held = held_ref[source][:, :1] > 0.0
        out_ref[source] = jnp.where(held, value, 0.0).astype(BF16)

    if isinstance(ops[0], tuple):
        for source in range(count):
            reading = own_ref[...]
            for (one, other), back_ref in zip(ops, back_refs):
                if source in (one, other):
                    owner = one + other - source
                    reading = jnp.where(me == owner, back_ref[...].astype(F32), reading)
            finish(source, reading)
    else:
        finish(me, own_ref[...])
        for r, back_ref in zip(ops, back_refs):
            finish(lax.rem(me + r, count), back_ref[...].astype(F32))


def shards(
    ssm_input, bmat, cmat, dt_raw, a_log, d_skip, prompt_len, owner, dec_x, dec_b, dec_c, dec_dt
):
    count = lax.axis_size("seq")
    tensor = lax.axis_size("tp")
    tokens, heads = dt_raw.shape
    groups = heads // (H // G)
    names = groups * N
    lanes = heads * P_SIZE
    group_lanes = lanes // groups
    rows = count * STEPS
    chunks = CHUNKS if count <= 4 else groups
    width = lanes // chunks
    anywhere = pl.BlockSpec(memory_space=pl.ANY)
    in_hbm = pl.BlockSpec(memory_space=pltpu.HBM)
    in_vmem = pl.BlockSpec(memory_space=pltpu.VMEM)
    ride = count == 4 and width == 2 * names

    def sent_shape(hop, k):
        return shape((N + rows * (ride and (hop, k) in ((1, 0), (2, 1), (3, 1))), width), BF16)

    inputs = [
        ssm_input,
        bmat,
        a_log.reshape(1, heads),
        dec_c[0],
        cmat,
        d_skip.reshape(1, heads),
        prompt_len.reshape(1, -1),
        owner.reshape(1, -1),
        dec_x[0],
        dec_b[0],
        dec_dt[0],
    ]
    chunk_shapes = (shape((N, width)), shape((1, width)))
    results = call(
        functools.partial(first_kernel, len(inputs)),
        tuple(shape(value.shape, value.dtype) for value in inputs)
        + (
            shape((heads, tokens)),
            shape((heads, tokens)),
            shape((tokens, heads)),
            shape((1, heads)),
            shape((groups, N, tokens), BF16),
        )
        + chunk_shapes
        + (sent_shape(1, 0),),
        in_specs=[in_hbm] * (len(inputs) + 1),
        scratch_shapes=[
            pltpu.VMEM((heads, tokens), BF16),
            pltpu.SemaphoreType.DMA((len(inputs) + 2,)),
        ],
    )(*[pinned(value, pltpu.HBM) for value in inputs + [dt_raw.T]])
    x, b, a_row, asked_here, c, d_row, len_row, owner_row, x_dec, b_dec, dt_dec = results[:11]
    cum, row, weight, whole, turned = results[11:16]
    total, decay = [results[16]], [results[17]]
    all_asked = None if ride else lax.all_gather(dec_c[0], "seq")
    sent = {0: results[18]}

    def state_part(part, tie):
        out = call(
            functools.partial(state_kernel, part),
            chunk_shapes * len(part) + (sent_shape(1, 1),),
            in_specs=[in_vmem] * 4 + [anywhere],
        )(x, turned, weight, whole, tie)
        total.extend(out[0 : 2 * len(part) : 2])
        decay.extend(out[1 : 2 * len(part) : 2])
        return out[-1]

    def swap(value, *couples):
        partner = {}
        for one, other in couples:
            partner.update({one: other, other: one})
        pairs = []
        for d in range(count):
            for t in range(tensor):
                there = partner[d] * tensor + t if d in partner else d * tensor + (t ^ 1)
                pairs.append((d * tensor + t, there))
        return lax.ppermute(value, ("seq", "tp"), pairs)

    def forward(value, hop, k):
        with jax.named_scope(f"hop{hop}_chunk{k}"):
            rides = ride and (hop, k) in ((1, 0), (3, 1))
            return swap(value, *([(0, 1), (2, 3)] if rides else [(hop - 1, hop)]))

    def shift(value, by):
        return lax.ppermute(value, "seq", [(d, (d + by) % count) for d in range(count)])

    def inner_part(g, *after):
        return call(
            functools.partial(inner_kernel, g),
            shape((tokens, group_lanes)),
            in_specs=[in_vmem] * 6 + [anywhere] * len(after),
        )(x, b, c, cum, row, d_row, *after)

    def ask_part(*after):
        blocks = (moving[2, 1], got[2, 1], got[3, 1]) if ride else (all_asked,)
        return call(
            functools.partial(ask_kernel, ride),
            (shape((rows, lanes)), shape((rows, heads)), shape((rows, names), BF16)),
            in_specs=[in_vmem] * (6 + len(blocks)) + [anywhere] * len(after),
        )(x, b, cum, row, len_row, owner_row, *blocks, *after)

    def token(*after, flops=1):
        return call(
            token_kernel, shape((8, 128)), flops=flops, in_specs=[anywhere] * len(after)
        )(*after)

    def fresh_part(*after):
        return call(
            functools.partial(fresh_kernel, tokens),
            (shape((count, STEPS, lanes)),) * 2 + (shape((count, STEPS, 128)),),
            in_specs=[in_vmem] * 8 + [anywhere] * len(after),
        )(x_dec, b_dec, asked_here, dt_dec, a_row, d_row, len_row, owner_row, *after)

    def outer_part(parts, carry, before, *after):
        part = parts[-1]
        out = shape((len(part), tokens, width), BF16)
        operands = [c, cum, carry, *[got[count - 1, k] for k in part], *inner, *before]
        return call(
            functools.partial(outer_kernel, parts, count),
            (pltpu.HBM((tokens, lanes), BF16), shape((8, 128))) if before else out,
            in_specs=[in_vmem] * len(operands) + [anywhere] * len(after),
            out_specs=(in_hbm, in_vmem) if before else in_vmem,
            scratch_shapes=[out, pltpu.SemaphoreType.DMA((chunks,))] if before else [],
        )(*operands, *after)

    def read_part(ops, final, *after):
        arrived = [got[count - 1, k] for k in range(chunks)] if final else []
        operands = [local, gain, asked, carry, *arrived]
        return call(
            functools.partial(read_kernel, count, chunks, ops, final),
            (shape((STEPS, lanes), BF16),) * len(ops) + (shape((STEPS, lanes)),) * final,
            in_specs=[in_vmem] * len(operands) + [anywhere] * len(after),
        )(*operands, *after)

    got = {(1, 0): forward(sent[0], 1, 0)}
    inner = [inner_part(0)]
    for g in range(1, groups):
        inner.append(inner_part(g, inner[-1]))
    sent[1] = state_part(list(range(1, chunks)), inner[-1])
    got[1, 1] = forward(sent[1], 1, 1)
    order = sorted((k + hop, hop, k) for hop in range(1, count - 1) for k in range(chunks))
    moving = {}
    carry = tie = None
    for _, hop, k in order:
        more = hop == 1 and k + 2 < chunks
        operands = [got[hop, k], total[k], decay[k]]
        operands += [] if carry is None else [carry]
        operands += total[k + 2 : k + 3] * more + [sent[0], got[1, 0]] * (ride and (hop, k) == (1, 1))
        after = []
        if hop == count - 2 and k > 1:
            after = [token(got[hop + 1, k - 2], tie, flops=TOKEN_COST)]
        tie, carry, *following = call(
            functools.partial(pass_kernel, hop, k, more),
            (sent_shape(hop + 1, k), shape((chunks, N, width), BF16))
            + (sent_shape(1, k + 2),) * more,
            flops=PASS_COST if k % 2 == 0 else 1,
            in_specs=[in_vmem] * len(operands) + [anywhere] * len(after),
            input_output_aliases={} if carry is None else {3: 1},
        )(*operands, *after)
        moving[hop + 1, k] = tie
        got[hop + 1, k] = forward(tie, hop + 1, k)
        if more:
            got[1, k + 2] = forward(following[0], 1, k + 2)

    early, late = tuple(range(chunks // 2)), tuple(range(chunks // 2, chunks))
    four = count == 4
    local, gain, asked = ask_part(tie)
    back, ops = [], [(0, 1), (0, 2), (1, 2)] if four else []
    if four:
        reading = read_part(ops, False)
        for couple, value in zip(ops, reading):
            back.append(swap(value, couple))
    ends = [(2, 3), (1, 3), (0, 3)] if four else list(range(1, count))
    before = reading[0] if four else asked
    order_token = token(got[count - 1, chunks - 2], before, flops=TOKEN_COST)
    *reading, mine = read_part(ends, True, order_token)
    last_back = [
        swap(value, op) if four else shift(value, -op) for op, value in zip(ends, reading)
    ]
    outer = outer_part((early,), carry, [], mine)
    prefill, end_token = outer_part((early, late), carry, [outer])
    keep, fresh, held = fresh_part(end_token)
    end_token = token(keep, *back, flops=TOKEN_COST)
    ops, back = ops + ends, back + last_back

    decoded = call(
        functools.partial(finish_kernel, ops),
        jax.ShapeDtypeStruct((count, STEPS, lanes), BF16),
        in_specs=[in_vmem] * (4 + len(ops)) + [anywhere],
    )(keep, fresh, held, *back, mine, end_token)
    return (prefill, decoded[None])


def solution(mesh):
    placed = (
        P(("grp", "seq"), "tp"),
        P(("grp", "seq"), "tp"),
        P(("grp", "seq"), "tp"),
        P(("grp", "seq"), "tp"),
        P("tp"),
        P("tp"),
        P("grp"),
        P("grp"),
        P(("grp", "seq"), None, None, "tp"),
        P(("grp", "seq"), None, None, "tp"),
        P(("grp", "seq"), None, None, "tp"),
        P(("grp", "seq"), None, None, "tp"),
    )
    return jax.shard_map(
        shards,
        mesh=mesh,
        in_specs=placed,
        out_specs=(P(("grp", "seq"), "tp"), P(("grp", "seq"), None, None, "tp")),
        check_vma=False,
    )
```

```python
import functools
import math

import jax
import jax.numpy as jnp
from jax import lax
from jax.experimental import pallas as pl
from jax.experimental.pallas import tpu as pltpu
from jax.sharding import PartitionSpec as P

H = 128
P_SIZE = 64
N = 128
G = 8
SPAN = 128
STEPS = 4
LOG2E = math.log2(math.e)
F32 = jnp.float32
BF16 = jnp.bfloat16
CHUNKS = 4
TOKEN_COST = 10**8
PASS_COST = 5 * 10**8
VMEM_LIMIT = 32 * 1024 * 1024


def softplus(value):
    small = jnp.exp(-jnp.abs(value))
    series = small * (1.0 - small * (0.5 - small * (1.0 / 3.0 - small * 0.25)))
    return jnp.maximum(value, 0.0) + jnp.where(small < 0.02, series, jnp.log(1.0 + small))


def dot(left, right, left_dim=1, right_dim=0):
    return lax.dot_general(
        left, right, (((left_dim,), (right_dim,)), ((), ())), preferred_element_type=F32
    )


def split(value, pieces):
    result = []
    for _ in range(pieces):
        piece = value.astype(BF16)
        result.append(piece)
        value = value - piece.astype(F32)
    return result


def exact_dot(ones, value, pieces=3, left_dim=1):
    return sum(dot(ones, piece, left_dim) for piece in split(value, pieces))


def spread_matrix(heads, first, width):
    lane = lax.broadcasted_iota(jnp.int32, (heads, width), 1) + first
    head = lax.broadcasted_iota(jnp.int32, (heads, width), 0)
    return jnp.where(lane // P_SIZE == head, 1.0, 0.0).astype(BF16)


def over_lanes(value, first, width, pieces=2):
    return exact_dot_right(value, spread_matrix(value.shape[1], first, width), pieces)


def exact_dot_right(value, ones, pieces):
    return sum(dot(piece, ones) for piece in split(value, pieces))


def shape(dims, dtype=F32):
    return pltpu.VMEM(dims, dtype)


def pinned(value, space=pltpu.VMEM):
    return pltpu.with_memory_space_constraint(value, space)


def call(kernel, out_shape, flops=1, **options):
    name = getattr(kernel, "func", kernel).__name__
    return pl.pallas_call(
        kernel,
        name=name,
        out_shape=out_shape,
        compiler_params=pltpu.CompilerParams(vmem_limit_bytes=VMEM_LIMIT),
        cost_estimate=pl.CostEstimate(flops=flops, bytes_accessed=1, transcendentals=0),
        **options,
    )


def triangle(keep):
    row = lax.broadcasted_iota(jnp.int32, (SPAN, SPAN), 0)
    column = lax.broadcasted_iota(jnp.int32, (SPAN, SPAN), 1)
    return jnp.where(keep(row, column), 1.0, 0.0).astype(BF16)


def chunk_total(k, x_ref, turned, weight, whole, total_ref, decay_ref):
    width = total_ref.shape[1]
    first = k * width
    scaled = x_ref[:, first : first + width].astype(F32) * over_lanes(weight, first, width)
    total_ref[...] = dot(turned, scaled.astype(BF16))
    decay_ref[...] = over_lanes(whole, first, width, 3)


def first_kernel(kept, *refs):
    hbm, refs = refs[: kept + 1], refs[kept + 1 :]
    here, refs = refs[:kept], refs[kept:]
    cum_ref, row_ref, weight_ref, whole_ref, turned_ref = refs[:5]
    total_ref, decay_ref, sent_ref, dt_ref, sems = refs[5:]
    x_ref, b_ref, a_ref = here[:3]
    heads, tokens = dt_ref.shape
    spans = tokens // SPAN
    width = total_ref.shape[1]
    dt_copy = pltpu.make_async_copy(hbm[kept], dt_ref, sems.at[0])
    copies = [pltpu.make_async_copy(hbm[i], here[i], sems.at[i]) for i in range(1, kept)]
    x_copies = [
        pltpu.make_async_copy(hbm[0].at[:, lanes], x_ref.at[:, lanes], sems.at[kept + i])
        for i, lanes in enumerate((slice(0, width), slice(width, x_ref.shape[1])))
    ]
    for copy in [dt_copy, copies[1], copies[0], *x_copies, *copies[2:]]:
        copy.start()
    upper = triangle(lambda s, t: s <= t)
    eye = lax.broadcasted_iota(jnp.int32, (heads, heads), 0) == lax.broadcasted_iota(
        jnp.int32, (heads, heads), 1
    )
    dt_copy.wait()
    copies[1].wait()
    a_column = jnp.sum(jnp.where(eye, a_ref[...], 0.0), axis=1, keepdims=True)
    step = softplus(dt_ref[...].astype(F32))
    rate = step * (jnp.exp(a_column) * -LOG2E)
    cums = [exact_dot_right(rate[:, i * SPAN : (i + 1) * SPAN], upper, 3) for i in range(spans)]
    ends = [cum[:, SPAN - 1 : SPAN] for cum in cums]
    after = jnp.zeros_like(ends[0])
    weights = [None] * spans
    for i in reversed(range(spans)):
        after = after + ends[i]
        weights[i] = jnp.exp2(after - cums[i]) * step[:, i * SPAN : (i + 1) * SPAN]
    weight = jnp.concatenate(weights, axis=1).T
    whole = jnp.sum(jnp.where(eye, jnp.exp2(after), 0.0), axis=0, keepdims=True)
    weight_ref[...] = weight
    whole_ref[...] = whole
    copies[0].wait()
    turned = b_ref[:, :N].astype(F32).T.astype(BF16)
    x_copies[0].wait()
    chunk_total(0, x_ref, turned, weight, whole, total_ref, decay_ref)
    sent_ref[:N] = total_ref[...].astype(BF16)
    turned_ref[0] = turned
    for g in range(1, turned_ref.shape[0]):
        turned_ref[g] = b_ref[:, g * N : (g + 1) * N].astype(F32).T.astype(BF16)
    cum = jnp.concatenate(cums, axis=1)
    cum_ref[...] = cum
    row_ref[...] = jnp.log2(step) - cum
    x_copies[1].wait()
    for copy in copies[2:]:
        copy.wait()
    if sent_ref.shape[0] > N:
        own = flat(here[3]).astype(BF16)
        sent_ref[N:] = jnp.concatenate([own, own], axis=1)


def state_kernel(part, x_ref, turned_ref, weight_ref, whole_ref, *rest):
    results = rest[-2 * len(part) - 1 :]
    for i, k in enumerate(part):
        total_ref, decay_ref = results[2 * i : 2 * i + 2]
        g = k * total_ref.shape[1] // (H // G * P_SIZE)
        chunk_total(k, x_ref, turned_ref[g], weight_ref[...], whole_ref[...], total_ref, decay_ref)
    results[-1][...] = results[0][...].astype(BF16)


def flat(ref):
    return jnp.concatenate([ref[i].astype(F32) for i in range(ref.shape[0])], axis=0)


def token_kernel(*refs):
    refs[-1][...] = jnp.zeros_like(refs[-1])


def pass_kernel(hop, k, more, got_ref, total_ref, decay_ref, *rest):
    moving_ref, carry_ref = rest[len(rest) - 2 - more : len(rest) - more]
    me = lax.axis_index("seq")
    if hop == 1 and k == 0:
        following_ref = rest[0]
        carry_ref[...] = jnp.zeros_like(carry_ref)
    else:
        following_ref = rest[1]
    got = got_ref[:N]
    moving_ref[:N] = (total_ref[...] + decay_ref[...] * got.astype(F32)).astype(BF16)
    if moving_ref.shape[0] > N and hop == 1:
        own, other = [ref[N:].astype(F32) for ref in rest[1 + more : 3 + more]]
        lane = lax.broadcasted_iota(jnp.int32, own.shape, 1)
        mine = (lane // (own.shape[1] // 2)) == lax.rem(me, 2)
        moving_ref[N:] = jnp.where(mine, own, other).astype(BF16)
    elif moving_ref.shape[0] > N:
        moving_ref[N:] = got_ref[N:]

    @pl.when(me == hop)
    def _():
        carry_ref[k] = got

    if more:
        rest[-1][...] = following_ref[...].astype(BF16)


def pair_halves(x_part):
    first_half = lax.broadcasted_iota(jnp.int32, (1, 2 * P_SIZE), 1) < P_SIZE
    zero = jnp.zeros_like(x_part)
    return jnp.where(first_half, x_part, zero), jnp.where(first_half, zero, x_part)


def span_starts(cum, spans):
    ends = [cum[(i + 1) * SPAN - 1 : (i + 1) * SPAN, :] for i in range(spans)]
    starts = [jnp.zeros_like(ends[0])]
    for i in range(spans):
        starts.append(starts[i] + ends[i])
    return ends, starts


def inner_kernel(g, x_ref, b_ref, c_ref, cum_ref, row_ref, d_ref, *rest):
    inner_ref = rest[-1]
    heads, tokens = cum_ref.shape
    spans = tokens // SPAN
    per_group = H // G
    names = slice(g * N, (g + 1) * N)
    t_index = lax.broadcasted_iota(jnp.int32, (SPAN, SPAN), 0)
    s_index = lax.broadcasted_iota(jnp.int32, (SPAN, SPAN), 1)
    causal = t_index >= s_index
    rows = row_ref[...]
    cum = cum_ref[...].T
    ends, _ = span_starts(cum, spans)
    first_half = lax.broadcasted_iota(jnp.int32, (1, 2 * P_SIZE), 1) < P_SIZE
    scores = dot(c_ref[:, names], b_ref[:, names], 1, 1)
    for pair in range(per_group // 2):
        h0 = g * per_group + 2 * pair
        lanes = slice(h0 * P_SIZE, (h0 + 2) * P_SIZE)
        here = slice(2 * pair * P_SIZE, (2 * pair + 2) * P_SIZE)
        x_part = x_ref[:, lanes]
        halves = pair_halves(x_part)
        weights = [[None, None] for _ in range(spans)]
        for e in range(2):
            h = h0 + e
            row = rows[h : h + 1, :]
            for i in range(spans):
                column = jnp.broadcast_to(cum[i * SPAN : (i + 1) * SPAN, h : h + 1], (SPAN, SPAN))
                parts = []
                for j in range(i + 1):
                    shift = row[:, j * SPAN : (j + 1) * SPAN]
                    for m in range(j, i):
                        shift = shift + ends[m][:, h : h + 1]
                    score = scores[i * SPAN : (i + 1) * SPAN, j * SPAN : (j + 1) * SPAN]
                    part = score * jnp.exp2(column + shift)
                    if i == j:
                        part = jnp.where(causal, part, 0.0)
                    parts.append(part.astype(BF16))
                weights[i][e] = jnp.concatenate(parts, axis=1) if i else parts[0]
        skip = jnp.where(first_half, d_ref[:, h0 : h0 + 1], d_ref[:, h0 + 1 : h0 + 2])
        for i in range(spans):
            reach = (i + 1) * SPAN
            left = jnp.concatenate(weights[i], axis=1)
            right = jnp.concatenate([half[:reach] for half in halves], axis=0)
            mine = slice(i * SPAN, (i + 1) * SPAN)
            inner_ref[mine, here] = dot(left, right) + skip * x_part[mine].astype(F32)


def ask_kernel(ride, x_ref, b_ref, cum_ref, row_ref, len_ref, owner_ref, *rest):
    local_ref, gain_ref, asked_ref = rest[-3:]
    heads, tokens = cum_ref.shape
    spans = tokens // SPAN
    asks = local_ref.shape[0]
    per_group = H // G
    groups = heads // per_group
    me = lax.axis_index("seq")
    if ride:
        near, middle, far = [ref[N:].astype(F32) for ref in rest[:3]]
        far = jnp.where((me == 1) | (me == 2), middle, far)
        halves = (jnp.where(me < 2, near, far), jnp.where(me < 2, far, near))
        names = near.shape[1] // 2
        blocks = [half[:, i * names : (i + 1) * names] for half in halves for i in range(2)]
        blocks = jnp.concatenate(blocks, axis=0).astype(BF16)
        row = lax.broadcasted_iota(jnp.int32, (asks, blocks.shape[0]), 0)
        column = lax.broadcasted_iota(jnp.int32, (asks, blocks.shape[0]), 1)
        wanted = row // STEPS * asks + me * STEPS + row % STEPS
        asked = dot(jnp.where(column == wanted, 1.0, 0.0).astype(BF16), blocks).astype(BF16)
    else:
        blocks = [rest[0][r, me].astype(F32) for r in range(asks // STEPS)]
        asked = jnp.concatenate(blocks, axis=0).astype(BF16)
    asked_ref[...] = asked
    block = lax.broadcasted_iota(jnp.int32, (asks, 1), 0) // STEPS
    spot = len_ref[...] - 1 - me * tokens
    mine = (owner_ref[...] == block) & (spot >= 0) & (spot < tokens)
    spot = jnp.sum(jnp.where(mine, spot, 0).astype(F32), axis=1, keepdims=True).astype(jnp.int32)
    position = lax.broadcasted_iota(jnp.int32, (asks, tokens), 1)
    picked = jnp.where(position == spot, 1.0, 0.0).astype(BF16)
    upto = position <= spot
    rows = row_ref[...]
    cum = cum_ref[...].T
    ends, starts = span_starts(cum, spans)
    near_ask = exact_dot(picked, cum)
    ask_start = starts[0]
    for i in range(1, spans):
        ask_start = jnp.where(spot >= i * SPAN, starts[i], ask_start)
    gain_ref[...] = jnp.exp2(near_ask + ask_start)
    columns = []
    for j in range(spans):
        column = near_ask
        for i in range(j + 1, spans):
            column = jnp.where(spot // SPAN == i, near_ask + sum(ends[j + 1 : i], ends[j]), column)
        columns.append(column)
    for g in range(groups):
        names = slice(g * N, (g + 1) * N)
        scores = jnp.where(upto, dot(asked[:, names], b_ref[:, names], 1, 1), 0.0)
        for pair in range(per_group // 2):
            h0 = g * per_group + 2 * pair
            lanes = slice(h0 * P_SIZE, (h0 + 2) * P_SIZE)
            parts = []
            for h in (h0, h0 + 1):
                for j in range(spans):
                    span = slice(j * SPAN, (j + 1) * SPAN)
                    part = scores[:, span] * jnp.exp2(columns[j][:, h : h + 1] + rows[h : h + 1, span])
                    parts.append(jnp.where(upto[:, span], part, 0.0).astype(BF16))
            right = jnp.concatenate(pair_halves(x_ref[:, lanes]), axis=0)
            local_ref[:, lanes] = dot(jnp.concatenate(parts, axis=1), right)


def read_kernel(count, chunks, ops, final, local_ref, gain_ref, asked_ref, carry_ref, *rest):
    got_refs, rest = rest[: chunks * final], rest[chunks * final :]
    read_refs = rest[-(len(ops) + final) :]
    me = lax.axis_index("seq")
    lanes = local_ref.shape[1]
    width = lanes // chunks
    for k in range(chunks):
        first = k * width
        here = slice(first, first + width)
        g = first // (H // G * P_SIZE)
        state = carry_ref[k]
        if final:
            state = jnp.where(me == count - 1, got_refs[k][:N], state)
        carried = dot(asked_ref[:, g * N : (g + 1) * N], state)
        reading = local_ref[:, here] + over_lanes(gain_ref[...], first, width) * carried
        parts = [reading[r * STEPS : (r + 1) * STEPS] for r in range(count)]
        for op, read_ref in zip(ops, read_refs):
            if isinstance(op, tuple):
                part = jnp.where(me == op[0], parts[op[1]], parts[op[0]])
            else:
                part = parts[0]
                for r in range(1, count):
                    part = jnp.where(lax.rem(me + count - op, count) == r, parts[r], part)
            read_ref[:, here] = part.astype(read_ref.dtype)
        if final:
            own = parts[0]
            for r in range(1, count):
                own = jnp.where(me == r, parts[r], own)
            read_refs[-1][:, here] = own


def outer_kernel(parts, count, c_ref, cum_ref, carry_ref, *rest):
    final = len(parts) > 1
    part = parts[-1]
    got_refs = rest[: len(part)]
    inner_refs = rest[len(part) : len(part) + cum_ref.shape[0] // (H // G)]
    if final:
        early_ref, out_hbm, token_ref, out_ref, sems = rest[-5:]
        token_ref[...] = jnp.zeros_like(token_ref)
    else:
        out_ref = rest[-1]
    heads, tokens = cum_ref.shape
    spans = tokens // SPAN
    width = got_refs[0].shape[1]
    group_lanes = H // G * P_SIZE
    copies = []

    def send(source, k):
        lanes = slice(k * width, (k + 1) * width)
        copies.append(pltpu.make_async_copy(source, out_hbm.at[:, lanes], sems.at[k]))
        copies[-1].start()

    if final:
        for i, k in enumerate(parts[0]):
            send(early_ref.at[i], k)
    last = lax.axis_index("seq") == count - 1
    start = jnp.zeros((heads, 1), F32)
    gains = []
    for i in range(spans):
        cum = cum_ref[:, i * SPAN : (i + 1) * SPAN]
        gains.append(jnp.exp2(cum + start))
        start = start + cum[:, SPAN - 1 : SPAN]
    gain = jnp.concatenate(gains, axis=1).T
    for i, k in enumerate(part):
        first = k * width
        g = first // group_lanes
        state = jnp.where(last, got_refs[i][:N], carry_ref[k])
        carried = dot(c_ref[:, g * N : (g + 1) * N], state)
        inner = inner_refs[g][:, first - g * group_lanes : first - g * group_lanes + width]
        out_ref[i] = (inner + over_lanes(gain, first, width) * carried).astype(BF16)
        if final:
            send(out_ref.at[i], k)
    for copy in copies:
        copy.wait()


def fresh_kernel(tokens, x_ref, b_ref, c_ref, dt_ref, a_ref, d_ref, len_ref, owner_ref, *rest):
    keep_ref, fresh_ref, held_ref = rest[-3:]
    count, _, heads = dt_ref.shape
    rows = count * STEPS
    place = lax.broadcasted_iota(jnp.int32, (rows, 1), 0) // STEPS * tokens
    spot = len_ref[...] - 1 - place
    mine = (owner_ref[...] == lax.axis_index("seq")) & (spot >= 0) & (spot < tokens)
    held = jnp.sum(jnp.where(mine, 1.0, 0.0), axis=1, keepdims=True)
    held = jnp.broadcast_to(held, (rows, held_ref.shape[2]))
    per_group = H // G
    groups = heads // per_group
    width = x_ref.shape[2]
    turn = lax.broadcasted_iota(jnp.int32, (rows, 1), 0) % STEPS
    step = softplus(flat(dt_ref))
    rate = step * (jnp.exp(a_ref[...]) * -LOG2E)

    def earlier(value, gap):
        if not gap:
            return value
        moved = jnp.concatenate([jnp.zeros_like(value[:gap]), value[:-gap]], axis=0)
        return jnp.where(turn >= gap, moved, 0.0)

    running = sum(earlier(rate, gap) for gap in range(STEPS))
    keep = over_lanes(jnp.exp2(running), 0, width)
    x_values = flat(x_ref)
    b_values = flat(b_ref)
    c_values = flat(c_ref)
    head = lax.broadcasted_iota(jnp.int32, (rows, heads), 1)
    fresh = over_lanes(d_ref[...], 0, width, 3) * x_values
    since = jnp.zeros_like(rate)
    for gap in range(STEPS):
        if gap:
            since = since + earlier(rate, gap - 1)
        products = c_values * earlier(b_values, gap)
        pair = jnp.zeros((rows, heads), F32)
        for g in range(groups):
            score = jnp.sum(products[:, g * N : (g + 1) * N], axis=1, keepdims=True)
            pair = jnp.where(head // per_group == g, score, pair)
        factor = jnp.where(turn >= gap, jnp.exp2(since) * earlier(step, gap) * pair, 0.0)
        fresh = fresh + over_lanes(factor, 0, width) * earlier(x_values, gap)
    for i in range(rows // STEPS):
        keep_ref[i] = keep[i * STEPS : (i + 1) * STEPS]
        fresh_ref[i] = fresh[i * STEPS : (i + 1) * STEPS]
        held_ref[i] = held[i * STEPS : (i + 1) * STEPS]


def finish_kernel(ops, keep_ref, fresh_ref, held_ref, *rest):
    count = keep_ref.shape[0]
    back_refs, own_ref, out_ref = rest[: len(ops)], rest[len(ops)], rest[-1]
    me = lax.axis_index("seq")

    def finish(source, reading):
        value = reading * keep_ref[source] + fresh_ref[source]
        held = held_ref[source][:, :1] > 0.0
        out_ref[source] = jnp.where(held, value, 0.0).astype(BF16)

    if isinstance(ops[0], tuple):
        for source in range(count):
            reading = own_ref[...]
            for (one, other), back_ref in zip(ops, back_refs):
                if source in (one, other):
                    owner = one + other - source
                    reading = jnp.where(me == owner, back_ref[...].astype(F32), reading)
            finish(source, reading)
    else:
        finish(me, own_ref[...])
        for r, back_ref in zip(ops, back_refs):
            finish(lax.rem(me + r, count), back_ref[...].astype(F32))


def shards(
    ssm_input, bmat, cmat, dt_raw, a_log, d_skip, prompt_len, owner, dec_x, dec_b, dec_c, dec_dt
):
    count = lax.axis_size("seq")
    tensor = lax.axis_size("tp")
    tokens, heads = dt_raw.shape
    groups = heads // (H // G)
    names = groups * N
    lanes = heads * P_SIZE
    group_lanes = lanes // groups
    rows = count * STEPS
    chunks = CHUNKS if count <= 4 else groups
    width = lanes // chunks
    anywhere = pl.BlockSpec(memory_space=pl.ANY)
    in_hbm = pl.BlockSpec(memory_space=pltpu.HBM)
    in_vmem = pl.BlockSpec(memory_space=pltpu.VMEM)
    ride = count == 4 and width == 2 * names

    def sent_shape(hop, k):
        return shape((N + rows * (ride and (hop, k) in ((1, 0), (2, 1), (3, 1))), width), BF16)

    inputs = [
        ssm_input,
        bmat,
        a_log.reshape(1, heads),
        dec_c[0],
        cmat,
        d_skip.reshape(1, heads),
        prompt_len.reshape(1, -1),
        owner.reshape(1, -1),
        dec_x[0],
        dec_b[0],
        dec_dt[0],
    ]
    chunk_shapes = (shape((N, width)), shape((1, width)))
    results = call(
        functools.partial(first_kernel, len(inputs)),
        tuple(shape(value.shape, value.dtype) for value in inputs)
        + (
            shape((heads, tokens)),
            shape((heads, tokens)),
            shape((tokens, heads)),
            shape((1, heads)),
            shape((groups, N, tokens), BF16),
        )
        + chunk_shapes
        + (sent_shape(1, 0),),
        in_specs=[in_hbm] * (len(inputs) + 1),
        scratch_shapes=[
            pltpu.VMEM((heads, tokens), BF16),
            pltpu.SemaphoreType.DMA((len(inputs) + 2,)),
        ],
    )(*[pinned(value, pltpu.HBM) for value in inputs + [dt_raw.T]])
    x, b, a_row, asked_here, c, d_row, len_row, owner_row, x_dec, b_dec, dt_dec = results[:11]
    cum, row, weight, whole, turned = results[11:16]
    total, decay = [results[16]], [results[17]]
    all_asked = None if ride else lax.all_gather(dec_c[0], "seq")
    sent = {0: results[18]}

    def state_part(part, tie):
        out = call(
            functools.partial(state_kernel, part),
            chunk_shapes * len(part) + (sent_shape(1, 1),),
            in_specs=[in_vmem] * 4 + [anywhere],
        )(x, turned, weight, whole, tie)
        total.extend(out[0 : 2 * len(part) : 2])
        decay.extend(out[1 : 2 * len(part) : 2])
        return out[-1]

    def swap(value, *couples):
        partner = {}
        for one, other in couples:
            partner.update({one: other, other: one})
        pairs = []
        for d in range(count):
            for t in range(tensor):
                there = partner[d] * tensor + t if d in partner else d * tensor + (t ^ 1)
                pairs.append((d * tensor + t, there))
        return lax.ppermute(value, ("seq", "tp"), pairs)

    def forward(value, hop, k):
        with jax.named_scope(f"hop{hop}_chunk{k}"):
            rides = ride and (hop, k) in ((1, 0), (3, 1))
            return swap(value, *([(0, 1), (2, 3)] if rides else [(hop - 1, hop)]))

    def shift(value, by):
        return lax.ppermute(value, "seq", [(d, (d + by) % count) for d in range(count)])

    def inner_part(g, *after):
        return call(
            functools.partial(inner_kernel, g),
            shape((tokens, group_lanes)),
            in_specs=[in_vmem] * 6 + [anywhere] * len(after),
        )(x, b, c, cum, row, d_row, *after)

    def ask_part(*after):
        blocks = (moving[2, 1], got[2, 1], got[3, 1]) if ride else (all_asked,)
        return call(
            functools.partial(ask_kernel, ride),
            (shape((rows, lanes)), shape((rows, heads)), shape((rows, names), BF16)),
            in_specs=[in_vmem] * (6 + len(blocks)) + [anywhere] * len(after),
        )(x, b, cum, row, len_row, owner_row, *blocks, *after)

    def token(*after, flops=1):
        return call(
            token_kernel, shape((8, 128)), flops=flops, in_specs=[anywhere] * len(after)
        )(*after)

    def fresh_part(*after):
        return call(
            functools.partial(fresh_kernel, tokens),
            (shape((count, STEPS, lanes)),) * 2 + (shape((count, STEPS, 128)),),
            in_specs=[in_vmem] * 8 + [anywhere] * len(after),
        )(x_dec, b_dec, asked_here, dt_dec, a_row, d_row, len_row, owner_row, *after)

    def outer_part(parts, carry, before, *after):
        part = parts[-1]
        out = shape((len(part), tokens, width), BF16)
        operands = [c, cum, carry, *[got[count - 1, k] for k in part], *inner, *before]
        return call(
            functools.partial(outer_kernel, parts, count),
            (pltpu.HBM((tokens, lanes), BF16), shape((8, 128))) if before else out,
            in_specs=[in_vmem] * len(operands) + [anywhere] * len(after),
            out_specs=(in_hbm, in_vmem) if before else in_vmem,
            scratch_shapes=[out, pltpu.SemaphoreType.DMA((chunks,))] if before else [],
        )(*operands, *after)

    def read_part(ops, final, *after):
        arrived = [got[count - 1, k] for k in range(chunks)] if final else []
        operands = [local, gain, asked, carry, *arrived]
        return call(
            functools.partial(read_kernel, count, chunks, ops, final),
            (shape((STEPS, lanes), BF16),) * len(ops) + (shape((STEPS, lanes)),) * final,
            in_specs=[in_vmem] * len(operands) + [anywhere] * len(after),
        )(*operands, *after)

    got = {(1, 0): forward(sent[0], 1, 0)}
    inner = [inner_part(0)]
    for g in range(1, groups):
        inner.append(inner_part(g, inner[-1]))
    sent[1] = state_part(list(range(1, chunks)), inner[-1])
    got[1, 1] = forward(sent[1], 1, 1)
    order = sorted((k + hop, hop, k) for hop in range(1, count - 1) for k in range(chunks))
    moving = {}
    carry = tie = None
    for _, hop, k in order:
        more = hop == 1 and k + 2 < chunks
        operands = [got[hop, k], total[k], decay[k]]
        operands += [] if carry is None else [carry]
        operands += total[k + 2 : k + 3] * more + [sent[0], got[1, 0]] * (ride and (hop, k) == (1, 1))
        after = []
        if (hop, k) == (1, 1):
            keep, fresh, held = fresh_part(tie)
            after = [keep]
        if hop == count - 2 and k > 1:
            after = [token(got[hop + 1, k - 2], tie, flops=TOKEN_COST)]
        tie, carry, *following = call(
            functools.partial(pass_kernel, hop, k, more),
            (sent_shape(hop + 1, k), shape((chunks, N, width), BF16))
            + (sent_shape(1, k + 2),) * more,
            flops=PASS_COST if k % 2 == 0 else 1,
            in_specs=[in_vmem] * len(operands) + [anywhere] * len(after),
            input_output_aliases={} if carry is None else {3: 1},
        )(*operands, *after)
        moving[hop + 1, k] = tie
        got[hop + 1, k] = forward(tie, hop + 1, k)
        if more:
            got[1, k + 2] = forward(following[0], 1, k + 2)

    early, late = tuple(range(chunks // 2)), tuple(range(chunks // 2, chunks))
    four = count == 4
    local, gain, asked = ask_part(tie)
    back, ops = [], [(0, 1), (0, 2), (1, 2)] if four else []
    if four:
        reading = read_part(ops, False)
        for couple, value in zip(ops, reading):
            back.append(swap(value, couple))
    ends = [(0, 3), (1, 3), (2, 3)] if four else list(range(1, count))
    before = reading[0] if four else asked
    order_token = token(got[count - 1, chunks - 2], before, flops=TOKEN_COST)
    *reading, mine = read_part(ends, True, order_token)
    last_back = [
        swap(value, op) if four else shift(value, -op) for op, value in zip(ends, reading)
    ]
    outer = outer_part((early,), carry, [], mine)
    prefill, end_token = outer_part((early, late), carry, [outer])
    end_token = token(end_token, *back, flops=TOKEN_COST)
    ops, back = ops + ends, back + last_back

    decoded = call(
        functools.partial(finish_kernel, ops),
        jax.ShapeDtypeStruct((count, STEPS, lanes), BF16),
        in_specs=[in_vmem] * (4 + len(ops)) + [anywhere],
    )(keep, fresh, held, *back, mine, end_token)
    return (prefill, decoded[None])


def solution(mesh):
    placed = (
        P(("grp", "seq"), "tp"),
        P(("grp", "seq"), "tp"),
        P(("grp", "seq"), "tp"),
        P(("grp", "seq"), "tp"),
        P("tp"),
        P("tp"),
        P("grp"),
        P("grp"),
        P(("grp", "seq"), None, None, "tp"),
        P(("grp", "seq"), None, None, "tp"),
        P(("grp", "seq"), None, None, "tp"),
        P(("grp", "seq"), None, None, "tp"),
    )
    return jax.shard_map(
        shards,
        mesh=mesh,
        in_specs=placed,
        out_specs=(P(("grp", "seq"), "tp"), P(("grp", "seq"), None, None, "tp")),
        check_vma=False,
    )
```

```python
import functools
import math

import jax
import jax.numpy as jnp
from jax import lax
from jax.experimental import pallas as pl
from jax.experimental.pallas import tpu as pltpu
from jax.sharding import PartitionSpec as P

H = 128
P_SIZE = 64
N = 128
G = 8
SPAN = 128
STEPS = 4
LOG2E = math.log2(math.e)
F32 = jnp.float32
BF16 = jnp.bfloat16
CHUNKS = 4
TOKEN_COST = 10**8
PASS_COST = 8 * 10**8
VMEM_LIMIT = 32 * 1024 * 1024


def softplus(value):
    small = jnp.exp(-jnp.abs(value))
    series = small * (1.0 - small * (0.5 - small * (1.0 / 3.0 - small * 0.25)))
    return jnp.maximum(value, 0.0) + jnp.where(small < 0.02, series, jnp.log(1.0 + small))


def dot(left, right, left_dim=1, right_dim=0):
    return lax.dot_general(
        left, right, (((left_dim,), (right_dim,)), ((), ())), preferred_element_type=F32
    )


def split(value, pieces):
    result = []
    for _ in range(pieces):
        piece = value.astype(BF16)
        result.append(piece)
        value = value - piece.astype(F32)
    return result


def exact_dot(ones, value, pieces=3, left_dim=1):
    return sum(dot(ones, piece, left_dim) for piece in split(value, pieces))


def spread_matrix(heads, first, width):
    lane = lax.broadcasted_iota(jnp.int32, (heads, width), 1) + first
    head = lax.broadcasted_iota(jnp.int32, (heads, width), 0)
    return jnp.where(lane // P_SIZE == head, 1.0, 0.0).astype(BF16)


def over_lanes(value, first, width, pieces=2):
    return exact_dot_right(value, spread_matrix(value.shape[1], first, width), pieces)


def exact_dot_right(value, ones, pieces):
    return sum(dot(piece, ones) for piece in split(value, pieces))


def shape(dims, dtype=F32):
    return pltpu.VMEM(dims, dtype)


def pinned(value, space=pltpu.VMEM):
    return pltpu.with_memory_space_constraint(value, space)


def call(kernel, out_shape, flops=1, **options):
    name = getattr(kernel, "func", kernel).__name__
    return pl.pallas_call(
        kernel,
        name=name,
        out_shape=out_shape,
        compiler_params=pltpu.CompilerParams(vmem_limit_bytes=VMEM_LIMIT),
        cost_estimate=pl.CostEstimate(flops=flops, bytes_accessed=1, transcendentals=0),
        **options,
    )


def triangle(keep):
    row = lax.broadcasted_iota(jnp.int32, (SPAN, SPAN), 0)
    column = lax.broadcasted_iota(jnp.int32, (SPAN, SPAN), 1)
    return jnp.where(keep(row, column), 1.0, 0.0).astype(BF16)


def chunk_total(first, x_ref, turned, weight, total_ref):
    width = total_ref.shape[1]
    scaled = x_ref[:, first : first + width].astype(F32) * over_lanes(weight, first, width)
    total_ref[...] = dot(turned, scaled.astype(BF16))


def first_kernel(kept, *refs):
    hbm, refs = refs[: kept + 1], refs[kept + 1 :]
    here, refs = refs[:kept], refs[kept:]
    cum_ref, row_ref, weight_ref, whole_ref = refs[:4]
    total_ref, sent_ref, dt_ref, sems = refs[4:]
    x_ref, b_ref, a_ref = here[:3]
    heads, tokens = dt_ref.shape
    spans = tokens // SPAN
    width = total_ref.shape[1]
    dt_copy = pltpu.make_async_copy(hbm[kept], dt_ref, sems.at[0])
    copies = [pltpu.make_async_copy(hbm[i], here[i], sems.at[i]) for i in range(1, kept)]
    x_copies = [
        pltpu.make_async_copy(hbm[0].at[:, lanes], x_ref.at[:, lanes], sems.at[kept + i])
        for i, lanes in enumerate((slice(0, width), slice(width, x_ref.shape[1])))
    ]
    for copy in [dt_copy, copies[1], copies[0], *x_copies, *copies[2:]]:
        copy.start()
    upper = triangle(lambda s, t: s <= t)
    eye = lax.broadcasted_iota(jnp.int32, (heads, heads), 0) == lax.broadcasted_iota(
        jnp.int32, (heads, heads), 1
    )
    dt_copy.wait()
    copies[1].wait()
    a_column = jnp.sum(jnp.where(eye, a_ref[...], 0.0), axis=1, keepdims=True)
    step = softplus(dt_ref[...].astype(F32))
    rate = step * (jnp.exp(a_column) * -LOG2E)
    cums = [exact_dot_right(rate[:, i * SPAN : (i + 1) * SPAN], upper, 3) for i in range(spans)]
    ends = [cum[:, SPAN - 1 : SPAN] for cum in cums]
    after = jnp.zeros_like(ends[0])
    weights = [None] * spans
    for i in reversed(range(spans)):
        after = after + ends[i]
        weights[i] = jnp.exp2(after - cums[i]) * step[:, i * SPAN : (i + 1) * SPAN]
    weight = jnp.concatenate(weights, axis=1).T
    whole = jnp.sum(jnp.where(eye, jnp.exp2(after), 0.0), axis=0, keepdims=True)
    weight_ref[...] = weight
    whole_ref[...] = whole
    copies[0].wait()
    turned = b_ref[:, :N].astype(F32).T.astype(BF16)
    x_copies[0].wait()
    chunk_total(0, x_ref, turned, weight, total_ref)
    sent_ref[:N] = total_ref[...].astype(BF16)
    cum = jnp.concatenate(cums, axis=1)
    cum_ref[...] = cum
    row_ref[...] = jnp.log2(step) - cum
    x_copies[1].wait()
    for copy in copies[2:]:
        copy.wait()
    if sent_ref.shape[0] > N:
        own = flat(here[3]).astype(BF16)
        padding = jnp.zeros((own.shape[0], sent_ref.shape[1] - own.shape[1]), BF16)
        sent_ref[N:] = jnp.concatenate([own, padding], axis=1)


def state_kernel(bounds, x_ref, b_ref, weight_ref, whole_ref, *rest):
    chunks = len(bounds) - 1
    results = rest[-2 * chunks :]
    decay_refs, total_refs, sent_ref = results[:chunks], results[chunks:-1], results[-1]
    turned = [
        b_ref[:, g * N : (g + 1) * N].astype(F32).T.astype(BF16)
        for g in range(b_ref.shape[1] // N)
    ]
    for k in range(chunks):
        first = bounds[k]
        decay_refs[k][...] = over_lanes(whole_ref[...], first, bounds[k + 1] - first, 3)
        if k:
            g = first // (H // G * P_SIZE)
            chunk_total(first, x_ref, turned[g], weight_ref[...], total_refs[k - 1])
    sent_ref[...] = total_refs[0][...].astype(BF16)


def flat(ref):
    return jnp.concatenate([ref[i].astype(F32) for i in range(ref.shape[0])], axis=0)


def token_kernel(*refs):
    refs[-1][...] = jnp.zeros_like(refs[-1])


def pass_kernel(hop, first, more, got_ref, total_ref, decay_ref, *rest):
    moving_ref, carry_ref = rest[len(rest) - 2 - more : len(rest) - more]
    me = lax.axis_index("seq")
    groups = carry_ref.shape[1] // (H // G * P_SIZE)
    if hop == 1 and first == 0:
        following_ref = rest[0]
        carry_ref[...] = jnp.zeros_like(carry_ref)
    else:
        following_ref = rest[1]
    got = got_ref[:N]
    moving_ref[:N] = (total_ref[...] + decay_ref[...] * got.astype(F32)).astype(BF16)
    if moving_ref.shape[0] > N and hop == 1:
        names = groups * N
        own, other = [ref[N:, :names].astype(F32) for ref in rest[1 + more : 3 + more]]
        even = lax.rem(me, 2) == 0
        padding = jnp.zeros((own.shape[0], moving_ref.shape[1] - 2 * names), F32)
        pair = [jnp.where(even, own, other), jnp.where(even, other, own), padding]
        moving_ref[N:] = jnp.concatenate(pair, axis=1).astype(BF16)
    elif moving_ref.shape[0] > N:
        moving_ref[N:] = got_ref[N:]

    @pl.when(me == hop)
    def _():
        carry_ref[:, first : first + got.shape[1]] = got

    if more:
        rest[-1][...] = following_ref[...].astype(BF16)


def pair_halves(x_part):
    first_half = lax.broadcasted_iota(jnp.int32, (1, 2 * P_SIZE), 1) < P_SIZE
    zero = jnp.zeros_like(x_part)
    return jnp.where(first_half, x_part, zero), jnp.where(first_half, zero, x_part)


def span_starts(cum, spans):
    ends = [cum[(i + 1) * SPAN - 1 : (i + 1) * SPAN, :] for i in range(spans)]
    starts = [jnp.zeros_like(ends[0])]
    for i in range(spans):
        starts.append(starts[i] + ends[i])
    return ends, starts


def inner_kernel(g, x_ref, b_ref, c_ref, cum_ref, row_ref, d_ref, *rest):
    inner_ref = rest[-1]
    heads, tokens = cum_ref.shape
    spans = tokens // SPAN
    per_group = H // G
    names = slice(g * N, (g + 1) * N)
    t_index = lax.broadcasted_iota(jnp.int32, (SPAN, SPAN), 0)
    s_index = lax.broadcasted_iota(jnp.int32, (SPAN, SPAN), 1)
    causal = t_index >= s_index
    rows = row_ref[...]
    cum = cum_ref[...].T
    ends, _ = span_starts(cum, spans)
    first_half = lax.broadcasted_iota(jnp.int32, (1, 2 * P_SIZE), 1) < P_SIZE
    scores = dot(c_ref[:, names], b_ref[:, names], 1, 1)
    for pair in range(per_group // 2):
        h0 = g * per_group + 2 * pair
        lanes = slice(h0 * P_SIZE, (h0 + 2) * P_SIZE)
        here = slice(2 * pair * P_SIZE, (2 * pair + 2) * P_SIZE)
        x_part = x_ref[:, lanes]
        halves = pair_halves(x_part)
        weights = [[None, None] for _ in range(spans)]
        for e in range(2):
            h = h0 + e
            row = rows[h : h + 1, :]
            for i in range(spans):
                column = jnp.broadcast_to(cum[i * SPAN : (i + 1) * SPAN, h : h + 1], (SPAN, SPAN))
                parts = []
                for j in range(i + 1):
                    shift = row[:, j * SPAN : (j + 1) * SPAN]
                    for m in range(j, i):
                        shift = shift + ends[m][:, h : h + 1]
                    score = scores[i * SPAN : (i + 1) * SPAN, j * SPAN : (j + 1) * SPAN]
                    part = score * jnp.exp2(column + shift)
                    if i == j:
                        part = jnp.where(causal, part, 0.0)
                    parts.append(part.astype(BF16))
                weights[i][e] = jnp.concatenate(parts, axis=1) if i else parts[0]
        skip = jnp.where(first_half, d_ref[:, h0 : h0 + 1], d_ref[:, h0 + 1 : h0 + 2])
        for i in range(spans):
            reach = (i + 1) * SPAN
            left = jnp.concatenate(weights[i], axis=1)
            right = jnp.concatenate([half[:reach] for half in halves], axis=0)
            mine = slice(i * SPAN, (i + 1) * SPAN)
            inner_ref[mine, here] = dot(left, right) + skip * x_part[mine].astype(F32)


def ask_kernel(ride, x_ref, b_ref, cum_ref, row_ref, len_ref, owner_ref, *rest):
    local_ref, gain_ref, asked_ref = rest[-3:]
    heads, tokens = cum_ref.shape
    spans = tokens // SPAN
    asks = local_ref.shape[0]
    per_group = H // G
    groups = heads // per_group
    me = lax.axis_index("seq")
    if ride:
        near, middle, far = [ref[N:].astype(F32) for ref in rest[:3]]
        far = jnp.where((me == 1) | (me == 2), middle, far)
        halves = (jnp.where(me < 2, near, far), jnp.where(me < 2, far, near))
        names = b_ref.shape[1]
        blocks = [half[:, i * names : (i + 1) * names] for half in halves for i in range(2)]
        blocks = jnp.concatenate(blocks, axis=0).astype(BF16)
        row = lax.broadcasted_iota(jnp.int32, (asks, blocks.shape[0]), 0)
        column = lax.broadcasted_iota(jnp.int32, (asks, blocks.shape[0]), 1)
        wanted = row // STEPS * asks + me * STEPS + row % STEPS
        asked = dot(jnp.where(column == wanted, 1.0, 0.0).astype(BF16), blocks).astype(BF16)
    else:
        blocks = [rest[0][r, me].astype(F32) for r in range(asks // STEPS)]
        asked = jnp.concatenate(blocks, axis=0).astype(BF16)
    asked_ref[...] = asked
    block = lax.broadcasted_iota(jnp.int32, (asks, 1), 0) // STEPS
    spot = len_ref[...] - 1 - me * tokens
    mine = (owner_ref[...] == block) & (spot >= 0) & (spot < tokens)
    spot = jnp.sum(jnp.where(mine, spot, 0).astype(F32), axis=1, keepdims=True).astype(jnp.int32)
    position = lax.broadcasted_iota(jnp.int32, (asks, tokens), 1)
    picked = jnp.where(position == spot, 1.0, 0.0).astype(BF16)
    upto = position <= spot
    rows = row_ref[...]
    cum = cum_ref[...].T
    ends, starts = span_starts(cum, spans)
    near_ask = exact_dot(picked, cum)
    ask_start = starts[0]
    for i in range(1, spans):
        ask_start = jnp.where(spot >= i * SPAN, starts[i], ask_start)
    gain_ref[...] = jnp.exp2(near_ask + ask_start)
    columns = []
    for j in range(spans):
        column = near_ask
        for i in range(j + 1, spans):
            column = jnp.where(spot // SPAN == i, near_ask + sum(ends[j + 1 : i], ends[j]), column)
        columns.append(column)
    for g in range(groups):
        names = slice(g * N, (g + 1) * N)
        scores = jnp.where(upto, dot(asked[:, names], b_ref[:, names], 1, 1), 0.0)
        for pair in range(per_group // 2):
            h0 = g * per_group + 2 * pair
            lanes = slice(h0 * P_SIZE, (h0 + 2) * P_SIZE)
            parts = []
            for h in (h0, h0 + 1):
                for j in range(spans):
                    span = slice(j * SPAN, (j + 1) * SPAN)
                    part = scores[:, span] * jnp.exp2(columns[j][:, h : h + 1] + rows[h : h + 1, span])
                    parts.append(jnp.where(upto[:, span], part, 0.0).astype(BF16))
            right = jnp.concatenate(pair_halves(x_ref[:, lanes]), axis=0)
            local_ref[:, lanes] = dot(jnp.concatenate(parts, axis=1), right)


def read_kernel(count, bounds, ops, final, local_ref, gain_ref, asked_ref, carry_ref, *rest):
    chunks = len(bounds) - 1
    got_refs, rest = rest[: chunks * final], rest[chunks * final :]
    read_refs = rest[-(len(ops) + final) :]
    me = lax.axis_index("seq")
    for k in range(chunks):
        first = bounds[k]
        width = bounds[k + 1] - first
        here = slice(first, first + width)
        g = first // (H // G * P_SIZE)
        state = carry_ref[:, here]
        if final:
            state = jnp.where(me == count - 1, got_refs[k][:N], state)
        carried = dot(asked_ref[:, g * N : (g + 1) * N], state)
        reading = local_ref[:, here] + over_lanes(gain_ref[...], first, width) * carried
        parts = [reading[r * STEPS : (r + 1) * STEPS] for r in range(count)]
        for op, read_ref in zip(ops, read_refs):
            if isinstance(op, tuple):
                part = jnp.where(me == op[0], parts[op[1]], parts[op[0]])
            else:
                part = parts[0]
                for r in range(1, count):
                    part = jnp.where(lax.rem(me + count - op, count) == r, parts[r], part)
            read_ref[:, here] = part.astype(read_ref.dtype)
        if final:
            own = parts[0]
            for r in range(1, count):
                own = jnp.where(me == r, parts[r], own)
            read_refs[-1][:, here] = own


def outer_kernel(parts, bounds, count, c_ref, cum_ref, carry_ref, *rest):
    final = len(parts) > 1
    part = parts[-1]
    got_refs = rest[: len(part)]
    inner_refs = rest[len(part) : len(part) + cum_ref.shape[0] // (H // G)]
    if final:
        early_ref, out_hbm, token_ref, out_ref, sems = rest[-5:]
        token_ref[...] = jnp.zeros_like(token_ref)
    else:
        out_ref = rest[-1]
    heads, tokens = cum_ref.shape
    spans = tokens // SPAN
    group_lanes = H // G * P_SIZE
    copies = []

    def send(source, first, width):
        lanes = slice(first, first + width)
        copies.append(pltpu.make_async_copy(source, out_hbm.at[:, lanes], sems.at[len(copies)]))
        copies[-1].start()

    if final:
        send(early_ref, 0, early_ref.shape[1])
    last = lax.axis_index("seq") == count - 1
    start = jnp.zeros((heads, 1), F32)
    gains = []
    for i in range(spans):
        cum = cum_ref[:, i * SPAN : (i + 1) * SPAN]
        gains.append(jnp.exp2(cum + start))
        start = start + cum[:, SPAN - 1 : SPAN]
    gain = jnp.concatenate(gains, axis=1).T
    for i, k in enumerate(part):
        first = bounds[k]
        width = bounds[k + 1] - first
        g = first // group_lanes
        state = jnp.where(last, got_refs[i][:N], carry_ref[:, first : first + width])
        carried = dot(c_ref[:, g * N : (g + 1) * N], state)
        inner = inner_refs[g][:, first - g * group_lanes : first - g * group_lanes + width]
        here = slice(first - bounds[part[0]], first - bounds[part[0]] + width)
        out_ref[:, here] = (inner + over_lanes(gain, first, width) * carried).astype(BF16)
        if final:
            send(out_ref.at[:, here], first, width)
    for copy in copies:
        copy.wait()


def fresh_kernel(tokens, x_ref, b_ref, c_ref, dt_ref, a_ref, d_ref, len_ref, owner_ref, *rest):
    keep_ref, fresh_ref, held_ref = rest[-3:]
    count, _, heads = dt_ref.shape
    rows = count * STEPS
    place = lax.broadcasted_iota(jnp.int32, (rows, 1), 0) // STEPS * tokens
    spot = len_ref[...] - 1 - place
    mine = (owner_ref[...] == lax.axis_index("seq")) & (spot >= 0) & (spot < tokens)
    held = jnp.sum(jnp.where(mine, 1.0, 0.0), axis=1, keepdims=True)
    held = jnp.broadcast_to(held, (rows, held_ref.shape[2]))
    per_group = H // G
    groups = heads // per_group
    width = x_ref.shape[2]
    turn = lax.broadcasted_iota(jnp.int32, (rows, 1), 0) % STEPS
    step = softplus(flat(dt_ref))
    rate = step * (jnp.exp(a_ref[...]) * -LOG2E)

    def earlier(value, gap):
        if not gap:
            return value
        moved = jnp.concatenate([jnp.zeros_like(value[:gap]), value[:-gap]], axis=0)
        return jnp.where(turn >= gap, moved, 0.0)

    running = sum(earlier(rate, gap) for gap in range(STEPS))
    keep = over_lanes(jnp.exp2(running), 0, width)
    x_values = flat(x_ref)
    b_values = flat(b_ref)
    c_values = flat(c_ref)
    head = lax.broadcasted_iota(jnp.int32, (rows, heads), 1)
    fresh = over_lanes(d_ref[...], 0, width, 3) * x_values
    since = jnp.zeros_like(rate)
    for gap in range(STEPS):
        if gap:
            since = since + earlier(rate, gap - 1)
        products = c_values * earlier(b_values, gap)
        pair = jnp.zeros((rows, heads), F32)
        for g in range(groups):
            score = jnp.sum(products[:, g * N : (g + 1) * N], axis=1, keepdims=True)
            pair = jnp.where(head // per_group == g, score, pair)
        factor = jnp.where(turn >= gap, jnp.exp2(since) * earlier(step, gap) * pair, 0.0)
        fresh = fresh + over_lanes(factor, 0, width) * earlier(x_values, gap)
    for i in range(rows // STEPS):
        keep_ref[i] = keep[i * STEPS : (i + 1) * STEPS]
        fresh_ref[i] = fresh[i * STEPS : (i + 1) * STEPS]
        held_ref[i] = held[i * STEPS : (i + 1) * STEPS]


def finish_kernel(ops, keep_ref, fresh_ref, held_ref, *rest):
    count = keep_ref.shape[0]
    back_refs, own_ref, out_ref = rest[: len(ops)], rest[len(ops)], rest[-1]
    me = lax.axis_index("seq")

    def finish(source, reading):
        value = reading * keep_ref[source] + fresh_ref[source]
        held = held_ref[source][:, :1] > 0.0
        out_ref[source] = jnp.where(held, value, 0.0).astype(BF16)

    if isinstance(ops[0], tuple):
        for source in range(count):
            reading = own_ref[...]
            for (one, other), back_ref in zip(ops, back_refs):
                if source in (one, other):
                    owner = one + other - source
                    reading = jnp.where(me == owner, back_ref[...].astype(F32), reading)
            finish(source, reading)
    else:
        finish(me, own_ref[...])
        for r, back_ref in zip(ops, back_refs):
            finish(lax.rem(me + r, count), back_ref[...].astype(F32))


def shards(
    ssm_input, bmat, cmat, dt_raw, a_log, d_skip, prompt_len, owner, dec_x, dec_b, dec_c, dec_dt
):
    count = lax.axis_size("seq")
    tensor = lax.axis_size("tp")
    tokens, heads = dt_raw.shape
    groups = heads // (H // G)
    names = groups * N
    lanes = heads * P_SIZE
    group_lanes = lanes // groups
    rows = count * STEPS
    chunks = CHUNKS if count <= 4 else groups
    bounds = tuple(lanes * k // chunks for k in range(chunks + 1))
    if chunks > groups:
        bounds = bounds[:1] + (bounds[1] - 128,) + bounds[2:]
    widths = [bounds[k + 1] - bounds[k] for k in range(chunks)]
    anywhere = pl.BlockSpec(memory_space=pl.ANY)
    in_hbm = pl.BlockSpec(memory_space=pltpu.HBM)
    in_vmem = pl.BlockSpec(memory_space=pltpu.VMEM)
    ride = count == 4 and widths[0] >= names and widths[1] >= 2 * names

    def sent_shape(hop, k):
        return shape((N + rows * (ride and (hop, k) in ((1, 0), (2, 1), (3, 1))), widths[k]), BF16)

    inputs = [
        ssm_input,
        bmat,
        a_log.reshape(1, heads),
        dec_c[0],
        cmat,
        d_skip.reshape(1, heads),
        prompt_len.reshape(1, -1),
        owner.reshape(1, -1),
        dec_x[0],
        dec_b[0],
        dec_dt[0],
    ]
    total_shapes = tuple(shape((N, width)) for width in widths)
    decay_shapes = tuple(shape((1, width)) for width in widths)
    results = call(
        functools.partial(first_kernel, len(inputs)),
        tuple(shape(value.shape, value.dtype) for value in inputs)
        + (
            shape((heads, tokens)),
            shape((heads, tokens)),
            shape((tokens, heads)),
            shape((1, heads)),
            total_shapes[0],
            sent_shape(1, 0),
        ),
        in_specs=[in_hbm] * (len(inputs) + 1),
        scratch_shapes=[
            pltpu.VMEM((heads, tokens), BF16),
            pltpu.SemaphoreType.DMA((len(inputs) + 2,)),
        ],
    )(*[pinned(value, pltpu.HBM) for value in inputs + [dt_raw.T]])
    x, b, a_row, asked_here, c, d_row, len_row, owner_row, x_dec, b_dec, dt_dec = results[:11]
    cum, row, weight, whole = results[11:15]
    total, sent = [results[15]], {0: results[16]}
    all_asked = None if ride else lax.all_gather(dec_c[0], "seq")

    def state_part(tie):
        return call(
            functools.partial(state_kernel, bounds),
            decay_shapes + total_shapes[1:] + (sent_shape(1, 1),),
            in_specs=[in_vmem] * 4 + [anywhere],
        )(x, b, weight, whole, tie)

    def swap(value, *couples):
        partner = {}
        for one, other in couples:
            partner.update({one: other, other: one})
        pairs = []
        for d in range(count):
            for t in range(tensor):
                there = partner[d] * tensor + t if d in partner else d * tensor + (t ^ 1)
                pairs.append((d * tensor + t, there))
        return lax.ppermute(value, ("seq", "tp"), pairs)

    def forward(value, hop, k):
        with jax.named_scope(f"hop{hop}_chunk{k}"):
            rides = ride and (hop, k) in ((1, 0), (3, 1))
            return swap(value, *([(0, 1), (2, 3)] if rides else [(hop - 1, hop)]))

    def shift(value, by):
        return lax.ppermute(value, "seq", [(d, (d + by) % count) for d in range(count)])

    def inner_part(g, *after):
        return call(
            functools.partial(inner_kernel, g),
            shape((tokens, group_lanes)),
            in_specs=[in_vmem] * 6 + [anywhere] * len(after),
        )(x, b, c, cum, row, d_row, *after)

    def ask_part(*after):
        blocks = (moving[2, 1], got[2, 1], got[3, 1]) if ride else (all_asked,)
        return call(
            functools.partial(ask_kernel, ride),
            (shape((rows, lanes)), shape((rows, heads)), shape((rows, names), BF16)),
            in_specs=[in_vmem] * (6 + len(blocks)) + [anywhere] * len(after),
        )(x, b, cum, row, len_row, owner_row, *blocks, *after)

    def token(*after, flops=1):
        return call(
            token_kernel, shape((8, 128)), flops=flops, in_specs=[anywhere] * len(after)
        )(*after)

    def fresh_part(*after):
        return call(
            functools.partial(fresh_kernel, tokens),
            (shape((count, STEPS, lanes)),) * 2 + (shape((count, STEPS, 128)),),
            in_specs=[in_vmem] * 8 + [anywhere] * len(after),
        )(x_dec, b_dec, asked_here, dt_dec, a_row, d_row, len_row, owner_row, *after)

    def outer_part(parts, carry, before, *after):
        part = parts[-1]
        out = shape((tokens, sum(widths[k] for k in part)), BF16)
        operands = [c, cum, carry, *[got[count - 1, k] for k in part], *inner, *before]
        return call(
            functools.partial(outer_kernel, parts, bounds, count),
            (pltpu.HBM((tokens, lanes), BF16), shape((8, 128))) if before else out,
            in_specs=[in_vmem] * len(operands) + [anywhere] * len(after),
            out_specs=(in_hbm, in_vmem) if before else in_vmem,
            scratch_shapes=[out, pltpu.SemaphoreType.DMA((chunks,))] if before else [],
        )(*operands, *after)

    def read_part(ops, final, *after):
        arrived = [got[count - 1, k] for k in range(chunks)] if final else []
        operands = [local, gain, asked, carry, *arrived]
        return call(
            functools.partial(read_kernel, count, bounds, ops, final),
            (shape((STEPS, lanes), BF16),) * len(ops) + (shape((STEPS, lanes)),) * final,
            in_specs=[in_vmem] * len(operands) + [anywhere] * len(after),
        )(*operands, *after)

    got = {(1, 0): forward(sent[0], 1, 0)}
    inner = [inner_part(0)]
    for g in range(1, groups):
        inner.append(inner_part(g, inner[-1]))
    *parts, sent[1] = state_part(inner[-1])
    decay, total = parts[:chunks], total + parts[chunks:]
    got[1, 1] = forward(sent[1], 1, 1)
    order = sorted((k + hop, hop, k) for hop in range(1, count - 1) for k in range(chunks))
    moving = {}
    carry = tie = None
    for _, hop, k in order:
        more = hop == 1 and k + 2 < chunks
        operands = [got[hop, k], total[k], decay[k]]
        operands += [] if carry is None else [carry]
        operands += total[k + 2 : k + 3] * more + [sent[0], got[1, 0]] * (ride and (hop, k) == (1, 1))
        after = []
        if (hop, k) == (1, 1):
            keep, fresh, held = fresh_part(tie)
            after = [keep]
        if hop == count - 2 and k > 1:
            after = [token(got[hop + 1, k - 2], tie, flops=5 * TOKEN_COST)]
        tie, carry, *following = call(
            functools.partial(pass_kernel, hop, bounds[k], more),
            (sent_shape(hop + 1, k), shape((N, lanes), BF16))
            + ((sent_shape(1, k + 2),) if more else ()),
            flops=PASS_COST if k % 2 == 0 else 1,
            in_specs=[in_vmem] * len(operands) + [anywhere] * len(after),
            input_output_aliases={} if carry is None else {3: 1},
        )(*operands, *after)
        moving[hop + 1, k] = tie
        got[hop + 1, k] = forward(tie, hop + 1, k)
        if more:
            got[1, k + 2] = forward(following[0], 1, k + 2)

    early, late = tuple(range(chunks // 2)), tuple(range(chunks // 2, chunks))
    four = count == 4
    local, gain, asked = ask_part(tie)
    back, ops = [], [(0, 1), (0, 2), (1, 2)] if four else []
    if four:
        reading = read_part(ops, False)
        for couple, value in zip(ops, reading):
            back.append(swap(value, couple))
    ends = [(0, 3), (2, 3), (1, 3)] if four else list(range(1, count))
    before = reading[0] if four else asked
    order_token = token(got[count - 1, chunks - 2], before, flops=TOKEN_COST)
    *reading, mine = read_part(ends, True, order_token)
    last_back = [
        swap(value, op) if four else shift(value, -op) for op, value in zip(ends, reading)
    ]
    outer = outer_part((early,), carry, [], mine)
    prefill, end_token = outer_part((early, late), carry, [outer])
    end_token = token(end_token, *back, flops=TOKEN_COST)
    ops, back = ops + ends, back + last_back

    decoded = call(
        functools.partial(finish_kernel, ops),
        jax.ShapeDtypeStruct((count, STEPS, lanes), BF16),
        in_specs=[in_vmem] * (4 + len(ops)) + [anywhere],
    )(keep, fresh, held, *back, mine, end_token)
    return (prefill, decoded[None])


def solution(mesh):
    placed = (
        P(("grp", "seq"), "tp"),
        P(("grp", "seq"), "tp"),
        P(("grp", "seq"), "tp"),
        P(("grp", "seq"), "tp"),
        P("tp"),
        P("tp"),
        P("grp"),
        P("grp"),
        P(("grp", "seq"), None, None, "tp"),
        P(("grp", "seq"), None, None, "tp"),
        P(("grp", "seq"), None, None, "tp"),
        P(("grp", "seq"), None, None, "tp"),
    )
    return jax.shard_map(
        shards,
        mesh=mesh,
        in_specs=placed,
        out_specs=(P(("grp", "seq"), "tp"), P(("grp", "seq"), None, None, "tp")),
        check_vma=False,
    )
```

```python
import functools
import math

import jax
import jax.numpy as jnp
from jax import lax
from jax.experimental import pallas as pl
from jax.experimental.pallas import tpu as pltpu
from jax.sharding import PartitionSpec as P

H = 128
P_SIZE = 64
N = 128
G = 8
SPAN = 128
STEPS = 4
LOG2E = math.log2(math.e)
F32 = jnp.float32
BF16 = jnp.bfloat16
CHUNKS = 4
TOKEN_COST = 10**8
PASS_COST = 8 * 10**8
VMEM_LIMIT = 32 * 1024 * 1024


def softplus(value):
    small = jnp.exp(-jnp.abs(value))
    series = small * (1.0 - small * (0.5 - small * (1.0 / 3.0 - small * 0.25)))
    return jnp.maximum(value, 0.0) + jnp.where(small < 0.02, series, jnp.log(1.0 + small))


def dot(left, right, left_dim=1, right_dim=0):
    return lax.dot_general(
        left, right, (((left_dim,), (right_dim,)), ((), ())), preferred_element_type=F32
    )


def split(value, pieces):
    result = []
    for _ in range(pieces):
        piece = value.astype(BF16)
        result.append(piece)
        value = value - piece.astype(F32)
    return result


def exact_dot(ones, value, pieces=3, left_dim=1):
    return sum(dot(ones, piece, left_dim) for piece in split(value, pieces))


def spread_matrix(heads, first, width):
    lane = lax.broadcasted_iota(jnp.int32, (heads, width), 1) + first
    head = lax.broadcasted_iota(jnp.int32, (heads, width), 0)
    return jnp.where(lane // P_SIZE == head, 1.0, 0.0).astype(BF16)


def over_lanes(value, first, width, pieces=2):
    return exact_dot_right(value, spread_matrix(value.shape[1], first, width), pieces)


def exact_dot_right(value, ones, pieces):
    return sum(dot(piece, ones) for piece in split(value, pieces))


def shape(dims, dtype=F32):
    return pltpu.VMEM(dims, dtype)


def pinned(value, space=pltpu.VMEM):
    return pltpu.with_memory_space_constraint(value, space)


def call(kernel, out_shape, flops=1, **options):
    name = getattr(kernel, "func", kernel).__name__
    return pl.pallas_call(
        kernel,
        name=name,
        out_shape=out_shape,
        compiler_params=pltpu.CompilerParams(vmem_limit_bytes=VMEM_LIMIT),
        cost_estimate=pl.CostEstimate(flops=flops, bytes_accessed=1, transcendentals=0),
        **options,
    )


def triangle(keep):
    row = lax.broadcasted_iota(jnp.int32, (SPAN, SPAN), 0)
    column = lax.broadcasted_iota(jnp.int32, (SPAN, SPAN), 1)
    return jnp.where(keep(row, column), 1.0, 0.0).astype(BF16)


def chunk_total(first, x_ref, turned, weight, total_ref):
    width = total_ref.shape[1]
    scaled = x_ref[:, first : first + width].astype(F32) * over_lanes(weight, first, width)
    total_ref[...] = dot(turned, scaled.astype(BF16))


def first_kernel(kept, *refs):
    hbm, refs = refs[: kept + 1], refs[kept + 1 :]
    here, refs = refs[:kept], refs[kept:]
    cum_ref, row_ref, weight_ref, whole_ref = refs[:4]
    total_ref, sent_ref, dt_ref, sems = refs[4:]
    x_ref, b_ref, a_ref = here[:3]
    heads, tokens = dt_ref.shape
    spans = tokens // SPAN
    width = total_ref.shape[1]
    dt_copy = pltpu.make_async_copy(hbm[kept], dt_ref, sems.at[0])
    copies = [pltpu.make_async_copy(hbm[i], here[i], sems.at[i]) for i in range(1, kept)]
    x_copies = [
        pltpu.make_async_copy(hbm[0].at[:, lanes], x_ref.at[:, lanes], sems.at[kept + i])
        for i, lanes in enumerate((slice(0, width), slice(width, x_ref.shape[1])))
    ]
    for copy in [dt_copy, copies[1], copies[0], *x_copies, *copies[2:]]:
        copy.start()
    upper = triangle(lambda s, t: s <= t)
    eye = lax.broadcasted_iota(jnp.int32, (heads, heads), 0) == lax.broadcasted_iota(
        jnp.int32, (heads, heads), 1
    )
    dt_copy.wait()
    copies[1].wait()
    a_column = jnp.sum(jnp.where(eye, a_ref[...], 0.0), axis=1, keepdims=True)
    step = softplus(dt_ref[...].astype(F32))
    rate = step * (jnp.exp(a_column) * -LOG2E)
    cums = [exact_dot_right(rate[:, i * SPAN : (i + 1) * SPAN], upper, 3) for i in range(spans)]
    ends = [cum[:, SPAN - 1 : SPAN] for cum in cums]
    after = jnp.zeros_like(ends[0])
    weights = [None] * spans
    for i in reversed(range(spans)):
        after = after + ends[i]
        weights[i] = jnp.exp2(after - cums[i]) * step[:, i * SPAN : (i + 1) * SPAN]
    weight = jnp.concatenate(weights, axis=1).T
    whole = jnp.sum(jnp.where(eye, jnp.exp2(after), 0.0), axis=0, keepdims=True)
    weight_ref[...] = weight
    whole_ref[...] = whole
    copies[0].wait()
    turned = b_ref[:, :N].astype(F32).T.astype(BF16)
    x_copies[0].wait()
    chunk_total(0, x_ref, turned, weight, total_ref)
    sent_ref[:N] = total_ref[...].astype(BF16)
    cum = jnp.concatenate(cums, axis=1)
    cum_ref[...] = cum
    row_ref[...] = jnp.log2(step) - cum
    x_copies[1].wait()
    for copy in copies[2:]:
        copy.wait()
    if sent_ref.shape[0] > N:
        own = flat(here[3]).astype(BF16)
        padding = jnp.zeros((own.shape[0], sent_ref.shape[1] - own.shape[1]), BF16)
        sent_ref[N:] = jnp.concatenate([own, padding], axis=1)


def state_kernel(bounds, x_ref, b_ref, weight_ref, whole_ref, *rest):
    chunks = len(bounds) - 1
    results = rest[-2 * chunks :]
    decay_refs, total_refs, sent_ref = results[:chunks], results[chunks:-1], results[-1]
    turned = [
        b_ref[:, g * N : (g + 1) * N].astype(F32).T.astype(BF16)
        for g in range(b_ref.shape[1] // N)
    ]
    for k in range(chunks):
        first = bounds[k]
        decay_refs[k][...] = over_lanes(whole_ref[...], first, bounds[k + 1] - first, 3)
        if k:
            g = first // (H // G * P_SIZE)
            chunk_total(first, x_ref, turned[g], weight_ref[...], total_refs[k - 1])
    sent_ref[...] = total_refs[0][...].astype(BF16)


def flat(ref):
    return jnp.concatenate([ref[i].astype(F32) for i in range(ref.shape[0])], axis=0)


def token_kernel(*refs):
    refs[-1][...] = jnp.zeros_like(refs[-1])


def pass_kernel(hop, first, more, got_ref, total_ref, decay_ref, *rest):
    moving_ref, carry_ref = rest[len(rest) - 2 - more : len(rest) - more]
    me = lax.axis_index("seq")
    groups = carry_ref.shape[1] // (H // G * P_SIZE)
    if hop == 1 and first == 0:
        following_ref = rest[0]
        carry_ref[...] = jnp.zeros_like(carry_ref)
    else:
        following_ref = rest[1]
    got = got_ref[:N]
    moving_ref[:N] = (total_ref[...] + decay_ref[...] * got.astype(F32)).astype(BF16)
    if moving_ref.shape[0] > N and hop == 1:
        names = groups * N
        own, other = [ref[N:, :names].astype(F32) for ref in rest[1 + more : 3 + more]]
        even = lax.rem(me, 2) == 0
        padding = jnp.zeros((own.shape[0], moving_ref.shape[1] - 2 * names), F32)
        pair = [jnp.where(even, own, other), jnp.where(even, other, own), padding]
        moving_ref[N:] = jnp.concatenate(pair, axis=1).astype(BF16)
    elif moving_ref.shape[0] > N:
        moving_ref[N:] = got_ref[N:]

    @pl.when(me == hop)
    def _():
        carry_ref[:, first : first + got.shape[1]] = got

    if more:
        rest[-1][...] = following_ref[...].astype(BF16)


def pair_halves(x_part):
    first_half = lax.broadcasted_iota(jnp.int32, (1, 2 * P_SIZE), 1) < P_SIZE
    zero = jnp.zeros_like(x_part)
    return jnp.where(first_half, x_part, zero), jnp.where(first_half, zero, x_part)


def span_starts(cum, spans):
    ends = [cum[(i + 1) * SPAN - 1 : (i + 1) * SPAN, :] for i in range(spans)]
    starts = [jnp.zeros_like(ends[0])]
    for i in range(spans):
        starts.append(starts[i] + ends[i])
    return ends, starts


def inner_kernel(g, x_ref, b_ref, c_ref, cum_ref, row_ref, d_ref, *rest):
    inner_ref = rest[-1]
    heads, tokens = cum_ref.shape
    spans = tokens // SPAN
    per_group = H // G
    names = slice(g * N, (g + 1) * N)
    t_index = lax.broadcasted_iota(jnp.int32, (SPAN, SPAN), 0)
    s_index = lax.broadcasted_iota(jnp.int32, (SPAN, SPAN), 1)
    causal = t_index >= s_index
    rows = row_ref[...]
    cum = cum_ref[...].T
    ends, _ = span_starts(cum, spans)
    first_half = lax.broadcasted_iota(jnp.int32, (1, 2 * P_SIZE), 1) < P_SIZE
    scores = dot(c_ref[:, names], b_ref[:, names], 1, 1)
    for pair in range(per_group // 2):
        h0 = g * per_group + 2 * pair
        lanes = slice(h0 * P_SIZE, (h0 + 2) * P_SIZE)
        here = slice(2 * pair * P_SIZE, (2 * pair + 2) * P_SIZE)
        x_part = x_ref[:, lanes]
        halves = pair_halves(x_part)
        weights = [[None, None] for _ in range(spans)]
        for e in range(2):
            h = h0 + e
            row = rows[h : h + 1, :]
            for i in range(spans):
                column = jnp.broadcast_to(cum[i * SPAN : (i + 1) * SPAN, h : h + 1], (SPAN, SPAN))
                parts = []
                for j in range(i + 1):
                    shift = row[:, j * SPAN : (j + 1) * SPAN]
                    for m in range(j, i):
                        shift = shift + ends[m][:, h : h + 1]
                    score = scores[i * SPAN : (i + 1) * SPAN, j * SPAN : (j + 1) * SPAN]
                    part = score * jnp.exp2(column + shift)
                    if i == j:
                        part = jnp.where(causal, part, 0.0)
                    parts.append(part.astype(BF16))
                weights[i][e] = jnp.concatenate(parts, axis=1) if i else parts[0]
        skip = jnp.where(first_half, d_ref[:, h0 : h0 + 1], d_ref[:, h0 + 1 : h0 + 2])
        for i in range(spans):
            reach = (i + 1) * SPAN
            left = jnp.concatenate(weights[i], axis=1)
            right = jnp.concatenate([half[:reach] for half in halves], axis=0)
            mine = slice(i * SPAN, (i + 1) * SPAN)
            inner_ref[mine, here] = dot(left, right) + skip * x_part[mine].astype(F32)


def ask_kernel(ride, x_ref, b_ref, cum_ref, row_ref, len_ref, owner_ref, *rest):
    local_ref, gain_ref, asked_ref = rest[-3:]
    heads, tokens = cum_ref.shape
    spans = tokens // SPAN
    asks = local_ref.shape[0]
    per_group = H // G
    groups = heads // per_group
    me = lax.axis_index("seq")
    if ride:
        near, middle, far = [ref[N:].astype(F32) for ref in rest[:3]]
        far = jnp.where((me == 1) | (me == 2), middle, far)
        halves = (jnp.where(me < 2, near, far), jnp.where(me < 2, far, near))
        names = b_ref.shape[1]
        blocks = [half[:, i * names : (i + 1) * names] for half in halves for i in range(2)]
        blocks = jnp.concatenate(blocks, axis=0).astype(BF16)
        row = lax.broadcasted_iota(jnp.int32, (asks, blocks.shape[0]), 0)
        column = lax.broadcasted_iota(jnp.int32, (asks, blocks.shape[0]), 1)
        wanted = row // STEPS * asks + me * STEPS + row % STEPS
        asked = dot(jnp.where(column == wanted, 1.0, 0.0).astype(BF16), blocks).astype(BF16)
    else:
        blocks = [rest[0][r, me].astype(F32) for r in range(asks // STEPS)]
        asked = jnp.concatenate(blocks, axis=0).astype(BF16)
    asked_ref[...] = asked
    block = lax.broadcasted_iota(jnp.int32, (asks, 1), 0) // STEPS
    spot = len_ref[...] - 1 - me * tokens
    mine = (owner_ref[...] == block) & (spot >= 0) & (spot < tokens)
    spot = jnp.sum(jnp.where(mine, spot, 0).astype(F32), axis=1, keepdims=True).astype(jnp.int32)
    position = lax.broadcasted_iota(jnp.int32, (asks, tokens), 1)
    picked = jnp.where(position == spot, 1.0, 0.0).astype(BF16)
    upto = position <= spot
    rows = row_ref[...]
    cum = cum_ref[...].T
    ends, starts = span_starts(cum, spans)
    near_ask = exact_dot(picked, cum)
    ask_start = starts[0]
    for i in range(1, spans):
        ask_start = jnp.where(spot >= i * SPAN, starts[i], ask_start)
    gain_ref[...] = jnp.exp2(near_ask + ask_start)
    columns = []
    for j in range(spans):
        column = near_ask
        for i in range(j + 1, spans):
            column = jnp.where(spot // SPAN == i, near_ask + sum(ends[j + 1 : i], ends[j]), column)
        columns.append(column)
    for g in range(groups):
        names = slice(g * N, (g + 1) * N)
        scores = jnp.where(upto, dot(asked[:, names], b_ref[:, names], 1, 1), 0.0)
        for pair in range(per_group // 2):
            h0 = g * per_group + 2 * pair
            lanes = slice(h0 * P_SIZE, (h0 + 2) * P_SIZE)
            parts = []
            for h in (h0, h0 + 1):
                for j in range(spans):
                    span = slice(j * SPAN, (j + 1) * SPAN)
                    part = scores[:, span] * jnp.exp2(columns[j][:, h : h + 1] + rows[h : h + 1, span])
                    parts.append(jnp.where(upto[:, span], part, 0.0).astype(BF16))
            right = jnp.concatenate(pair_halves(x_ref[:, lanes]), axis=0)
            local_ref[:, lanes] = dot(jnp.concatenate(parts, axis=1), right)


def read_kernel(count, bounds, ops, final, local_ref, gain_ref, asked_ref, carry_ref, *rest):
    chunks = len(bounds) - 1
    got_refs, rest = rest[: chunks * final], rest[chunks * final :]
    read_refs = rest[-(len(ops) + final) :]
    me = lax.axis_index("seq")
    for k in range(chunks):
        first = bounds[k]
        width = bounds[k + 1] - first
        here = slice(first, first + width)
        g = first // (H // G * P_SIZE)
        state = carry_ref[:, here]
        if final:
            state = jnp.where(me == count - 1, got_refs[k][:N], state)
        carried = dot(asked_ref[:, g * N : (g + 1) * N], state)
        reading = local_ref[:, here] + over_lanes(gain_ref[...], first, width) * carried
        parts = [reading[r * STEPS : (r + 1) * STEPS] for r in range(count)]
        for op, read_ref in zip(ops, read_refs):
            if isinstance(op, tuple):
                part = jnp.where(me == op[0], parts[op[1]], parts[op[0]])
            else:
                part = parts[0]
                for r in range(1, count):
                    part = jnp.where(lax.rem(me + count - op, count) == r, parts[r], part)
            read_ref[:, here] = part.astype(read_ref.dtype)
        if final:
            own = parts[0]
            for r in range(1, count):
                own = jnp.where(me == r, parts[r], own)
            read_refs[-1][:, here] = own


def outer_kernel(parts, bounds, count, c_ref, cum_ref, carry_ref, *rest):
    final = len(parts) > 1
    part = parts[-1]
    got_refs = rest[: len(part)]
    inner_refs = rest[len(part) : len(part) + cum_ref.shape[0] // (H // G)]
    if final:
        early_ref, out_hbm, token_ref, out_ref, sems = rest[-5:]
        token_ref[...] = jnp.zeros_like(token_ref)
    else:
        out_ref = rest[-1]
    heads, tokens = cum_ref.shape
    spans = tokens // SPAN
    group_lanes = H // G * P_SIZE
    copies = []

    def send(source, first, width):
        lanes = slice(first, first + width)
        copies.append(pltpu.make_async_copy(source, out_hbm.at[:, lanes], sems.at[len(copies)]))
        copies[-1].start()

    if final:
        send(early_ref, 0, early_ref.shape[1])
    last = lax.axis_index("seq") == count - 1
    start = jnp.zeros((heads, 1), F32)
    gains = []
    for i in range(spans):
        cum = cum_ref[:, i * SPAN : (i + 1) * SPAN]
        gains.append(jnp.exp2(cum + start))
        start = start + cum[:, SPAN - 1 : SPAN]
    gain = jnp.concatenate(gains, axis=1).T
    for i, k in enumerate(part):
        first = bounds[k]
        width = bounds[k + 1] - first
        g = first // group_lanes
        state = jnp.where(last, got_refs[i][:N], carry_ref[:, first : first + width])
        carried = dot(c_ref[:, g * N : (g + 1) * N], state)
        inner = inner_refs[g][:, first - g * group_lanes : first - g * group_lanes + width]
        here = slice(first - bounds[part[0]], first - bounds[part[0]] + width)
        out_ref[:, here] = (inner + over_lanes(gain, first, width) * carried).astype(BF16)
        if final:
            send(out_ref.at[:, here], first, width)
    for copy in copies:
        copy.wait()


def fresh_kernel(tokens, x_ref, b_ref, c_ref, dt_ref, a_ref, d_ref, len_ref, owner_ref, *rest):
    keep_ref, fresh_ref, held_ref = rest[-3:]
    count, _, heads = dt_ref.shape
    rows = count * STEPS
    place = lax.broadcasted_iota(jnp.int32, (rows, 1), 0) // STEPS * tokens
    spot = len_ref[...] - 1 - place
    mine = (owner_ref[...] == lax.axis_index("seq")) & (spot >= 0) & (spot < tokens)
    held = jnp.sum(jnp.where(mine, 1.0, 0.0), axis=1, keepdims=True)
    held = jnp.broadcast_to(held, (rows, held_ref.shape[2]))
    per_group = H // G
    groups = heads // per_group
    width = x_ref.shape[2]
    turn = lax.broadcasted_iota(jnp.int32, (rows, 1), 0) % STEPS
    step = softplus(flat(dt_ref))
    rate = step * (jnp.exp(a_ref[...]) * -LOG2E)

    def earlier(value, gap):
        if not gap:
            return value
        moved = jnp.concatenate([jnp.zeros_like(value[:gap]), value[:-gap]], axis=0)
        return jnp.where(turn >= gap, moved, 0.0)

    running = sum(earlier(rate, gap) for gap in range(STEPS))
    keep = over_lanes(jnp.exp2(running), 0, width)
    x_values = flat(x_ref)
    b_values = flat(b_ref)
    c_values = flat(c_ref)
    head = lax.broadcasted_iota(jnp.int32, (rows, heads), 1)
    fresh = over_lanes(d_ref[...], 0, width, 3) * x_values
    since = jnp.zeros_like(rate)
    for gap in range(STEPS):
        if gap:
            since = since + earlier(rate, gap - 1)
        products = c_values * earlier(b_values, gap)
        pair = jnp.zeros((rows, heads), F32)
        for g in range(groups):
            score = jnp.sum(products[:, g * N : (g + 1) * N], axis=1, keepdims=True)
            pair = jnp.where(head // per_group == g, score, pair)
        factor = jnp.where(turn >= gap, jnp.exp2(since) * earlier(step, gap) * pair, 0.0)
        fresh = fresh + over_lanes(factor, 0, width) * earlier(x_values, gap)
    for i in range(rows // STEPS):
        keep_ref[i] = keep[i * STEPS : (i + 1) * STEPS]
        fresh_ref[i] = fresh[i * STEPS : (i + 1) * STEPS]
        held_ref[i] = held[i * STEPS : (i + 1) * STEPS]


def finish_kernel(ops, keep_ref, fresh_ref, held_ref, *rest):
    count = keep_ref.shape[0]
    back_refs, own_ref, out_ref = rest[: len(ops)], rest[len(ops)], rest[-1]
    me = lax.axis_index("seq")

    def finish(source, reading):
        value = reading * keep_ref[source] + fresh_ref[source]
        held = held_ref[source][:, :1] > 0.0
        out_ref[source] = jnp.where(held, value, 0.0).astype(BF16)

    if isinstance(ops[0], tuple):
        for source in range(count):
            reading = own_ref[...]
            for (one, other), back_ref in zip(ops, back_refs):
                if source in (one, other):
                    owner = one + other - source
                    reading = jnp.where(me == owner, back_ref[...].astype(F32), reading)
            finish(source, reading)
    else:
        finish(me, own_ref[...])
        for r, back_ref in zip(ops, back_refs):
            finish(lax.rem(me + r, count), back_ref[...].astype(F32))


def shards(
    ssm_input, bmat, cmat, dt_raw, a_log, d_skip, prompt_len, owner, dec_x, dec_b, dec_c, dec_dt
):
    count = lax.axis_size("seq")
    tensor = lax.axis_size("tp")
    tokens, heads = dt_raw.shape
    groups = heads // (H // G)
    names = groups * N
    lanes = heads * P_SIZE
    group_lanes = lanes // groups
    rows = count * STEPS
    chunks = CHUNKS if count <= 4 else groups
    bounds = tuple(lanes * k // chunks for k in range(chunks + 1))
    if chunks > groups:
        bounds = bounds[:1] + (bounds[1] - 128,) + bounds[2:]
    widths = [bounds[k + 1] - bounds[k] for k in range(chunks)]
    anywhere = pl.BlockSpec(memory_space=pl.ANY)
    in_hbm = pl.BlockSpec(memory_space=pltpu.HBM)
    in_vmem = pl.BlockSpec(memory_space=pltpu.VMEM)
    ride = count == 4 and widths[0] >= names and widths[1] >= 2 * names

    def sent_shape(hop, k):
        return shape((N + rows * (ride and (hop, k) in ((1, 0), (2, 1), (3, 1))), widths[k]), BF16)

    inputs = [
        ssm_input,
        bmat,
        a_log.reshape(1, heads),
        dec_c[0],
        cmat,
        d_skip.reshape(1, heads),
        prompt_len.reshape(1, -1),
        owner.reshape(1, -1),
        dec_x[0],
        dec_b[0],
        dec_dt[0],
    ]
    total_shapes = tuple(shape((N, width)) for width in widths)
    decay_shapes = tuple(shape((1, width)) for width in widths)
    results = call(
        functools.partial(first_kernel, len(inputs)),
        tuple(shape(value.shape, value.dtype) for value in inputs)
        + (
            shape((heads, tokens)),
            shape((heads, tokens)),
            shape((tokens, heads)),
            shape((1, heads)),
            total_shapes[0],
            sent_shape(1, 0),
        ),
        in_specs=[in_hbm] * (len(inputs) + 1),
        scratch_shapes=[
            pltpu.VMEM((heads, tokens), BF16),
            pltpu.SemaphoreType.DMA((len(inputs) + 2,)),
        ],
    )(*[pinned(value, pltpu.HBM) for value in inputs + [dt_raw.T]])
    x, b, a_row, asked_here, c, d_row, len_row, owner_row, x_dec, b_dec, dt_dec = results[:11]
    cum, row, weight, whole = results[11:15]
    total, sent = [results[15]], {0: results[16]}
    all_asked = None if ride else lax.all_gather(dec_c[0], "seq")

    def state_part(tie):
        return call(
            functools.partial(state_kernel, bounds),
            decay_shapes + total_shapes[1:] + (sent_shape(1, 1),),
            in_specs=[in_vmem] * 4 + [anywhere],
        )(x, b, weight, whole, tie)

    def swap(value, *couples):
        partner = {}
        for one, other in couples:
            partner.update({one: other, other: one})
        pairs = []
        for d in range(count):
            for t in range(tensor):
                there = partner[d] * tensor + t if d in partner else d * tensor + (t ^ 1)
                pairs.append((d * tensor + t, there))
        return lax.ppermute(value, ("seq", "tp"), pairs)

    def forward(value, hop, k):
        with jax.named_scope(f"hop{hop}_chunk{k}"):
            rides = ride and (hop, k) in ((1, 0), (3, 1))
            return swap(value, *([(0, 1), (2, 3)] if rides else [(hop - 1, hop)]))

    def shift(value, by):
        return lax.ppermute(value, "seq", [(d, (d + by) % count) for d in range(count)])

    def inner_part(g, *after):
        return call(
            functools.partial(inner_kernel, g),
            shape((tokens, group_lanes)),
            in_specs=[in_vmem] * 6 + [anywhere] * len(after),
        )(x, b, c, cum, row, d_row, *after)

    def ask_part(*after):
        blocks = (moving[2, 1], got[2, 1], got[3, 1]) if ride else (all_asked,)
        return call(
            functools.partial(ask_kernel, ride),
            (shape((rows, lanes)), shape((rows, heads)), shape((rows, names), BF16)),
            in_specs=[in_vmem] * (6 + len(blocks)) + [anywhere] * len(after),
        )(x, b, cum, row, len_row, owner_row, *blocks, *after)

    def token(*after, flops=1):
        return call(
            token_kernel, shape((8, 128)), flops=flops, in_specs=[anywhere] * len(after)
        )(*after)

    def fresh_part(*after):
        return call(
            functools.partial(fresh_kernel, tokens),
            (shape((count, STEPS, lanes)),) * 2 + (shape((count, STEPS, 128)),),
            in_specs=[in_vmem] * 8 + [anywhere] * len(after),
        )(x_dec, b_dec, asked_here, dt_dec, a_row, d_row, len_row, owner_row, *after)

    def outer_part(parts, carry, before, *after):
        part = parts[-1]
        out = shape((tokens, sum(widths[k] for k in part)), BF16)
        operands = [c, cum, carry, *[got[count - 1, k] for k in part], *inner, *before]
        return call(
            functools.partial(outer_kernel, parts, bounds, count),
            (pltpu.HBM((tokens, lanes), BF16), shape((8, 128))) if before else out,
            in_specs=[in_vmem] * len(operands) + [anywhere] * len(after),
            out_specs=(in_hbm, in_vmem) if before else in_vmem,
            scratch_shapes=[out, pltpu.SemaphoreType.DMA((chunks,))] if before else [],
        )(*operands, *after)

    def read_part(ops, final, *after):
        arrived = [got[count - 1, k] for k in range(chunks)] if final else []
        operands = [local, gain, asked, carry, *arrived]
        return call(
            functools.partial(read_kernel, count, bounds, ops, final),
            (shape((STEPS, lanes), BF16),) * len(ops) + (shape((STEPS, lanes)),) * final,
            in_specs=[in_vmem] * len(operands) + [anywhere] * len(after),
        )(*operands, *after)

    got = {(1, 0): forward(sent[0], 1, 0)}
    inner = [inner_part(0)]
    *parts, sent[1] = state_part(inner[-1])
    decay, total = parts[:chunks], total + parts[chunks:]
    got[1, 1] = forward(sent[1], 1, 1)
    order = sorted((k + hop, hop, k) for hop in range(1, count - 1) for k in range(chunks))
    moving = {}
    carry = tie = None
    for _, hop, k in order:
        more = hop == 1 and k + 2 < chunks
        operands = [got[hop, k], total[k], decay[k]]
        operands += [] if carry is None else [carry]
        operands += total[k + 2 : k + 3] * more + [sent[0], got[1, 0]] * (ride and (hop, k) == (1, 1))
        after = []
        if (hop, k) == (1, 1):
            for g in range(1, groups):
                inner.append(inner_part(g, tie))
            keep, fresh, held = fresh_part(inner[-1])
            after = [keep]
        if hop == count - 2 and k > 1:
            after = [token(got[hop + 1, k - 2], tie, flops=5 * TOKEN_COST)]
        tie, carry, *following = call(
            functools.partial(pass_kernel, hop, bounds[k], more),
            (sent_shape(hop + 1, k), shape((N, lanes), BF16))
            + ((sent_shape(1, k + 2),) if more else ()),
            flops=PASS_COST if k % 2 == 0 else 1,
            in_specs=[in_vmem] * len(operands) + [anywhere] * len(after),
            input_output_aliases={} if carry is None else {3: 1},
        )(*operands, *after)
        moving[hop + 1, k] = tie
        got[hop + 1, k] = forward(tie, hop + 1, k)
        if more:
            got[1, k + 2] = forward(following[0], 1, k + 2)

    early, late = tuple(range(chunks // 2)), tuple(range(chunks // 2, chunks))
    four = count == 4
    local, gain, asked = ask_part(tie)
    back, ops = [], [(0, 1), (0, 2), (1, 2)] if four else []
    if four:
        reading = read_part(ops, False)
        for couple, value in zip(ops, reading):
            back.append(swap(value, couple))
    ends = [(0, 3), (1, 3), (2, 3)] if four else list(range(1, count))
    before = reading[0] if four else asked
    order_token = token(got[count - 1, chunks - 2], before, flops=TOKEN_COST)
    *reading, mine = read_part(ends, True, order_token)
    last_back = [
        swap(value, op) if four else shift(value, -op) for op, value in zip(ends, reading)
    ]
    outer = outer_part((early,), carry, [], mine)
    prefill, end_token = outer_part((early, late), carry, [outer])
    end_token = token(end_token, *back, flops=TOKEN_COST)
    ops, back = ops + ends, back + last_back

    decoded = call(
        functools.partial(finish_kernel, ops),
        jax.ShapeDtypeStruct((count, STEPS, lanes), BF16),
        in_specs=[in_vmem] * (4 + len(ops)) + [anywhere],
    )(keep, fresh, held, *back, mine, end_token)
    return (prefill, decoded[None])


def solution(mesh):
    placed = (
        P(("grp", "seq"), "tp"),
        P(("grp", "seq"), "tp"),
        P(("grp", "seq"), "tp"),
        P(("grp", "seq"), "tp"),
        P("tp"),
        P("tp"),
        P("grp"),
        P("grp"),
        P(("grp", "seq"), None, None, "tp"),
        P(("grp", "seq"), None, None, "tp"),
        P(("grp", "seq"), None, None, "tp"),
        P(("grp", "seq"), None, None, "tp"),
    )
    return jax.shard_map(
        shards,
        mesh=mesh,
        in_specs=placed,
        out_specs=(P(("grp", "seq"), "tp"), P(("grp", "seq"), None, None, "tp")),
        check_vma=False,
    )
```

```python
import functools
import math

import jax
import jax.numpy as jnp
from jax import lax
from jax.experimental import pallas as pl
from jax.experimental.pallas import tpu as pltpu
from jax.sharding import PartitionSpec as P

H = 128
P_SIZE = 64
N = 128
G = 8
SPAN = 128
STEPS = 4
LOG2E = math.log2(math.e)
F32 = jnp.float32
BF16 = jnp.bfloat16
CHUNKS = 4
TOKEN_COST = 10**8
PASS_COSTS = {
    (1, 0): 8 * 10**8,
    (2, 0): 5 * 10**8,
    (1, 2): 8 * 10**8,
    (2, 1): 4 * 10**8,
    (2, 2): 4 * 10**8,
}
GAP_COSTS = (8 * 10**8, 5 * 10**8)
VMEM_LIMIT = 32 * 1024 * 1024


def softplus(value):
    small = jnp.exp(-jnp.abs(value))
    series = small * (1.0 - small * (0.5 - small * (1.0 / 3.0 - small * 0.25)))
    return jnp.maximum(value, 0.0) + jnp.where(small < 0.02, series, jnp.log(1.0 + small))


def dot(left, right, left_dim=1, right_dim=0):
    return lax.dot_general(
        left, right, (((left_dim,), (right_dim,)), ((), ())), preferred_element_type=F32
    )


def split(value, pieces):
    result = []
    for _ in range(pieces):
        piece = value.astype(BF16)
        result.append(piece)
        value = value - piece.astype(F32)
    return result


def exact_dot(ones, value, pieces=3, left_dim=1):
    return sum(dot(ones, piece, left_dim) for piece in split(value, pieces))


def spread_matrix(heads, first, width):
    lane = lax.broadcasted_iota(jnp.int32, (heads, width), 1) + first
    head = lax.broadcasted_iota(jnp.int32, (heads, width), 0)
    return jnp.where(lane // P_SIZE == head, 1.0, 0.0).astype(BF16)


def over_lanes(value, first, width, pieces=2):
    return exact_dot_right(value, spread_matrix(value.shape[1], first, width), pieces)


def exact_dot_right(value, ones, pieces):
    return sum(dot(piece, ones) for piece in split(value, pieces))


def shape(dims, dtype=F32):
    return pltpu.VMEM(dims, dtype)


def pinned(value, space=pltpu.VMEM):
    return pltpu.with_memory_space_constraint(value, space)


def call(kernel, out_shape, flops=1, **options):
    name = getattr(kernel, "func", kernel).__name__
    return pl.pallas_call(
        kernel,
        name=name,
        out_shape=out_shape,
        compiler_params=pltpu.CompilerParams(vmem_limit_bytes=VMEM_LIMIT),
        cost_estimate=pl.CostEstimate(flops=flops, bytes_accessed=1, transcendentals=0),
        **options,
    )


def triangle(keep):
    row = lax.broadcasted_iota(jnp.int32, (SPAN, SPAN), 0)
    column = lax.broadcasted_iota(jnp.int32, (SPAN, SPAN), 1)
    return jnp.where(keep(row, column), 1.0, 0.0).astype(BF16)


def by_group(first, last):
    group_lanes = H // G * P_SIZE
    pieces = []
    while first < last:
        g = first // group_lanes
        end = min(last, (g + 1) * group_lanes)
        pieces.append((g, first, end))
        first = end
    return pieces


def chunk_total(first, x_ref, turned, weight, total_ref):
    for g, start, end in by_group(first, first + total_ref.shape[1]):
        scaled = x_ref[:, start:end].astype(F32) * over_lanes(weight, start, end - start)
        total_ref[:, start - first : end - first] = dot(turned[g], scaled.astype(BF16))


def first_kernel(kept, *refs):
    hbm, refs = refs[: kept + 1], refs[kept + 1 :]
    here, refs = refs[:kept], refs[kept:]
    cum_ref, row_ref, weight_ref, whole_ref = refs[:4]
    total_ref, sent_ref, dt_ref, sems = refs[4:]
    x_ref, b_ref, a_ref = here[:3]
    heads, tokens = dt_ref.shape
    spans = tokens // SPAN
    width = total_ref.shape[1]
    dt_copy = pltpu.make_async_copy(hbm[kept], dt_ref, sems.at[0])
    copies = [pltpu.make_async_copy(hbm[i], here[i], sems.at[i]) for i in range(1, kept)]
    x_copies = [
        pltpu.make_async_copy(hbm[0].at[:, lanes], x_ref.at[:, lanes], sems.at[kept + i])
        for i, lanes in enumerate((slice(0, width), slice(width, x_ref.shape[1])))
    ]
    for copy in [dt_copy, copies[1], copies[0], *x_copies, *copies[2:]]:
        copy.start()
    upper = triangle(lambda s, t: s <= t)
    eye = lax.broadcasted_iota(jnp.int32, (heads, heads), 0) == lax.broadcasted_iota(
        jnp.int32, (heads, heads), 1
    )
    dt_copy.wait()
    copies[1].wait()
    a_column = jnp.sum(jnp.where(eye, a_ref[...], 0.0), axis=1, keepdims=True)
    step = softplus(dt_ref[...].astype(F32))
    rate = step * (jnp.exp(a_column) * -LOG2E)
    cums = [exact_dot_right(rate[:, i * SPAN : (i + 1) * SPAN], upper, 3) for i in range(spans)]
    ends = [cum[:, SPAN - 1 : SPAN] for cum in cums]
    after = jnp.zeros_like(ends[0])
    weights = [None] * spans
    for i in reversed(range(spans)):
        after = after + ends[i]
        weights[i] = jnp.exp2(after - cums[i]) * step[:, i * SPAN : (i + 1) * SPAN]
    weight = jnp.concatenate(weights, axis=1).T
    whole = jnp.sum(jnp.where(eye, jnp.exp2(after), 0.0), axis=0, keepdims=True)
    weight_ref[...] = weight
    whole_ref[...] = whole
    copies[0].wait()
    turned = b_ref[:, :N].astype(F32).T.astype(BF16)
    x_copies[0].wait()
    chunk_total(0, x_ref, [turned], weight, total_ref)
    sent_ref[:N] = total_ref[...].astype(BF16)
    cum = jnp.concatenate(cums, axis=1)
    cum_ref[...] = cum
    row_ref[...] = jnp.log2(step) - cum
    x_copies[1].wait()
    for copy in copies[2:]:
        copy.wait()
    if sent_ref.shape[0] > N:
        own = flat(here[3]).astype(BF16)
        sent_ref[N:, : own.shape[1]] = own


def state_kernel(bounds, x_ref, b_ref, weight_ref, whole_ref, *rest):
    chunks = len(bounds) - 1
    results = rest[-2 * chunks :]
    decay_refs, total_refs, sent_ref = results[:chunks], results[chunks:-1], results[-1]
    turned = [
        b_ref[:, g * N : (g + 1) * N].astype(F32).T.astype(BF16)
        for g in range(b_ref.shape[1] // N)
    ]
    for k in range(chunks):
        first = bounds[k]
        decay_refs[k][...] = over_lanes(whole_ref[...], first, bounds[k + 1] - first, 3)
        if k:
            chunk_total(first, x_ref, turned, weight_ref[...], total_refs[k - 1])
    sent_ref[...] = total_refs[0][...].astype(BF16)


def flat(ref):
    return jnp.concatenate([ref[i].astype(F32) for i in range(ref.shape[0])], axis=0)


def token_kernel(*refs):
    refs[-1][...] = jnp.zeros_like(refs[-1])


def pass_kernel(hop, first, more, got_ref, total_ref, decay_ref, *rest):
    moving_ref, carry_ref = rest[len(rest) - 2 - more : len(rest) - more]
    me = lax.axis_index("seq")
    groups = carry_ref.shape[1] // (H // G * P_SIZE)
    if hop == 1 and first == 0:
        following_ref = rest[0]
        carry_ref[...] = jnp.zeros_like(carry_ref)
    else:
        following_ref = rest[1]
    got = got_ref[:N]
    moving_ref[:N] = (total_ref[...] + decay_ref[...] * got.astype(F32)).astype(BF16)
    if moving_ref.shape[0] > N and hop == 1:
        names = groups * N
        own, other = [ref[N:, :names].astype(F32) for ref in rest[1 + more : 3 + more]]
        even = lax.rem(me, 2) == 0
        moving_ref[N:, :names] = jnp.where(even, own, other).astype(BF16)
        moving_ref[N:, names : 2 * names] = jnp.where(even, other, own).astype(BF16)
    elif moving_ref.shape[0] > N:
        moving_ref[N:] = got_ref[N:]

    @pl.when(me == hop)
    def _():
        carry_ref[:, first : first + got.shape[1]] = got

    if more:
        rest[-1][...] = following_ref[...].astype(BF16)


def pair_halves(x_part):
    first_half = lax.broadcasted_iota(jnp.int32, (1, 2 * P_SIZE), 1) < P_SIZE
    zero = jnp.zeros_like(x_part)
    return jnp.where(first_half, x_part, zero), jnp.where(first_half, zero, x_part)


def span_starts(cum, spans):
    ends = [cum[(i + 1) * SPAN - 1 : (i + 1) * SPAN, :] for i in range(spans)]
    starts = [jnp.zeros_like(ends[0])]
    for i in range(spans):
        starts.append(starts[i] + ends[i])
    return ends, starts


def inner_kernel(g, x_ref, b_ref, c_ref, cum_ref, row_ref, d_ref, *rest):
    inner_ref = rest[-1]
    heads, tokens = cum_ref.shape
    spans = tokens // SPAN
    per_group = H // G
    names = slice(g * N, (g + 1) * N)
    t_index = lax.broadcasted_iota(jnp.int32, (SPAN, SPAN), 0)
    s_index = lax.broadcasted_iota(jnp.int32, (SPAN, SPAN), 1)
    causal = t_index >= s_index
    rows = row_ref[...]
    cum = cum_ref[...].T
    ends, _ = span_starts(cum, spans)
    first_half = lax.broadcasted_iota(jnp.int32, (1, 2 * P_SIZE), 1) < P_SIZE
    scores = dot(c_ref[:, names], b_ref[:, names], 1, 1)
    for pair in range(per_group // 2):
        h0 = g * per_group + 2 * pair
        lanes = slice(h0 * P_SIZE, (h0 + 2) * P_SIZE)
        here = slice(2 * pair * P_SIZE, (2 * pair + 2) * P_SIZE)
        x_part = x_ref[:, lanes]
        halves = pair_halves(x_part)
        weights = [[None, None] for _ in range(spans)]
        for e in range(2):
            h = h0 + e
            row = rows[h : h + 1, :]
            for i in range(spans):
                column = jnp.broadcast_to(cum[i * SPAN : (i + 1) * SPAN, h : h + 1], (SPAN, SPAN))
                parts = []
                for j in range(i + 1):
                    shift = row[:, j * SPAN : (j + 1) * SPAN]
                    for m in range(j, i):
                        shift = shift + ends[m][:, h : h + 1]
                    score = scores[i * SPAN : (i + 1) * SPAN, j * SPAN : (j + 1) * SPAN]
                    part = score * jnp.exp2(column + shift)
                    if i == j:
                        part = jnp.where(causal, part, 0.0)
                    parts.append(part.astype(BF16))
                weights[i][e] = jnp.concatenate(parts, axis=1) if i else parts[0]
        skip = jnp.where(first_half, d_ref[:, h0 : h0 + 1], d_ref[:, h0 + 1 : h0 + 2])
        for i in range(spans):
            reach = (i + 1) * SPAN
            left = jnp.concatenate(weights[i], axis=1)
            right = jnp.concatenate([half[:reach] for half in halves], axis=0)
            mine = slice(i * SPAN, (i + 1) * SPAN)
            inner_ref[mine, here] = dot(left, right) + skip * x_part[mine].astype(F32)


def ask_kernel(ride, x_ref, b_ref, cum_ref, row_ref, len_ref, owner_ref, *rest):
    local_ref, gain_ref, asked_ref = rest[-3:]
    heads, tokens = cum_ref.shape
    spans = tokens // SPAN
    asks = local_ref.shape[0]
    per_group = H // G
    groups = heads // per_group
    me = lax.axis_index("seq")
    if ride:
        near, middle, far = [ref[N:].astype(F32) for ref in rest[:3]]
        far = jnp.where((me == 1) | (me == 2), middle, far)
        halves = (jnp.where(me < 2, near, far), jnp.where(me < 2, far, near))
        names = b_ref.shape[1]
        blocks = [half[:, i * names : (i + 1) * names] for half in halves for i in range(2)]
        blocks = jnp.concatenate(blocks, axis=0).astype(BF16)
        row = lax.broadcasted_iota(jnp.int32, (asks, blocks.shape[0]), 0)
        column = lax.broadcasted_iota(jnp.int32, (asks, blocks.shape[0]), 1)
        wanted = row // STEPS * asks + me * STEPS + row % STEPS
        asked = dot(jnp.where(column == wanted, 1.0, 0.0).astype(BF16), blocks).astype(BF16)
    else:
        blocks = [rest[0][r, me].astype(F32) for r in range(asks // STEPS)]
        asked = jnp.concatenate(blocks, axis=0).astype(BF16)
    asked_ref[...] = asked
    block = lax.broadcasted_iota(jnp.int32, (asks, 1), 0) // STEPS
    spot = len_ref[...] - 1 - me * tokens
    mine = (owner_ref[...] == block) & (spot >= 0) & (spot < tokens)
    spot = jnp.sum(jnp.where(mine, spot, 0).astype(F32), axis=1, keepdims=True).astype(jnp.int32)
    position = lax.broadcasted_iota(jnp.int32, (asks, tokens), 1)
    picked = jnp.where(position == spot, 1.0, 0.0).astype(BF16)
    upto = position <= spot
    rows = row_ref[...]
    cum = cum_ref[...].T
    ends, starts = span_starts(cum, spans)
    near_ask = exact_dot(picked, cum)
    ask_start = starts[0]
    for i in range(1, spans):
        ask_start = jnp.where(spot >= i * SPAN, starts[i], ask_start)
    gain_ref[...] = jnp.exp2(near_ask + ask_start)
    columns = []
    for j in range(spans):
        column = near_ask
        for i in range(j + 1, spans):
            column = jnp.where(spot // SPAN == i, near_ask + sum(ends[j + 1 : i], ends[j]), column)
        columns.append(column)
    for g in range(groups):
        names = slice(g * N, (g + 1) * N)
        scores = jnp.where(upto, dot(asked[:, names], b_ref[:, names], 1, 1), 0.0)
        for pair in range(per_group // 2):
            h0 = g * per_group + 2 * pair
            lanes = slice(h0 * P_SIZE, (h0 + 2) * P_SIZE)
            parts = []
            for h in (h0, h0 + 1):
                for j in range(spans):
                    span = slice(j * SPAN, (j + 1) * SPAN)
                    part = scores[:, span] * jnp.exp2(columns[j][:, h : h + 1] + rows[h : h + 1, span])
                    parts.append(jnp.where(upto[:, span], part, 0.0).astype(BF16))
            right = jnp.concatenate(pair_halves(x_ref[:, lanes]), axis=0)
            local_ref[:, lanes] = dot(jnp.concatenate(parts, axis=1), right)


def read_kernel(count, bounds, ops, final, local_ref, gain_ref, asked_ref, carry_ref, *rest):
    chunks = len(bounds) - 1
    got_refs, rest = rest[: chunks * final], rest[chunks * final :]
    read_refs = rest[-(len(ops) + final) :]
    me = lax.axis_index("seq")
    for k in range(chunks):
        first = bounds[k]
        width = bounds[k + 1] - first
        here = slice(first, first + width)
        state = carry_ref[:, here]
        if final:
            state = jnp.where(me == count - 1, got_refs[k][:N], state)
        carried = [
            dot(asked_ref[:, g * N : (g + 1) * N], state[:, start - first : end - first])
            for g, start, end in by_group(first, first + width)
        ]
        carried = jnp.concatenate(carried, axis=1)
        reading = local_ref[:, here] + over_lanes(gain_ref[...], first, width) * carried
        parts = [reading[r * STEPS : (r + 1) * STEPS] for r in range(count)]
        for op, read_ref in zip(ops, read_refs):
            if isinstance(op, tuple):
                part = jnp.where(me == op[0], parts[op[1]], parts[op[0]])
            else:
                part = parts[0]
                for r in range(1, count):
                    part = jnp.where(lax.rem(me + count - op, count) == r, parts[r], part)
            read_ref[:, here] = part.astype(read_ref.dtype)
        if final:
            own = parts[0]
            for r in range(1, count):
                own = jnp.where(me == r, parts[r], own)
            read_refs[-1][:, here] = own


def outer_kernel(parts, bounds, count, c_ref, cum_ref, carry_ref, *rest):
    final = len(parts) > 1
    part = parts[-1]
    got_refs = rest[: len(part)]
    inner_refs = rest[len(part) : len(part) + cum_ref.shape[0] // (H // G)]
    if final:
        early_ref, out_hbm, token_ref, out_ref, sems = rest[-5:]
        token_ref[...] = jnp.zeros_like(token_ref)
    else:
        out_ref = rest[-1]
    heads, tokens = cum_ref.shape
    spans = tokens // SPAN
    group_lanes = H // G * P_SIZE
    copies = []

    def send(source, first, width):
        lanes = slice(first, first + width)
        copies.append(pltpu.make_async_copy(source, out_hbm.at[:, lanes], sems.at[len(copies)]))
        copies[-1].start()

    if final:
        send(early_ref, 0, early_ref.shape[1])
    last = lax.axis_index("seq") == count - 1
    start = jnp.zeros((heads, 1), F32)
    gains = []
    for i in range(spans):
        cum = cum_ref[:, i * SPAN : (i + 1) * SPAN]
        gains.append(jnp.exp2(cum + start))
        start = start + cum[:, SPAN - 1 : SPAN]
    gain = jnp.concatenate(gains, axis=1).T
    for i, k in enumerate(part):
        first = bounds[k]
        state = jnp.where(last, got_refs[i][:N], carry_ref[:, first : bounds[k + 1]])
        for g, start, end in by_group(first, bounds[k + 1]):
            carried = dot(c_ref[:, g * N : (g + 1) * N], state[:, start - first : end - first])
            inner = inner_refs[g][:, start - g * group_lanes : end - g * group_lanes]
            here = slice(start - bounds[part[0]], end - bounds[part[0]])
            out = inner + over_lanes(gain, start, end - start) * carried
            out_ref[:, here] = out.astype(BF16)
            if final:
                send(out_ref.at[:, here], start, end - start)
    for copy in copies:
        copy.wait()


def fresh_kernel(tokens, x_ref, b_ref, c_ref, dt_ref, a_ref, d_ref, len_ref, owner_ref, *rest):
    keep_ref, fresh_ref, held_ref = rest[-3:]
    count, _, heads = dt_ref.shape
    rows = count * STEPS
    place = lax.broadcasted_iota(jnp.int32, (rows, 1), 0) // STEPS * tokens
    spot = len_ref[...] - 1 - place
    mine = (owner_ref[...] == lax.axis_index("seq")) & (spot >= 0) & (spot < tokens)
    held = jnp.sum(jnp.where(mine, 1.0, 0.0), axis=1, keepdims=True)
    held = jnp.broadcast_to(held, (rows, held_ref.shape[2]))
    per_group = H // G
    groups = heads // per_group
    width = x_ref.shape[2]
    turn = lax.broadcasted_iota(jnp.int32, (rows, 1), 0) % STEPS
    step = softplus(flat(dt_ref))
    rate = step * (jnp.exp(a_ref[...]) * -LOG2E)

    def earlier(value, gap):
        if not gap:
            return value
        moved = jnp.concatenate([jnp.zeros_like(value[:gap]), value[:-gap]], axis=0)
        return jnp.where(turn >= gap, moved, 0.0)

    running = sum(earlier(rate, gap) for gap in range(STEPS))
    keep = over_lanes(jnp.exp2(running), 0, width)
    x_values = flat(x_ref)
    b_values = flat(b_ref)
    c_values = flat(c_ref)
    head = lax.broadcasted_iota(jnp.int32, (rows, heads), 1)
    fresh = over_lanes(d_ref[...], 0, width, 3) * x_values
    since = jnp.zeros_like(rate)
    for gap in range(STEPS):
        if gap:
            since = since + earlier(rate, gap - 1)
        products = c_values * earlier(b_values, gap)
        pair = jnp.zeros((rows, heads), F32)
        for g in range(groups):
            score = jnp.sum(products[:, g * N : (g + 1) * N], axis=1, keepdims=True)
            pair = jnp.where(head // per_group == g, score, pair)
        factor = jnp.where(turn >= gap, jnp.exp2(since) * earlier(step, gap) * pair, 0.0)
        fresh = fresh + over_lanes(factor, 0, width) * earlier(x_values, gap)
    for i in range(rows // STEPS):
        keep_ref[i] = keep[i * STEPS : (i + 1) * STEPS]
        fresh_ref[i] = fresh[i * STEPS : (i + 1) * STEPS]
        held_ref[i] = held[i * STEPS : (i + 1) * STEPS]


def finish_kernel(ops, keep_ref, fresh_ref, held_ref, *rest):
    count = keep_ref.shape[0]
    back_refs, own_ref, out_ref = rest[: len(ops)], rest[len(ops)], rest[-1]
    me = lax.axis_index("seq")

    def finish(source, reading):
        value = reading * keep_ref[source] + fresh_ref[source]
        held = held_ref[source][:, :1] > 0.0
        out_ref[source] = jnp.where(held, value, 0.0).astype(BF16)

    if isinstance(ops[0], tuple):
        for source in range(count):
            reading = own_ref[...]
            for (one, other), back_ref in zip(ops, back_refs):
                if source in (one, other):
                    owner = one + other - source
                    reading = jnp.where(me == owner, back_ref[...].astype(F32), reading)
            finish(source, reading)
    else:
        finish(me, own_ref[...])
        for r, back_ref in zip(ops, back_refs):
            finish(lax.rem(me + r, count), back_ref[...].astype(F32))


def shards(
    ssm_input, bmat, cmat, dt_raw, a_log, d_skip, prompt_len, owner, dec_x, dec_b, dec_c, dec_dt
):
    count = lax.axis_size("seq")
    tensor = lax.axis_size("tp")
    tokens, heads = dt_raw.shape
    groups = heads // (H // G)
    names = groups * N
    lanes = heads * P_SIZE
    group_lanes = lanes // groups
    rows = count * STEPS
    chunks = CHUNKS if count <= 4 else groups
    bounds = tuple(lanes * k // chunks for k in range(chunks + 1))
    if chunks > groups:
        bounds = bounds[:1] + (bounds[1] - 128, bounds[2] - 128) + bounds[3:]
    widths = [bounds[k + 1] - bounds[k] for k in range(chunks)]
    anywhere = pl.BlockSpec(memory_space=pl.ANY)
    in_hbm = pl.BlockSpec(memory_space=pltpu.HBM)
    in_vmem = pl.BlockSpec(memory_space=pltpu.VMEM)
    ride = count == 4 and widths[0] >= names and widths[1] >= 2 * names

    def sent_shape(hop, k):
        return shape((N + rows * (ride and (hop, k) in ((1, 0), (2, 1), (3, 1))), widths[k]), BF16)

    inputs = [
        ssm_input,
        bmat,
        a_log.reshape(1, heads),
        dec_c[0],
        cmat,
        d_skip.reshape(1, heads),
        prompt_len.reshape(1, -1),
        owner.reshape(1, -1),
        dec_x[0],
        dec_b[0],
        dec_dt[0],
    ]
    total_shapes = tuple(shape((N, width)) for width in widths)
    decay_shapes = tuple(shape((1, width)) for width in widths)
    results = call(
        functools.partial(first_kernel, len(inputs)),
        tuple(shape(value.shape, value.dtype) for value in inputs)
        + (
            shape((heads, tokens)),
            shape((heads, tokens)),
            shape((tokens, heads)),
            shape((1, heads)),
            total_shapes[0],
            sent_shape(1, 0),
        ),
        in_specs=[in_hbm] * (len(inputs) + 1),
        scratch_shapes=[
            pltpu.VMEM((heads, tokens), BF16),
            pltpu.SemaphoreType.DMA((len(inputs) + 2,)),
        ],
    )(*[pinned(value, pltpu.HBM) for value in inputs + [dt_raw.T]])
    x, b, a_row, asked_here, c, d_row, len_row, owner_row, x_dec, b_dec, dt_dec = results[:11]
    cum, row, weight, whole = results[11:15]
    total, sent = [results[15]], {0: results[16]}
    all_asked = None if ride else lax.all_gather(dec_c[0], "seq")

    def state_part(tie):
        return call(
            functools.partial(state_kernel, bounds),
            decay_shapes + total_shapes[1:] + (sent_shape(1, 1),),
            in_specs=[in_vmem] * 4 + [anywhere],
        )(x, b, weight, whole, tie)

    def swap(value, *couples):
        partner = {}
        for one, other in couples:
            partner.update({one: other, other: one})
        pairs = []
        for d in range(count):
            for t in range(tensor):
                there = partner[d] * tensor + t if d in partner else d * tensor + (t ^ 1)
                pairs.append((d * tensor + t, there))
        return lax.ppermute(value, ("seq", "tp"), pairs)

    def forward(value, hop, k):
        with jax.named_scope(f"hop{hop}_chunk{k}"):
            rides = ride and (hop, k) in ((1, 0), (3, 1))
            return swap(value, *([(0, 1), (2, 3)] if rides else [(hop - 1, hop)]))

    def shift(value, by):
        return lax.ppermute(value, "seq", [(d, (d + by) % count) for d in range(count)])

    def inner_part(g, *after):
        return call(
            functools.partial(inner_kernel, g),
            shape((tokens, group_lanes)),
            in_specs=[in_vmem] * 6 + [anywhere] * len(after),
        )(x, b, c, cum, row, d_row, *after)

    def ask_part(*after):
        blocks = (moving[2, 1], got[2, 1], got[3, 1]) if ride else (all_asked,)
        return call(
            functools.partial(ask_kernel, ride),
            (shape((rows, lanes)), shape((rows, heads)), shape((rows, names), BF16)),
            in_specs=[in_vmem] * (6 + len(blocks)) + [anywhere] * len(after),
        )(x, b, cum, row, len_row, owner_row, *blocks, *after)

    def token(*after, flops=1):
        return call(
            token_kernel, shape((8, 128)), flops=flops, in_specs=[anywhere] * len(after)
        )(*after)

    def fresh_part(*after):
        return call(
            functools.partial(fresh_kernel, tokens),
            (shape((count, STEPS, lanes)),) * 2 + (shape((count, STEPS, 128)),),
            in_specs=[in_vmem] * 8 + [anywhere] * len(after),
        )(x_dec, b_dec, asked_here, dt_dec, a_row, d_row, len_row, owner_row, *after)

    def outer_part(parts, carry, before, *after):
        part = parts[-1]
        out = shape((tokens, sum(widths[k] for k in part)), BF16)
        operands = [c, cum, carry, *[got[count - 1, k] for k in part], *inner, *before]
        return call(
            functools.partial(outer_kernel, parts, bounds, count),
            (pltpu.HBM((tokens, lanes), BF16), shape((8, 128))) if before else out,
            in_specs=[in_vmem] * len(operands) + [anywhere] * len(after),
            out_specs=(in_hbm, in_vmem) if before else in_vmem,
            scratch_shapes=[out, pltpu.SemaphoreType.DMA((chunks + groups,))] if before else [],
        )(*operands, *after)

    def read_part(ops, final, *after):
        arrived = [got[count - 1, k] for k in range(chunks)] if final else []
        operands = [local, gain, asked, carry, *arrived]
        return call(
            functools.partial(read_kernel, count, bounds, ops, final),
            (shape((STEPS, lanes), BF16),) * len(ops) + (shape((STEPS, lanes)),) * final,
            in_specs=[in_vmem] * len(operands) + [anywhere] * len(after),
        )(*operands, *after)

    got = {(1, 0): forward(sent[0], 1, 0)}
    inner = [inner_part(0)]
    *parts, sent[1] = state_part(inner[-1])
    decay, total = parts[:chunks], total + parts[chunks:]
    got[1, 1] = forward(sent[1], 1, 1)
    order = sorted((k + hop, hop, k) for hop in range(1, count - 1) for k in range(chunks))
    moving = {}
    carry = tie = None
    for _, hop, k in order:
        more = hop == 1 and k + 2 < chunks
        operands = [got[hop, k], total[k], decay[k]]
        operands += [] if carry is None else [carry]
        operands += total[k + 2 : k + 3] * more + [sent[0], got[1, 0]] * (ride and (hop, k) == (1, 1))
        after = []
        if (hop, k) == (1, 1):
            for g in range(1, groups):
                inner.append(inner_part(g, tie))
            keep, fresh, held = fresh_part(inner[-1])
            after = [keep]
        if hop == count - 2 and k > 1:
            after = [token(got[hop + 1, k - 2], tie, flops=GAP_COSTS[k - 2])]
        tie, carry, *following = call(
            functools.partial(pass_kernel, hop, bounds[k], more),
            (sent_shape(hop + 1, k), shape((N, lanes), BF16))
            + ((sent_shape(1, k + 2),) if more else ()),
            flops=PASS_COSTS.get((hop, k), 1),
            in_specs=[in_vmem] * len(operands) + [anywhere] * len(after),
            input_output_aliases={} if carry is None else {3: 1},
        )(*operands, *after)
        moving[hop + 1, k] = tie
        got[hop + 1, k] = forward(tie, hop + 1, k)
        if more:
            got[1, k + 2] = forward(following[0], 1, k + 2)

    early, late = tuple(range(chunks // 2)), tuple(range(chunks // 2, chunks))
    four = count == 4
    local, gain, asked = ask_part(tie)
    back, ops = [], [(0, 1), (0, 2), (1, 2)] if four else []
    if four:
        reading = read_part(ops, False)
        for couple, value in zip(ops, reading):
            back.append(swap(value, couple))
    ends = [(0, 3), (1, 3), (2, 3)] if four else list(range(1, count))
    before = reading[0] if four else asked
    order_token = token(got[count - 1, chunks - 2], before, flops=TOKEN_COST)
    *reading, mine = read_part(ends, True, order_token)
    last_back = [
        swap(value, op) if four else shift(value, -op) for op, value in zip(ends, reading)
    ]
    outer = outer_part((early,), carry, [], mine)
    prefill, end_token = outer_part((early, late), carry, [outer])
    end_token = token(end_token, *back, flops=TOKEN_COST)
    ops, back = ops + ends, back + last_back

    decoded = call(
        functools.partial(finish_kernel, ops),
        jax.ShapeDtypeStruct((count, STEPS, lanes), BF16),
        in_specs=[in_vmem] * (4 + len(ops)) + [anywhere],
    )(keep, fresh, held, *back, mine, end_token)
    return (prefill, decoded[None])


def solution(mesh):
    placed = (
        P(("grp", "seq"), "tp"),
        P(("grp", "seq"), "tp"),
        P(("grp", "seq"), "tp"),
        P(("grp", "seq"), "tp"),
        P("tp"),
        P("tp"),
        P("grp"),
        P("grp"),
        P(("grp", "seq"), None, None, "tp"),
        P(("grp", "seq"), None, None, "tp"),
        P(("grp", "seq"), None, None, "tp"),
        P(("grp", "seq"), None, None, "tp"),
    )
    return jax.shard_map(
        shards,
        mesh=mesh,
        in_specs=placed,
        out_specs=(P(("grp", "seq"), "tp"), P(("grp", "seq"), None, None, "tp")),
        check_vma=False,
    )
```

```python
import functools
import math

import jax
import jax.numpy as jnp
from jax import lax
from jax.experimental import pallas as pl
from jax.experimental.pallas import tpu as pltpu
from jax.sharding import PartitionSpec as P

H = 128
P_SIZE = 64
N = 128
G = 8
SPAN = 128
STEPS = 4
LOG2E = math.log2(math.e)
F32 = jnp.float32
BF16 = jnp.bfloat16
CHUNKS = 4
TOKEN_COST = 10**8
PASS_COSTS = {
    (1, 0): 8 * 10**8,
    (2, 0): 5 * 10**8,
    (1, 2): 8 * 10**8,
    (2, 1): 4 * 10**8,
    (2, 2): 4 * 10**8,
}
GAP_COSTS = (8 * 10**8, 5 * 10**8)
VMEM_LIMIT = 32 * 1024 * 1024


def softplus(value):
    small = jnp.exp(-jnp.abs(value))
    series = small * (1.0 - small * (0.5 - small * (1.0 / 3.0 - small * 0.25)))
    return jnp.maximum(value, 0.0) + jnp.where(small < 0.02, series, jnp.log(1.0 + small))


def dot(left, right, left_dim=1, right_dim=0):
    return lax.dot_general(
        left, right, (((left_dim,), (right_dim,)), ((), ())), preferred_element_type=F32
    )


def split(value, pieces):
    result = []
    for _ in range(pieces):
        piece = value.astype(BF16)
        result.append(piece)
        value = value - piece.astype(F32)
    return result


def exact_dot(ones, value, pieces=3, left_dim=1):
    return sum(dot(ones, piece, left_dim) for piece in split(value, pieces))


def spread_matrix(heads, first, width):
    lane = lax.broadcasted_iota(jnp.int32, (heads, width), 1) + first
    head = lax.broadcasted_iota(jnp.int32, (heads, width), 0)
    return jnp.where(lane // P_SIZE == head, 1.0, 0.0).astype(BF16)


def over_lanes(value, first, width, pieces=2):
    return exact_dot_right(value, spread_matrix(value.shape[1], first, width), pieces)


def exact_dot_right(value, ones, pieces):
    parts = [piece.astype(F32) for piece in split(value, pieces)]
    stacked = jnp.concatenate(parts, axis=1).astype(BF16)
    return dot(stacked, jnp.concatenate([ones] * pieces, axis=0))


def shape(dims, dtype=F32):
    return pltpu.VMEM(dims, dtype)


def pinned(value, space=pltpu.VMEM):
    return pltpu.with_memory_space_constraint(value, space)


def call(kernel, out_shape, flops=1, **options):
    name = getattr(kernel, "func", kernel).__name__
    return pl.pallas_call(
        kernel,
        name=name,
        out_shape=out_shape,
        compiler_params=pltpu.CompilerParams(vmem_limit_bytes=VMEM_LIMIT),
        cost_estimate=pl.CostEstimate(flops=flops, bytes_accessed=1, transcendentals=0),
        **options,
    )


def triangle(keep):
    row = lax.broadcasted_iota(jnp.int32, (SPAN, SPAN), 0)
    column = lax.broadcasted_iota(jnp.int32, (SPAN, SPAN), 1)
    return jnp.where(keep(row, column), 1.0, 0.0).astype(BF16)


def by_group(first, last):
    group_lanes = H // G * P_SIZE
    pieces = []
    while first < last:
        g = first // group_lanes
        end = min(last, (g + 1) * group_lanes)
        pieces.append((g, first, end))
        first = end
    return pieces


def chunk_total(first, x_ref, turned, weight, total_ref):
    for g, start, end in by_group(first, first + total_ref.shape[1]):
        scaled = x_ref[:, start:end].astype(F32) * over_lanes(weight, start, end - start)
        total_ref[:, start - first : end - first] = dot(turned[g], scaled.astype(BF16))


def first_kernel(kept, *refs):
    hbm, refs = refs[: kept + 1], refs[kept + 1 :]
    here, refs = refs[:kept], refs[kept:]
    cum_ref, row_ref, weight_ref, whole_ref = refs[:4]
    total_ref, sent_ref, dt_ref, sems = refs[4:]
    x_ref, b_ref, a_ref = here[:3]
    heads, tokens = dt_ref.shape
    spans = tokens // SPAN
    width = total_ref.shape[1]
    dt_copy = pltpu.make_async_copy(hbm[kept], dt_ref, sems.at[0])
    copies = [pltpu.make_async_copy(hbm[i], here[i], sems.at[i]) for i in range(1, kept)]
    x_copies = [
        pltpu.make_async_copy(hbm[0].at[:, lanes], x_ref.at[:, lanes], sems.at[kept + i])
        for i, lanes in enumerate((slice(0, width), slice(width, x_ref.shape[1])))
    ]
    for copy in [dt_copy, copies[1], copies[0], *x_copies, *copies[2:]]:
        copy.start()
    upper = triangle(lambda s, t: s <= t)
    eye = lax.broadcasted_iota(jnp.int32, (heads, heads), 0) == lax.broadcasted_iota(
        jnp.int32, (heads, heads), 1
    )
    dt_copy.wait()
    copies[1].wait()
    a_column = jnp.sum(jnp.where(eye, a_ref[...], 0.0), axis=1, keepdims=True)
    step = softplus(dt_ref[...].astype(F32))
    rate = step * (jnp.exp(a_column) * -LOG2E)
    cums = [exact_dot_right(rate[:, i * SPAN : (i + 1) * SPAN], upper, 3) for i in range(spans)]
    ends = [cum[:, SPAN - 1 : SPAN] for cum in cums]
    after = jnp.zeros_like(ends[0])
    weights = [None] * spans
    for i in reversed(range(spans)):
        after = after + ends[i]
        weights[i] = jnp.exp2(after - cums[i]) * step[:, i * SPAN : (i + 1) * SPAN]
    weight = jnp.concatenate(weights, axis=1).T
    whole = jnp.sum(jnp.where(eye, jnp.exp2(after), 0.0), axis=0, keepdims=True)
    weight_ref[...] = weight
    whole_ref[...] = whole
    copies[0].wait()
    turned = b_ref[:, :N].astype(F32).T.astype(BF16)
    x_copies[0].wait()
    chunk_total(0, x_ref, [turned], weight, total_ref)
    sent_ref[:N] = total_ref[...].astype(BF16)
    cum = jnp.concatenate(cums, axis=1)
    cum_ref[...] = cum
    row_ref[...] = jnp.log2(step) - cum
    x_copies[1].wait()
    for copy in copies[2:]:
        copy.wait()
    if sent_ref.shape[0] > N:
        own = flat(here[3]).astype(BF16)
        sent_ref[N:, : own.shape[1]] = own


def state_kernel(bounds, x_ref, b_ref, weight_ref, whole_ref, *rest):
    chunks = len(bounds) - 1
    results = rest[-2 * chunks :]
    decay_refs, total_refs, sent_ref = results[:chunks], results[chunks:-1], results[-1]
    turned = [
        b_ref[:, g * N : (g + 1) * N].astype(F32).T.astype(BF16)
        for g in range(b_ref.shape[1] // N)
    ]
    for k in range(chunks):
        first = bounds[k]
        decay_refs[k][...] = over_lanes(whole_ref[...], first, bounds[k + 1] - first, 3)
        if k:
            chunk_total(first, x_ref, turned, weight_ref[...], total_refs[k - 1])
    sent_ref[...] = total_refs[0][...].astype(BF16)


def flat(ref):
    return jnp.concatenate([ref[i].astype(F32) for i in range(ref.shape[0])], axis=0)


def token_kernel(*refs):
    refs[-1][...] = jnp.zeros_like(refs[-1])


def pass_kernel(hop, first, more, got_ref, total_ref, decay_ref, *rest):
    moving_ref, carry_ref = rest[len(rest) - 2 - more : len(rest) - more]
    me = lax.axis_index("seq")
    groups = carry_ref.shape[1] // (H // G * P_SIZE)
    if hop == 1 and first == 0:
        following_ref = rest[0]
        carry_ref[...] = jnp.zeros_like(carry_ref)
    else:
        following_ref = rest[1]
    got = got_ref[:N]
    moving_ref[:N] = (total_ref[...] + decay_ref[...] * got.astype(F32)).astype(BF16)
    if moving_ref.shape[0] > N and hop == 1:
        names = groups * N
        own, other = [ref[N:, :names].astype(F32) for ref in rest[1 + more : 3 + more]]
        even = lax.rem(me, 2) == 0
        moving_ref[N:, :names] = jnp.where(even, own, other).astype(BF16)
        moving_ref[N:, names : 2 * names] = jnp.where(even, other, own).astype(BF16)
    elif moving_ref.shape[0] > N:
        moving_ref[N:] = got_ref[N:]

    @pl.when(me == hop)
    def _():
        carry_ref[:, first : first + got.shape[1]] = got

    if more:
        rest[-1][...] = following_ref[...].astype(BF16)


def pair_halves(x_part):
    first_half = lax.broadcasted_iota(jnp.int32, (1, 2 * P_SIZE), 1) < P_SIZE
    zero = jnp.zeros_like(x_part)
    return jnp.where(first_half, x_part, zero), jnp.where(first_half, zero, x_part)


def span_starts(cum, spans):
    ends = [cum[(i + 1) * SPAN - 1 : (i + 1) * SPAN, :] for i in range(spans)]
    starts = [jnp.zeros_like(ends[0])]
    for i in range(spans):
        starts.append(starts[i] + ends[i])
    return ends, starts


def inner_kernel(g, x_ref, b_ref, c_ref, cum_ref, row_ref, d_ref, *rest):
    inner_ref = rest[-1]
    heads, tokens = cum_ref.shape
    spans = tokens // SPAN
    per_group = H // G
    names = slice(g * N, (g + 1) * N)
    t_index = lax.broadcasted_iota(jnp.int32, (SPAN, SPAN), 0)
    s_index = lax.broadcasted_iota(jnp.int32, (SPAN, SPAN), 1)
    causal = t_index >= s_index
    rows = row_ref[...]
    cum = cum_ref[...].T
    ends, _ = span_starts(cum, spans)
    first_half = lax.broadcasted_iota(jnp.int32, (1, 2 * P_SIZE), 1) < P_SIZE
    scores = dot(c_ref[:, names], b_ref[:, names], 1, 1)
    for pair in range(per_group // 2):
        h0 = g * per_group + 2 * pair
        lanes = slice(h0 * P_SIZE, (h0 + 2) * P_SIZE)
        here = slice(2 * pair * P_SIZE, (2 * pair + 2) * P_SIZE)
        x_part = x_ref[:, lanes]
        halves = pair_halves(x_part)
        weights = [[None, None] for _ in range(spans)]
        for e in range(2):
            h = h0 + e
            row = rows[h : h + 1, :]
            for i in range(spans):
                column = jnp.broadcast_to(cum[i * SPAN : (i + 1) * SPAN, h : h + 1], (SPAN, SPAN))
                parts = []
                for j in range(i + 1):
                    shift = row[:, j * SPAN : (j + 1) * SPAN]
                    for m in range(j, i):
                        shift = shift + ends[m][:, h : h + 1]
                    score = scores[i * SPAN : (i + 1) * SPAN, j * SPAN : (j + 1) * SPAN]
                    part = score * jnp.exp2(column + shift)
                    if i == j:
                        part = jnp.where(causal, part, 0.0)
                    parts.append(part.astype(BF16))
                weights[i][e] = jnp.concatenate(parts, axis=1) if i else parts[0]
        skip = jnp.where(first_half, d_ref[:, h0 : h0 + 1], d_ref[:, h0 + 1 : h0 + 2])
        for i in range(spans):
            reach = (i + 1) * SPAN
            left = jnp.concatenate(weights[i], axis=1)
            right = jnp.concatenate([half[:reach] for half in halves], axis=0)
            mine = slice(i * SPAN, (i + 1) * SPAN)
            inner_ref[mine, here] = dot(left, right) + skip * x_part[mine].astype(F32)


def ask_kernel(ride, x_ref, b_ref, cum_ref, row_ref, len_ref, owner_ref, *rest):
    local_ref, gain_ref, asked_ref = rest[-3:]
    heads, tokens = cum_ref.shape
    spans = tokens // SPAN
    asks = local_ref.shape[0]
    per_group = H // G
    groups = heads // per_group
    me = lax.axis_index("seq")
    if ride:
        near, middle, far = [ref[N:].astype(F32) for ref in rest[:3]]
        far = jnp.where((me == 1) | (me == 2), middle, far)
        halves = (jnp.where(me < 2, near, far), jnp.where(me < 2, far, near))
        names = b_ref.shape[1]
        blocks = [half[:, i * names : (i + 1) * names] for half in halves for i in range(2)]
        blocks = jnp.concatenate(blocks, axis=0).astype(BF16)
        row = lax.broadcasted_iota(jnp.int32, (asks, blocks.shape[0]), 0)
        column = lax.broadcasted_iota(jnp.int32, (asks, blocks.shape[0]), 1)
        wanted = row // STEPS * asks + me * STEPS + row % STEPS
        asked = dot(jnp.where(column == wanted, 1.0, 0.0).astype(BF16), blocks).astype(BF16)
    else:
        blocks = [rest[0][r, me].astype(F32) for r in range(asks // STEPS)]
        asked = jnp.concatenate(blocks, axis=0).astype(BF16)
    asked_ref[...] = asked
    block = lax.broadcasted_iota(jnp.int32, (asks, 1), 0) // STEPS
    spot = len_ref[...] - 1 - me * tokens
    mine = (owner_ref[...] == block) & (spot >= 0) & (spot < tokens)
    spot = jnp.sum(jnp.where(mine, spot, 0).astype(F32), axis=1, keepdims=True).astype(jnp.int32)
    position = lax.broadcasted_iota(jnp.int32, (asks, tokens), 1)
    picked = jnp.where(position == spot, 1.0, 0.0).astype(BF16)
    upto = position <= spot
    rows = row_ref[...]
    cum = cum_ref[...].T
    ends, starts = span_starts(cum, spans)
    near_ask = exact_dot(picked, cum)
    ask_start = starts[0]
    for i in range(1, spans):
        ask_start = jnp.where(spot >= i * SPAN, starts[i], ask_start)
    gain_ref[...] = jnp.exp2(near_ask + ask_start)
    columns = []
    for j in range(spans):
        column = near_ask
        for i in range(j + 1, spans):
            column = jnp.where(spot // SPAN == i, near_ask + sum(ends[j + 1 : i], ends[j]), column)
        columns.append(column)
    for g in range(groups):
        names = slice(g * N, (g + 1) * N)
        scores = jnp.where(upto, dot(asked[:, names], b_ref[:, names], 1, 1), 0.0)
        for pair in range(per_group // 2):
            h0 = g * per_group + 2 * pair
            lanes = slice(h0 * P_SIZE, (h0 + 2) * P_SIZE)
            parts = []
            for h in (h0, h0 + 1):
                for j in range(spans):
                    span = slice(j * SPAN, (j + 1) * SPAN)
                    part = scores[:, span] * jnp.exp2(columns[j][:, h : h + 1] + rows[h : h + 1, span])
                    parts.append(jnp.where(upto[:, span], part, 0.0).astype(BF16))
            right = jnp.concatenate(pair_halves(x_ref[:, lanes]), axis=0)
            local_ref[:, lanes] = dot(jnp.concatenate(parts, axis=1), right)


def read_kernel(count, bounds, ops, final, local_ref, gain_ref, asked_ref, carry_ref, *rest):
    chunks = len(bounds) - 1
    got_refs, rest = rest[: chunks * final], rest[chunks * final :]
    read_refs = rest[-(len(ops) + final) :]
    me = lax.axis_index("seq")
    for k in range(chunks):
        first = bounds[k]
        width = bounds[k + 1] - first
        here = slice(first, first + width)
        state = carry_ref[:, here]
        if final:
            state = jnp.where(me == count - 1, got_refs[k][:N], state)
        carried = [
            dot(asked_ref[:, g * N : (g + 1) * N], state[:, start - first : end - first])
            for g, start, end in by_group(first, first + width)
        ]
        carried = jnp.concatenate(carried, axis=1)
        reading = local_ref[:, here] + over_lanes(gain_ref[...], first, width) * carried
        parts = [reading[r * STEPS : (r + 1) * STEPS] for r in range(count)]
        for op, read_ref in zip(ops, read_refs):
            if isinstance(op, tuple):
                part = jnp.where(me == op[0], parts[op[1]], parts[op[0]])
            else:
                part = parts[0]
                for r in range(1, count):
                    part = jnp.where(lax.rem(me + count - op, count) == r, parts[r], part)
            read_ref[:, here] = part.astype(read_ref.dtype)
        if final:
            own = parts[0]
            for r in range(1, count):
                own = jnp.where(me == r, parts[r], own)
            read_refs[-1][:, here] = own


def outer_kernel(parts, bounds, count, c_ref, cum_ref, carry_ref, *rest):
    final = len(parts) > 1
    part = parts[-1]
    got_refs = rest[: len(part)]
    inner_refs = rest[len(part) : len(part) + cum_ref.shape[0] // (H // G)]
    if final:
        early_ref, out_hbm, token_ref, out_ref, sems = rest[-5:]
        token_ref[...] = jnp.zeros_like(token_ref)
    else:
        out_ref = rest[-1]
    heads, tokens = cum_ref.shape
    spans = tokens // SPAN
    group_lanes = H // G * P_SIZE
    copies = []

    def send(source, first, width):
        lanes = slice(first, first + width)
        copies.append(pltpu.make_async_copy(source, out_hbm.at[:, lanes], sems.at[len(copies)]))
        copies[-1].start()

    if final:
        send(early_ref, 0, early_ref.shape[1])
    last = lax.axis_index("seq") == count - 1
    start = jnp.zeros((heads, 1), F32)
    gains = []
    for i in range(spans):
        cum = cum_ref[:, i * SPAN : (i + 1) * SPAN]
        gains.append(jnp.exp2(cum + start))
        start = start + cum[:, SPAN - 1 : SPAN]
    gain = jnp.concatenate(gains, axis=1).T
    for i, k in enumerate(part):
        first = bounds[k]
        state = jnp.where(last, got_refs[i][:N], carry_ref[:, first : bounds[k + 1]])
        for g, start, end in by_group(first, bounds[k + 1]):
            carried = dot(c_ref[:, g * N : (g + 1) * N], state[:, start - first : end - first])
            inner = inner_refs[g][:, start - g * group_lanes : end - g * group_lanes]
            here = slice(start - bounds[part[0]], end - bounds[part[0]])
            out = inner + over_lanes(gain, start, end - start) * carried
            out_ref[:, here] = out.astype(BF16)
            if final:
                send(out_ref.at[:, here], start, end - start)
    for copy in copies:
        copy.wait()


def fresh_kernel(tokens, x_ref, b_ref, c_ref, dt_ref, a_ref, d_ref, len_ref, owner_ref, *rest):
    keep_ref, fresh_ref, held_ref = rest[-3:]
    count, _, heads = dt_ref.shape
    rows = count * STEPS
    place = lax.broadcasted_iota(jnp.int32, (rows, 1), 0) // STEPS * tokens
    spot = len_ref[...] - 1 - place
    mine = (owner_ref[...] == lax.axis_index("seq")) & (spot >= 0) & (spot < tokens)
    held = jnp.sum(jnp.where(mine, 1.0, 0.0), axis=1, keepdims=True)
    held = jnp.broadcast_to(held, (rows, held_ref.shape[2]))
    per_group = H // G
    groups = heads // per_group
    width = x_ref.shape[2]
    turn = lax.broadcasted_iota(jnp.int32, (rows, 1), 0) % STEPS
    step = softplus(flat(dt_ref))
    rate = step * (jnp.exp(a_ref[...]) * -LOG2E)

    def earlier(value, gap):
        if not gap:
            return value
        moved = jnp.concatenate([jnp.zeros_like(value[:gap]), value[:-gap]], axis=0)
        return jnp.where(turn >= gap, moved, 0.0)

    running = sum(earlier(rate, gap) for gap in range(STEPS))
    keep = over_lanes(jnp.exp2(running), 0, width)
    x_values = flat(x_ref)
    b_values = flat(b_ref)
    c_values = flat(c_ref)
    head = lax.broadcasted_iota(jnp.int32, (rows, heads), 1)
    fresh = over_lanes(d_ref[...], 0, width, 3) * x_values
    since = jnp.zeros_like(rate)
    for gap in range(STEPS):
        if gap:
            since = since + earlier(rate, gap - 1)
        products = c_values * earlier(b_values, gap)
        pair = jnp.zeros((rows, heads), F32)
        for g in range(groups):
            score = jnp.sum(products[:, g * N : (g + 1) * N], axis=1, keepdims=True)
            pair = jnp.where(head // per_group == g, score, pair)
        factor = jnp.where(turn >= gap, jnp.exp2(since) * earlier(step, gap) * pair, 0.0)
        fresh = fresh + over_lanes(factor, 0, width) * earlier(x_values, gap)
    for i in range(rows // STEPS):
        keep_ref[i] = keep[i * STEPS : (i + 1) * STEPS]
        fresh_ref[i] = fresh[i * STEPS : (i + 1) * STEPS]
        held_ref[i] = held[i * STEPS : (i + 1) * STEPS]


def finish_kernel(ops, keep_ref, fresh_ref, held_ref, *rest):
    count = keep_ref.shape[0]
    back_refs, own_ref, out_ref = rest[: len(ops)], rest[len(ops)], rest[-1]
    me = lax.axis_index("seq")

    def finish(source, reading):
        value = reading * keep_ref[source] + fresh_ref[source]
        held = held_ref[source][:, :1] > 0.0
        out_ref[source] = jnp.where(held, value, 0.0).astype(BF16)

    if isinstance(ops[0], tuple):
        for source in range(count):
            reading = own_ref[...]
            for (one, other), back_ref in zip(ops, back_refs):
                if source in (one, other):
                    owner = one + other - source
                    reading = jnp.where(me == owner, back_ref[...].astype(F32), reading)
            finish(source, reading)
    else:
        finish(me, own_ref[...])
        for r, back_ref in zip(ops, back_refs):
            finish(lax.rem(me + r, count), back_ref[...].astype(F32))


def shards(
    ssm_input, bmat, cmat, dt_raw, a_log, d_skip, prompt_len, owner, dec_x, dec_b, dec_c, dec_dt
):
    count = lax.axis_size("seq")
    tensor = lax.axis_size("tp")
    tokens, heads = dt_raw.shape
    groups = heads // (H // G)
    names = groups * N
    lanes = heads * P_SIZE
    group_lanes = lanes // groups
    rows = count * STEPS
    chunks = CHUNKS if count <= 4 else groups
    bounds = tuple(lanes * k // chunks for k in range(chunks + 1))
    if chunks > groups:
        bounds = bounds[:1] + (bounds[1] - 128, bounds[2] - 128) + bounds[3:]
    widths = [bounds[k + 1] - bounds[k] for k in range(chunks)]
    anywhere = pl.BlockSpec(memory_space=pl.ANY)
    in_hbm = pl.BlockSpec(memory_space=pltpu.HBM)
    in_vmem = pl.BlockSpec(memory_space=pltpu.VMEM)
    ride = count == 4 and widths[0] >= names and widths[1] >= 2 * names

    def sent_shape(hop, k):
        return shape((N + rows * (ride and (hop, k) in ((1, 0), (2, 1), (3, 1))), widths[k]), BF16)

    inputs = [
        ssm_input,
        bmat,
        a_log.reshape(1, heads),
        dec_c[0],
        cmat,
        d_skip.reshape(1, heads),
        prompt_len.reshape(1, -1),
        owner.reshape(1, -1),
        dec_x[0],
        dec_b[0],
        dec_dt[0],
    ]
    total_shapes = tuple(shape((N, width)) for width in widths)
    decay_shapes = tuple(shape((1, width)) for width in widths)
    results = call(
        functools.partial(first_kernel, len(inputs)),
        tuple(shape(value.shape, value.dtype) for value in inputs)
        + (
            shape((heads, tokens)),
            shape((heads, tokens)),
            shape((tokens, heads)),
            shape((1, heads)),
            total_shapes[0],
            sent_shape(1, 0),
        ),
        in_specs=[in_hbm] * (len(inputs) + 1),
        scratch_shapes=[
            pltpu.VMEM((heads, tokens), BF16),
            pltpu.SemaphoreType.DMA((len(inputs) + 2,)),
        ],
    )(*[pinned(value, pltpu.HBM) for value in inputs + [dt_raw.T]])
    x, b, a_row, asked_here, c, d_row, len_row, owner_row, x_dec, b_dec, dt_dec = results[:11]
    cum, row, weight, whole = results[11:15]
    total, sent = [results[15]], {0: results[16]}
    all_asked = None if ride else lax.all_gather(dec_c[0], "seq")

    def state_part(tie):
        return call(
            functools.partial(state_kernel, bounds),
            decay_shapes + total_shapes[1:] + (sent_shape(1, 1),),
            in_specs=[in_vmem] * 4 + [anywhere],
        )(x, b, weight, whole, tie)

    def swap(value, *couples):
        partner = {}
        for one, other in couples:
            partner.update({one: other, other: one})
        pairs = []
        for d in range(count):
            for t in range(tensor):
                there = partner[d] * tensor + t if d in partner else d * tensor + (t ^ 1)
                pairs.append((d * tensor + t, there))
        return lax.ppermute(value, ("seq", "tp"), pairs)

    def forward(value, hop, k):
        with jax.named_scope(f"hop{hop}_chunk{k}"):
            rides = ride and (hop, k) in ((1, 0), (3, 1))
            return swap(value, *([(0, 1), (2, 3)] if rides else [(hop - 1, hop)]))

    def shift(value, by):
        return lax.ppermute(value, "seq", [(d, (d + by) % count) for d in range(count)])

    def inner_part(g, *after):
        return call(
            functools.partial(inner_kernel, g),
            shape((tokens, group_lanes)),
            in_specs=[in_vmem] * 6 + [anywhere] * len(after),
        )(x, b, c, cum, row, d_row, *after)

    def ask_part(*after):
        blocks = (moving[2, 1], got[2, 1], got[3, 1]) if ride else (all_asked,)
        return call(
            functools.partial(ask_kernel, ride),
            (shape((rows, lanes)), shape((rows, heads)), shape((rows, names), BF16)),
            in_specs=[in_vmem] * (6 + len(blocks)) + [anywhere] * len(after),
        )(x, b, cum, row, len_row, owner_row, *blocks, *after)

    def token(*after, flops=1):
        return call(
            token_kernel, shape((8, 128)), flops=flops, in_specs=[anywhere] * len(after)
        )(*after)

    def fresh_part(*after):
        return call(
            functools.partial(fresh_kernel, tokens),
            (shape((count, STEPS, lanes)),) * 2 + (shape((count, STEPS, 128)),),
            in_specs=[in_vmem] * 8 + [anywhere] * len(after),
        )(x_dec, b_dec, asked_here, dt_dec, a_row, d_row, len_row, owner_row, *after)

    def outer_part(parts, carry, before, *after):
        part = parts[-1]
        out = shape((tokens, sum(widths[k] for k in part)), BF16)
        operands = [c, cum, carry, *[got[count - 1, k] for k in part], *inner, *before]
        return call(
            functools.partial(outer_kernel, parts, bounds, count),
            (pltpu.HBM((tokens, lanes), BF16), shape((8, 128))) if before else out,
            in_specs=[in_vmem] * len(operands) + [anywhere] * len(after),
            out_specs=(in_hbm, in_vmem) if before else in_vmem,
            scratch_shapes=[out, pltpu.SemaphoreType.DMA((chunks + groups,))] if before else [],
        )(*operands, *after)

    def read_part(ops, final, *after):
        arrived = [got[count - 1, k] for k in range(chunks)] if final else []
        operands = [local, gain, asked, carry, *arrived]
        return call(
            functools.partial(read_kernel, count, bounds, ops, final),
            (shape((STEPS, lanes), BF16),) * len(ops) + (shape((STEPS, lanes)),) * final,
            in_specs=[in_vmem] * len(operands) + [anywhere] * len(after),
        )(*operands, *after)

    got = {(1, 0): forward(sent[0], 1, 0)}
    inner = [inner_part(0)]
    *parts, sent[1] = state_part(inner[-1])
    decay, total = parts[:chunks], total + parts[chunks:]
    got[1, 1] = forward(sent[1], 1, 1)
    order = sorted((k + hop, hop, k) for hop in range(1, count - 1) for k in range(chunks))
    moving = {}
    carry = tie = None
    for _, hop, k in order:
        more = hop == 1 and k + 2 < chunks
        operands = [got[hop, k], total[k], decay[k]]
        operands += [] if carry is None else [carry]
        operands += total[k + 2 : k + 3] * more + [sent[0], got[1, 0]] * (ride and (hop, k) == (1, 1))
        after = []
        if (hop, k) == (1, 1):
            for g in range(1, groups):
                inner.append(inner_part(g, tie))
            keep, fresh, held = fresh_part(inner[-1])
            after = [keep]
        if hop == count - 2 and k > 1:
            after = [token(got[hop + 1, k - 2], tie, flops=GAP_COSTS[k - 2])]
        tie, carry, *following = call(
            functools.partial(pass_kernel, hop, bounds[k], more),
            (sent_shape(hop + 1, k), shape((N, lanes), BF16))
            + ((sent_shape(1, k + 2),) if more else ()),
            flops=PASS_COSTS.get((hop, k), 1),
            in_specs=[in_vmem] * len(operands) + [anywhere] * len(after),
            input_output_aliases={} if carry is None else {3: 1},
        )(*operands, *after)
        moving[hop + 1, k] = tie
        got[hop + 1, k] = forward(tie, hop + 1, k)
        if more:
            got[1, k + 2] = forward(following[0], 1, k + 2)

    early, late = tuple(range(chunks // 2)), tuple(range(chunks // 2, chunks))
    four = count == 4
    local, gain, asked = ask_part(tie)
    back, ops = [], [(0, 1), (0, 2), (1, 2)] if four else []
    if four:
        reading = read_part(ops, False)
        for couple, value in zip(ops, reading):
            back.append(swap(value, couple))
    ends = [(0, 3), (1, 3), (2, 3)] if four else list(range(1, count))
    before = reading[0] if four else asked
    order_token = token(got[count - 1, chunks - 2], before, flops=TOKEN_COST)
    *reading, mine = read_part(ends, True, order_token)
    last_back = [
        swap(value, op) if four else shift(value, -op) for op, value in zip(ends, reading)
    ]
    outer = outer_part((early,), carry, [], mine)
    prefill, end_token = outer_part((early, late), carry, [outer])
    end_token = token(end_token, *back, flops=TOKEN_COST)
    ops, back = ops + ends, back + last_back

    decoded = call(
        functools.partial(finish_kernel, ops),
        jax.ShapeDtypeStruct((count, STEPS, lanes), BF16),
        in_specs=[in_vmem] * (4 + len(ops)) + [anywhere],
    )(keep, fresh, held, *back, mine, end_token)
    return (prefill, decoded[None])


def solution(mesh):
    placed = (
        P(("grp", "seq"), "tp"),
        P(("grp", "seq"), "tp"),
        P(("grp", "seq"), "tp"),
        P(("grp", "seq"), "tp"),
        P("tp"),
        P("tp"),
        P("grp"),
        P("grp"),
        P(("grp", "seq"), None, None, "tp"),
        P(("grp", "seq"), None, None, "tp"),
        P(("grp", "seq"), None, None, "tp"),
        P(("grp", "seq"), None, None, "tp"),
    )
    return jax.shard_map(
        shards,
        mesh=mesh,
        in_specs=placed,
        out_specs=(P(("grp", "seq"), "tp"), P(("grp", "seq"), None, None, "tp")),
        check_vma=False,
    )
```

```python
import functools
import math

import jax
import jax.numpy as jnp
from jax import lax
from jax.experimental import pallas as pl
from jax.experimental.pallas import tpu as pltpu
from jax.sharding import PartitionSpec as P

H = 128
P_SIZE = 64
N = 128
G = 8
SPAN = 128
STEPS = 4
LOG2E = math.log2(math.e)
F32 = jnp.float32
BF16 = jnp.bfloat16
CHUNKS = 4
TOKEN_COST = 10**8
PASS_COSTS = {
    (1, 0): 8 * 10**8,
    (2, 0): 5 * 10**8,
    (1, 2): 8 * 10**8,
    (2, 1): 4 * 10**8,
    (2, 2): 4 * 10**8,
}
GAP_COSTS = (8 * 10**8, 5 * 10**8)
VMEM_LIMIT = 32 * 1024 * 1024


def softplus(value):
    small = jnp.exp(-jnp.abs(value))
    series = small * (1.0 - small * (0.5 - small * (1.0 / 3.0 - small * 0.25)))
    return jnp.maximum(value, 0.0) + jnp.where(small < 0.02, series, jnp.log(1.0 + small))


def dot(left, right, left_dim=1, right_dim=0):
    return lax.dot_general(
        left, right, (((left_dim,), (right_dim,)), ((), ())), preferred_element_type=F32
    )


def split(value, pieces):
    result = []
    for _ in range(pieces):
        piece = value.astype(BF16)
        result.append(piece)
        value = value - piece.astype(F32)
    return result


def exact_dot(ones, value, pieces=3, left_dim=1):
    return sum(dot(ones, piece, left_dim) for piece in split(value, pieces))


def spread_matrix(heads, first, width):
    lane = lax.broadcasted_iota(jnp.int32, (heads, width), 1) + first
    head = lax.broadcasted_iota(jnp.int32, (heads, width), 0)
    return jnp.where(lane // P_SIZE == head, 1.0, 0.0).astype(BF16)


def over_lanes(value, first, width, pieces=2):
    return exact_dot_right(value, spread_matrix(value.shape[1], first, width), pieces)


def exact_dot_right(value, ones, pieces):
    return sum(dot(piece, ones) for piece in split(value, pieces))


def shape(dims, dtype=F32):
    return pltpu.VMEM(dims, dtype)


def pinned(value, space=pltpu.VMEM):
    return pltpu.with_memory_space_constraint(value, space)


def call(kernel, out_shape, flops=1, **options):
    name = getattr(kernel, "func", kernel).__name__
    return pl.pallas_call(
        kernel,
        name=name,
        out_shape=out_shape,
        compiler_params=pltpu.CompilerParams(vmem_limit_bytes=VMEM_LIMIT),
        cost_estimate=pl.CostEstimate(flops=flops, bytes_accessed=1, transcendentals=0),
        **options,
    )


def triangle(keep):
    row = lax.broadcasted_iota(jnp.int32, (SPAN, SPAN), 0)
    column = lax.broadcasted_iota(jnp.int32, (SPAN, SPAN), 1)
    return jnp.where(keep(row, column), 1.0, 0.0).astype(BF16)


def by_group(first, last):
    group_lanes = H // G * P_SIZE
    pieces = []
    while first < last:
        g = first // group_lanes
        end = min(last, (g + 1) * group_lanes)
        pieces.append((g, first, end))
        first = end
    return pieces


def chunk_total(first, x_ref, turned, weight, total_ref):
    for g, start, end in by_group(first, first + total_ref.shape[1]):
        scaled = x_ref[:, start:end].astype(F32) * over_lanes(weight, start, end - start)
        total_ref[:, start - first : end - first] = dot(turned[g], scaled.astype(BF16))


def first_kernel(kept, *refs):
    hbm, refs = refs[: kept + 1], refs[kept + 1 :]
    here, refs = refs[:kept], refs[kept:]
    cum_ref, row_ref, weight_ref, whole_ref = refs[:4]
    total_ref, sent_ref, dt_ref, sems = refs[4:]
    x_ref, b_ref, a_ref = here[:3]
    heads, tokens = dt_ref.shape
    spans = tokens // SPAN
    width = total_ref.shape[1]
    dt_copy = pltpu.make_async_copy(hbm[kept], dt_ref, sems.at[0])
    copies = [pltpu.make_async_copy(hbm[i], here[i], sems.at[i]) for i in range(1, kept)]
    x_copies = [
        pltpu.make_async_copy(hbm[0].at[:, lanes], x_ref.at[:, lanes], sems.at[kept + i])
        for i, lanes in enumerate((slice(0, width), slice(width, x_ref.shape[1])))
    ]
    for copy in [dt_copy, copies[1], copies[0], *x_copies, *copies[2:]]:
        copy.start()
    upper = triangle(lambda s, t: s <= t)
    eye = lax.broadcasted_iota(jnp.int32, (heads, heads), 0) == lax.broadcasted_iota(
        jnp.int32, (heads, heads), 1
    )
    dt_copy.wait()
    copies[1].wait()
    a_column = jnp.sum(jnp.where(eye, a_ref[...], 0.0), axis=1, keepdims=True)
    step = softplus(dt_ref[...].astype(F32))
    rate = step * (jnp.exp(a_column) * -LOG2E)
    cums = [exact_dot_right(rate[:, i * SPAN : (i + 1) * SPAN], upper, 3) for i in range(spans)]
    ends = [cum[:, SPAN - 1 : SPAN] for cum in cums]
    after = jnp.zeros_like(ends[0])
    weights = [None] * spans
    for i in reversed(range(spans)):
        after = after + ends[i]
        weights[i] = jnp.exp2(after - cums[i]) * step[:, i * SPAN : (i + 1) * SPAN]
    weight = jnp.concatenate(weights, axis=1).T
    whole = jnp.sum(jnp.where(eye, jnp.exp2(after), 0.0), axis=0, keepdims=True)
    weight_ref[...] = weight
    whole_ref[...] = whole
    copies[0].wait()
    turned = b_ref[:, :N].astype(F32).T.astype(BF16)
    x_copies[0].wait()
    chunk_total(0, x_ref, [turned], weight, total_ref)
    sent_ref[:N] = total_ref[...].astype(BF16)
    cum = jnp.concatenate(cums, axis=1)
    cum_ref[...] = cum
    row_ref[...] = jnp.log2(step) - cum
    x_copies[1].wait()
    for copy in copies[2:]:
        copy.wait()
    if sent_ref.shape[0] > N:
        own = flat(here[3]).astype(BF16)
        sent_ref[N:, : own.shape[1]] = own


def state_kernel(bounds, x_ref, b_ref, weight_ref, whole_ref, *rest):
    chunks = len(bounds) - 1
    results = rest[-2 * chunks :]
    decay_refs, total_refs, sent_ref = results[:chunks], results[chunks:-1], results[-1]
    turned = [
        b_ref[:, g * N : (g + 1) * N].astype(F32).T.astype(BF16)
        for g in range(b_ref.shape[1] // N)
    ]
    for k in range(chunks):
        first = bounds[k]
        decay_refs[k][...] = over_lanes(whole_ref[...], first, bounds[k + 1] - first, 3)
        if k:
            chunk_total(first, x_ref, turned, weight_ref[...], total_refs[k - 1])
    sent_ref[...] = total_refs[0][...].astype(BF16)


def flat(ref):
    return jnp.concatenate([ref[i].astype(F32) for i in range(ref.shape[0])], axis=0)


def token_kernel(*refs):
    refs[-1][...] = jnp.zeros_like(refs[-1])


def pass_kernel(hop, first, more, got_ref, total_ref, decay_ref, *rest):
    moving_ref, carry_ref = rest[len(rest) - 2 - more : len(rest) - more]
    me = lax.axis_index("seq")
    groups = carry_ref.shape[1] // (H // G * P_SIZE)
    if hop == 1 and first == 0:
        following_ref = rest[0]
        carry_ref[...] = jnp.zeros_like(carry_ref)
    else:
        following_ref = rest[1]
    got = got_ref[:N]
    moving_ref[:N] = (total_ref[...] + decay_ref[...] * got.astype(F32)).astype(BF16)
    if moving_ref.shape[0] > N and hop == 1:
        names = groups * N
        own, other = [ref[N:, :names].astype(F32) for ref in rest[1 + more : 3 + more]]
        even = lax.rem(me, 2) == 0
        moving_ref[N:, :names] = jnp.where(even, own, other).astype(BF16)
        moving_ref[N:, names : 2 * names] = jnp.where(even, other, own).astype(BF16)
    elif moving_ref.shape[0] > N:
        moving_ref[N:] = got_ref[N:]

    @pl.when(me == hop)
    def _():
        carry_ref[:, first : first + got.shape[1]] = got

    if more:
        rest[-1][...] = following_ref[...].astype(BF16)


def pair_halves(x_part):
    first_half = lax.broadcasted_iota(jnp.int32, (1, 2 * P_SIZE), 1) < P_SIZE
    zero = jnp.zeros_like(x_part)
    return jnp.where(first_half, x_part, zero), jnp.where(first_half, zero, x_part)


def span_starts(cum, spans):
    ends = [cum[(i + 1) * SPAN - 1 : (i + 1) * SPAN, :] for i in range(spans)]
    starts = [jnp.zeros_like(ends[0])]
    for i in range(spans):
        starts.append(starts[i] + ends[i])
    return ends, starts


def inner_kernel(g, x_ref, b_ref, c_ref, cum_ref, row_ref, d_ref, *rest):
    inner_ref = rest[-1]
    heads, tokens = cum_ref.shape
    spans = tokens // SPAN
    per_group = H // G
    names = slice(g * N, (g + 1) * N)
    t_index = lax.broadcasted_iota(jnp.int32, (SPAN, SPAN), 0)
    s_index = lax.broadcasted_iota(jnp.int32, (SPAN, SPAN), 1)
    causal = t_index >= s_index
    rows = row_ref[...]
    cum = cum_ref[...].T
    ends, _ = span_starts(cum, spans)
    first_half = lax.broadcasted_iota(jnp.int32, (1, 2 * P_SIZE), 1) < P_SIZE
    scores = dot(c_ref[:, names], b_ref[:, names], 1, 1)
    for pair in range(per_group // 2):
        h0 = g * per_group + 2 * pair
        lanes = slice(h0 * P_SIZE, (h0 + 2) * P_SIZE)
        here = slice(2 * pair * P_SIZE, (2 * pair + 2) * P_SIZE)
        x_part = x_ref[:, lanes]
        halves = pair_halves(x_part)
        weights = [[None, None] for _ in range(spans)]
        for e in range(2):
            h = h0 + e
            row = rows[h : h + 1, :]
            for i in range(spans):
                column = jnp.broadcast_to(cum[i * SPAN : (i + 1) * SPAN, h : h + 1], (SPAN, SPAN))
                parts = []
                for j in range(i + 1):
                    shift = row[:, j * SPAN : (j + 1) * SPAN]
                    for m in range(j, i):
                        shift = shift + ends[m][:, h : h + 1]
                    score = scores[i * SPAN : (i + 1) * SPAN, j * SPAN : (j + 1) * SPAN]
                    part = score * jnp.exp2(column + shift)
                    if i == j:
                        part = jnp.where(causal, part, 0.0)
                    parts.append(part.astype(BF16))
                weights[i][e] = jnp.concatenate(parts, axis=1) if i else parts[0]
        skip = jnp.where(first_half, d_ref[:, h0 : h0 + 1], d_ref[:, h0 + 1 : h0 + 2])
        for i in range(spans):
            reach = (i + 1) * SPAN
            left = jnp.concatenate(weights[i], axis=1)
            right = jnp.concatenate([half[:reach] for half in halves], axis=0)
            mine = slice(i * SPAN, (i + 1) * SPAN)
            inner_ref[mine, here] = dot(left, right) + skip * x_part[mine].astype(F32)


def ask_kernel(ride, x_ref, b_ref, cum_ref, row_ref, len_ref, owner_ref, *rest):
    local_ref, gain_ref, asked_ref = rest[-3:]
    heads, tokens = cum_ref.shape
    spans = tokens // SPAN
    asks = local_ref.shape[0]
    per_group = H // G
    groups = heads // per_group
    me = lax.axis_index("seq")
    if ride:
        near, middle, far = [ref[N:].astype(F32) for ref in rest[:3]]
        far = jnp.where((me == 1) | (me == 2), middle, far)
        halves = (jnp.where(me < 2, near, far), jnp.where(me < 2, far, near))
        names = b_ref.shape[1]
        blocks = [half[:, i * names : (i + 1) * names] for half in halves for i in range(2)]
        blocks = jnp.concatenate(blocks, axis=0).astype(BF16)
        row = lax.broadcasted_iota(jnp.int32, (asks, blocks.shape[0]), 0)
        column = lax.broadcasted_iota(jnp.int32, (asks, blocks.shape[0]), 1)
        wanted = row // STEPS * asks + me * STEPS + row % STEPS
        asked = dot(jnp.where(column == wanted, 1.0, 0.0).astype(BF16), blocks).astype(BF16)
    else:
        blocks = [rest[0][r, me].astype(F32) for r in range(asks // STEPS)]
        asked = jnp.concatenate(blocks, axis=0).astype(BF16)
    asked_ref[...] = asked
    block = lax.broadcasted_iota(jnp.int32, (asks, 1), 0) // STEPS
    spot = len_ref[...] - 1 - me * tokens
    mine = (owner_ref[...] == block) & (spot >= 0) & (spot < tokens)
    spot = jnp.sum(jnp.where(mine, spot, 0).astype(F32), axis=1, keepdims=True).astype(jnp.int32)
    position = lax.broadcasted_iota(jnp.int32, (asks, tokens), 1)
    picked = jnp.where(position == spot, 1.0, 0.0).astype(BF16)
    upto = position <= spot
    rows = row_ref[...]
    cum = cum_ref[...].T
    ends, starts = span_starts(cum, spans)
    near_ask = exact_dot(picked, cum)
    ask_start = starts[0]
    for i in range(1, spans):
        ask_start = jnp.where(spot >= i * SPAN, starts[i], ask_start)
    gain_ref[...] = jnp.exp2(near_ask + ask_start)
    columns = []
    for j in range(spans):
        column = near_ask
        for i in range(j + 1, spans):
            column = jnp.where(spot // SPAN == i, near_ask + sum(ends[j + 1 : i], ends[j]), column)
        columns.append(column)
    for g in range(groups):
        names = slice(g * N, (g + 1) * N)
        scores = jnp.where(upto, dot(asked[:, names], b_ref[:, names], 1, 1), 0.0)
        for pair in range(per_group // 2):
            h0 = g * per_group + 2 * pair
            lanes = slice(h0 * P_SIZE, (h0 + 2) * P_SIZE)
            parts = []
            for h in (h0, h0 + 1):
                for j in range(spans):
                    span = slice(j * SPAN, (j + 1) * SPAN)
                    part = scores[:, span] * jnp.exp2(columns[j][:, h : h + 1] + rows[h : h + 1, span])
                    parts.append(jnp.where(upto[:, span], part, 0.0).astype(BF16))
            right = jnp.concatenate(pair_halves(x_ref[:, lanes]), axis=0)
            local_ref[:, lanes] = dot(jnp.concatenate(parts, axis=1), right)


def read_kernel(count, bounds, ops, final, local_ref, gain_ref, asked_ref, carry_ref, *rest):
    chunks = len(bounds) - 1
    got_refs, rest = rest[: chunks * final], rest[chunks * final :]
    read_refs = rest[-(len(ops) + final) :]
    me = lax.axis_index("seq")
    for k in range(chunks):
        first = bounds[k]
        width = bounds[k + 1] - first
        here = slice(first, first + width)
        state = carry_ref[:, here]
        if final:
            state = jnp.where(me == count - 1, got_refs[k][:N], state)
        carried = [
            dot(asked_ref[:, g * N : (g + 1) * N], state[:, start - first : end - first])
            for g, start, end in by_group(first, first + width)
        ]
        carried = jnp.concatenate(carried, axis=1)
        reading = local_ref[:, here] + over_lanes(gain_ref[...], first, width) * carried
        parts = [reading[r * STEPS : (r + 1) * STEPS] for r in range(count)]
        for op, read_ref in zip(ops, read_refs):
            if isinstance(op, tuple):
                part = jnp.where(me == op[0], parts[op[1]], parts[op[0]])
            else:
                part = parts[0]
                for r in range(1, count):
                    part = jnp.where(lax.rem(me + count - op, count) == r, parts[r], part)
            read_ref[:, here] = part.astype(read_ref.dtype)
        if final:
            own = parts[0]
            for r in range(1, count):
                own = jnp.where(me == r, parts[r], own)
            read_refs[-1][:, here] = own


def outer_kernel(parts, bounds, count, c_ref, cum_ref, carry_ref, *rest):
    part = parts[-1]
    final = True
    got_refs = rest[: len(part)]
    inner_refs = rest[len(part) : len(part) + cum_ref.shape[0] // (H // G)]
    out_hbm, token_ref, out_ref, sems = rest[-4:]
    token_ref[...] = jnp.zeros_like(token_ref)
    heads, tokens = cum_ref.shape
    spans = tokens // SPAN
    group_lanes = H // G * P_SIZE
    copies = []

    def send(source, first, width):
        lanes = slice(first, first + width)
        copies.append(pltpu.make_async_copy(source, out_hbm.at[:, lanes], sems.at[len(copies)]))
        copies[-1].start()

    last = lax.axis_index("seq") == count - 1
    start = jnp.zeros((heads, 1), F32)
    gains = []
    for i in range(spans):
        cum = cum_ref[:, i * SPAN : (i + 1) * SPAN]
        gains.append(jnp.exp2(cum + start))
        start = start + cum[:, SPAN - 1 : SPAN]
    gain = jnp.concatenate(gains, axis=1).T
    for i, k in enumerate(part):
        first = bounds[k]
        state = jnp.where(last, got_refs[i][:N], carry_ref[:, first : bounds[k + 1]])
        for g, start, end in by_group(first, bounds[k + 1]):
            carried = dot(c_ref[:, g * N : (g + 1) * N], state[:, start - first : end - first])
            inner = inner_refs[g][:, start - g * group_lanes : end - g * group_lanes]
            here = slice(start - bounds[part[0]], end - bounds[part[0]])
            out = inner + over_lanes(gain, start, end - start) * carried
            out_ref[:, here] = out.astype(BF16)
            if final:
                send(out_ref.at[:, here], start, end - start)
    for copy in copies:
        copy.wait()


def fresh_kernel(tokens, x_ref, b_ref, c_ref, dt_ref, a_ref, d_ref, len_ref, owner_ref, *rest):
    keep_ref, fresh_ref, held_ref = rest[-3:]
    count, _, heads = dt_ref.shape
    rows = count * STEPS
    place = lax.broadcasted_iota(jnp.int32, (rows, 1), 0) // STEPS * tokens
    spot = len_ref[...] - 1 - place
    mine = (owner_ref[...] == lax.axis_index("seq")) & (spot >= 0) & (spot < tokens)
    held = jnp.sum(jnp.where(mine, 1.0, 0.0), axis=1, keepdims=True)
    held = jnp.broadcast_to(held, (rows, held_ref.shape[2]))
    per_group = H // G
    groups = heads // per_group
    width = x_ref.shape[2]
    turn = lax.broadcasted_iota(jnp.int32, (rows, 1), 0) % STEPS
    step = softplus(flat(dt_ref))
    rate = step * (jnp.exp(a_ref[...]) * -LOG2E)

    def earlier(value, gap):
        if not gap:
            return value
        moved = jnp.concatenate([jnp.zeros_like(value[:gap]), value[:-gap]], axis=0)
        return jnp.where(turn >= gap, moved, 0.0)

    running = sum(earlier(rate, gap) for gap in range(STEPS))
    keep = over_lanes(jnp.exp2(running), 0, width)
    x_values = flat(x_ref)
    b_values = flat(b_ref)
    c_values = flat(c_ref)
    head = lax.broadcasted_iota(jnp.int32, (rows, heads), 1)
    fresh = over_lanes(d_ref[...], 0, width, 3) * x_values
    since = jnp.zeros_like(rate)
    for gap in range(STEPS):
        if gap:
            since = since + earlier(rate, gap - 1)
        products = c_values * earlier(b_values, gap)
        pair = jnp.zeros((rows, heads), F32)
        for g in range(groups):
            score = jnp.sum(products[:, g * N : (g + 1) * N], axis=1, keepdims=True)
            pair = jnp.where(head // per_group == g, score, pair)
        factor = jnp.where(turn >= gap, jnp.exp2(since) * earlier(step, gap) * pair, 0.0)
        fresh = fresh + over_lanes(factor, 0, width) * earlier(x_values, gap)
    for i in range(rows // STEPS):
        keep_ref[i] = keep[i * STEPS : (i + 1) * STEPS]
        fresh_ref[i] = fresh[i * STEPS : (i + 1) * STEPS]
        held_ref[i] = held[i * STEPS : (i + 1) * STEPS]


def finish_kernel(ops, keep_ref, fresh_ref, held_ref, *rest):
    count = keep_ref.shape[0]
    back_refs, own_ref, out_ref = rest[: len(ops)], rest[len(ops)], rest[-1]
    me = lax.axis_index("seq")

    def finish(source, reading):
        value = reading * keep_ref[source] + fresh_ref[source]
        held = held_ref[source][:, :1] > 0.0
        out_ref[source] = jnp.where(held, value, 0.0).astype(BF16)

    if isinstance(ops[0], tuple):
        for source in range(count):
            reading = own_ref[...]
            for (one, other), back_ref in zip(ops, back_refs):
                if source in (one, other):
                    owner = one + other - source
                    reading = jnp.where(me == owner, back_ref[...].astype(F32), reading)
            finish(source, reading)
    else:
        finish(me, own_ref[...])
        for r, back_ref in zip(ops, back_refs):
            finish(lax.rem(me + r, count), back_ref[...].astype(F32))


def shards(
    ssm_input, bmat, cmat, dt_raw, a_log, d_skip, prompt_len, owner, dec_x, dec_b, dec_c, dec_dt
):
    count = lax.axis_size("seq")
    tensor = lax.axis_size("tp")
    tokens, heads = dt_raw.shape
    groups = heads // (H // G)
    names = groups * N
    lanes = heads * P_SIZE
    group_lanes = lanes // groups
    rows = count * STEPS
    chunks = CHUNKS if count <= 4 else groups
    bounds = tuple(lanes * k // chunks for k in range(chunks + 1))
    if chunks > groups:
        bounds = bounds[:1] + (bounds[1] - 128, bounds[2] - 128) + bounds[3:]
    widths = [bounds[k + 1] - bounds[k] for k in range(chunks)]
    anywhere = pl.BlockSpec(memory_space=pl.ANY)
    in_hbm = pl.BlockSpec(memory_space=pltpu.HBM)
    in_vmem = pl.BlockSpec(memory_space=pltpu.VMEM)
    ride = count == 4 and widths[0] >= names and widths[1] >= 2 * names

    def sent_shape(hop, k):
        return shape((N + rows * (ride and (hop, k) in ((1, 0), (2, 1), (3, 1))), widths[k]), BF16)

    inputs = [
        ssm_input,
        bmat,
        a_log.reshape(1, heads),
        dec_c[0],
        cmat,
        d_skip.reshape(1, heads),
        prompt_len.reshape(1, -1),
        owner.reshape(1, -1),
        dec_x[0],
        dec_b[0],
        dec_dt[0],
    ]
    total_shapes = tuple(shape((N, width)) for width in widths)
    decay_shapes = tuple(shape((1, width)) for width in widths)
    results = call(
        functools.partial(first_kernel, len(inputs)),
        tuple(shape(value.shape, value.dtype) for value in inputs)
        + (
            shape((heads, tokens)),
            shape((heads, tokens)),
            shape((tokens, heads)),
            shape((1, heads)),
            total_shapes[0],
            sent_shape(1, 0),
        ),
        in_specs=[in_hbm] * (len(inputs) + 1),
        scratch_shapes=[
            pltpu.VMEM((heads, tokens), BF16),
            pltpu.SemaphoreType.DMA((len(inputs) + 2,)),
        ],
    )(*[pinned(value, pltpu.HBM) for value in inputs + [dt_raw.T]])
    x, b, a_row, asked_here, c, d_row, len_row, owner_row, x_dec, b_dec, dt_dec = results[:11]
    cum, row, weight, whole = results[11:15]
    total, sent = [results[15]], {0: results[16]}
    all_asked = None if ride else lax.all_gather(dec_c[0], "seq")

    def state_part(tie):
        return call(
            functools.partial(state_kernel, bounds),
            decay_shapes + total_shapes[1:] + (sent_shape(1, 1),),
            in_specs=[in_vmem] * 4 + [anywhere],
        )(x, b, weight, whole, tie)

    def swap(value, *couples):
        partner = {}
        for one, other in couples:
            partner.update({one: other, other: one})
        pairs = []
        for d in range(count):
            for t in range(tensor):
                there = partner[d] * tensor + t if d in partner else d * tensor + (t ^ 1)
                pairs.append((d * tensor + t, there))
        return lax.ppermute(value, ("seq", "tp"), pairs)

    def forward(value, hop, k):
        with jax.named_scope(f"hop{hop}_chunk{k}"):
            rides = ride and (hop, k) in ((1, 0), (3, 1))
            return swap(value, *([(0, 1), (2, 3)] if rides else [(hop - 1, hop)]))

    def shift(value, by):
        return lax.ppermute(value, "seq", [(d, (d + by) % count) for d in range(count)])

    def inner_part(g, *after):
        return call(
            functools.partial(inner_kernel, g),
            shape((tokens, group_lanes)),
            in_specs=[in_vmem] * 6 + [anywhere] * len(after),
        )(x, b, c, cum, row, d_row, *after)

    def ask_part(*after):
        blocks = (moving[2, 1], got[2, 1], got[3, 1]) if ride else (all_asked,)
        return call(
            functools.partial(ask_kernel, ride),
            (shape((rows, lanes)), shape((rows, heads)), shape((rows, names), BF16)),
            in_specs=[in_vmem] * (6 + len(blocks)) + [anywhere] * len(after),
        )(x, b, cum, row, len_row, owner_row, *blocks, *after)

    def token(*after, flops=1):
        return call(
            token_kernel, shape((8, 128)), flops=flops, in_specs=[anywhere] * len(after)
        )(*after)

    def fresh_part(*after):
        return call(
            functools.partial(fresh_kernel, tokens),
            (shape((count, STEPS, lanes)),) * 2 + (shape((count, STEPS, 128)),),
            in_specs=[in_vmem] * 8 + [anywhere] * len(after),
        )(x_dec, b_dec, asked_here, dt_dec, a_row, d_row, len_row, owner_row, *after)

    def outer_part(parts, carry, before, *after):
        part = parts[-1]
        out = shape((tokens, sum(widths[k] for k in part)), BF16)
        operands = [c, cum, carry, *[got[count - 1, k] for k in part], *inner, *before]
        return call(
            functools.partial(outer_kernel, parts, bounds, count),
            (pltpu.HBM((tokens, lanes), BF16), shape((8, 128))),
            in_specs=[in_vmem] * len(operands) + [anywhere] * len(after),
            out_specs=(in_hbm, in_vmem),
            scratch_shapes=[out, pltpu.SemaphoreType.DMA((chunks + groups,))],
        )(*operands, *after)

    def read_part(ops, final, *after):
        arrived = [got[count - 1, k] for k in range(chunks)] if final else []
        operands = [local, gain, asked, carry, *arrived]
        return call(
            functools.partial(read_kernel, count, bounds, ops, final),
            (shape((STEPS, lanes), BF16),) * len(ops) + (shape((STEPS, lanes)),) * final,
            in_specs=[in_vmem] * len(operands) + [anywhere] * len(after),
        )(*operands, *after)

    got = {(1, 0): forward(sent[0], 1, 0)}
    inner = [inner_part(0)]
    *parts, sent[1] = state_part(inner[-1])
    decay, total = parts[:chunks], total + parts[chunks:]
    got[1, 1] = forward(sent[1], 1, 1)
    order = sorted((k + hop, hop, k) for hop in range(1, count - 1) for k in range(chunks))
    moving = {}
    carry = tie = None
    for _, hop, k in order:
        more = hop == 1 and k + 2 < chunks
        operands = [got[hop, k], total[k], decay[k]]
        operands += [] if carry is None else [carry]
        operands += total[k + 2 : k + 3] * more + [sent[0], got[1, 0]] * (ride and (hop, k) == (1, 1))
        after = []
        if (hop, k) == (1, 1):
            for g in range(1, groups):
                inner.append(inner_part(g, tie))
            keep, fresh, held = fresh_part(inner[-1])
            after = [keep]
        if hop == count - 2 and k > 1:
            after = [token(got[hop + 1, k - 2], tie, flops=GAP_COSTS[k - 2])]
        tie, carry, *following = call(
            functools.partial(pass_kernel, hop, bounds[k], more),
            (sent_shape(hop + 1, k), shape((N, lanes), BF16))
            + ((sent_shape(1, k + 2),) if more else ()),
            flops=PASS_COSTS.get((hop, k), 1),
            in_specs=[in_vmem] * len(operands) + [anywhere] * len(after),
            input_output_aliases={} if carry is None else {3: 1},
        )(*operands, *after)
        moving[hop + 1, k] = tie
        got[hop + 1, k] = forward(tie, hop + 1, k)
        if more:
            got[1, k + 2] = forward(following[0], 1, k + 2)

    early, late = tuple(range(chunks // 2)), tuple(range(chunks // 2, chunks))
    four = count == 4
    local, gain, asked = ask_part(tie)
    back, ops = [], [(0, 1), (0, 2), (1, 2)] if four else []
    if four:
        reading = read_part(ops, False)
        for couple, value in zip(ops, reading):
            back.append(swap(value, couple))
    ends = [(0, 3), (1, 3), (2, 3)] if four else list(range(1, count))
    before = reading[0] if four else asked
    order_token = token(got[count - 1, chunks - 2], before, flops=TOKEN_COST)
    *reading, mine = read_part(ends, True, order_token)
    last_back = [
        swap(value, op) if four else shift(value, -op) for op, value in zip(ends, reading)
    ]
    prefill, end_token = outer_part((early + late,), carry, [], mine)
    end_token = token(end_token, *back, flops=TOKEN_COST)
    ops, back = ops + ends, back + last_back

    decoded = call(
        functools.partial(finish_kernel, ops),
        jax.ShapeDtypeStruct((count, STEPS, lanes), BF16),
        in_specs=[in_vmem] * (4 + len(ops)) + [anywhere],
    )(keep, fresh, held, *back, mine, end_token)
    return (prefill, decoded[None])


def solution(mesh):
    placed = (
        P(("grp", "seq"), "tp"),
        P(("grp", "seq"), "tp"),
        P(("grp", "seq"), "tp"),
        P(("grp", "seq"), "tp"),
        P("tp"),
        P("tp"),
        P("grp"),
        P("grp"),
        P(("grp", "seq"), None, None, "tp"),
        P(("grp", "seq"), None, None, "tp"),
        P(("grp", "seq"), None, None, "tp"),
        P(("grp", "seq"), None, None, "tp"),
    )
    return jax.shard_map(
        shards,
        mesh=mesh,
        in_specs=placed,
        out_specs=(P(("grp", "seq"), "tp"), P(("grp", "seq"), None, None, "tp")),
        check_vma=False,
    )
```
